32 devices in a mesh: seq: 4 (over y, x), mp: 8 (over z, core).
Axes of the slice: x: 2, y: 2, z: 4, core: 2. Of those that a mesh axis runs over, the one named last changes fastest.
Arguments:
- layer_in: bfloat16 [8, 1536, 1024], P('mp', 'seq'), may hold values from -6 to 6
- out_grad: bfloat16 [8, 1536, 1024], P('mp', 'seq'), may hold values from -6 to 6
- seq_lengths: int32 [8, 3], P('mp'), may hold values from 1 to 1248, 1536 in all within a row
- dealing: int32 [8, 1536], P('mp'), may hold values from 0 to 1535, each once within a row
- log_decay: float32 [8, 1536, 8], P('mp', 'seq'), may hold values from -0.75 to 0
- w_qkv: bfloat16 [1024, 4096], P(('seq', 'mp')), may hold values from -0.1875 to 0.1875
- w_out_gate: bfloat16 [1024, 2048], P(('seq', 'mp')), may hold values from -0.1875 to 0.1875
- w_beta: bfloat16 [1024, 8], P(('seq', 'mp')), may hold values from -0.1875 to 0.1875
- conv_w: bfloat16 [4096, 4], P(('seq', 'mp')), may hold values from -3 to 3
- gain_in: bfloat16 [1024], P(('seq', 'mp')), may hold values from 0.099609375 to 1.8984375
- gain_o: bfloat16 [256], P(('seq', 'mp')), may hold values from 0.099609375 to 1.8984375
- w_out: bfloat16 [2048, 1024], P(None, ('seq', 'mp')), may hold values from -0.125 to 0.125
- gain_mid: bfloat16 [1024], P(('seq', 'mp')), may hold values from 0.099609375 to 1.8984375
- w_gate_up: bfloat16 [1024, 5632], P(('seq', 'mp')), may hold values from -0.1875 to 0.1875
- w_down: bfloat16 [2816, 1024], P(None, ('seq', 'mp')), may hold values from -0.109375 to 0.109375
Outputs:
- mixed_out: bfloat16 [8, 1536, 1024], P('mp', 'seq')
- input_grad: bfloat16 [8, 1536, 1024], P('mp', 'seq')
- grad_w_qkv: float32 [1024, 4096], P(('seq', 'mp'))
- grad_w_out_gate: float32 [1024, 2048], P(('seq', 'mp'))
- grad_w_beta: float32 [1024, 8], P(('seq', 'mp'))
- grad_conv_w: float32 [4096, 4], P(('seq', 'mp'))
- grad_gain_in: float32 [1024], P(('seq', 'mp'))
- grad_gain_o: float32 [256], P(('seq', 'mp'))
- grad_w_out: float32 [2048, 1024], P(None, ('seq', 'mp'))
- grad_gain_mid: float32 [1024], P(('seq', 'mp'))
- grad_w_gate_up: float32 [1024, 5632], P(('seq', 'mp'))
- grad_w_down: float32 [2816, 1024], P(None, ('seq', 'mp'))
The draws below stay inside these ranges and needn't reach their ends.
Inputs may be any that keep to these rules, and one draw needn't show every extreme that they name: `seq_lengths`: each row holds the lengths of 3 sequences packed in this order, summing to 1536; the largest is exactly 1248. `dealing`: each row is a permutation of the group's rows.
All inputs are finite; a program needn't handle non-finite values.
Results may differ from the reference program's by a relative error of at most 0.012.
The reference program's roundings to bfloat16 on the way (of `normed`, `proj`, `attn_out`, `mid_normed` and `hidden`) count: a program that leaves them out, or rounds other values in their place, can miss the bound.
Values may be sent and summed in bfloat16 or wider, within the bound.
No kernel may reach another device: no remote copies, remote signals or barrier semaphores. Data moves between devices by JAX's collectives and lax.ppermute only.
A program may use at most 320 MiB of HBM per device.

```python
import math
import jax
import jax.numpy as jnp
import numpy as np
from jax import lax

D = 1024
HEAD_COUNT = 8
DK = 128
DV = 256
FF = 2816
KW = 4
STRETCH = 64
NSEQ = 3
GROUP_TOKENS = 1536
SEQUENCE_GROUPS = 8
LONGEST = 1248
CONV_CH = 4096


def draw_log_decay(key, part):
    key = jax.random.fold_in(key, 7)
    key_rows = jax.random.split(key, 6)
    fast_share = 0.5
    fast = jax.random.uniform(key_rows[0], (SEQUENCE_GROUPS, 1, HEAD_COUNT)) < fast_share
    fast_rate = jnp.exp(jax.random.uniform(key_rows[1], (SEQUENCE_GROUPS, 1, HEAD_COUNT), minval=math.log(1.0 / 50.0), maxval=math.log(1.0 / 30.0)))
    slow_rate = jnp.exp(jax.random.uniform(key_rows[2], (SEQUENCE_GROUPS, 1, HEAD_COUNT), minval=math.log(0.1 / GROUP_TOKENS), maxval=math.log(0.5 / GROUP_TOKENS)))
    decay_speed = jnp.where(fast, fast_rate, slow_rate)
    random_noise = jax.random.uniform(key_rows[3], (SEQUENCE_GROUPS, GROUP_TOKENS, HEAD_COUNT), minval=0.5, maxval=1.5)
    sudden_spike = jax.random.uniform(key_rows[4], (SEQUENCE_GROUPS, GROUP_TOKENS, HEAD_COUNT)) < 4.0 / GROUP_TOKENS
    retained_state = jax.random.uniform(key_rows[5], (SEQUENCE_GROUPS, GROUP_TOKENS, HEAD_COUNT), minval=0.5, maxval=0.8)
    return (-decay_speed * random_noise + jnp.where(sudden_spike, jnp.log(retained_state), 0.0)).astype(jnp.float32)


def shard_levels(stream_key, extent, pieces, smallest, largest):
    factor_of, own = 1.0, jax.random.fold_in(stream_key, 6)
    for dim, shards_of in pieces:
        steps = jnp.exp(jax.random.uniform(jax.random.fold_in(own, dim), (shards_of,), jnp.float32, smallest / len(pieces), largest / len(pieces)))
        factor_of = factor_of * jnp.repeat(steps, extent[dim] // shards_of).reshape([-1 if axis == dim else 1 for axis in range(len(extent))])
    return factor_of


def length_profile(amount, total, reach, skew):
    portions = [(1 << 20) // math.isqrt(rank ** skew) + 1 for rank in range(2, amount + 1)]
    spare, counts = total - reach - (amount - 1), [1] * (amount - 1)
    while spare > 0:
        free = [i for i in range(amount - 1) if counts[i] < reach]
        pool, budget = sum([portions[i] for i in free]), spare
        for i in free:
            more = min(reach - counts[i], max(1, budget * portions[i] // pool), spare)
            counts[i] = counts[i] + more
            spare = spare - more
    return np.array([reach] + counts)


def uneven_parts(own_key, count, total, most, slope):
    if count == 2:
        one = jax.random.randint(own_key, (), max(1, total - most), min(most, total - 1) + 1)
        return jnp.stack([one, total - one])
    sizes = jnp.asarray(length_profile(count, total, most, slope), jnp.int32)
    pairs = (count - 1) // 2
    source_of, taker = sizes[1:1 + 2 * pairs:2], sizes[2:2 + 2 * pairs:2]
    slack = jnp.minimum(source_of - 1, most - taker)
    passed = jax.random.randint(jax.random.fold_in(own_key, 1), (pairs,), 0, 1 << 20) % (slack + 1)
    sizes = sizes.at[1:1 + 2 * pairs:2].set(source_of - passed).at[2:2 + 2 * pairs:2].set(taker + passed)
    return sizes[jax.random.permutation(jax.random.fold_in(own_key, 2), count)]


def noise(key, shape, width, limit, pieces=(), kind=jnp.bfloat16):
    values = width * jax.random.normal(key, shape, jnp.float32)
    if pieces:
        values = values * shard_levels(key, shape, pieces, -0.22, 0.18)
    return jnp.clip(values, -limit, limit).astype(kind)


def setup_inputs(seed: int = 0) -> dict:
    key_list = jax.random.split(jax.random.key(seed), 16)
    layer_in = noise(key_list[0], (SEQUENCE_GROUPS, GROUP_TOKENS, D), 1.0, 6.0, ((0, 8), (1, 4)))
    out_grad = noise(key_list[1], (SEQUENCE_GROUPS, GROUP_TOKENS, D), 1.0, 6.0, ((0, 8), (1, 4)))
    seq_lengths = jax.vmap(lambda own: uneven_parts(own, NSEQ, GROUP_TOKENS, LONGEST, 2))(jax.random.split(key_list[2], SEQUENCE_GROUPS)).reshape((SEQUENCE_GROUPS, NSEQ)).astype(jnp.int32)
    dealing = jax.vmap(lambda own: jax.random.permutation(own, GROUP_TOKENS))(jax.random.split(key_list[3], SEQUENCE_GROUPS)).reshape((SEQUENCE_GROUPS, GROUP_TOKENS)).astype(jnp.int32)
    log_decay = draw_log_decay(jax.random.fold_in(key_list[15], 71), 0)
    w_qkv = noise(key_list[5], (D, CONV_CH), D ** -0.5, 0.1875, ((0, 32),))
    w_out_gate = noise(key_list[6], (D, HEAD_COUNT * DV), D ** -0.5, 0.1875, ((0, 32),))
    w_beta = noise(key_list[7], (D, HEAD_COUNT), D ** -0.5, 0.1875, ((0, 32),))
    conv_w = noise(key_list[8], (CONV_CH, KW), KW ** -0.5, 3.0, ((0, 32),))
    gain_in = jnp.clip(1.0 + 0.18 * jax.random.normal(key_list[9], (D,), jnp.float32), 0.099609375, 1.8984375).astype(jnp.bfloat16)
    gain_o = jnp.clip(1.0 + 0.18 * jax.random.normal(key_list[10], (DV,), jnp.float32), 0.099609375, 1.8984375).astype(jnp.bfloat16)
    w_out = noise(key_list[11], (HEAD_COUNT * DV, D), (HEAD_COUNT * DV) ** -0.5, 0.125, ((1, 32),))
    gain_mid = jnp.clip(1.0 + 0.18 * jax.random.normal(key_list[12], (D,), jnp.float32), 0.099609375, 1.8984375).astype(jnp.bfloat16)
    w_gate_up = noise(key_list[13], (D, 2 * FF), D ** -0.5, 0.1875, ((0, 32),))
    w_down = noise(key_list[14], (FF, D), FF ** -0.5, 0.109375, ((1, 32),))
    return dict(layer_in=layer_in, out_grad=out_grad, seq_lengths=seq_lengths, dealing=dealing, log_decay=log_decay, w_qkv=w_qkv, w_out_gate=w_out_gate, w_beta=w_beta, conv_w=conv_w, gain_in=gain_in, gain_o=gain_o, w_out=w_out, gain_mid=gain_mid, w_gate_up=w_gate_up, w_down=w_down)


EXACT_PRECISION = lax.Precision.HIGHEST

@jax.custom_vjp
def low(v):
    return lax.optimization_barrier(v.astype(jnp.bfloat16)).astype(jnp.float32)

@jax.custom_vjp
def low_back(v):
    return v

def low_keep(v):
    return (low(v), None)

def low_pass(retained_state, grad):
    return (grad,)

def back_keep(v):
    return (v, None)

def back_low(retained_state, grad):
    return (low(grad),)
low.defvjp(low_keep, low_pass)
low_back.defvjp(back_keep, back_low)

def dense(left, right):
    return jnp.dot(left, right, precision=EXACT_PRECISION, preferred_element_type=jnp.float32)

def batch_mm(left, right):
    return jnp.einsum('hij,hjk->hik', left, right, precision=EXACT_PRECISION)

def rms_scale(values, gain):
    return values * lax.rsqrt(lax.optimization_barrier(jnp.mean(values * values, axis=-1, keepdims=True)) + 1e-05) * gain

def segments(positions, lengths):
    ends = jnp.cumsum(lengths)
    counted = lax.optimization_barrier(jnp.sum((positions[:, None] >= ends[None, :]).astype(jnp.int32), axis=1))
    return jnp.where(positions < 0, -1, counted).astype(jnp.int32)

def conv_mix(extended, seg_ext, conv_f):
    taps = conv_f.shape[1]
    count = extended.shape[0] - taps + 1
    seg_now = seg_ext[taps - 1:]
    total = jnp.zeros((count, extended.shape[1]), jnp.float32)
    for offset in range(taps):
        keeper = (seg_ext[offset:offset + count] == seg_now).astype(jnp.float32)
        total = total + extended[offset:offset + count] * keeper[:, None] * conv_f[:, offset][None, :]
    return jax.nn.silu(total)

def split_feats(feats, heads, key_dim, val_dim):
    count = feats.shape[0]
    queries = feats[:, :heads * key_dim].reshape(count, heads, key_dim)
    raw_keys = feats[:, heads * key_dim:2 * heads * key_dim].reshape(count, heads, key_dim)
    values = feats[:, 2 * heads * key_dim:].reshape(count, heads, val_dim)
    keys_n = raw_keys * lax.rsqrt(lax.optimization_barrier(jnp.sum(raw_keys * raw_keys, axis=-1, keepdims=True)) + 1e-06)
    return (queries, keys_n, values)

def unit_inverse(lower_mat):
    size = lower_mat.shape[-1]
    ident = jnp.eye(size, dtype=jnp.float32)
    result = ident - lower_mat
    power = lower_mat
    span = 2
    while span < size:
        power = batch_mm(power, power)
        result = batch_mm(result, ident + power)
        span = span * 2
    return result

def stretch_terms(queries, keys_n, values, beta, decay, seg, seg_prev):
    size = queries.shape[1]
    cum = jnp.cumsum(decay, axis=1)
    index = jnp.arange(size)
    strict = index[:, None] > index[None, :]
    within = (index[:, None] >= index[None, :]) & (seg[:, None] == seg[None, :])
    keep_in = (seg == seg_prev).astype(jnp.float32)
    keep_out = (seg == seg[size - 1]).astype(jnp.float32)
    diff = cum[:, :, None] - cum[:, None, :]
    dmat = jnp.where(within[None], jnp.exp(jnp.where(within[None], diff, 0.0)), 0.0)
    inner = jnp.einsum('hik,hjk->hij', keys_n, keys_n, precision=EXACT_PRECISION)
    lower_mat = jnp.where(strict[None], beta[:, :, None] * inner * dmat, 0.0)
    inverse = unit_inverse(lower_mat)
    elog = jnp.exp(cum) * keep_in[None, :]
    umat = batch_mm(inverse, beta[:, :, None] * values)
    wmat = batch_mm(inverse, (beta * elog)[:, :, None] * keys_n)
    qkd = jnp.einsum('hik,hjk->hij', queries, keys_n, precision=EXACT_PRECISION) * dmat
    gmat = queries * elog[:, :, None] - batch_mm(qkd, wmat)
    o_local = batch_mm(qkd, umat)
    last = cum[:, size - 1]
    key_boundary = keys_n * (jnp.exp(last[:, None] - cum) * keep_out[None, :])[:, :, None]
    carried_factor = jnp.exp(last) * keep_in[size - 1]
    return (o_local, gmat, wmat, umat, key_boundary, carried_factor)

def to_blocks(array, stretches):
    return array.reshape((stretches, STRETCH) + array.shape[1:]).swapaxes(1, 2)

def recurrence(queries, keys_n, values, beta, decay, seg, seg_prev):
    count, heads = (queries.shape[0], queries.shape[1])
    stretches = count // STRETCH
    items = (to_blocks(queries, stretches), to_blocks(keys_n, stretches), to_blocks(values, stretches), to_blocks(beta, stretches), to_blocks(decay, stretches), seg.reshape(stretches, STRETCH), seg_prev)

    def advance(memory_state, item):
        o_local, gmat, wmat, umat, key_boundary, carried_factor = stretch_terms(*item)
        output = o_local + batch_mm(gmat, memory_state)
        shifted_state = umat - batch_mm(wmat, memory_state)
        newest_state = carried_factor[:, None, None] * memory_state + jnp.einsum('izg,izu->igu', key_boundary, shifted_state, precision=EXACT_PRECISION)
        return (newest_state, output)
    state_zero = jnp.zeros((heads, queries.shape[2], values.shape[2]), jnp.float32)
    final, output_rows = lax.scan(jax.checkpoint(advance), state_zero, items)
    return output_rows.transpose(0, 2, 1, 3).reshape(count, heads, values.shape[2])

def gated_norm(output_rows, gate_logit, gain):
    scaled = output_rows * lax.rsqrt(lax.optimization_barrier(jnp.mean(output_rows * output_rows, axis=-1, keepdims=True)) + 1e-05) * gain
    return scaled * jax.nn.silu(gate_logit)

def layer(packed, seg, seg_ext, seg_prev, decay, weights):
    w_qkv, w_out_gate, w_beta, conv_w, gain_in, gain_o, w_out, gain_mid, w_gate_up, w_down = weights
    count = packed.shape[0]
    normed = low(rms_scale(packed, gain_in))
    proj = low_back(low(dense(normed, w_qkv)))
    extended = jnp.concatenate([jnp.zeros((KW - 1, proj.shape[1]), jnp.float32), proj], 0)
    feats = conv_mix(extended, seg_ext, conv_w)
    queries, keys_n, values = split_feats(feats, HEAD_COUNT, DK, DV)
    beta = jax.nn.sigmoid(low_back(dense(normed, w_beta)))
    gate_logit = low_back(dense(normed, w_out_gate)).reshape(count, HEAD_COUNT, DV)
    output_rows = recurrence(queries, keys_n, values, beta, decay, seg, seg_prev)
    attn_out = low(gated_norm(output_rows, gate_logit, gain_o).reshape(count, HEAD_COUNT * DV))
    residual = packed + low_back(dense(attn_out, w_out))
    mid_normed = low(rms_scale(residual, gain_mid))
    gate_up = low_back(dense(mid_normed, w_gate_up))
    hidden = low(jax.nn.silu(gate_up[:, :FF]) * gate_up[:, FF:])
    return residual + low_back(dense(hidden, w_down))

def reference(layer_in, out_grad, seq_lengths, dealing, log_decay, w_qkv, w_out_gate, w_beta, conv_w, gain_in, gain_o, w_out, gain_mid, w_gate_up, w_down):
    weights = tuple((w.astype(jnp.float32) for w in (w_qkv, w_out_gate, w_beta, conv_w, gain_in, gain_o, w_out, gain_mid, w_gate_up, w_down)))
    positions = jnp.arange(GROUP_TOKENS, dtype=jnp.int32)
    ext_positions = jnp.arange(GROUP_TOKENS + KW - 1, dtype=jnp.int32) - (KW - 1)
    stretch_prev = jnp.arange(GROUP_TOKENS // STRETCH, dtype=jnp.int32) * STRETCH - 1

    def one_group(totals, items):
        rows_in, rows_grad, lengths, order, decay = items
        packed = rows_in.astype(jnp.float32)[order]
        packed_grad = rows_grad.astype(jnp.float32)[order]
        seg = segments(positions, lengths)
        seg_ext = segments(ext_positions, lengths)
        seg_prev = segments(stretch_prev, lengths)

        def forward(values_in, weight_set):
            return layer(values_in, seg, seg_ext, seg_prev, decay, weight_set)
        layer_out, pull = jax.vjp(forward, packed, weights)
        in_grad, weight_grads = pull(packed_grad)
        inverse = jnp.zeros((GROUP_TOKENS,), jnp.int32).at[order].set(positions)
        totals = jax.tree.map(lambda a, b: a + b, totals, weight_grads)
        return (totals, (layer_out[inverse].astype(jnp.bfloat16), in_grad[inverse].astype(jnp.bfloat16)))
    start = tuple((jnp.zeros(w.shape, jnp.float32) for w in weights))
    totals, (outs, in_grads) = lax.scan(one_group, start, (layer_in, out_grad, seq_lengths, dealing, log_decay))
    return (outs, in_grads, totals[0], totals[1], totals[2], totals[3], totals[4], totals[5], totals[6], totals[7], totals[8], totals[9])
```

```python
import functools

import jax
import jax.numpy as jnp
from jax import lax
from jax.experimental import pallas as pl
from jax.experimental.pallas import tpu as pltpu
from jax.sharding import PartitionSpec as P

HEAD_COUNT = 8
DK = 128
DV = 256
BLOCK = 128
PER_STEP = 2
F32 = jnp.float32
BF16 = jnp.bfloat16


def mm(left, right):
    return jnp.dot(left.astype(BF16), right.astype(BF16), preferred_element_type=F32)


def mm_nt(left, right):
    return lax.dot_general(
        left.astype(BF16),
        right.astype(BF16),
        (((1,), (1,)), ((), ())),
        preferred_element_type=F32,
    )


def mm_tn(left, right):
    return lax.dot_general(
        left.astype(BF16),
        right.astype(BF16),
        (((0,), (0,)), ((), ())),
        preferred_element_type=F32,
    )


def masks():
    rows = lax.broadcasted_iota(jnp.int32, (BLOCK, BLOCK), 0)
    cols = lax.broadcasted_iota(jnp.int32, (BLOCK, BLOCK), 1)
    return rows, cols


def unit_inverses(mats, rows, cols):
    ident = (rows == cols).astype(F32)
    near = (rows // 16) == (cols // 16)
    power = [jnp.where(near, a, 0.0) for a in mats]
    result = [ident - p for p in power]
    span = 2
    while span < 16:
        power = [mm(p, p) for p in power]
        result = [t + mm(t, p) for t, p in zip(result, power)]
        span *= 2
    size = 16
    while size < BLOCK:
        off = ((rows // (2 * size)) == (cols // (2 * size))) & ((rows // size) != (cols // size))
        reach = [mm(jnp.where(off, a, 0.0), t) for a, t in zip(mats, result)]
        result = [t - mm(t, x) for t, x in zip(result, reach)]
        size *= 2
    return result


def convolve(ext_ref, conv_ref, col_ref, start, first, width):
    cols = pl.ds(first, width)
    total = ext_ref[pl.ds(16 + start, BLOCK), cols] * conv_ref[3:4, cols]
    for tap in range(3):
        keep = col_ref[pl.ds(start, BLOCK), tap : tap + 1]
        total += ext_ref[pl.ds(13 + tap + start, BLOCK), cols] * keep * conv_ref[tap : tap + 1, cols]
    return total


def column(col_ref, start, index):
    return col_ref[pl.ds(start, BLOCK), index : index + 1]


def strength(logit_ref, start, head, heads):
    return jax.nn.sigmoid(column(logit_ref, start, head))


def exact_nt(left, right):
    left_high, right_high = left.astype(BF16), right.astype(BF16)
    left_low = left - left_high.astype(F32)
    right_low = right - right_high.astype(F32)
    return mm_nt(left_high, right_high) + (mm_nt(left_high, right_low) + mm_nt(left_low, right_high))


def decay_matrix(col_ref, row_ref, start, head, heads, rows, cols):
    cum_i = column(col_ref, start, 5 + head)
    cum_j = row_ref[head : head + 1, pl.ds(start, BLOCK)]
    seg_i = column(col_ref, start, 3)
    seg_j = row_ref[heads : heads + 1, pl.ds(start, BLOCK)]
    within = (rows >= cols) & (seg_i == seg_j)
    return jnp.where(within, jnp.exp(jnp.where(within, cum_i - cum_j, 0.0)), 0.0)


def silu(values):
    return values * jax.nn.sigmoid(values)


def forward_kernel(
    heads, edge_ref, proj_ref, conv_ref, col_ref, row_ref, logit_ref,
    o_ref, s_ref, n_ref, t_ref, w_ref, p_ref, ext_ref, state_ref,
):
    steps = proj_ref.shape[0] // BLOCK

    @pl.when(pl.program_id(0) == 0)
    def _():
        state_ref[...] = jnp.zeros_like(state_ref)

    ext_ref[:16, :] = edge_ref[...].astype(F32)
    ext_ref[16:, :] = proj_ref[...].astype(F32)
    rows, cols = masks()
    strict = rows > cols
    units = [(g, h) for g in range(steps) for h in range(heads)]
    queries, keys, values, mats, decays, betas = {}, {}, {}, [], {}, {}
    for g, h in units:
        start = g * BLOCK
        taken = functools.partial(convolve, ext_ref, conv_ref, col_ref, start)
        queries[g, h] = silu(taken(h * DK, DK))
        raw = silu(taken((heads + h) * DK, DK))
        keys[g, h] = raw * lax.rsqrt(jnp.sum(raw * raw, axis=1, keepdims=True) + 1e-06)
        values[g, h] = silu(taken(2 * heads * DK + h * DV, DV))
        decays[g, h] = decay_matrix(col_ref, row_ref, start, h, heads, rows, cols)
        betas[g, h] = strength(logit_ref, start, h, heads)
        beta = betas[g, h]
        inner = mm_nt(keys[g, h], keys[g, h])
        mats.append(jnp.where(strict, beta * inner * decays[g, h], 0.0))
    inverses = unit_inverses(mats, rows, cols)
    umats, wmats, pmats, boundary, reads = {}, {}, {}, {}, {}
    for (g, h), inverse in zip(units, inverses):
        start = g * BLOCK
        beta = betas[g, h]
        elog = column(col_ref, start, 5 + heads + h)
        flog = column(col_ref, start, 5 + 2 * heads + h)
        inverse = inverse.astype(BF16)
        t_ref[g, h] = inverse
        umats[g, h] = mm(inverse, beta * values[g, h])
        wmats[g, h] = mm(inverse, (beta * elog) * keys[g, h]).astype(BF16)
        w_ref[g, h] = wmats[g, h]
        pmats[g, h] = (exact_nt(queries[g, h], keys[g, h]) * decays[g, h]).astype(BF16)
        p_ref[g, h] = pmats[g, h]
        boundary[g, h] = (keys[g, h] * flog).T.astype(BF16)
        reads[g, h] = (queries[g, h] * elog).astype(BF16)
    for g in range(steps):
        start = g * BLOCK
        for h in range(heads):
            state = state_ref[h]
            low = state.astype(BF16)
            s_ref[g, h] = low
            news = (umats[g, h] - mm(wmats[g, h], low)).astype(BF16)
            n_ref[g, h] = news
            carried = col_ref[pl.ds(start + BLOCK - 1, 1), 5 + heads + h : 6 + heads + h]
            state_ref[h] = carried * state + mm(boundary[g, h], news)
            output = mm(reads[g, h], low) + mm(pmats[g, h], news)
            o_ref[pl.ds(start, BLOCK), h * DV : (h + 1) * DV] = output.astype(BF16)


def backward_kernel(
    heads, edge_ref, proj_ref, conv_ref, col_ref, row_ref, logit_ref,
    s_ref, n_ref, t_ref, w_ref, p_ref, do_ref, *refs,
):
    grad_ref, gconv_ref, ext_ref, shift_ref, dstate_ref, head_ref = refs[-6:]
    count = proj_ref.shape[0]
    steps = count // BLOCK
    channels = proj_ref.shape[1]

    @pl.when(pl.program_id(0) == 0)
    def _():
        dstate_ref[...] = jnp.zeros_like(dstate_ref)
        head_ref[...] = jnp.zeros_like(head_ref)
        gconv_ref[...] = jnp.zeros_like(gconv_ref)

    ext_ref[:16, :] = edge_ref[...].astype(F32)
    ext_ref[16:, :] = proj_ref[...].astype(F32)
    for tap in range(3):
        shift_ref[tap, count : count + 8, :] = head_ref[tap]
    rows, cols = masks()
    strict = rows > cols
    units = [(g, h) for g in reversed(range(steps)) for h in range(heads)]
    queries, keys, pre, reads, first, gains = {}, {}, {}, {}, {}, {}
    for g, h in units:
        start = g * BLOCK
        taken = functools.partial(convolve, ext_ref, conv_ref, col_ref, start)
        elog = column(col_ref, start, 5 + heads + h)
        out_grad = do_ref[pl.ds(start, BLOCK), h * DV : (h + 1) * DV]
        queries[g, h] = silu(taken(h * DK, DK))
        raw = silu(taken((heads + h) * DK, DK))
        scale = lax.rsqrt(jnp.sum(raw * raw, axis=1, keepdims=True) + 1e-06)
        keys[g, h] = (raw * scale, scale)
        first[g, h] = mm_tn(p_ref[g, h], out_grad)
        gains[g, h] = mm_tn(queries[g, h] * elog, out_grad)
    news_grads, state_grads = {}, {}
    for g in reversed(range(steps)):
        start = g * BLOCK
        for h in range(heads):
            flog = column(col_ref, start, 5 + 2 * heads + h)
            dstate = dstate_ref[h]
            low = dstate.astype(BF16)
            state_grads[g, h] = low
            news_grad = (first[g, h] + mm(keys[g, h][0] * flog, low)).astype(BF16)
            news_grads[g, h] = news_grad
            carried = col_ref[pl.ds(start + BLOCK - 1, 1), 5 + heads + h : 6 + heads + h]
            dstate_ref[h] = gains[g, h] + carried * dstate - mm_tn(w_ref[g, h], news_grad)
    lane = lax.broadcasted_iota(jnp.int32, (BLOCK, 128), 1)

    def through_conv(g, first_col, width, grad):
        start = g * BLOCK
        cols_ = pl.ds(first_col, width)
        value = convolve(ext_ref, conv_ref, col_ref, start, first_col, width)
        gate = jax.nn.sigmoid(value)
        grad = grad * (gate * (1.0 + value * (1.0 - gate)))
        shift_ref[3, pl.ds(start, BLOCK), cols_] = grad * conv_ref[3:4, cols_]
        sums = []
        for tap in range(3):
            kept = grad * col_ref[pl.ds(start, BLOCK), tap : tap + 1]
            shift_ref[tap, pl.ds(start, BLOCK), cols_] = kept * conv_ref[tap : tap + 1, cols_]
            sums.append(
                jnp.sum(kept * ext_ref[pl.ds(13 + tap + start, BLOCK), cols_], axis=0, keepdims=True)
            )
        sums.append(
            jnp.sum(grad * ext_ref[pl.ds(16 + start, BLOCK), cols_], axis=0, keepdims=True)
        )
        for tap in range(4):
            gconv_ref[tap : tap + 1, cols_] += sums[tap]

    logit_grads = {}
    for g, h in units:
        start = g * BLOCK
        beta = strength(logit_ref, start, h, heads)
        elog = column(col_ref, start, 5 + heads + h)
        flog = column(col_ref, start, 5 + 2 * heads + h)
        key, scale = keys[g, h]
        query = queries[g, h]
        out_grad = do_ref[pl.ds(start, BLOCK), h * DV : (h + 1) * DV]
        decay = decay_matrix(col_ref, row_ref, start, h, heads, rows, cols)
        key_low = key.astype(BF16)
        inner = mm_nt(key_low, key_low) * decay
        news, state, dstate = n_ref[g, h], s_ref[g, h], state_grads[g, h]
        rhs_grad = mm_tn(t_ref[g, h], news_grads[g, h])
        rhs_low = rhs_grad.astype(BF16)
        within = (mm_nt(out_grad, news) * decay).astype(BF16)
        mat_grad = jnp.where(strict, -mm_nt(rhs_low, news), 0.0)
        pair = (mat_grad * beta * decay).astype(BF16)
        back = mm_nt(rhs_low, state)
        q_grad = mm(within, key_low) + elog * mm_nt(out_grad, state)
        k_grad = (
            mm_tn(within, query)
            + mm(pair, key_low)
            + mm_tn(pair, key_low)
            + flog * mm_nt(news, dstate)
            - (beta * elog) * back
        )
        value = silu(convolve(ext_ref, conv_ref, col_ref, start, 2 * heads * DK + h * DV, DV))
        beta_grad = (
            jnp.sum(mat_grad * inner - elog * (key * back), axis=1, keepdims=True)
            + jnp.sum(rhs_grad * value, axis=1, keepdims=True)
        )
        logit_grads[g, h] = beta_grad * beta * (1.0 - beta)
        raw_grad = scale * (k_grad - key * jnp.sum(k_grad * key, axis=1, keepdims=True))
        through_conv(g, h * DK, DK, q_grad)
        through_conv(g, (heads + h) * DK, DK, raw_grad)
        through_conv(g, 2 * heads * DK + h * DV, DV, beta * rhs_grad)
    for g in range(steps):
        total = jnp.zeros((BLOCK, 128), F32)
        for h in range(heads):
            total = jnp.where(lane == h, logit_grads[g, h], total)
        grad_ref[pl.ds(g * BLOCK, BLOCK), channels:] = total.astype(BF16)
    total = shift_ref[3, :count, :]
    for tap in range(3):
        total += shift_ref[tap, pl.ds(3 - tap, count), :]
    grad_ref[:, :channels] = total.astype(BF16)
    for tap in range(3):
        head_ref[tap] = shift_ref[tap, :8, :]


def saved_shapes(blocks, heads):
    return (
        jax.ShapeDtypeStruct((blocks, heads, DK, DV), BF16),
        jax.ShapeDtypeStruct((blocks, heads, BLOCK, DV), BF16),
        jax.ShapeDtypeStruct((blocks, heads, BLOCK, BLOCK), BF16),
        jax.ShapeDtypeStruct((blocks, heads, BLOCK, DK), BF16),
        jax.ShapeDtypeStruct((blocks, heads, BLOCK, BLOCK), BF16),
    )


def saved_specs(shapes, index):
    return [
        pl.BlockSpec((PER_STEP,) + shape.shape[1:], lambda i: (index(i), 0, 0, 0))
        for shape in shapes
    ]


def common_specs(step, channels, logits, index):
    return [
        pl.BlockSpec((16, channels), lambda i: (jnp.maximum(index(i) * (step // 16) - 1, 0), 0)),
        pl.BlockSpec((step, channels), lambda i: (index(i), 0)),
        pl.BlockSpec((8, channels), lambda i: (0, 0)),
        pl.BlockSpec((step, 128), lambda i: (index(i), 0)),
        pl.BlockSpec((8, step), lambda i: (0, index(i))),
        pl.BlockSpec((step, logits), lambda i: (index(i), 0)),
    ]


VMEM_BYTES = 56 * 1024 * 1024
SMALL_COST = pl.CostEstimate(flops=10**6, bytes_accessed=10**6, transcendentals=0)
ANYWHERE = pl.BlockSpec(memory_space=pl.ANY)
WHOLE = pl.BlockSpec(memory_space=pltpu.VMEM)
SCALAR = pl.BlockSpec(memory_space=pltpu.SMEM)


def params():
    return pltpu.CompilerParams(dimension_semantics=("arbitrary",), vmem_limit_bytes=VMEM_BYTES)


def forward_recurrence(proj, conv, cols, rows, logits, heads):
    count, channels = proj.shape
    step = BLOCK * PER_STEP
    shapes = saved_shapes(count // BLOCK, heads)
    index = lambda i: i
    return pl.pallas_call(
        functools.partial(forward_kernel, heads),
        grid=(count // step,),
        in_specs=common_specs(step, channels, 128, index),
        out_specs=[pl.BlockSpec((step, heads * DV), lambda i: (i, 0))] + saved_specs(shapes, index),
        out_shape=(jax.ShapeDtypeStruct((count, heads * DV), BF16),) + shapes,
        scratch_shapes=[
            pltpu.VMEM((step + 16, channels), F32),
            pltpu.VMEM((heads, DK, DV), F32),
        ],
        compiler_params=params(),
        cost_estimate=SMALL_COST,
        name="recurrence_forward",
    )(proj, proj, conv, cols, rows, logits)


def backward_recurrence(proj, conv, cols, rows, logits, saved, out_grad, heads, tokens):
    count, channels = proj.shape
    step = BLOCK * PER_STEP
    last = count // step - 1
    index = lambda i: last - i
    return pl.pallas_call(
        functools.partial(backward_kernel, heads),
        grid=(count // step,),
        in_specs=common_specs(step, channels, 128, index)
        + saved_specs(saved, index)
        + [pl.BlockSpec((step, heads * DV), lambda i: (index(i), 0))]
        + [ANYWHERE] * len(tokens),
        out_specs=[
            pl.BlockSpec((step, channels + 128), lambda i: (index(i), 0)),
            pl.BlockSpec((8, channels), lambda i: (0, 0)),
        ],
        out_shape=(
            jax.ShapeDtypeStruct((count, channels + 128), BF16),
            jax.ShapeDtypeStruct((8, channels), F32),
        ),
        scratch_shapes=[
            pltpu.VMEM((step + 16, channels), F32),
            pltpu.VMEM((4, step + 8, channels), F32),
            pltpu.VMEM((heads, DK, DV), F32),
            pltpu.VMEM((3, 8, channels), F32),
        ],
        compiler_params=params(),
        cost_estimate=SMALL_COST,
        name="recurrence_backward",
    )(proj, proj, conv, cols, rows, logits, *saved, out_grad, *tokens)


def project_kernel(
    channels, rank_ref, x_ref, gain_ref, w_ref, col_ref, normed_ref, gate_ref, proj_ref, logit_ref, all_ref, rows_ref
):
    step = pl.program_id(0)
    count = x_ref.shape[0]
    chunks = rows_ref.shape[0] // count

    @pl.when(step == 0)
    def _():
        width = w_ref.shape[0] * w_ref.shape[2]
        for k in range(w_ref.shape[1]):
            place = pl.ds(pl.multiple_of((rank_ref[0] ^ k) * width, width), width)
            all_ref[place, :] = w_ref[:, k].reshape(width, w_ref.shape[3])

    @pl.when(step < chunks)
    def _():
        x = x_ref[...].astype(F32)
        scale = lax.rsqrt(jnp.mean(x * x, axis=1, keepdims=True) + 1e-05)
        normed = (x * scale * gain_ref[...]).astype(BF16)
        normed_ref[...] = normed
        total = mm(normed, all_ref[...])
        gate_ref[...] = total[:, channels + 128 :]
        logit = total[:, channels : channels + 128]
        high = logit.astype(BF16)
        place = pl.ds(pl.multiple_of(step * count, count), count)
        rows_ref[place, : channels + 128] = total[:, : channels + 128].astype(BF16)
        rows_ref[place, channels + 128 :] = (logit - high.astype(F32)).astype(BF16)

    @pl.when(step >= chunks)
    def _():
        order = lax.broadcasted_iota(jnp.int32, (proj_ref.shape[0], rows_ref.shape[0]), 1)
        picked = (col_ref[:, 4:5].astype(jnp.int32) == order).astype(F32)
        packed = mm(picked, rows_ref[...])
        proj_ref[...] = packed[:, :channels].astype(BF16)
        logit_ref[...] = packed[:, channels : channels + 128] + packed[:, channels + 128 :]


def project(rank, x_all, gain, weights, cols, count, channels):
    total, width = x_all.shape
    gates = weights.shape[3] - channels - 128
    chunks = total // count
    block = 256
    first = lambda i: jnp.minimum(i, chunks - 1)
    later = lambda i: jnp.maximum(i - chunks, 0)
    return pl.pallas_call(
        functools.partial(project_kernel, channels),
        grid=(chunks + total // block,),
        in_specs=[
            SCALAR,
            pl.BlockSpec((count, width), lambda i: (first(i), 0)),
            pl.BlockSpec((1, width), lambda i: (0, 0)),
            pl.BlockSpec(weights.shape, lambda i: (0, 0, 0, 0)),
            pl.BlockSpec((block, 128), lambda i: (later(i), 0)),
        ],
        out_specs=[
            pl.BlockSpec((count, width), lambda i: (first(i), 0)),
            pl.BlockSpec((count, gates), lambda i: (first(i), 0)),
            pl.BlockSpec((block, channels), lambda i: (later(i), 0)),
            pl.BlockSpec((block, 128), lambda i: (later(i), 0)),
            pl.BlockSpec((width, weights.shape[3]), lambda i: (0, 0)),
        ],
        out_shape=(
            jax.ShapeDtypeStruct((total, width), BF16),
            jax.ShapeDtypeStruct((total, gates), F32),
            jax.ShapeDtypeStruct((total, channels), BF16),
            jax.ShapeDtypeStruct((total, 128), F32),
            jax.ShapeDtypeStruct((width, weights.shape[3]), BF16),
        ),
        scratch_shapes=[pltpu.VMEM((total, channels + 256), BF16)],
        compiler_params=params(),
        cost_estimate=SMALL_COST,
        name="project",
    )(rank, x_all, gain, weights, cols)


def gate_kernel(heads, count, o_ref, place_ref, gate_ref, gain_ref, *refs):
    dealt_ref, chunk_refs = refs[-1 - place_ref.shape[1] // count], refs[-(place_ref.shape[1] // count) :]
    for k, chunk_ref in enumerate(chunk_refs):
        order = lax.broadcasted_iota(jnp.int32, (count, o_ref.shape[0]), 0) + k * count
        picked = (place_ref[...].astype(jnp.int32) == order).astype(F32)
        rows = mm(picked, o_ref[...])
        place = pl.ds(k * count, count)
        dealt_ref[place, :] = rows.astype(BF16)
        for h in range(heads):
            lanes = slice(h * DV, (h + 1) * DV)
            value = rows[:, lanes]
            scale = lax.rsqrt(jnp.mean(value * value, axis=1, keepdims=True) + 1e-05)
            gated = value * scale * gain_ref[...] * silu(gate_ref[place, lanes])
            chunk_ref[:, lanes] = gated.astype(BF16)


def gate_rows(output, place, gate_logit, gain, count, heads, tokens):
    total, cols = output.shape
    chunks = total // count
    whole = pl.BlockSpec(memory_space=pltpu.VMEM)
    outs = pl.pallas_call(
        functools.partial(gate_kernel, heads, count),
        in_specs=[whole] * 4 + [ANYWHERE] * len(tokens),
        out_specs=[whole] * (chunks + 1),
        out_shape=[jax.ShapeDtypeStruct((total, cols), BF16)]
        + [jax.ShapeDtypeStruct((count, cols), BF16)] * chunks,
        compiler_params=pltpu.CompilerParams(vmem_limit_bytes=VMEM_BYTES),
        cost_estimate=SMALL_COST,
        name="gate_rows",
    )(output, place, gate_logit, gain, *tokens)
    return outs[0], outs[1:]


def ungate_kernel(heads, chunks, dealt_ref, col_ref, gate_ref, gain_ref, *refs):
    grad_refs = refs[:chunks]
    gate_grad_ref, o_grad_ref, gain_grad_ref, rows_ref = refs[-4:]
    count = grad_refs[0].shape[0]
    total = dealt_ref.shape[0]
    sums = jnp.zeros((1, DV), F32)
    for k in range(chunks):
        place = pl.ds(k * count, count)
        for h in range(heads):
            lanes = slice(h * DV, (h + 1) * DV)
            value = dealt_ref[place, lanes].astype(F32)
            grad = grad_refs[k][:, lanes].astype(F32)
            logit = gate_ref[place, lanes]
            scale = lax.rsqrt(jnp.mean(value * value, axis=1, keepdims=True) + 1e-05)
            unit = value * scale
            gate = jax.nn.sigmoid(logit)
            slid = logit * gate
            sums += jnp.sum(grad * unit * slid, axis=0, keepdims=True)
            grad = grad * gain_ref[...]
            slope = gate * (1.0 + logit * (1.0 - gate))
            gate_grad_ref[place, lanes] = (grad * unit * slope).astype(BF16)
            grad = grad * slid
            inner = jnp.mean(grad * unit, axis=1, keepdims=True)
            rows_ref[place, lanes] = (scale * (grad - unit * inner)).astype(BF16)
    gain_grad_ref[...] = sums
    for k in range(chunks):
        place = pl.ds(k * count, count)
        order = lax.broadcasted_iota(jnp.int32, (count, total), 1)
        picked = (col_ref[place, 4:5].astype(jnp.int32) == order).astype(F32)
        o_grad_ref[place, :] = mm(picked, rows_ref[...]).astype(BF16)


def ungate_rows(dealt_rows, cols, gate_logit, gain, grads, heads, tokens):
    total, width = dealt_rows.shape
    whole = pl.BlockSpec(memory_space=pltpu.VMEM)
    return pl.pallas_call(
        functools.partial(ungate_kernel, heads, len(grads)),
        in_specs=[whole] * (4 + len(grads)) + [ANYWHERE] * len(tokens),
        out_specs=[whole] * 3,
        out_shape=(
            jax.ShapeDtypeStruct((total, width), BF16),
            jax.ShapeDtypeStruct((total, width), BF16),
            jax.ShapeDtypeStruct((1, DV), F32),
        ),
        scratch_shapes=[pltpu.VMEM((total, width), BF16)],
        compiler_params=pltpu.CompilerParams(vmem_limit_bytes=VMEM_BYTES),
        cost_estimate=SMALL_COST,
        name="ungate_rows",
    )(dealt_rows, cols, gate_logit, gain, *grads, *tokens)


def unpack_kernel(grad_ref, place_ref, normed_ref, w_ref, *refs):
    dealt_ref, g_ref, sums_ref, picked_ref = refs[-4:]
    step = pl.program_id(0)
    total = grad_ref.shape[0]

    @pl.when(step == 0)
    def _():
        part = 256
        for k in range(total // part):
            order = lax.broadcasted_iota(jnp.int32, (part, total), 0) + k * part
            picked = (place_ref[...].astype(jnp.int32) == order).astype(F32)
            picked_ref[k * part : (k + 1) * part, :] = picked.astype(BF16)
        sums_ref[...] = jnp.zeros_like(sums_ref)

    grad = mm(picked_ref[...], grad_ref[...]).astype(BF16)
    dealt_ref[...] = grad
    share = mm_tn(normed_ref[...], grad)
    g_ref[...] = share.astype(BF16)
    sums_ref[...] += jnp.sum(share * w_ref[...].astype(F32), axis=1, keepdims=True)


def unpack(grad, place, normed, weights, tokens):
    total, cols = grad.shape
    width = normed.shape[1]
    tile = 384
    return pl.pallas_call(
        unpack_kernel,
        grid=(cols // tile,),
        in_specs=[
            pl.BlockSpec((total, tile), lambda i: (0, i)),
            pl.BlockSpec(place.shape, lambda i: (0, 0)),
            pl.BlockSpec(normed.shape, lambda i: (0, 0)),
            pl.BlockSpec((width, tile), lambda i: (0, i)),
        ]
        + [ANYWHERE] * len(tokens),
        out_specs=[
            pl.BlockSpec((total, tile), lambda i: (0, i)),
            pl.BlockSpec((width, tile), lambda i: (0, i)),
            pl.BlockSpec((width, 1), lambda i: (0, 0)),
        ],
        out_shape=(
            jax.ShapeDtypeStruct((total, cols), BF16),
            jax.ShapeDtypeStruct((width, cols), BF16),
            jax.ShapeDtypeStruct((width, 1), F32),
        ),
        scratch_shapes=[pltpu.VMEM((total, total), BF16)],
        compiler_params=params(),
        cost_estimate=SMALL_COST,
        name="unpack",
    )(grad, place, normed, weights, *tokens)


def unproject_kernel(wide, grad_ref, gate_ref, w_ref, *refs):
    part_ref, turned_ref = refs[-2:]

    @pl.when(pl.program_id(0) == 0)
    def _():
        turned_ref[...] = w_ref[...].T

    part = mm(grad_ref[...], turned_ref[:wide, :]) + mm(gate_ref[...], turned_ref[wide:, :])
    part_ref[...] = part.astype(BF16)


def unproject(grad, gate_grad, weights, count, tokens):
    total, cols = grad.shape
    width = weights.shape[0]
    return pl.pallas_call(
        functools.partial(unproject_kernel, cols),
        grid=(total // count,),
        in_specs=[
            pl.BlockSpec((count, cols), lambda i: (i, 0)),
            pl.BlockSpec((count, gate_grad.shape[1]), lambda i: (i, 0)),
            pl.BlockSpec(weights.shape, lambda i: (0, 0)),
        ]
        + [ANYWHERE] * len(tokens),
        out_specs=pl.BlockSpec((count, width), lambda i: (i, 0)),
        out_shape=jax.ShapeDtypeStruct((total, width), BF16),
        scratch_shapes=[pltpu.VMEM(weights.shape[::-1], BF16)],
        compiler_params=params(),
        cost_estimate=SMALL_COST,
        name="unproject",
    )(grad, gate_grad, weights, *tokens)


def copy_kernel(value_ref, *refs):
    refs[-1][...] = value_ref[...]


def copied(value, *tokens):
    whole = pl.BlockSpec(memory_space=pltpu.VMEM)
    return pl.pallas_call(
        copy_kernel,
        in_specs=[whole] + [ANYWHERE] * len(tokens),
        out_specs=whole,
        out_shape=jax.ShapeDtypeStruct(value.shape, value.dtype),
        cost_estimate=SMALL_COST,
        name="copied",
    )(value, *tokens)


def weight_grad_kernel(parts, sums, *refs):
    total = mm_tn(refs[0][...], refs[parts][...])
    for k in range(1, parts):
        total += mm_tn(refs[k][...], refs[parts + k][...])
    if sums:
        refs[-2][...] = total.astype(BF16)
        refs[-1][...] = jnp.sum(total * refs[2 * parts][...].astype(F32), axis=1, keepdims=True)
    else:
        refs[-1][...] = total.astype(BF16)


def weight_grad(lefts, rights, tile, *tokens, weights=None):
    parts = len(lefts)
    count, width = lefts[0].shape
    cols = rights[0].shape[1]
    sums = weights is not None
    outs = pl.pallas_call(
        functools.partial(weight_grad_kernel, parts, sums),
        grid=(cols // tile,),
        in_specs=[pl.BlockSpec((count, width), lambda i: (0, 0))] * parts
        + [pl.BlockSpec((count, tile), lambda i: (0, i))] * parts
        + [pl.BlockSpec((width, tile), lambda i: (0, i))] * sums
        + [ANYWHERE] * len(tokens),
        out_specs=[pl.BlockSpec((width, tile), lambda i: (0, i))]
        + [pl.BlockSpec((width, 1), lambda i: (0, 0))] * sums,
        out_shape=[jax.ShapeDtypeStruct((width, cols), BF16)]
        + [jax.ShapeDtypeStruct((width, 1), F32)] * sums,
        compiler_params=params(),
        cost_estimate=pl.CostEstimate(
            flops=4 * parts * count * width * cols, bytes_accessed=10**7, transcendentals=0
        ),
        name="weight_grad",
    )(*lefts, *rights, *([weights] if sums else []), *tokens)
    return outs if sums else outs[0]


def out_project_kernel(rank_ref, x_ref, gain_ref, *refs):
    residual_ref, mid_ref, all_ref = refs[-3:]
    chunks = (len(refs) - 3) // 2
    rank = rank_ref[0]
    for k in range(chunks):
        width = refs[k].shape[1]
        all_ref[:, pl.ds(pl.multiple_of((rank ^ k) * width, width), width)] = refs[k][...]
    for k in range(chunks):
        width = refs[chunks + k].shape[0]
        cols = pl.ds(pl.multiple_of((rank ^ k) * width, width), width)
        residual_ref[:, cols] = x_ref[:, cols].astype(F32) + mm_nt(all_ref[...], refs[chunks + k][...])
    residual = residual_ref[...]
    scale = lax.rsqrt(jnp.mean(residual * residual, axis=1, keepdims=True) + 1e-05)
    mid_ref[...] = (residual * scale * gain_ref[...]).astype(BF16)


def out_project(rank, x, gain, attn, blocks):
    count, width = x.shape
    return pl.pallas_call(
        out_project_kernel,
        in_specs=[SCALAR] + [WHOLE] * (2 + len(attn) + len(blocks)),
        out_specs=[WHOLE] * 2,
        out_shape=(
            jax.ShapeDtypeStruct((count, width), F32),
            jax.ShapeDtypeStruct((count, width), BF16),
        ),
        scratch_shapes=[pltpu.VMEM((count, blocks[0].shape[1]), BF16)],
        compiler_params=pltpu.CompilerParams(vmem_limit_bytes=VMEM_BYTES),
        cost_estimate=SMALL_COST,
        name="out_project",
    )(rank, x, gain, *attn, *blocks)


def mid_back_kernel(chunks, rank_ref, grad_ref, residual_ref, gain_ref, *refs):
    parts, blocks, outs = refs[:chunks], refs[chunks : 2 * chunks], refs[-chunks - 4 :]
    res_grad_ref, low_ref, gain_grad_ref, chunk_refs, all_ref = outs[0], outs[1], outs[2], outs[3:-1], outs[-1]
    rank = rank_ref[0]
    mid_grad = parts[0][...].astype(F32)
    for k in range(1, chunks):
        mid_grad += parts[k][...].astype(F32)
    residual = residual_ref[...]
    scale = lax.rsqrt(jnp.mean(residual * residual, axis=1, keepdims=True) + 1e-05)
    unit = residual * scale
    gain_grad_ref[...] = jnp.sum(mid_grad * unit, axis=0, keepdims=True)
    scaled = mid_grad * gain_ref[...]
    inner = jnp.mean(scaled * unit, axis=1, keepdims=True)
    res_grad = grad_ref[...].astype(F32) + scale * (scaled - unit * inner)
    res_grad_ref[...] = res_grad
    low_ref[...] = res_grad.astype(BF16)
    for k in range(chunks):
        width = blocks[k].shape[0]
        cols = pl.ds(pl.multiple_of((rank ^ k) * width, width), width)
        share = mm(low_ref[:, cols], blocks[k][...])
        if k == 0:
            all_ref[...] = share
        else:
            all_ref[...] += share
    for k in range(chunks):
        width = chunk_refs[k].shape[1]
        cols = pl.ds(pl.multiple_of((rank ^ k) * width, width), width)
        chunk_refs[k][...] = all_ref[:, cols].astype(BF16)


def mid_back(rank, grad, residual, gain, parts, blocks, tokens):
    count, width = residual.shape
    chunks = len(parts)
    wide = blocks[0].shape[1]
    outs = pl.pallas_call(
        functools.partial(mid_back_kernel, chunks),
        in_specs=[SCALAR] + [WHOLE] * (3 + 2 * chunks) + [ANYWHERE] * len(tokens),
        out_specs=[WHOLE] * (3 + chunks),
        out_shape=[
            jax.ShapeDtypeStruct((count, width), F32),
            jax.ShapeDtypeStruct((count, width), BF16),
            jax.ShapeDtypeStruct((1, width), F32),
        ]
        + [jax.ShapeDtypeStruct((count, wide // chunks), BF16)] * chunks,
        scratch_shapes=[pltpu.VMEM((count, wide), F32)],
        compiler_params=pltpu.CompilerParams(vmem_limit_bytes=VMEM_BYTES),
        cost_estimate=SMALL_COST,
        name="mid_back",
    )(rank, grad, residual, gain, *parts, *blocks, *tokens)
    return outs[0], outs[1], outs[2], outs[3:]


def in_back_kernel(chunks, x_ref, res_grad_ref, gain_ref, *refs):
    x = x_ref[...].astype(F32)
    grad = refs[0][...].astype(F32)
    for k in range(1, chunks):
        grad += refs[k][...].astype(F32)
    scale = lax.rsqrt(jnp.mean(x * x, axis=1, keepdims=True) + 1e-05)
    unit = x * scale
    scaled = grad * gain_ref[...]
    inner = jnp.mean(scaled * unit, axis=1, keepdims=True)
    refs[-1][...] = (res_grad_ref[...] + scale * (scaled - unit * inner)).astype(BF16)


def in_back(x, res_grad, gain, parts, tokens):
    return pl.pallas_call(
        functools.partial(in_back_kernel, len(parts)),
        in_specs=[WHOLE] * (3 + len(parts)) + [ANYWHERE] * len(tokens),
        out_specs=WHOLE,
        out_shape=jax.ShapeDtypeStruct(x.shape, BF16),
        compiler_params=pltpu.CompilerParams(vmem_limit_bytes=VMEM_BYTES),
        cost_estimate=SMALL_COST,
        name="in_back",
    )(x, res_grad, gain, *parts, *tokens)


def swapped(value, axis, mask):
    devices = lax.axis_size(axis)
    return lax.ppermute(value, axis, [(i, i ^ mask) for i in range(devices)])


def spread(value):
    return [value] + [swapped(value, "seq", k) for k in range(1, lax.axis_size("seq"))]


def returned(chunks):
    return [chunks[0]] + [swapped(chunks[k], "seq", k) for k in range(1, len(chunks))]


def gathered_rows(pieces):
    own = lax.all_to_all(pieces, "seq", 0, 0, tiled=True)
    return lax.all_gather(own, "mp", axis=0, tiled=False)


def gathered_near(pieces):
    rank = lax.axis_index("seq")
    chunks = [lax.dynamic_index_in_dim(pieces, rank ^ k, 0, keepdims=False) for k in range(pieces.shape[0])]
    return lax.all_gather(jnp.stack(returned(chunks)), "mp", axis=0, tiled=False)


class RowSum:
    def __init__(self, grad):
        self.seq_count, self.mp_count = lax.axis_size("seq"), lax.axis_size("mp")
        self.rank = lax.axis_index("mp")
        self.cols = grad.shape[1]
        self.short = self.mp_count <= 8
        if not self.short:
            parts = grad.astype(F32).reshape(self.seq_count, self.mp_count, -1, self.cols)
            self.grad = parts.transpose(1, 0, 2, 3).reshape(-1, self.cols)
            return
        self.grad = grad.reshape(self.seq_count, self.mp_count // 2, 2, -1, self.cols)
        self.core = self.rank % 2
        sent = lax.dynamic_index_in_dim(self.grad, 1 - self.core, 2, keepdims=False)
        self.got = swapped(sent, "mp", 1)

    def join(self):
        if self.short:
            kept = lax.dynamic_index_in_dim(self.grad, self.core, 2, keepdims=False)
            self.half = (kept.astype(F32) + self.got.astype(F32)).astype(BF16)
            return self.half
        return self.grad

    def send(self, half):
        if not self.short:
            own = lax.psum_scatter(half, "mp", scatter_dimension=0, tiled=True)
            self.own = own.reshape(self.seq_count, -1, self.cols)
            self.parts = [self.own]
            return
        chip = self.rank // 2
        self.parts = [lax.dynamic_index_in_dim(half, chip, 1, keepdims=False)]
        for j in range(1, self.mp_count // 2):
            piece = lax.dynamic_index_in_dim(half, chip ^ j, 1, keepdims=False)
            self.parts.append(swapped(piece, "mp", 2 * j))

    def total(self):
        if self.short:
            self.own = sum(p.astype(F32) for p in self.parts)
        return self.own.astype(BF16)


def dealt(own):
    return lax.all_to_all(own, "seq", 0, 0, tiled=True).astype(F32)


def left_product(left, right):
    return lax.dot_general(
        left, right, (((0,), (0,)), ((), ())), preferred_element_type=jnp.float32
    )


def right_product(left, right):
    return lax.dot_general(
        left, right, (((1,), (1,)), ((), ())), preferred_element_type=jnp.float32
    )


def dot(left, right):
    return jnp.dot(left, right, preferred_element_type=jnp.float32)


def silu_slope(values):
    gate = jax.nn.sigmoid(values)
    return gate * (1.0 + values * (1.0 - gate))


def body(
    layer_in,
    out_grad,
    seq_lengths,
    dealing,
    log_decay,
    w_qkv,
    w_out_gate,
    w_beta,
    conv_w,
    gain_in,
    gain_o,
    w_out,
    gain_mid,
    w_gate_up,
    w_down,
):
    seq_count, mp_count = lax.axis_size("seq"), lax.axis_size("mp")
    rank = lax.axis_index("seq")
    count = layer_in.shape[1]
    rows = w_qkv.shape[0]
    heads = HEAD_COUNT // seq_count
    key_cols, val_cols = heads * DK, heads * DV
    half = w_down.shape[0] // seq_count
    wide = -(-half // 128) * 128
    taps = conv_w.shape[1]
    total = dealing.shape[1]
    devices = seq_count * mp_count

    mix_pieces, ffn_pieces = [], []
    turned_down = w_down.T
    small = jnp.concatenate([conv_w.T.reshape(-1), gain_in, gain_mid, gain_o])
    small_count = small.shape[0]
    spare = 128 - heads
    filler = jnp.concatenate([small, jnp.zeros((rows * spare - small_count,), BF16)])
    filler = filler.reshape(rows, spare)
    wide_filler = jnp.zeros((rows, wide - half), BF16)
    all_keys, ffn = HEAD_COUNT * DK, w_down.shape[0]
    for j in range(seq_count):
        mix_pieces.append(
            jnp.concatenate(
                [
                    w_qkv[:, j * key_cols : (j + 1) * key_cols],
                    w_qkv[:, all_keys + j * key_cols : all_keys + (j + 1) * key_cols],
                    w_qkv[:, 2 * all_keys + j * val_cols : 2 * all_keys + (j + 1) * val_cols],
                    w_beta[:, j * heads : (j + 1) * heads],
                    filler,
                    w_out_gate[:, j * val_cols : (j + 1) * val_cols],
                ],
                1,
            )
        )
        ffn_pieces.append(
            jnp.concatenate(
                [
                    w_gate_up[:, j * half : (j + 1) * half],
                    wide_filler,
                    w_gate_up[:, ffn + j * half : ffn + (j + 1) * half],
                    wide_filler,
                    turned_down[:, j * half : (j + 1) * half],
                    wide_filler,
                ],
                1,
            )
        )
    channels = 2 * key_cols + val_cols
    gathered = gathered_near(jnp.stack(mix_pieces))
    smalls = gathered[:, :, :, channels + heads : channels + 128].transpose(1, 0, 2, 3)
    smalls = jnp.take(smalls, rank ^ jnp.arange(seq_count), axis=0)
    smalls = smalls.reshape(devices, -1)[:, :small_count]
    out_block = lax.all_gather(w_out.T, "mp", axis=0, tiled=True)
    ffn_w = gathered_rows(jnp.stack(ffn_pieces)).transpose(1, 0, 2, 3).reshape(devices * rows, -1)
    w_gu, down_turned = ffn_w[:, : 2 * wide], ffn_w[:, 2 * wide :]

    own_taps = conv_w.shape[0] * taps
    full_conv = smalls[:, :own_taps].reshape(-1, taps, conv_w.shape[0]).transpose(1, 0, 2)
    full_conv = full_conv.reshape(taps, -1).astype(F32)
    conv = jnp.concatenate(
        [
            lax.dynamic_slice_in_dim(full_conv, rank * key_cols, key_cols, 1),
            lax.dynamic_slice_in_dim(full_conv, all_keys + rank * key_cols, key_cols, 1),
            lax.dynamic_slice_in_dim(full_conv, 2 * all_keys + rank * val_cols, val_cols, 1),
        ],
        1,
    )
    conv = jnp.concatenate([conv, jnp.zeros((8 - taps, channels), F32)], 0)
    gains = smalls[:, own_taps:].astype(F32)
    full_gin = gains[:, :rows].reshape(-1)
    full_gmid = gains[:, rows : 2 * rows].reshape(-1)
    full_go = gains[:, 2 * rows :].reshape(-1)

    chunks_in = spread(layer_in[0])
    decay_chunks = spread(log_decay[0].T)
    out_blocks = spread(copied(out_block, chunks_in[1], chunks_in[2]))
    order = dealing[0]
    place = ((order // count) ^ rank) * count + order % count
    index = jnp.arange(total, dtype=jnp.int32)

    decay = jnp.zeros((heads, total), F32)
    for k in range(seq_count):
        own = lax.dynamic_slice_in_dim(decay_chunks[k], rank * heads, heads, 0)
        decay = lax.dynamic_update_slice_in_dim(decay, own, (rank ^ k) * count, 1)
    decay = decay.reshape(heads, -1, BLOCK)
    cum = jnp.cumsum(decay, axis=2)
    ends = jnp.cumsum(seq_lengths[0])
    seg = jnp.sum((index[None, :] >= ends[:, None]).astype(jnp.int32), axis=0)
    seg_blocks = seg.reshape(-1, BLOCK)
    seg_before = jnp.concatenate([jnp.full((1,), -1, jnp.int32), seg_blocks[:-1, -1]])
    keep_in = (seg_blocks == seg_before[:, None]).astype(F32)
    keep_out = (seg_blocks == seg_blocks[:, -1:]).astype(F32)
    elog = (jnp.exp(cum) * keep_in[None]).reshape(heads, total)
    flog = (jnp.exp(cum[:, :, -1:] - cum) * keep_out[None]).reshape(heads, total)
    cum = cum.reshape(heads, total)
    keeps = []
    for tap in range(taps - 1):
        by = taps - 1 - tap
        before = jnp.concatenate([jnp.full((by,), -1, jnp.int32), seg[:-by]])
        keeps.append((before == seg).astype(F32)[None])
    seg_row = seg.astype(F32)[None]
    place_row = place.astype(F32)[None]
    row_info = jnp.concatenate([cum, seg_row, jnp.zeros((8 - heads - 1, total), F32)], 0)
    col_info = jnp.concatenate(
        keeps
        + [seg_row, place_row, cum, elog, flog, jnp.zeros((128 - 5 - 3 * heads, total), F32)],
        0,
    ).T

    rank_word = rank.astype(jnp.int32).reshape(1)
    normed, gate_logit, proj, logit_parts, mix = project(
        rank_word, jnp.concatenate(chunks_in, 0), full_gin[None], gathered, col_info, count, channels
    )
    chunks_grad = spread(copied(out_grad[0], proj))
    outs = forward_recurrence(proj, conv, col_info, row_info, logit_parts, heads)
    dealt_rows, attn = gate_rows(
        outs[0], place_row, gate_logit, full_go[None], count, heads, chunks_grad[1:] + out_blocks[1:]
    )
    attn_parts = returned(attn)
    residual, mid_own = out_project(rank_word, layer_in[0], full_gmid[None], attn_parts, out_blocks)

    mids = [mid_own, swapped(mid_own, "seq", 1), swapped(mid_own, "seq", 2)]
    hiddens, gu_grads, layer_parts, mid_parts = [], [], [], []
    for k in range(seq_count):
        if k == 1:
            mids.append(swapped(copied(mid_own, mids[1], mid_parts[0]), "seq", 3))
        gate_up = dot(mids[k], w_gu)
        gate, up = gate_up[:, :wide], gate_up[:, wide:]
        hiddens.append((silu(gate) * up).astype(BF16))
        hidden_grad = dot(chunks_grad[k], down_turned)
        gu_grads.append(
            jnp.concatenate(
                [hidden_grad * up * silu_slope(gate), hidden_grad * silu(gate)], 1
            ).astype(BF16)
        )
        mid_parts.append(right_product(gu_grads[k], w_gu).astype(BF16))
    for k in range(seq_count):
        layer_parts.append(
            right_product(hiddens[k], down_turned).astype(BF16)
        )
    mid_parts = returned(mid_parts)
    g_down = weight_grad(chunks_grad, hiddens, wide, mid_parts[1])
    down_sum = RowSum(g_down)
    res_grad, out_proj_grad, g_mid, attn_grads = mid_back(
        rank_word, out_grad[0], residual, full_gmid[None], mid_parts, out_blocks, [g_down]
    )
    g_gu = weight_grad(mids, gu_grads, wide, attn_grads[0])
    attn_grads = returned(attn_grads)
    down_half = down_sum.join()
    down_sum.send(down_half)
    ffn_sum = RowSum(g_gu)
    opg_chunks = spread(copied(out_proj_grad, *attn_grads[1:]))
    layer_parts = returned(layer_parts)

    gate_grad, o_grad, g_go = ungate_rows(
        dealt_rows, col_info, gate_logit, full_go[None], attn_grads, heads, [g_gu]
    )
    ffn_half = ffn_sum.join()
    ffn_sum.send(ffn_half)
    proj_grad, g_conv = backward_recurrence(
        proj, conv, col_info, row_info, logit_parts, outs[1:], o_grad, heads,
        down_sum.parts[1:] + [ffn_half],
    )
    g_gate, gate_sums = weight_grad(
        [normed], [gate_grad], val_cols, proj_grad, weights=mix[:, channels + 128 :]
    )
    g_out = weight_grad(opg_chunks, attn, val_cols, proj_grad, *ffn_sum.parts[1:])
    out_sum = RowSum(jnp.concatenate([g_gate, g_out], 1))
    out_half = out_sum.join()
    out_sum.send(out_half)
    proj_grad, g_proj, proj_sums = unpack(proj_grad, place_row, normed, mix, [out_half] + layer_parts[1:])
    normed_low = unproject(proj_grad, gate_grad, mix, count, [])
    g_gin = (proj_sums + gate_sums)[:, 0] / full_gin
    conv_full = jnp.zeros((taps, conv_w.shape[0] * devices), F32)
    conv_full = lax.dynamic_update_slice_in_dim(
        conv_full, g_conv[:taps, :key_cols], rank * key_cols, 1
    )
    conv_full = lax.dynamic_update_slice_in_dim(
        conv_full, g_conv[:taps, key_cols : 2 * key_cols], all_keys + rank * key_cols, 1
    )
    conv_full = lax.dynamic_update_slice_in_dim(
        conv_full, g_conv[:taps, 2 * key_cols :], 2 * all_keys + rank * val_cols, 1
    )
    conv_full = conv_full.reshape(taps, devices, -1).transpose(1, 0, 2).reshape(devices, -1)
    small_cols = -(-small_count // rows)
    small_grad = jnp.concatenate(
        [
            conv_full,
            g_gin.reshape(devices, -1),
            g_mid.reshape(devices, -1),
            g_go.reshape(devices, -1),
            jnp.zeros((devices, small_cols * rows - small_count), F32),
        ],
        1,
    )
    small_grad = small_grad.reshape(devices * rows, small_cols).astype(BF16)
    mix_sum = RowSum(
        jnp.concatenate([g_proj[:, : channels + heads], small_grad], 1)
    )
    mix_half = mix_sum.join()
    mix_sum.send(mix_half)
    normed_chunks = returned(
        [normed_low[k * count : (k + 1) * count] for k in range(seq_count)]
    )
    ffn_pieces = dealt(jnp.concatenate([down_sum.total(), ffn_sum.total(), out_sum.total()], 2))
    layer_out = residual + sum(c.astype(F32) for c in layer_parts)
    mix_pieces = dealt(mix_sum.total())
    in_grad = in_back(layer_in[0], res_grad, full_gin[None], normed_chunks, [mix_half])

    small_sum = jnp.sum(mix_pieces[:, :, channels + heads :], axis=0).reshape(-1)[:small_count]
    grad_conv = small_sum[:own_taps].reshape(taps, -1).T
    small_sum = small_sum[own_taps:]

    def columns(pieces, first, width):
        return jnp.concatenate([pieces[j, :, first : first + width] for j in range(seq_count)], 1)

    grad_qkv = jnp.concatenate(
        [
            columns(mix_pieces, 0, key_cols),
            columns(mix_pieces, key_cols, key_cols),
            columns(mix_pieces, 2 * key_cols, val_cols),
        ],
        1,
    )
    return (
        layer_out.astype(BF16)[None],
        in_grad.astype(BF16)[None],
        grad_qkv,
        columns(ffn_pieces, 3 * wide, val_cols),
        columns(mix_pieces, channels, heads),
        grad_conv,
        small_sum[:rows],
        small_sum[2 * rows :],
        columns(ffn_pieces, 3 * wide + val_cols, val_cols).T,
        small_sum[rows : 2 * rows],
        jnp.concatenate([columns(ffn_pieces, wide, half), columns(ffn_pieces, 2 * wide, half)], 1),
        columns(ffn_pieces, 0, half).T,
    )


def solution(mesh):
    in_specs = (
        P("mp", "seq", None),
        P("mp", "seq", None),
        P("mp", None),
        P("mp", None),
        P("mp", "seq", None),
        P(("seq", "mp"), None),
        P(("seq", "mp"), None),
        P(("seq", "mp"), None),
        P(("seq", "mp"), None),
        P(("seq", "mp")),
        P(("seq", "mp")),
        P(None, ("seq", "mp")),
        P(("seq", "mp")),
        P(("seq", "mp"), None),
        P(None, ("seq", "mp")),
    )
    out_specs = (
        P("mp", "seq", None),
        P("mp", "seq", None),
        P(("seq", "mp"), None),
        P(("seq", "mp"), None),
        P(("seq", "mp"), None),
        P(("seq", "mp"), None),
        P(("seq", "mp")),
        P(("seq", "mp")),
        P(None, ("seq", "mp")),
        P(("seq", "mp")),
        P(("seq", "mp"), None),
        P(None, ("seq", "mp")),
    )
    return jax.shard_map(body, mesh=mesh, in_specs=in_specs, out_specs=out_specs, check_vma=False)
```

```python
import functools

import jax
import jax.numpy as jnp
from jax import lax
from jax.experimental import pallas as pl
from jax.experimental.pallas import tpu as pltpu
from jax.sharding import PartitionSpec as P

HEAD_COUNT = 8
DK = 128
DV = 256
BLOCK = 128
PER_STEP = 2
F32 = jnp.float32
BF16 = jnp.bfloat16


def mm(left, right):
    return jnp.dot(left.astype(BF16), right.astype(BF16), preferred_element_type=F32)


def mm_nt(left, right):
    return lax.dot_general(
        left.astype(BF16),
        right.astype(BF16),
        (((1,), (1,)), ((), ())),
        preferred_element_type=F32,
    )


def mm_tn(left, right):
    return lax.dot_general(
        left.astype(BF16),
        right.astype(BF16),
        (((0,), (0,)), ((), ())),
        preferred_element_type=F32,
    )


def masks():
    rows = lax.broadcasted_iota(jnp.int32, (BLOCK, BLOCK), 0)
    cols = lax.broadcasted_iota(jnp.int32, (BLOCK, BLOCK), 1)
    return rows, cols


def unit_inverses(mats, rows, cols):
    ident = (rows == cols).astype(F32)
    near = (rows // 16) == (cols // 16)
    power = [jnp.where(near, a, 0.0) for a in mats]
    result = [ident - p for p in power]
    span = 2
    while span < 16:
        power = [mm(p, p) for p in power]
        result = [t + mm(t, p) for t, p in zip(result, power)]
        span *= 2
    size = 16
    while size < BLOCK:
        off = ((rows // (2 * size)) == (cols // (2 * size))) & ((rows // size) != (cols // size))
        reach = [mm(jnp.where(off, a, 0.0), t) for a, t in zip(mats, result)]
        result = [t - mm(t, x) for t, x in zip(result, reach)]
        size *= 2
    return result


def convolve(ext_ref, conv_ref, col_ref, start, first, width):
    cols = pl.ds(first, width)
    total = ext_ref[pl.ds(16 + start, BLOCK), cols] * conv_ref[3:4, cols]
    for tap in range(3):
        keep = col_ref[pl.ds(start, BLOCK), tap : tap + 1]
        total += ext_ref[pl.ds(13 + tap + start, BLOCK), cols] * keep * conv_ref[tap : tap + 1, cols]
    return total


def column(col_ref, start, index):
    return col_ref[pl.ds(start, BLOCK), index : index + 1]


def strength(logit_ref, start, head, heads):
    return jax.nn.sigmoid(column(logit_ref, start, head))


def exact_nt(left, right):
    left_high, right_high = left.astype(BF16), right.astype(BF16)
    left_low = left - left_high.astype(F32)
    right_low = right - right_high.astype(F32)
    return mm_nt(left_high, right_high) + (mm_nt(left_high, right_low) + mm_nt(left_low, right_high))


def decay_matrix(col_ref, row_ref, start, head, heads, rows, cols):
    cum_i = column(col_ref, start, 5 + head)
    cum_j = row_ref[head : head + 1, pl.ds(start, BLOCK)]
    seg_i = column(col_ref, start, 3)
    seg_j = row_ref[heads : heads + 1, pl.ds(start, BLOCK)]
    within = (rows >= cols) & (seg_i == seg_j)
    return jnp.where(within, jnp.exp(jnp.where(within, cum_i - cum_j, 0.0)), 0.0)


def silu(values):
    return values * jax.nn.sigmoid(values)


def forward_kernel(
    heads, edge_ref, proj_ref, conv_ref, col_ref, row_ref, logit_ref, *refs,
):
    o_ref, s_ref, n_ref, t_ref, w_ref, p_ref, ext_ref, state_ref = refs[-8:]
    steps = proj_ref.shape[0] // BLOCK

    @pl.when(pl.program_id(0) == 0)
    def _():
        state_ref[...] = jnp.zeros_like(state_ref)

    ext_ref[:16, :] = edge_ref[...].astype(F32)
    ext_ref[16:, :] = proj_ref[...].astype(F32)
    rows, cols = masks()
    strict = rows > cols
    units = [(g, h) for g in range(steps) for h in range(heads)]
    queries, keys, values, mats, decays, betas = {}, {}, {}, [], {}, {}
    for g, h in units:
        start = g * BLOCK
        taken = functools.partial(convolve, ext_ref, conv_ref, col_ref, start)
        queries[g, h] = silu(taken(h * DK, DK))
        raw = silu(taken((heads + h) * DK, DK))
        keys[g, h] = raw * lax.rsqrt(jnp.sum(raw * raw, axis=1, keepdims=True) + 1e-06)
        values[g, h] = silu(taken(2 * heads * DK + h * DV, DV))
        decays[g, h] = decay_matrix(col_ref, row_ref, start, h, heads, rows, cols)
        betas[g, h] = strength(logit_ref, start, h, heads)
        beta = betas[g, h]
        inner = mm_nt(keys[g, h], keys[g, h])
        mats.append(jnp.where(strict, beta * inner * decays[g, h], 0.0))
    inverses = unit_inverses(mats, rows, cols)
    umats, wmats, pmats, boundary, reads = {}, {}, {}, {}, {}
    for (g, h), inverse in zip(units, inverses):
        start = g * BLOCK
        beta = betas[g, h]
        elog = column(col_ref, start, 5 + heads + h)
        flog = column(col_ref, start, 5 + 2 * heads + h)
        inverse = inverse.astype(BF16)
        t_ref[g, h] = inverse
        umats[g, h] = mm(inverse, beta * values[g, h])
        wmats[g, h] = mm(inverse, (beta * elog) * keys[g, h]).astype(BF16)
        w_ref[g, h] = wmats[g, h]
        pmats[g, h] = (exact_nt(queries[g, h], keys[g, h]) * decays[g, h]).astype(BF16)
        p_ref[g, h] = pmats[g, h]
        boundary[g, h] = (keys[g, h] * flog).T.astype(BF16)
        reads[g, h] = (queries[g, h] * elog).astype(BF16)
    for g in range(steps):
        start = g * BLOCK
        for h in range(heads):
            state = state_ref[h]
            low = state.astype(BF16)
            s_ref[g, h] = low
            news = (umats[g, h] - mm(wmats[g, h], low)).astype(BF16)
            n_ref[g, h] = news
            carried = col_ref[pl.ds(start + BLOCK - 1, 1), 5 + heads + h : 6 + heads + h]
            state_ref[h] = carried * state + mm(boundary[g, h], news)
            output = mm(reads[g, h], low) + mm(pmats[g, h], news)
            o_ref[pl.ds(start, BLOCK), h * DV : (h + 1) * DV] = output.astype(BF16)


def backward_kernel(
    heads, edge_ref, proj_ref, conv_ref, col_ref, row_ref, logit_ref,
    s_ref, n_ref, t_ref, w_ref, p_ref, do_ref, *refs,
):
    grad_ref, gconv_ref, ext_ref, shift_ref, dstate_ref, head_ref = refs[-6:]
    count = proj_ref.shape[0]
    steps = count // BLOCK
    channels = proj_ref.shape[1]

    @pl.when(pl.program_id(0) == 0)
    def _():
        dstate_ref[...] = jnp.zeros_like(dstate_ref)
        head_ref[...] = jnp.zeros_like(head_ref)
        gconv_ref[...] = jnp.zeros_like(gconv_ref)

    ext_ref[:16, :] = edge_ref[...].astype(F32)
    ext_ref[16:, :] = proj_ref[...].astype(F32)
    for tap in range(3):
        shift_ref[tap, count : count + 8, :] = head_ref[tap]
    rows, cols = masks()
    strict = rows > cols
    units = [(g, h) for g in reversed(range(steps)) for h in range(heads)]
    queries, keys, pre, reads, first, gains = {}, {}, {}, {}, {}, {}
    for g, h in units:
        start = g * BLOCK
        taken = functools.partial(convolve, ext_ref, conv_ref, col_ref, start)
        elog = column(col_ref, start, 5 + heads + h)
        out_grad = do_ref[pl.ds(start, BLOCK), h * DV : (h + 1) * DV]
        queries[g, h] = silu(taken(h * DK, DK))
        raw = silu(taken((heads + h) * DK, DK))
        scale = lax.rsqrt(jnp.sum(raw * raw, axis=1, keepdims=True) + 1e-06)
        keys[g, h] = (raw * scale, scale)
        first[g, h] = mm_tn(p_ref[g, h], out_grad)
        gains[g, h] = mm_tn(queries[g, h] * elog, out_grad)
    news_grads, state_grads = {}, {}
    for g in reversed(range(steps)):
        start = g * BLOCK
        for h in range(heads):
            flog = column(col_ref, start, 5 + 2 * heads + h)
            dstate = dstate_ref[h]
            low = dstate.astype(BF16)
            state_grads[g, h] = low
            news_grad = (first[g, h] + mm(keys[g, h][0] * flog, low)).astype(BF16)
            news_grads[g, h] = news_grad
            carried = col_ref[pl.ds(start + BLOCK - 1, 1), 5 + heads + h : 6 + heads + h]
            dstate_ref[h] = gains[g, h] + carried * dstate - mm_tn(w_ref[g, h], news_grad)
    lane = lax.broadcasted_iota(jnp.int32, (BLOCK, 128), 1)

    def through_conv(g, first_col, width, grad):
        start = g * BLOCK
        cols_ = pl.ds(first_col, width)
        value = convolve(ext_ref, conv_ref, col_ref, start, first_col, width)
        gate = jax.nn.sigmoid(value)
        grad = grad * (gate * (1.0 + value * (1.0 - gate)))
        shift_ref[3, pl.ds(start, BLOCK), cols_] = grad * conv_ref[3:4, cols_]
        sums = []
        for tap in range(3):
            kept = grad * col_ref[pl.ds(start, BLOCK), tap : tap + 1]
            shift_ref[tap, pl.ds(start, BLOCK), cols_] = kept * conv_ref[tap : tap + 1, cols_]
            sums.append(
                jnp.sum(kept * ext_ref[pl.ds(13 + tap + start, BLOCK), cols_], axis=0, keepdims=True)
            )
        sums.append(
            jnp.sum(grad * ext_ref[pl.ds(16 + start, BLOCK), cols_], axis=0, keepdims=True)
        )
        for tap in range(4):
            gconv_ref[tap : tap + 1, cols_] += sums[tap]

    logit_grads = {}
    for g, h in units:
        start = g * BLOCK
        beta = strength(logit_ref, start, h, heads)
        elog = column(col_ref, start, 5 + heads + h)
        flog = column(col_ref, start, 5 + 2 * heads + h)
        key, scale = keys[g, h]
        query = queries[g, h]
        out_grad = do_ref[pl.ds(start, BLOCK), h * DV : (h + 1) * DV]
        decay = decay_matrix(col_ref, row_ref, start, h, heads, rows, cols)
        key_low = key.astype(BF16)
        inner = mm_nt(key_low, key_low) * decay
        news, state, dstate = n_ref[g, h], s_ref[g, h], state_grads[g, h]
        rhs_grad = mm_tn(t_ref[g, h], news_grads[g, h])
        rhs_low = rhs_grad.astype(BF16)
        within = (mm_nt(out_grad, news) * decay).astype(BF16)
        mat_grad = jnp.where(strict, -mm_nt(rhs_low, news), 0.0)
        pair = (mat_grad * beta * decay).astype(BF16)
        back = mm_nt(rhs_low, state)
        q_grad = mm(within, key_low) + elog * mm_nt(out_grad, state)
        k_grad = (
            mm_tn(within, query)
            + mm(pair, key_low)
            + mm_tn(pair, key_low)
            + flog * mm_nt(news, dstate)
            - (beta * elog) * back
        )
        value = silu(convolve(ext_ref, conv_ref, col_ref, start, 2 * heads * DK + h * DV, DV))
        beta_grad = (
            jnp.sum(mat_grad * inner - elog * (key * back), axis=1, keepdims=True)
            + jnp.sum(rhs_grad * value, axis=1, keepdims=True)
        )
        logit_grads[g, h] = beta_grad * beta * (1.0 - beta)
        raw_grad = scale * (k_grad - key * jnp.sum(k_grad * key, axis=1, keepdims=True))
        through_conv(g, h * DK, DK, q_grad)
        through_conv(g, (heads + h) * DK, DK, raw_grad)
        through_conv(g, 2 * heads * DK + h * DV, DV, beta * rhs_grad)
    for g in range(steps):
        total = jnp.zeros((BLOCK, 128), F32)
        for h in range(heads):
            total = jnp.where(lane == h, logit_grads[g, h], total)
        grad_ref[pl.ds(g * BLOCK, BLOCK), channels : channels + 128] = total.astype(BF16)
        grad_ref[pl.ds(g * BLOCK, BLOCK), channels + 128 :] = jnp.zeros((BLOCK, 128), BF16)
    total = shift_ref[3, :count, :]
    for tap in range(3):
        total += shift_ref[tap, pl.ds(3 - tap, count), :]
    grad_ref[:, :channels] = total.astype(BF16)
    for tap in range(3):
        head_ref[tap] = shift_ref[tap, :8, :]


def saved_shapes(blocks, heads):
    return (
        jax.ShapeDtypeStruct((blocks, heads, DK, DV), BF16),
        jax.ShapeDtypeStruct((blocks, heads, BLOCK, DV), BF16),
        jax.ShapeDtypeStruct((blocks, heads, BLOCK, BLOCK), BF16),
        jax.ShapeDtypeStruct((blocks, heads, BLOCK, DK), BF16),
        jax.ShapeDtypeStruct((blocks, heads, BLOCK, BLOCK), BF16),
    )


def saved_specs(shapes, index):
    return [
        pl.BlockSpec((PER_STEP,) + shape.shape[1:], lambda i: (index(i), 0, 0, 0))
        for shape in shapes
    ]


def common_specs(step, channels, logits, index):
    return [
        pl.BlockSpec((16, channels), lambda i: (jnp.maximum(index(i) * (step // 16) - 1, 0), 0)),
        pl.BlockSpec((step, channels), lambda i: (index(i), 0)),
        pl.BlockSpec((8, channels), lambda i: (0, 0)),
        pl.BlockSpec((step, 128), lambda i: (index(i), 0)),
        pl.BlockSpec((8, step), lambda i: (0, index(i))),
        pl.BlockSpec((step, logits), lambda i: (index(i), 0)),
    ]


VMEM_BYTES = 56 * 1024 * 1024
SMALL_COST = pl.CostEstimate(flops=10**6, bytes_accessed=10**6, transcendentals=0)
ANYWHERE = pl.BlockSpec(memory_space=pl.ANY)
WHOLE = pl.BlockSpec(memory_space=pltpu.VMEM)
SCALAR = pl.BlockSpec(memory_space=pltpu.SMEM)


def params():
    return pltpu.CompilerParams(dimension_semantics=("arbitrary",), vmem_limit_bytes=VMEM_BYTES)


def forward_recurrence(proj, conv, cols, rows, logits, heads, tokens):
    count, channels = proj.shape
    step = BLOCK * PER_STEP
    shapes = saved_shapes(count // BLOCK, heads)
    index = lambda i: i
    return pl.pallas_call(
        functools.partial(forward_kernel, heads),
        grid=(count // step,),
        in_specs=common_specs(step, channels, 128, index) + [ANYWHERE] * len(tokens),
        out_specs=[pl.BlockSpec((step, heads * DV), lambda i: (i, 0))] + saved_specs(shapes, index),
        out_shape=(jax.ShapeDtypeStruct((count, heads * DV), BF16),) + shapes,
        scratch_shapes=[
            pltpu.VMEM((step + 16, channels), F32),
            pltpu.VMEM((heads, DK, DV), F32),
        ],
        compiler_params=params(),
        cost_estimate=SMALL_COST,
        name="recurrence_forward",
    )(proj, proj, conv, cols, rows, logits, *tokens)


def backward_recurrence(proj, conv, cols, rows, logits, saved, out_grad, heads, tokens):
    count, channels = proj.shape
    step = BLOCK * PER_STEP
    last = count // step - 1
    index = lambda i: last - i
    return pl.pallas_call(
        functools.partial(backward_kernel, heads),
        grid=(count // step,),
        in_specs=common_specs(step, channels, 128, index)
        + saved_specs(saved, index)
        + [pl.BlockSpec((step, heads * DV), lambda i: (index(i), 0))]
        + [ANYWHERE] * len(tokens),
        out_specs=[
            pl.BlockSpec((step, channels + 256), lambda i: (index(i), 0)),
            pl.BlockSpec((8, channels), lambda i: (0, 0)),
        ],
        out_shape=(
            jax.ShapeDtypeStruct((count, channels + 256), BF16),
            jax.ShapeDtypeStruct((8, channels), F32),
        ),
        scratch_shapes=[
            pltpu.VMEM((step + 16, channels), F32),
            pltpu.VMEM((4, step + 8, channels), F32),
            pltpu.VMEM((heads, DK, DV), F32),
            pltpu.VMEM((3, 8, channels), F32),
        ],
        compiler_params=params(),
        cost_estimate=SMALL_COST,
        name="recurrence_backward",
    )(proj, proj, conv, cols, rows, logits, *saved, out_grad, *tokens)


def project_kernel(
    channels, chunks, handed, rank_ref, gain_ref, w_ref, col_ref, *refs
):
    x_refs = refs[:chunks]
    normed_ref, gate_ref, proj_ref, logit_ref, all_ref = refs[chunks + handed : chunks + handed + 5]
    rows_ref = refs[-1]
    step = pl.program_id(0)
    count = x_refs[0].shape[0]

    @pl.when(step == 0)
    def _():
        width = w_ref.shape[0] * w_ref.shape[2]
        for k in range(w_ref.shape[1]):
            place = pl.ds(pl.multiple_of((rank_ref[0] ^ k) * width, width), width)
            all_ref[place, :] = w_ref[:, k].reshape(width, w_ref.shape[3])

    for k in range(chunks):

        @pl.when(step == k)
        def _():
            x = x_refs[k][...].astype(F32)
            scale = lax.rsqrt(jnp.mean(x * x, axis=1, keepdims=True) + 1e-05)
            normed = (x * scale * gain_ref[...]).astype(BF16)
            normed_ref[...] = normed
            total = mm(normed, all_ref[...])
            gates = gate_ref.shape[1]
            gate_ref[...] = total[:, :gates]
            logit = total[:, gates + channels :]
            high = logit.astype(BF16)
            place = slice(k * count, (k + 1) * count)
            rows_ref[place, : channels + 128] = total[:, gates:].astype(BF16)
            rows_ref[place, channels + 128 :] = (logit - high.astype(F32)).astype(BF16)

    @pl.when(step >= chunks)
    def _():
        order = lax.broadcasted_iota(jnp.int32, (proj_ref.shape[0], rows_ref.shape[0]), 1)
        picked = (col_ref[:, 4:5].astype(jnp.int32) == order).astype(F32)
        packed = mm(picked, rows_ref[...])
        proj_ref[...] = packed[:, :channels].astype(BF16)
        logit_ref[...] = packed[:, channels : channels + 128] + packed[:, channels + 128 :]


def project(rank, x_chunks, gain, weights, cols, channels, passed, tokens):
    count, width = x_chunks[0].shape
    total = count * len(x_chunks)
    gates = weights.shape[3] - channels - 128
    chunks = total // count
    block = 256
    first = lambda i: jnp.minimum(i, chunks - 1)
    later = lambda i: jnp.maximum(i - chunks, 0)
    outs = pl.pallas_call(
        functools.partial(project_kernel, channels, chunks, len(passed) + len(tokens)),
        grid=(chunks + total // block,),
        in_specs=[
            SCALAR,
            pl.BlockSpec((1, width), lambda i: (0, 0)),
            pl.BlockSpec(weights.shape, lambda i: (0, 0, 0, 0)),
            pl.BlockSpec((block, 128), lambda i: (later(i), 0)),
        ]
        + [pl.BlockSpec((count, width), lambda i: (0, 0))] * chunks
        + [ANYWHERE] * (len(passed) + len(tokens)),
        out_specs=[
            pl.BlockSpec((count, width), lambda i: (first(i), 0)),
            pl.BlockSpec((count, gates), lambda i: (first(i), 0)),
            pl.BlockSpec((block, channels), lambda i: (later(i), 0)),
            pl.BlockSpec((block, 128), lambda i: (later(i), 0)),
            pl.BlockSpec((width, weights.shape[3]), lambda i: (0, 0)),
        ]
        + [ANYWHERE] * len(passed),
        out_shape=[
            jax.ShapeDtypeStruct((total, width), BF16),
            jax.ShapeDtypeStruct((total, gates), F32),
            jax.ShapeDtypeStruct((total, channels), BF16),
            jax.ShapeDtypeStruct((total, 128), F32),
            jax.ShapeDtypeStruct((width, weights.shape[3]), BF16),
        ]
        + [jax.ShapeDtypeStruct(p.shape, p.dtype) for p in passed],
        input_output_aliases={4 + chunks + i: 5 + i for i in range(len(passed))},
        scratch_shapes=[pltpu.VMEM((total, channels + 256), BF16)],
        compiler_params=params(),
        cost_estimate=SMALL_COST,
        name="project",
    )(rank, gain, weights, cols, *x_chunks, *passed, *tokens)
    return outs[:5], outs[5:]


def gate_kernel(heads, count, first, o_ref, place_ref, gate_ref, gain_ref, *refs):
    chunks = place_ref.shape[1] // count
    dealt_ref, chunk_refs = refs[first], refs[first + 1 : first + 1 + chunks]
    for k, chunk_ref in enumerate(chunk_refs):
        order = lax.broadcasted_iota(jnp.int32, (count, o_ref.shape[0]), 0) + k * count
        picked = (place_ref[...].astype(jnp.int32) == order).astype(F32)
        rows = mm(picked, o_ref[...])
        place = pl.ds(k * count, count)
        dealt_ref[place, :] = rows.astype(BF16)
        for h in range(heads):
            lanes = slice(h * DV, (h + 1) * DV)
            value = rows[:, lanes]
            scale = lax.rsqrt(jnp.mean(value * value, axis=1, keepdims=True) + 1e-05)
            gated = value * scale * gain_ref[...] * silu(gate_ref[place, lanes])
            chunk_ref[:, lanes] = gated.astype(BF16)


def gate_rows(output, place, gate_logit, gain, count, heads, passed, tokens):
    total, cols = output.shape
    chunks = total // count
    others = len(passed) + len(tokens)
    outs = pl.pallas_call(
        functools.partial(gate_kernel, heads, count, others),
        in_specs=[WHOLE] * 4 + [ANYWHERE] * others,
        out_specs=[WHOLE] * (chunks + 1) + [ANYWHERE] * len(passed),
        out_shape=[jax.ShapeDtypeStruct((total, cols), BF16)]
        + [jax.ShapeDtypeStruct((count, cols), BF16)] * chunks
        + [jax.ShapeDtypeStruct(a.shape, a.dtype) for a in passed],
        input_output_aliases={4 + i: 1 + chunks + i for i in range(len(passed))},
        compiler_params=pltpu.CompilerParams(vmem_limit_bytes=VMEM_BYTES),
        cost_estimate=SMALL_COST,
        name="gate_rows",
    )(output, place, gate_logit, gain, *passed, *tokens)
    return outs[0], outs[1 : 1 + chunks], outs[1 + chunks :]


def ungate_kernel(heads, chunks, outs, dealt_ref, col_ref, gate_ref, gain_ref, *refs):
    grad_refs = refs[:chunks]
    gate_grad_ref, o_grad_ref, gain_grad_ref, rows_ref = *refs[outs : outs + 3], refs[-1]
    count = grad_refs[0].shape[0]
    total = dealt_ref.shape[0]
    sums = jnp.zeros((1, DV), F32)
    for k in range(chunks):
        place = pl.ds(k * count, count)
        for h in range(heads):
            lanes = slice(h * DV, (h + 1) * DV)
            value = dealt_ref[place, lanes].astype(F32)
            grad = grad_refs[k][:, lanes].astype(F32)
            logit = gate_ref[place, lanes]
            scale = lax.rsqrt(jnp.mean(value * value, axis=1, keepdims=True) + 1e-05)
            unit = value * scale
            gate = jax.nn.sigmoid(logit)
            slid = logit * gate
            sums += jnp.sum(grad * unit * slid, axis=0, keepdims=True)
            grad = grad * gain_ref[...]
            slope = gate * (1.0 + logit * (1.0 - gate))
            gate_grad_ref[place, lanes] = (grad * unit * slope).astype(BF16)
            grad = grad * slid
            inner = jnp.mean(grad * unit, axis=1, keepdims=True)
            rows_ref[place, lanes] = (scale * (grad - unit * inner)).astype(BF16)
    gain_grad_ref[...] = sums
    for k in range(chunks):
        place = pl.ds(k * count, count)
        order = lax.broadcasted_iota(jnp.int32, (count, total), 1)
        picked = (col_ref[place, 4:5].astype(jnp.int32) == order).astype(F32)
        o_grad_ref[place, :] = mm(picked, rows_ref[...]).astype(BF16)


def ungate_rows(dealt_rows, cols, gate_logit, gain, grads, heads, passed, tokens):
    total, width = dealt_rows.shape
    whole = pl.BlockSpec(memory_space=pltpu.VMEM)
    first = 4 + len(grads)
    outs = pl.pallas_call(
        functools.partial(ungate_kernel, heads, len(grads), len(grads) + len(passed) + len(tokens)),
        in_specs=[whole] * first + [ANYWHERE] * (len(passed) + len(tokens)),
        out_specs=[whole] * 3 + [ANYWHERE] * len(passed),
        out_shape=[
            jax.ShapeDtypeStruct((total, width), BF16),
            jax.ShapeDtypeStruct((total, width), BF16),
            jax.ShapeDtypeStruct((1, DV), F32),
        ]
        + [jax.ShapeDtypeStruct(p.shape, p.dtype) for p in passed],
        input_output_aliases={first + i: 3 + i for i in range(len(passed))},
        scratch_shapes=[pltpu.VMEM((total, width), BF16)],
        compiler_params=pltpu.CompilerParams(vmem_limit_bytes=VMEM_BYTES),
        cost_estimate=SMALL_COST,
        name="ungate_rows",
    )(dealt_rows, cols, gate_logit, gain, *grads, *passed, *tokens)
    return outs[:3], list(outs[3:])


def put_rows(total, split, core_ref, refs):
    total = total.astype(BF16)
    if split is None:
        refs[0][...] = total
        return
    halves = total.reshape(*split, 2, -1, total.shape[1])
    for core in range(2):

        @pl.when(core_ref[0] == core)
        def _():
            refs[0][...] = halves[:, :, core]
            refs[1][...] = halves[:, :, 1 - core]


def row_outputs(split, width, cols, tile):
    if split is None:
        shape, block = (width, cols), (width, tile)
        spec = pl.BlockSpec(block, lambda i: (0, i))
        return [spec], [jax.ShapeDtypeStruct(shape, BF16)]
    shape = (*split, width // (2 * split[0] * split[1]))
    spec = pl.BlockSpec((*shape, tile), lambda i: (0, 0, 0, i))
    return [spec] * 2, [jax.ShapeDtypeStruct((*shape, cols), BF16)] * 2


def unpack_kernel(split, heads, words_ref, grad_ref, gates_ref, place_ref, normed_ref, w_ref, conv_ref, gain_ref, mid_ref, o_ref, *refs):
    count = 2 if split else 1
    dealt_ref, sums_ref = refs[-4 - count], refs[-3 - count]
    row_refs, small_ref, picked_ref = refs[-2 - count : -2], refs[-2], refs[-1]
    step = pl.program_id(0)
    total = grad_ref.shape[0]
    gates = gates_ref.shape[1]
    tile = dealt_ref.shape[1] // 2

    @pl.when(step == 0)
    def _():
        part = 256
        for k in range(total // part):
            order = lax.broadcasted_iota(jnp.int32, (part, total), 0) + k * part
            picked = (place_ref[...].astype(jnp.int32) == order).astype(F32)
            picked_ref[k * part : (k + 1) * part, :] = picked.astype(BF16)
        dealt_ref[:, :gates] = gates_ref[...]
        dealt_ref[:, gates:tile] = mm(picked_ref[...], grad_ref[:, : tile - gates]).astype(BF16)
        share = mm(normed_ref[...], dealt_ref[:, :tile])
        sums_ref[...] = jnp.sum(share * w_ref[:, :tile].astype(F32), axis=1, keepdims=True)
        put_rows(share, split, words_ref, row_refs)

    @pl.when(step == 1)
    def _():
        dealt_ref[:, tile:] = mm(picked_ref[...], grad_ref[:, tile - gates :]).astype(BF16)
        share = mm(normed_ref[...], dealt_ref[:, tile:])
        used = w_ref.shape[1] - tile
        weights = w_ref[:, tile:].astype(F32)
        sums_ref[...] += jnp.sum(share[:, :used] * weights, axis=1, keepdims=True)
        if split:
            devices, rows = 2 * split[0] * split[1], share.shape[0] // (2 * split[0] * split[1])
            gin = jnp.broadcast_to(sums_ref[...], (share.shape[0], 128)).T[:1] / gain_ref[...]
            small_ref[...] = jnp.zeros_like(small_ref)
            gin = jnp.concatenate([gin[:, j * 128 : (j + 1) * 128] for j in range(8)], 0)
            mid = jnp.concatenate([mid_ref[:, j * 128 : (j + 1) * 128] for j in range(8)], 0)
            for d in range(devices):
                small_ref[d * rows + 4 : d * rows + 5, :] = o_ref[:, :128]
                small_ref[d * rows + 5 : d * rows + 6, :] = o_ref[:, 128:]
                small_ref[d * rows + 8 : d * rows + 16, :] = mid
                small_ref[d * rows + 16 : d * rows + 24, :] = gin
            rank = words_ref[2]
            keys = heads * DK // 128
            vals = heads * DV // 128
            owners = [rank * keys + j for j in range(keys)]
            owners += [HEAD_COUNT * DK // 128 + rank * keys + j for j in range(keys)]
            owners += [2 * HEAD_COUNT * DK // 128 + rank * vals + j for j in range(vals)]
            for j, owner in enumerate(owners):
                place = pl.ds(pl.multiple_of(owner * rows, rows), 8)
                old = small_ref[place, :]
                taps = lax.broadcasted_iota(jnp.int32, (8, 128), 0) < 4
                small_ref[place, :] = jnp.where(taps, conv_ref[:, j * 128 : (j + 1) * 128], old)
            share = jnp.concatenate([share[:, :-128], small_ref[...]], 1)
        put_rows(share, split, words_ref, row_refs)


def unpack(split, words, grad, gate_grad, place, normed, weights, g_conv, gain, g_mid, g_o, heads, tokens):
    total = grad.shape[0]
    cols = grad.shape[1] + gate_grad.shape[1]
    width = normed.shape[0]
    operands = (grad, gate_grad, place, normed, weights, g_conv, gain, g_mid, g_o)
    specs, shapes = row_outputs(split, width, cols, cols // 2)
    return pl.pallas_call(
        functools.partial(unpack_kernel, split, heads),
        grid=(2,),
        in_specs=[SCALAR]
        + [pl.BlockSpec(a.shape, lambda i: (0, 0)) for a in operands]
        + [ANYWHERE] * len(tokens),
        out_specs=[
            pl.BlockSpec((total, cols), lambda i: (0, 0)),
            pl.BlockSpec((width, 1), lambda i: (0, 0)),
        ]
        + specs,
        out_shape=[
            jax.ShapeDtypeStruct((total, cols), BF16),
            jax.ShapeDtypeStruct((width, 1), F32),
        ]
        + shapes,
        scratch_shapes=[pltpu.VMEM((width, 128), F32), pltpu.VMEM((total, total), BF16)],
        compiler_params=params(),
        cost_estimate=SMALL_COST,
        name="unpack",
    )(words, *operands, *tokens)


def unproject_kernel(chunks, first, grad_ref, w_ref, *refs):
    part_refs, turned_ref = refs[first : first + chunks], refs[-1]
    step = pl.program_id(0)

    @pl.when(step == 0)
    def _():
        turned_ref[...] = w_ref[...].T

    part = mm(grad_ref[:, : turned_ref.shape[0]], turned_ref[...])
    for k in range(chunks):

        @pl.when(step == k)
        def _():
            part_refs[k][...] = part.astype(BF16)


def unproject(grad, weights, count, passed, tokens):
    total, cols = grad.shape
    width = weights.shape[0]
    chunks = total // count
    outs = pl.pallas_call(
        functools.partial(unproject_kernel, chunks, len(passed) + len(tokens)),
        grid=(chunks,),
        in_specs=[
            pl.BlockSpec((count, cols), lambda i: (i, 0)),
            pl.BlockSpec(weights.shape, lambda i: (0, 0)),
        ]
        + [ANYWHERE] * (len(passed) + len(tokens)),
        out_specs=[pl.BlockSpec((count, width), lambda i: (0, 0))] * chunks
        + [ANYWHERE] * len(passed),
        out_shape=[jax.ShapeDtypeStruct((count, width), BF16)] * chunks
        + [jax.ShapeDtypeStruct(p.shape, p.dtype) for p in passed],
        input_output_aliases={2 + i: chunks + i for i in range(len(passed))},
        scratch_shapes=[pltpu.VMEM(weights.shape[::-1], BF16)],
        compiler_params=params(),
        cost_estimate=SMALL_COST,
        name="unproject",
    )(grad, weights, *passed, *tokens)
    return list(outs[:chunks]), list(outs[chunks:])


def hand_kernel(*refs):
    refs[-1][...] = jnp.zeros_like(refs[-1])


def handed(passed, tokens):
    outs = pl.pallas_call(
        hand_kernel,
        in_specs=[ANYWHERE] * (len(passed) + len(tokens)),
        out_specs=[ANYWHERE] * len(passed) + [WHOLE],
        out_shape=[jax.ShapeDtypeStruct(p.shape, p.dtype) for p in passed]
        + [jax.ShapeDtypeStruct((8, 128), F32)],
        input_output_aliases={i: i for i in range(len(passed))},
        cost_estimate=SMALL_COST,
        name="handed",
    )(*passed, *tokens)
    return outs[:-1]


def weight_grad_kernel(split, tiles, sums, words_ref, *refs):
    row_refs = refs[-2:] if split else refs[-1:]
    step = pl.program_id(0)
    for tile, pairs in enumerate(tiles):

        @pl.when(step == tile)
        def _():
            total = mm_tn(refs[pairs[0][0]][...], refs[pairs[0][1]][...])
            for left, right in pairs[1:]:
                total += mm_tn(refs[left][...], refs[right][...])
            put_rows(total, split, words_ref, row_refs)
            if sums is not None and tile == 0:
                refs[sums[1]][...] = jnp.sum(total * refs[sums[0]][...].astype(F32), axis=1, keepdims=True)


def weight_grad(split, words, groups, tile, tokens, weights=None):
    width = groups[0][0][0].shape[1]
    operands, specs, tiles = [words], [SCALAR], []
    first = 0
    for lefts, rights in groups:
        count = rights[0].shape[1] // tile
        base = len(operands) - 1
        for left in lefts:
            operands.append(left)
            specs.append(pl.BlockSpec((rights[0].shape[0], width), lambda i: (0, 0)))
        for right in rights:
            operands.append(right)
            specs.append(
                pl.BlockSpec(
                    (right.shape[0], tile),
                    lambda i, first=first, count=count: (0, jnp.clip(i - first, 0, count - 1)),
                )
            )
        tiles += [[(base + k, base + len(lefts) + k) for k in range(len(lefts))]] * count
        first += count
    sums = None
    out_specs, out_shapes = row_outputs(split, width, first * tile, tile)
    if weights is not None:
        operands.append(weights)
        specs.append(pl.BlockSpec((width, tile), lambda i: (0, 0)))
        sums = (len(operands) - 2, len(operands) - 1 + len(tokens))
        out_specs = [pl.BlockSpec((width, 1), lambda i: (0, 0))] + out_specs
        out_shapes = [jax.ShapeDtypeStruct((width, 1), F32)] + out_shapes
    return pl.pallas_call(
        functools.partial(weight_grad_kernel, split, tiles, sums),
        grid=(first,),
        in_specs=specs + [ANYWHERE] * len(tokens),
        out_specs=out_specs,
        out_shape=out_shapes,
        compiler_params=params(),
        cost_estimate=SMALL_COST,
        name="weight_grad",
    )(*operands, *tokens)


def join_kernel(pairs, *refs):
    for chip in range(refs[0].shape[1]):
        place = 0
        for k in range(pairs):
            keep_ref, got_ref = refs[2 * k], refs[2 * k + 1]
            width = keep_ref.shape[3]
            total = keep_ref[:, chip].astype(F32) + got_ref[:, chip].astype(F32)
            refs[-1][chip, :, :, place : place + width] = total.astype(BF16)
            place += width


def joined(pairs, tokens):
    seq_count, chips, rows, _ = pairs[0][0].shape
    cols = sum(keep.shape[3] for keep, _ in pairs)
    return pl.pallas_call(
        functools.partial(join_kernel, len(pairs)),
        in_specs=[WHOLE] * (2 * len(pairs)) + [ANYWHERE] * len(tokens),
        out_specs=WHOLE,
        out_shape=jax.ShapeDtypeStruct((chips, seq_count, rows, cols), BF16),
        compiler_params=pltpu.CompilerParams(vmem_limit_bytes=VMEM_BYTES),
        cost_estimate=SMALL_COST,
        name="joined",
    )(*[a for pair in pairs for a in pair], *tokens)


def layer_kernel(chunks, w_ref, low_ref, *refs):
    weights = w_ref[...].T
    count = low_ref.shape[0]
    refs[chunks][...] = mm(refs[0][...], weights).astype(BF16)
    for k in range(1, chunks):
        refs[chunks + k][:count, :] = low_ref[...]
        refs[chunks + k][count:, :] = mm(refs[k][...], weights).astype(BF16)


def layer_products(hiddens, weights, low):
    count, wide = hiddens[0].shape
    width = weights.shape[0]
    chunks = len(hiddens)
    rows = [count] + [2 * count] * (chunks - 1)
    return pl.pallas_call(
        functools.partial(layer_kernel, chunks),
        grid=(1,),
        in_specs=[
            pl.BlockSpec((width, wide), lambda i: (0, weights.shape[1] // wide - 1)),
            pl.BlockSpec((count, width), lambda i: (0, 0)),
        ]
        + [pl.BlockSpec((count, wide), lambda i: (0, 0))] * chunks,
        out_specs=[pl.BlockSpec((r, width), lambda i: (0, 0)) for r in rows],
        out_shape=[jax.ShapeDtypeStruct((r, width), BF16) for r in rows],
        compiler_params=params(),
        cost_estimate=SMALL_COST,
        name="layer_products",
    )(weights, low, *hiddens)


def position_kernel(heads, chunks, words_ref, lengths_ref, order_ref, decay_ref, *refs):
    col_ref, row_ref, place_ref, cum_ref = refs[-4:]
    total = order_ref.shape[1]
    count = total // chunks
    blocks, near = total // BLOCK, count // BLOCK
    rank = words_ref[2]
    ends = [lengths_ref[0]]
    for e in range(1, lengths_ref.shape[0]):
        ends.append(ends[-1] + lengths_ref[e])

    def segment(position):
        found = jnp.zeros(position.shape, jnp.int32)
        for end in ends:
            found += (position >= end).astype(jnp.int32)
        return jnp.where(position < 0, -1, found)

    for k in range(chunks):
        for h in range(heads):
            for b in range(near):
                value = jnp.zeros((1, BLOCK), F32)
                for part in range(3):
                    row = (part * heads + h) * near + b
                    value += decay_ref[k, row : row + 1, :].astype(F32)
                cum_ref[pl.ds(h * blocks + (rank ^ k) * near + b, 1), :] = value
    rows, cols = masks()
    upper = (rows <= cols).astype(F32)
    cums = jnp.dot(
        cum_ref[...], upper, precision=lax.Precision.HIGHEST, preferred_element_type=F32
    )
    order = order_ref[...]
    chunk = jnp.zeros_like(order)
    for k in range(1, chunks):
        chunk += (order >= k * count).astype(jnp.int32)
    place = (order + ((chunk ^ rank) - chunk) * count).astype(F32)
    place_ref[...] = place
    row_ref[...] = jnp.zeros_like(row_ref)
    lane = lax.broadcasted_iota(jnp.int32, (1, BLOCK), 1)
    for b in range(blocks):
        position = lane + b * BLOCK
        here = segment(position)
        low, high = jnp.full((1, BLOCK), b * BLOCK - 1), jnp.full((1, BLOCK), b * BLOCK + BLOCK - 1)
        keep_in = (here == segment(low)).astype(F32)
        keep_out = (here == segment(high)).astype(F32)
        found = [(segment(position - 3 + tap) == here).astype(F32) for tap in range(3)]
        found += [here.astype(F32), place[:, b * BLOCK : (b + 1) * BLOCK]]
        mine = [cums[h * blocks + b : h * blocks + b + 1, :] for h in range(heads)]
        found += mine
        found += [jnp.exp(c) * keep_in for c in mine]
        found += [jnp.exp(c[:, BLOCK - 1 :] - c) * keep_out for c in mine]
        found.append(jnp.zeros((128 - len(found), BLOCK), F32))
        col_ref[b * BLOCK : (b + 1) * BLOCK, :] = jnp.concatenate(found, 0).T
        for h in range(heads):
            row_ref[h : h + 1, b * BLOCK : (b + 1) * BLOCK] = mine[h]
        row_ref[heads : heads + 1, b * BLOCK : (b + 1) * BLOCK] = here.astype(F32)


def positions(words, lengths, order, decays, heads, tokens):
    total = order.shape[1]
    return pl.pallas_call(
        functools.partial(position_kernel, heads, decays.shape[0]),
        in_specs=[SCALAR, SCALAR, WHOLE, WHOLE] + [ANYWHERE] * len(tokens),
        out_specs=[WHOLE] * 3,
        out_shape=(
            jax.ShapeDtypeStruct((total, 128), F32),
            jax.ShapeDtypeStruct((8, total), F32),
            jax.ShapeDtypeStruct((1, total), F32),
        ),
        scratch_shapes=[pltpu.VMEM((heads * total // BLOCK, BLOCK), F32)],
        cost_estimate=SMALL_COST,
        compiler_params=pltpu.CompilerParams(vmem_limit_bytes=VMEM_BYTES),
        name="positions",
    )(words, lengths, order, decays, *tokens)


def out_rows_kernel(others, words_ref, mine_ref, normed_ref, *refs):
    out_ref, turned_ref = refs[-2:]
    core, chip = words_ref[0], words_ref[1]
    if others:
        chunks, chips, rows, _ = mine_ref.shape
        for k in range(chunks):
            for j in range(chips):
                device = k * 2 * chips + 2 * (chip ^ j)
                for ref, side in ((mine_ref, core), (refs[0], 1 - core)):
                    place = pl.ds(pl.multiple_of((device + side) * rows, rows), rows)
                    out_ref[place, :] = ref[k, j]
    else:
        out_ref[...] = mine_ref[...]
    turned_ref[...] = normed_ref[...].T


def out_rows(words, mine, others, normed, rows, tokens):
    return pl.pallas_call(
        functools.partial(out_rows_kernel, len(others)),
        in_specs=[SCALAR] + [WHOLE] * (2 + len(others)) + [ANYWHERE] * len(tokens),
        out_specs=[WHOLE] * 2,
        out_shape=(
            jax.ShapeDtypeStruct((rows, mine.shape[-1]), BF16),
            jax.ShapeDtypeStruct(normed.shape[::-1], BF16),
        ),
        compiler_params=pltpu.CompilerParams(vmem_limit_bytes=VMEM_BYTES),
        cost_estimate=SMALL_COST,
        name="out_rows",
    )(words, mine, normed, *others, *tokens)


def ffn_rows_kernel(words_ref, ffn_ref, *refs):
    width = ffn_ref.shape[0] * ffn_ref.shape[2]
    for k in range(ffn_ref.shape[1]):
        place = pl.ds(pl.multiple_of((words_ref[2] ^ k) * width, width), width)
        refs[-1][place, :] = ffn_ref[:, k].reshape(width, ffn_ref.shape[3])


def ffn_rows(words, ffn, tokens):
    return pl.pallas_call(
        ffn_rows_kernel,
        in_specs=[SCALAR, WHOLE] + [ANYWHERE] * len(tokens),
        out_specs=WHOLE,
        out_shape=jax.ShapeDtypeStruct((ffn.shape[0] * ffn.shape[1] * ffn.shape[2], ffn.shape[3]), BF16),
        compiler_params=pltpu.CompilerParams(vmem_limit_bytes=VMEM_BYTES),
        cost_estimate=SMALL_COST,
        name="ffn_rows",
    )(words, ffn, *tokens)


def out_project_kernel(chunks, rank_ref, x_ref, gain_ref, w_ref, *refs):
    residual_ref, mid_ref, all_ref = refs[-3:]
    rank = rank_ref[0]
    for k in range(chunks):
        width = refs[k].shape[1]
        all_ref[:, pl.ds(pl.multiple_of((rank ^ k) * width, width), width)] = refs[k][...]
    residual = x_ref[...].astype(F32) + mm_nt(all_ref[...], w_ref[...])
    residual_ref[...] = residual
    scale = lax.rsqrt(jnp.mean(residual * residual, axis=1, keepdims=True) + 1e-05)
    mid_ref[...] = (residual * scale * gain_ref[...]).astype(BF16)


def out_project(rank, x, gain, attn, weights):
    count, width = x.shape
    return pl.pallas_call(
        functools.partial(out_project_kernel, len(attn)),
        in_specs=[SCALAR] + [WHOLE] * (3 + len(attn)),
        out_specs=[WHOLE] * 2,
        out_shape=(
            jax.ShapeDtypeStruct((count, width), F32),
            jax.ShapeDtypeStruct((count, width), BF16),
        ),
        scratch_shapes=[pltpu.VMEM((count, weights.shape[1]), BF16)],
        compiler_params=pltpu.CompilerParams(vmem_limit_bytes=VMEM_BYTES),
        cost_estimate=SMALL_COST,
        name="out_project",
    )(rank, x, gain, weights, *attn)


def mid_back_kernel(chunks, handed, rank_ref, grad_ref, residual_ref, gain_ref, w_ref, *refs):
    parts = refs[:chunks]
    outs, all_ref = refs[chunks + handed :], refs[-1]
    res_grad_ref, low_ref, gain_grad_ref, chunk_refs = outs[0], outs[1], outs[2], outs[3 : 3 + chunks]
    rank = rank_ref[0]
    mid_grad = parts[0][...].astype(F32)
    for k in range(1, chunks):
        mid_grad += parts[k][...].astype(F32)
    residual = residual_ref[...]
    scale = lax.rsqrt(jnp.mean(residual * residual, axis=1, keepdims=True) + 1e-05)
    unit = residual * scale
    gain_grad_ref[...] = jnp.sum(mid_grad * unit, axis=0, keepdims=True)
    scaled = mid_grad * gain_ref[...]
    inner = jnp.mean(scaled * unit, axis=1, keepdims=True)
    res_grad = grad_ref[...].astype(F32) + scale * (scaled - unit * inner)
    res_grad_ref[...] = res_grad
    low = res_grad.astype(BF16)
    low_ref[...] = low
    all_ref[...] = mm(low, w_ref[...]).astype(BF16)
    for k in range(chunks):
        width = chunk_refs[k].shape[1]
        chunk_refs[k][...] = all_ref[:, pl.ds(pl.multiple_of((rank ^ k) * width, width), width)]


def mid_back(rank, grad, residual, gain, parts, weights, passed):
    count, width = residual.shape
    chunks = len(parts)
    wide = weights.shape[1]
    first = 5 + chunks
    outs = pl.pallas_call(
        functools.partial(mid_back_kernel, chunks, len(passed)),
        in_specs=[SCALAR] + [WHOLE] * (first - 1) + [ANYWHERE] * len(passed),
        out_specs=[WHOLE] * (3 + chunks) + [ANYWHERE] * len(passed),
        out_shape=[
            jax.ShapeDtypeStruct((count, width), F32),
            jax.ShapeDtypeStruct((count, width), BF16),
            jax.ShapeDtypeStruct((1, width), F32),
        ]
        + [jax.ShapeDtypeStruct((count, wide // chunks), BF16)] * chunks
        + [jax.ShapeDtypeStruct(p.shape, p.dtype) for p in passed],
        input_output_aliases={first + i: 3 + chunks + i for i in range(len(passed))},
        scratch_shapes=[pltpu.VMEM((count, wide), BF16)],
        compiler_params=pltpu.CompilerParams(vmem_limit_bytes=VMEM_BYTES),
        cost_estimate=SMALL_COST,
        name="mid_back",
    )(rank, grad, residual, gain, weights, *parts, *passed)
    return (*outs[:3], outs[3 : 3 + chunks], list(outs[3 + chunks :]))


def in_back_kernel(chunks, x_ref, res_grad_ref, gain_ref, *refs):
    x = x_ref[...].astype(F32)
    grad = refs[0][...].astype(F32)
    for k in range(1, chunks):
        grad += refs[k][...].astype(F32)
    scale = lax.rsqrt(jnp.mean(x * x, axis=1, keepdims=True) + 1e-05)
    unit = x * scale
    scaled = grad * gain_ref[...]
    inner = jnp.mean(scaled * unit, axis=1, keepdims=True)
    refs[-1][...] = (res_grad_ref[...] + scale * (scaled - unit * inner)).astype(BF16)


def in_back(x, res_grad, gain, parts, tokens):
    return pl.pallas_call(
        functools.partial(in_back_kernel, len(parts)),
        in_specs=[WHOLE] * (3 + len(parts)) + [ANYWHERE] * len(tokens),
        out_specs=WHOLE,
        out_shape=jax.ShapeDtypeStruct(x.shape, BF16),
        compiler_params=pltpu.CompilerParams(vmem_limit_bytes=VMEM_BYTES),
        cost_estimate=SMALL_COST,
        name="in_back",
    )(x, res_grad, gain, *parts, *tokens)


def swapped(value, axis, mask):
    devices = lax.axis_size(axis)
    return lax.ppermute(value, axis, [(i, i ^ mask) for i in range(devices)])


def pinned(value, other):
    return value + 0 * other[:1, :1].astype(value.dtype)


def spread(value):
    return [value] + [swapped(value, "seq", k) for k in range(1, lax.axis_size("seq"))]


def returned(chunks):
    return [chunks[0]] + [swapped(chunks[k], "seq", k) for k in range(1, len(chunks))]


class RowSum:
    def __init__(self, outs):
        self.outs = list(outs)

    def pair(self):
        if len(self.outs) == 2:
            self.got = swapped(self.outs[1], "mp", 1)

    def join(self, *tokens):
        seq_count, mp_count = lax.axis_size("seq"), lax.axis_size("mp")
        if len(self.outs) == 1:
            (grad,) = self.outs
            cols = grad.shape[1]
            parts = grad.astype(F32).reshape(seq_count, mp_count, -1, cols).transpose(1, 0, 2, 3)
            own = lax.psum_scatter(parts.reshape(-1, cols), "mp", scatter_dimension=0, tiled=True)
            self.half = grad
            self.parts = own.reshape(1, seq_count, -1, cols)
            return
        self.half = joined([(self.outs[0], self.got)], tokens)
        self.between()

    def between(self):
        mp_count = lax.axis_size("mp")
        groups = [list(range(core, mp_count, 2)) for core in range(2)]
        self.parts = lax.all_to_all(self.half, "mp", 0, 0, axis_index_groups=groups, tiled=True)

    def beside(self, other):
        if len(self.outs) == 1:
            both = RowSum([jnp.concatenate([self.outs[0], other.outs[0]], 1)])
            both.join()
            return both
        both = RowSum([])
        both.half = joined([(s.outs[0], s.got) for s in (self, other)], [])
        both.between()
        return both


def row_sums(sums, tokens):
    groups = [part.parts for part in sums]
    shape = groups[0].shape[1:3]
    cols = [group.shape[3] for group in groups]

    def kernel(*refs):
        place = 0
        for ref, width in zip(refs, cols):
            total = ref[0].astype(F32)
            for k in range(1, ref.shape[0]):
                total += ref[k].astype(F32)
            refs[-1][:, :, place : place + width] = total.astype(BF16)
            place = place + width

    return pl.pallas_call(
        kernel,
        in_specs=[WHOLE] * len(groups) + [ANYWHERE] * len(tokens),
        out_specs=WHOLE,
        out_shape=jax.ShapeDtypeStruct(shape + (sum(cols),), BF16),
        cost_estimate=SMALL_COST,
        compiler_params=pltpu.CompilerParams(vmem_limit_bytes=VMEM_BYTES),
        name="row_sums",
    )(*groups, *tokens)


def dealt(own):
    return lax.all_to_all(own, "seq", 0, 0, tiled=True)


def left_product(left, right):
    return lax.dot_general(
        left, right, (((0,), (0,)), ((), ())), preferred_element_type=jnp.float32
    )


def right_product(left, right):
    return lax.dot_general(
        left, right, (((1,), (1,)), ((), ())), preferred_element_type=jnp.float32
    )


def dot(left, right):
    return jnp.dot(left, right, preferred_element_type=jnp.float32)


def silu_slope(values):
    gate = jax.nn.sigmoid(values)
    return gate * (1.0 + values * (1.0 - gate))


def split_three(values):
    high = values.astype(BF16)
    rest = values - high.astype(F32)
    middle = rest.astype(BF16)
    return jnp.stack([high, middle, (rest - middle.astype(F32)).astype(BF16)])


def body(
    layer_in,
    out_grad,
    seq_lengths,
    dealing,
    log_decay,
    w_qkv,
    w_out_gate,
    w_beta,
    conv_w,
    gain_in,
    gain_o,
    w_out,
    gain_mid,
    w_gate_up,
    w_down,
):
    seq_count, mp_count = lax.axis_size("seq"), lax.axis_size("mp")
    rank, place_mp = lax.axis_index("seq"), lax.axis_index("mp")
    count = layer_in.shape[1]
    rows = w_qkv.shape[0]
    heads = HEAD_COUNT // seq_count
    key_cols, val_cols = heads * DK, heads * DV
    half = w_down.shape[0] // seq_count
    wide = -(-half // 256) * 256
    taps = conv_w.shape[1]
    total = dealing.shape[1]
    devices = seq_count * mp_count
    channels = 2 * key_cols + val_cols
    all_keys, ffn = HEAD_COUNT * DK, w_down.shape[0]
    split = (seq_count, mp_count // 2) if mp_count <= 8 else None
    words = jnp.stack([place_mp % 2, place_mp // 2, rank]).astype(jnp.int32)
    rank_word = rank.astype(jnp.int32).reshape(1)

    small = jnp.concatenate([conv_w.T.reshape(-1), gain_in, gain_mid, gain_o])
    small_count = small.shape[0]
    spare = 128 - heads
    filler = jnp.concatenate([small, jnp.zeros((rows * spare - small_count,), BF16)])
    filler = filler.reshape(rows, spare)
    wide_filler = jnp.zeros((rows, wide - half), BF16)
    turned_down = w_down.T
    decay_lanes = -(-3 * heads * count // (128 * rows)) * 128
    decays = split_three(log_decay[0].T)
    mix_cols = channels + 128 + val_cols
    pieces, ffn_pieces = [], []
    for j in range(seq_count):
        own_decay = decays[:, j * heads : (j + 1) * heads].reshape(-1)
        own_decay = jnp.concatenate(
            [own_decay, jnp.zeros((rows * decay_lanes - own_decay.shape[0],), BF16)]
        )
        pieces.append(
            jnp.concatenate(
                [
                    w_out_gate[:, j * val_cols : (j + 1) * val_cols],
                    w_qkv[:, j * key_cols : (j + 1) * key_cols],
                    w_qkv[:, all_keys + j * key_cols : all_keys + (j + 1) * key_cols],
                    w_qkv[:, 2 * all_keys + j * val_cols : 2 * all_keys + (j + 1) * val_cols],
                    w_beta[:, j * heads : (j + 1) * heads],
                    filler,
                    own_decay.reshape(rows, decay_lanes),
                ],
                1,
            )
        )
        ffn_pieces.append(
            jnp.concatenate(
                [
                    w_gate_up[:, j * half : (j + 1) * half],
                    wide_filler,
                    w_gate_up[:, ffn + j * half : ffn + (j + 1) * half],
                    wide_filler,
                    turned_down[:, j * half : (j + 1) * half],
                    wide_filler,
                ],
                1,
            )
        )
    def near(arrays):
        arrays = jnp.stack(arrays)
        return jnp.stack(
            returned(
                [lax.dynamic_index_in_dim(arrays, rank ^ k, 0, keepdims=False) for k in range(seq_count)]
            )
        )

    pieces = near([jnp.concatenate(p, 1) for p in zip(pieces, ffn_pieces)])
    ffn_pieces = pieces[:, :, -3 * wide :]
    gathered = lax.all_gather(pieces[:, :, :mix_cols], "mp", axis=0, tiled=False)
    chunks_in = spread(layer_in[0] + 0 * pieces[1, :1, :1])

    relative = rank ^ jnp.arange(seq_count)
    smalls = gathered[:, :, :, mix_cols - spare :].transpose(1, 0, 2, 3)
    smalls = jnp.take(smalls, relative, axis=0).reshape(devices, -1)[:, :small_count]
    own_taps = conv_w.shape[0] * taps
    full_conv = smalls[:, :own_taps].reshape(-1, taps, conv_w.shape[0]).transpose(1, 0, 2)
    full_conv = full_conv.reshape(taps, -1).astype(F32)
    conv = jnp.concatenate(
        [
            lax.dynamic_slice_in_dim(full_conv, rank * key_cols, key_cols, 1),
            lax.dynamic_slice_in_dim(full_conv, all_keys + rank * key_cols, key_cols, 1),
            lax.dynamic_slice_in_dim(full_conv, 2 * all_keys + rank * val_cols, val_cols, 1),
        ],
        1,
    )
    conv = jnp.concatenate([conv, jnp.zeros((8 - taps, channels), F32)], 0)
    gains = smalls[:, own_taps:].astype(F32)
    full_gin = gains[:, :rows].reshape(1, -1)
    full_gmid = gains[:, rows : 2 * rows].reshape(1, -1)
    full_go = gains[:, 2 * rows :].reshape(1, -1)

    out_turned = w_out.T
    out_near = []
    if split:
        out_near = [out_turned] + [swapped(out_turned, "mp", 2 * j) for j in range(1, mp_count // 2)]

    decays = pieces[:, :, mix_cols : -3 * wide].reshape(seq_count, -1)[:, : 3 * heads * count]
    col_info, row_info, place_row = positions(
        words, seq_lengths[0], dealing, decays.reshape(seq_count, -1, BLOCK), heads, out_near[1:]
    )

    passed = [ffn_pieces, out_grad[0] + 0 * pieces[1, :1, :1]]
    if split:
        passed.append(jnp.broadcast_to(jnp.stack(out_near), (seq_count, mp_count // 2, *out_turned.shape)))
    passed = handed(passed, chunks_in[1:] + [row_info])
    ffn_all = lax.all_gather(passed[0], "mp", axis=0, tiled=False)
    chunks_grad = spread(passed[1])
    out_mine = [lax.all_to_all(passed[2], "seq", 0, 0, tiled=True)] if split else []
    (normed, gate_logit, proj, logit_parts, mix), _ = project(
        rank_word, chunks_in, full_gin, gathered, col_info, channels,
        [], [conv, full_go, full_gmid],
    )
    outs = forward_recurrence(proj, conv, col_info, row_info, logit_parts, heads, [])
    dealt_rows, attn, out_mine = gate_rows(
        outs[0], place_row, gate_logit, full_go, count, heads, out_mine, chunks_grad[1:]
    )
    if split:
        out_others = [swapped(out_mine[0], "mp", 1)]
    else:
        out_mine, out_others = [lax.all_gather(out_turned, ("seq", "mp"), axis=0, tiled=True)], []
    attn_parts = returned(attn)
    out_w, normed_t = out_rows(words, out_mine[0], out_others, normed, devices * rows, [attn[0]])

    residual, mid_own = out_project(rank_word, layer_in[0], full_gmid, attn_parts, out_w)

    ffn_w = ffn_rows(words, ffn_all, [mid_own])
    w_gu, down_turned = ffn_w[:, : 2 * wide], ffn_w[:, 2 * wide :]
    mids = spread(mid_own)
    hiddens, gu_grads, mid_parts = ([None] * seq_count for _ in range(3))
    last_part = None
    for k in (0, 1, 3, 2):
        mid_k = mids[k] if last_part is None else pinned(mids[k], last_part)
        gate_up = dot(mid_k, w_gu)
        gate, up = gate_up[:, :wide], gate_up[:, wide:]
        hiddens[k] = (silu(gate) * up).astype(BF16)
        hidden_grad = dot(chunks_grad[k], down_turned)
        gu_grads[k] = jnp.concatenate(
            [hidden_grad * up * silu_slope(gate), hidden_grad * silu(gate)], 1
        ).astype(BF16)
        mid_parts[k] = last_part = right_product(gu_grads[k], w_gu).astype(BF16)
    mid_parts = returned(mid_parts)
    ffn_sum = RowSum(
        weight_grad(
            split, words, [(mids, gu_grads), (chunks_grad, hiddens)], wide, [last_part, mid_parts[1]]
        ),
    )
    res_grad, out_proj_grad, g_mid, attn_grads, ffn_sum.outs[-1:] = mid_back(
        rank_word, out_grad[0], residual, full_gmid, mid_parts, out_w, ffn_sum.outs[-1:]
    )
    attn_grads = returned(attn_grads)
    ffn_sum.pair()
    layer_own, *both = layer_products(hiddens, ffn_w, out_proj_grad)

    (gate_grad, o_grad, g_go), both = ungate_rows(
        dealt_rows, col_info, gate_logit, full_go, attn_grads, heads, both, []
    )
    ffn_sum.join(gate_grad)
    both = returned([None] + both)[1:]
    proj_grad, g_conv = backward_recurrence(
        proj, conv, col_info, row_info, logit_parts, outs[1:], o_grad, heads, [ffn_sum.half]
    )
    mix_grad, mix_sums, *mix_outs = unpack(
        split, words, proj_grad, gate_grad, place_row, normed_t, mix, g_conv, full_gin, g_mid, g_go,
        heads, [],
    )
    mix_sum = RowSum(mix_outs)
    mix_sum.pair()
    out_sum = RowSum(
        weight_grad(split, words, [([out_proj_grad] + both, attn)], val_cols, [mix_grad])
    )
    out_sum.pair()
    last_sum = mix_sum.beside(out_sum)
    normed_parts, _ = unproject(mix_grad, mix, count, [], [last_sum.half])
    normed_chunks = returned(normed_parts)
    in_grad = in_back(layer_in[0], res_grad, full_gin, normed_chunks, [])
    layer_out = residual + sum(
        c.astype(F32) for c in [layer_own] + [b[count:] for b in both]
    )
    all_pieces = dealt(row_sums([ffn_sum, last_sum], [in_grad]))
    ffn_pieces, all_pieces = all_pieces[:, :, : 3 * wide], all_pieces[:, :, 3 * wide :]
    gate_pieces, mix_pieces = all_pieces[:, :, :val_cols], all_pieces[:, :, val_cols:-val_cols]
    out_pieces = all_pieces[:, :, -val_cols:]

    def columns(pieces, first, width):
        parts = [pieces[j, :, first : first + width] for j in range(seq_count)]
        return jnp.concatenate(parts, 1).astype(F32)

    if split:
        small_sum = jnp.sum(mix_pieces[:, :, channels + 128 :].astype(F32), axis=0)
        device = rank * mp_count + place_mp
        grad_conv = small_sum[:taps].T
        grad_go = lax.dynamic_slice_in_dim(
            small_sum[4:6].reshape(-1), device * gain_o.shape[0], gain_o.shape[0]
        )
        grad_gmid = lax.dynamic_slice_in_dim(small_sum[8:16].reshape(-1), device * rows, rows)
        grad_gin = lax.dynamic_slice_in_dim(small_sum[16:24].reshape(-1), device * rows, rows)
    else:
        everywhere = ("seq", "mp")
        conv_full = jnp.zeros((taps, conv_w.shape[0] * devices), F32)
        for first, width in ((0, key_cols), (key_cols, key_cols), (2 * key_cols, val_cols)):
            conv_full = lax.dynamic_update_slice_in_dim(
                conv_full,
                g_conv[:taps, first : first + width],
                first * seq_count + rank * width,
                1,
            )
        grad_conv = lax.psum_scatter(conv_full.T, everywhere, scatter_dimension=0, tiled=True)
        g_gin = mix_sums[:, 0] / full_gin[0]
        grad_gin, grad_gmid, grad_go = (
            lax.psum_scatter(g, everywhere, scatter_dimension=0, tiled=True)
            for g in (g_gin, g_mid[0], g_go[0])
        )
    grad_qkv = jnp.concatenate(
        [
            columns(mix_pieces, 0, key_cols),
            columns(mix_pieces, key_cols, key_cols),
            columns(mix_pieces, 2 * key_cols, val_cols),
        ],
        1,
    )
    return (
        layer_out.astype(BF16)[None],
        in_grad[None],
        grad_qkv,
        columns(gate_pieces, 0, val_cols),
        columns(mix_pieces, channels, heads),
        grad_conv,
        grad_gin,
        grad_go,
        columns(out_pieces, 0, val_cols).T,
        grad_gmid,
        jnp.concatenate([columns(ffn_pieces, 0, half), columns(ffn_pieces, wide, half)], 1),
        columns(ffn_pieces, 2 * wide, half).T,
    )


def solution(mesh):
    in_specs = (
        P("mp", "seq", None),
        P("mp", "seq", None),
        P("mp", None),
        P("mp", None),
        P("mp", "seq", None),
        P(("seq", "mp"), None),
        P(("seq", "mp"), None),
        P(("seq", "mp"), None),
        P(("seq", "mp"), None),
        P(("seq", "mp")),
        P(("seq", "mp")),
        P(None, ("seq", "mp")),
        P(("seq", "mp")),
        P(("seq", "mp"), None),
        P(None, ("seq", "mp")),
    )
    out_specs = (
        P("mp", "seq", None),
        P("mp", "seq", None),
        P(("seq", "mp"), None),
        P(("seq", "mp"), None),
        P(("seq", "mp"), None),
        P(("seq", "mp"), None),
        P(("seq", "mp")),
        P(("seq", "mp")),
        P(None, ("seq", "mp")),
        P(("seq", "mp")),
        P(("seq", "mp"), None),
        P(None, ("seq", "mp")),
    )
    return jax.shard_map(body, mesh=mesh, in_specs=in_specs, out_specs=out_specs, check_vma=False)
```

```python
import functools

import jax
import jax.numpy as jnp
from jax import lax
from jax.experimental import pallas as pl
from jax.experimental.pallas import tpu as pltpu
from jax.sharding import PartitionSpec as P

HEAD_COUNT = 8
DK = 128
DV = 256
BLOCK = 128
FORWARD_STEP = 6
BACKWARD_STEP = 2
F32 = jnp.float32
BF16 = jnp.bfloat16


def mm(left, right):
    return jnp.dot(left.astype(BF16), right.astype(BF16), preferred_element_type=F32)


def mm_nt(left, right):
    return lax.dot_general(
        left.astype(BF16),
        right.astype(BF16),
        (((1,), (1,)), ((), ())),
        preferred_element_type=F32,
    )


def mm_tn(left, right):
    return lax.dot_general(
        left.astype(BF16),
        right.astype(BF16),
        (((0,), (0,)), ((), ())),
        preferred_element_type=F32,
    )


def masks():
    rows = lax.broadcasted_iota(jnp.int32, (BLOCK, BLOCK), 0)
    cols = lax.broadcasted_iota(jnp.int32, (BLOCK, BLOCK), 1)
    return rows, cols


def unit_inverses(mats, rows, cols):
    ident = (rows == cols).astype(F32)
    near = (rows // 16) == (cols // 16)
    power = [jnp.where(near, a, 0.0) for a in mats]
    result = [ident - p for p in power]
    span = 2
    while span < 16:
        power = [mm(p, p) for p in power]
        result = [t + mm(t, p) for t, p in zip(result, power)]
        span *= 2
    size = 16
    while size < BLOCK:
        off = ((rows // (2 * size)) == (cols // (2 * size))) & ((rows // size) != (cols // size))
        reach = [mm(jnp.where(off, a, 0.0), t) for a, t in zip(mats, result)]
        result = [t - mm(t, x) for t, x in zip(result, reach)]
        size *= 2
    return result


def convolve(ext_ref, conv_ref, col_ref, start, first, width):
    cols = pl.ds(first, width)
    total = ext_ref[pl.ds(16 + start, BLOCK), cols] * conv_ref[3:4, cols]
    for tap in range(3):
        keep = col_ref[pl.ds(start, BLOCK), tap : tap + 1]
        total += ext_ref[pl.ds(13 + tap + start, BLOCK), cols] * keep * conv_ref[tap : tap + 1, cols]
    return total


def column(col_ref, start, index):
    return col_ref[pl.ds(start, BLOCK), index : index + 1]


def strength(logit_ref, start, head, heads):
    return jax.nn.sigmoid(column(logit_ref, start, head))


def exact_nt(left, right):
    left_high, right_high = left.astype(BF16), right.astype(BF16)
    left_low = left - left_high.astype(F32)
    right_low = right - right_high.astype(F32)
    return mm_nt(left_high, right_high) + (mm_nt(left_high, right_low) + mm_nt(left_low, right_high))


def decay_matrix(col_ref, row_ref, start, head, heads, rows, cols):
    cum_i = column(col_ref, start, 5 + head)
    cum_j = row_ref[head : head + 1, pl.ds(start, BLOCK)]
    seg_i = column(col_ref, start, 3)
    seg_j = row_ref[heads : heads + 1, pl.ds(start, BLOCK)]
    within = (rows >= cols) & (seg_i == seg_j)
    return jnp.where(within, jnp.exp(jnp.where(within, cum_i - cum_j, 0.0)), 0.0)


def silu(values):
    return values * jax.nn.sigmoid(values)


def forward_kernel(
    heads, edge_ref, proj_ref, conv_ref, col_ref, row_ref, logit_ref, *refs,
):
    o_ref, s_ref, n_ref, t_ref, w_ref, p_ref, pre_ref, ext_ref, state_ref = refs[-9:]
    steps = proj_ref.shape[0] // BLOCK

    @pl.when(pl.program_id(0) == 0)
    def _():
        state_ref[...] = jnp.zeros_like(state_ref)

    ext_ref[:16, :] = edge_ref[...].astype(F32)
    ext_ref[16:, :] = proj_ref[...].astype(F32)
    rows, cols = masks()
    strict = rows > cols
    units = [(g, h) for g in range(steps) for h in range(heads)]
    queries, keys, values, mats, decays, betas = {}, {}, {}, [], {}, {}
    for g, h in units:
        start = g * BLOCK

        def taken(first, width):
            value = convolve(ext_ref, conv_ref, col_ref, start, first, width)
            pre_ref[pl.ds(start, BLOCK), first : first + width] = value
            return value

        queries[g, h] = silu(taken(h * DK, DK))
        raw = silu(taken((heads + h) * DK, DK))
        keys[g, h] = raw * lax.rsqrt(jnp.sum(raw * raw, axis=1, keepdims=True) + 1e-06)
        values[g, h] = silu(taken(2 * heads * DK + h * DV, DV))
        decays[g, h] = decay_matrix(col_ref, row_ref, start, h, heads, rows, cols)
        betas[g, h] = strength(logit_ref, start, h, heads)
        beta = betas[g, h]
        inner = mm_nt(keys[g, h], keys[g, h])
        mats.append(jnp.where(strict, beta * inner * decays[g, h], 0.0))
    inverses = unit_inverses(mats, rows, cols)
    umats, wmats, pmats, boundary, reads = {}, {}, {}, {}, {}
    for (g, h), inverse in zip(units, inverses):
        start = g * BLOCK
        beta = betas[g, h]
        elog = column(col_ref, start, 5 + heads + h)
        flog = column(col_ref, start, 5 + 2 * heads + h)
        inverse = inverse.astype(BF16)
        t_ref[g, h] = inverse
        umats[g, h] = mm(inverse, beta * values[g, h])
        wmats[g, h] = mm(inverse, (beta * elog) * keys[g, h]).astype(BF16)
        w_ref[g, h] = wmats[g, h]
        pmats[g, h] = (exact_nt(queries[g, h], keys[g, h]) * decays[g, h]).astype(BF16)
        p_ref[g, h] = pmats[g, h]
        boundary[g, h] = (keys[g, h] * flog).T.astype(BF16)
        reads[g, h] = (queries[g, h] * elog).astype(BF16)
    for g in range(steps):
        start = g * BLOCK
        for h in range(heads):
            state = state_ref[h]
            low = state.astype(BF16)
            s_ref[g, h] = low
            news = (umats[g, h] - mm(wmats[g, h], low)).astype(BF16)
            n_ref[g, h] = news
            carried = col_ref[pl.ds(start + BLOCK - 1, 1), 5 + heads + h : 6 + heads + h]
            state_ref[h] = carried * state + mm(boundary[g, h], news)
            output = mm(reads[g, h], low) + mm(pmats[g, h], news)
            o_ref[pl.ds(start, BLOCK), h * DV : (h + 1) * DV] = output.astype(BF16)


def backward_kernel(
    heads, edge_ref, proj_ref, conv_ref, col_ref, row_ref, logit_ref,
    s_ref, n_ref, t_ref, w_ref, p_ref, pre_ref, do_ref, *refs,
):
    grad_ref, gconv_ref, ext_ref, shift_ref, dstate_ref, head_ref = refs[-6:]
    count = proj_ref.shape[0]
    steps = count // BLOCK
    channels = proj_ref.shape[1]

    @pl.when(pl.program_id(0) == 0)
    def _():
        dstate_ref[...] = jnp.zeros_like(dstate_ref)
        head_ref[...] = jnp.zeros_like(head_ref)
        gconv_ref[...] = jnp.zeros_like(gconv_ref)

    ext_ref[:16, :] = edge_ref[...].astype(F32)
    ext_ref[16:, :] = proj_ref[...].astype(F32)
    for tap in range(3):
        shift_ref[tap, count : count + 8, :] = head_ref[tap]
    rows, cols = masks()
    strict = rows > cols
    units = [(g, h) for g in reversed(range(steps)) for h in range(heads)]
    queries, keys, pre, reads, first, gains = {}, {}, {}, {}, {}, {}
    for g, h in units:
        start = g * BLOCK

        def taken(first, width):
            return pre_ref[pl.ds(start, BLOCK), first : first + width]

        elog = column(col_ref, start, 5 + heads + h)
        out_grad = do_ref[pl.ds(start, BLOCK), h * DV : (h + 1) * DV]
        queries[g, h] = silu(taken(h * DK, DK))
        raw = silu(taken((heads + h) * DK, DK))
        scale = lax.rsqrt(jnp.sum(raw * raw, axis=1, keepdims=True) + 1e-06)
        keys[g, h] = (raw * scale, scale)
        first[g, h] = mm_tn(p_ref[g, h], out_grad)
        gains[g, h] = mm_tn(queries[g, h] * elog, out_grad)
    news_grads, state_grads = {}, {}
    for g in reversed(range(steps)):
        start = g * BLOCK
        for h in range(heads):
            flog = column(col_ref, start, 5 + 2 * heads + h)
            dstate = dstate_ref[h]
            low = dstate.astype(BF16)
            state_grads[g, h] = low
            news_grad = (first[g, h] + mm(keys[g, h][0] * flog, low)).astype(BF16)
            news_grads[g, h] = news_grad
            carried = col_ref[pl.ds(start + BLOCK - 1, 1), 5 + heads + h : 6 + heads + h]
            dstate_ref[h] = gains[g, h] + carried * dstate - mm_tn(w_ref[g, h], news_grad)
    lane = lax.broadcasted_iota(jnp.int32, (BLOCK, 128), 1)

    def through_conv(g, first_col, width, grad):
        start = g * BLOCK
        cols_ = pl.ds(first_col, width)
        value = pre_ref[pl.ds(start, BLOCK), first_col : first_col + width]
        gate = jax.nn.sigmoid(value)
        grad = grad * (gate * (1.0 + value * (1.0 - gate)))
        shift_ref[3, pl.ds(start, BLOCK), cols_] = grad * conv_ref[3:4, cols_]
        sums = []
        for tap in range(3):
            kept = grad * col_ref[pl.ds(start, BLOCK), tap : tap + 1]
            shift_ref[tap, pl.ds(start, BLOCK), cols_] = kept * conv_ref[tap : tap + 1, cols_]
            sums.append(
                jnp.sum(kept * ext_ref[pl.ds(13 + tap + start, BLOCK), cols_], axis=0, keepdims=True)
            )
        sums.append(
            jnp.sum(grad * ext_ref[pl.ds(16 + start, BLOCK), cols_], axis=0, keepdims=True)
        )
        for tap in range(4):
            gconv_ref[tap : tap + 1, cols_] += sums[tap]

    logit_grads = {}
    for g, h in units:
        start = g * BLOCK
        beta = strength(logit_ref, start, h, heads)
        elog = column(col_ref, start, 5 + heads + h)
        flog = column(col_ref, start, 5 + 2 * heads + h)
        key, scale = keys[g, h]
        query = queries[g, h]
        out_grad = do_ref[pl.ds(start, BLOCK), h * DV : (h + 1) * DV]
        decay = decay_matrix(col_ref, row_ref, start, h, heads, rows, cols)
        key_low = key.astype(BF16)
        inner = mm_nt(key_low, key_low) * decay
        news, state, dstate = n_ref[g, h], s_ref[g, h], state_grads[g, h]
        rhs_grad = mm_tn(t_ref[g, h], news_grads[g, h])
        rhs_low = rhs_grad.astype(BF16)
        within = (mm_nt(out_grad, news) * decay).astype(BF16)
        mat_grad = jnp.where(strict, -mm_nt(rhs_low, news), 0.0)
        pair = (mat_grad * beta * decay).astype(BF16)
        back = mm_nt(rhs_low, state)
        q_grad = mm(within, key_low) + elog * mm_nt(out_grad, state)
        k_grad = (
            mm_tn(within, query)
            + mm(pair, key_low)
            + mm_tn(pair, key_low)
            + flog * mm_nt(news, dstate)
            - (beta * elog) * back
        )
        value = silu(pre_ref[pl.ds(start, BLOCK), pl.ds(2 * heads * DK + h * DV, DV)])
        beta_grad = (
            jnp.sum(mat_grad * inner - elog * (key * back), axis=1, keepdims=True)
            + jnp.sum(rhs_grad * value, axis=1, keepdims=True)
        )
        logit_grads[g, h] = beta_grad * beta * (1.0 - beta)
        raw_grad = scale * (k_grad - key * jnp.sum(k_grad * key, axis=1, keepdims=True))
        through_conv(g, h * DK, DK, q_grad)
        through_conv(g, (heads + h) * DK, DK, raw_grad)
        through_conv(g, 2 * heads * DK + h * DV, DV, beta * rhs_grad)
    for g in range(steps):
        total = jnp.zeros((BLOCK, 128), F32)
        for h in range(heads):
            total = jnp.where(lane == h, logit_grads[g, h], total)
        grad_ref[pl.ds(g * BLOCK, BLOCK), channels : channels + 128] = total.astype(BF16)
        grad_ref[pl.ds(g * BLOCK, BLOCK), channels + 128 :] = jnp.zeros((BLOCK, 128), BF16)
    total = shift_ref[3, :count, :]
    for tap in range(3):
        total += shift_ref[tap, pl.ds(3 - tap, count), :]
    grad_ref[:, :channels] = total.astype(BF16)
    for tap in range(3):
        head_ref[tap] = shift_ref[tap, :8, :]


def saved_shapes(blocks, heads):
    return (
        jax.ShapeDtypeStruct((blocks, heads, DK, DV), BF16),
        jax.ShapeDtypeStruct((blocks, heads, BLOCK, DV), BF16),
        jax.ShapeDtypeStruct((blocks, heads, BLOCK, BLOCK), BF16),
        jax.ShapeDtypeStruct((blocks, heads, BLOCK, DK), BF16),
        jax.ShapeDtypeStruct((blocks, heads, BLOCK, BLOCK), BF16),
        jax.ShapeDtypeStruct((blocks * BLOCK, heads * (2 * DK + DV)), F32),
    )


def saved_specs(shapes, per_step, index):
    return [
        pl.BlockSpec((per_step,) + shape.shape[1:], lambda i: (index(i), 0, 0, 0))
        for shape in shapes[:-1]
    ] + [pl.BlockSpec((per_step * BLOCK, shapes[-1].shape[1]), lambda i: (index(i), 0))]


def common_specs(step, channels, logits, index):
    return [
        pl.BlockSpec((16, channels), lambda i: (jnp.maximum(index(i) * (step // 16) - 1, 0), 0)),
        pl.BlockSpec((step, channels), lambda i: (index(i), 0)),
        pl.BlockSpec((8, channels), lambda i: (0, 0)),
        pl.BlockSpec((step, 128), lambda i: (index(i), 0)),
        pl.BlockSpec((8, step), lambda i: (0, index(i))),
        pl.BlockSpec((step, logits), lambda i: (index(i), 0)),
    ]


MIB = 1024 * 1024
VMEM_BYTES = 24 * MIB
SMALL_COST = pl.CostEstimate(flops=10**6, bytes_accessed=10**6, transcendentals=0)
ANYWHERE = pl.BlockSpec(memory_space=pl.ANY)
WHOLE = pl.BlockSpec(memory_space=pltpu.VMEM)
SCALAR = pl.BlockSpec(memory_space=pltpu.SMEM)


def params(limit=VMEM_BYTES):
    return pltpu.CompilerParams(dimension_semantics=("arbitrary",), vmem_limit_bytes=limit)


def forward_recurrence(proj, conv, cols, rows, logits, heads, tokens):
    count, channels = proj.shape
    step = BLOCK * FORWARD_STEP
    shapes = saved_shapes(count // BLOCK, heads)
    index = lambda i: i
    return pl.pallas_call(
        functools.partial(forward_kernel, heads),
        grid=(count // step,),
        in_specs=common_specs(step, channels, 128, index) + [ANYWHERE] * len(tokens),
        out_specs=[pl.BlockSpec((step, heads * DV), lambda i: (i, 0))] + saved_specs(shapes, FORWARD_STEP, index),
        out_shape=(jax.ShapeDtypeStruct((count, heads * DV), BF16),) + shapes,
        scratch_shapes=[
            pltpu.VMEM((step + 16, channels), F32),
            pltpu.VMEM((heads, DK, DV), F32),
        ],
        compiler_params=params(56 * MIB),
        cost_estimate=SMALL_COST,
        name="recurrence_forward",
    )(proj, proj, conv, cols, rows, logits, *tokens)


def backward_recurrence(proj, conv, cols, rows, logits, saved, out_grad, heads, tokens):
    count, channels = proj.shape
    step = BLOCK * BACKWARD_STEP
    last = count // step - 1
    index = lambda i: last - i
    return pl.pallas_call(
        functools.partial(backward_kernel, heads),
        grid=(count // step,),
        in_specs=common_specs(step, channels, 128, index)
        + saved_specs(saved, BACKWARD_STEP, index)
        + [pl.BlockSpec((step, heads * DV), lambda i: (index(i), 0))]
        + [ANYWHERE] * len(tokens),
        out_specs=[
            pl.BlockSpec((step, channels + 256), lambda i: (index(i), 0)),
            pl.BlockSpec((8, channels), lambda i: (0, 0)),
        ],
        out_shape=(
            jax.ShapeDtypeStruct((count, channels + 256), BF16),
            jax.ShapeDtypeStruct((8, channels), F32),
        ),
        scratch_shapes=[
            pltpu.VMEM((step + 16, channels), F32),
            pltpu.VMEM((4, step + 8, channels), F32),
            pltpu.VMEM((heads, DK, DV), F32),
            pltpu.VMEM((3, 8, channels), F32),
        ],
        compiler_params=params(56 * MIB),
        cost_estimate=SMALL_COST,
        name="recurrence_backward",
    )(proj, proj, conv, cols, rows, logits, *saved, out_grad, *tokens)


def project_kernel(
    channels, chunks, handed, rank_ref, gain_ref, w_ref, col_ref, *refs
):
    x_refs = refs[:chunks]
    normed_ref, gate_ref, proj_ref, logit_ref, all_ref = refs[chunks + handed : chunks + handed + 5]
    rows_ref = refs[-1]
    step = pl.program_id(0)
    count = x_refs[0].shape[0]

    @pl.when(step == 0)
    def _():
        width = w_ref.shape[0] * w_ref.shape[2]
        for k in range(w_ref.shape[1]):
            place = pl.ds(pl.multiple_of((rank_ref[0] ^ k) * width, width), width)
            all_ref[place, :] = w_ref[:, k].reshape(width, w_ref.shape[3])

    for k in range(chunks):

        @pl.when(step == k)
        def _():
            x = x_refs[k][...].astype(F32)
            scale = lax.rsqrt(jnp.mean(x * x, axis=1, keepdims=True) + 1e-05)
            normed = (x * scale * gain_ref[...]).astype(BF16)
            normed_ref[...] = normed
            total = mm(normed, all_ref[...])
            gates = gate_ref.shape[1]
            gate_ref[...] = total[:, :gates]
            logit = total[:, gates + channels :]
            high = logit.astype(BF16)
            place = slice(k * count, (k + 1) * count)
            rows_ref[place, : channels + 128] = total[:, gates:].astype(BF16)
            rows_ref[place, channels + 128 :] = (logit - high.astype(F32)).astype(BF16)

    @pl.when(step >= chunks)
    def _():
        order = lax.broadcasted_iota(jnp.int32, (proj_ref.shape[0], rows_ref.shape[0]), 1)
        picked = (col_ref[:, 4:5].astype(jnp.int32) == order).astype(F32)
        packed = mm(picked, rows_ref[...])
        proj_ref[...] = packed[:, :channels].astype(BF16)
        logit_ref[...] = packed[:, channels : channels + 128] + packed[:, channels + 128 :]


def project(rank, x_chunks, gain, weights, cols, channels, passed, tokens):
    count, width = x_chunks[0].shape
    total = count * len(x_chunks)
    gates = weights.shape[3] - channels - 128
    chunks = total // count
    block = 256
    first = lambda i: jnp.minimum(i, chunks - 1)
    later = lambda i: jnp.maximum(i - chunks, 0)
    outs = pl.pallas_call(
        functools.partial(project_kernel, channels, chunks, len(passed) + len(tokens)),
        grid=(chunks + total // block,),
        in_specs=[
            SCALAR,
            pl.BlockSpec((1, width), lambda i: (0, 0)),
            pl.BlockSpec(weights.shape, lambda i: (0, 0, 0, 0)),
            pl.BlockSpec((block, 128), lambda i: (later(i), 0)),
        ]
        + [pl.BlockSpec((count, width), lambda i: (0, 0))] * chunks
        + [ANYWHERE] * (len(passed) + len(tokens)),
        out_specs=[
            pl.BlockSpec((count, width), lambda i: (first(i), 0)),
            pl.BlockSpec((count, gates), lambda i: (first(i), 0)),
            pl.BlockSpec((block, channels), lambda i: (later(i), 0)),
            pl.BlockSpec((block, 128), lambda i: (later(i), 0)),
            pl.BlockSpec((width, weights.shape[3]), lambda i: (0, 0)),
        ]
        + [ANYWHERE] * len(passed),
        out_shape=[
            jax.ShapeDtypeStruct((total, width), BF16),
            jax.ShapeDtypeStruct((total, gates), F32),
            jax.ShapeDtypeStruct((total, channels), BF16),
            jax.ShapeDtypeStruct((total, 128), F32),
            jax.ShapeDtypeStruct((width, weights.shape[3]), BF16),
        ]
        + [jax.ShapeDtypeStruct(p.shape, p.dtype) for p in passed],
        input_output_aliases={4 + chunks + i: 5 + i for i in range(len(passed))},
        scratch_shapes=[pltpu.VMEM((total, channels + 256), BF16)],
        compiler_params=params(56 * MIB),
        cost_estimate=SMALL_COST,
        name="project",
    )(rank, gain, weights, cols, *x_chunks, *passed, *tokens)
    return outs[:5], outs[5:]


def gate_kernel(heads, count, first, o_ref, place_ref, gate_ref, gain_ref, *refs):
    chunks = place_ref.shape[1] // count
    dealt_ref, chunk_refs = refs[first], refs[first + 1 : first + 1 + chunks]
    for k, chunk_ref in enumerate(chunk_refs):
        order = lax.broadcasted_iota(jnp.int32, (count, o_ref.shape[0]), 0) + k * count
        picked = (place_ref[...].astype(jnp.int32) == order).astype(F32)
        rows = mm(picked, o_ref[...])
        place = pl.ds(k * count, count)
        dealt_ref[place, :] = rows.astype(BF16)
        for h in range(heads):
            lanes = slice(h * DV, (h + 1) * DV)
            value = rows[:, lanes]
            scale = lax.rsqrt(jnp.mean(value * value, axis=1, keepdims=True) + 1e-05)
            gated = value * scale * gain_ref[...] * silu(gate_ref[place, lanes])
            chunk_ref[:, lanes] = gated.astype(BF16)


def gate_rows(output, place, gate_logit, gain, count, heads, passed, tokens):
    total, cols = output.shape
    chunks = total // count
    others = len(passed) + len(tokens)
    outs = pl.pallas_call(
        functools.partial(gate_kernel, heads, count, others),
        in_specs=[WHOLE] * 4 + [ANYWHERE] * others,
        out_specs=[WHOLE] * (chunks + 1) + [ANYWHERE] * len(passed),
        out_shape=[jax.ShapeDtypeStruct((total, cols), BF16)]
        + [jax.ShapeDtypeStruct((count, cols), BF16)] * chunks
        + [jax.ShapeDtypeStruct(a.shape, a.dtype) for a in passed],
        input_output_aliases={4 + i: 1 + chunks + i for i in range(len(passed))},
        compiler_params=pltpu.CompilerParams(vmem_limit_bytes=VMEM_BYTES),
        cost_estimate=SMALL_COST,
        name="gate_rows",
    )(output, place, gate_logit, gain, *passed, *tokens)
    return outs[0], outs[1 : 1 + chunks], outs[1 + chunks :]


def ungate_kernel(heads, chunks, outs, dealt_ref, col_ref, gate_ref, gain_ref, *refs):
    grad_refs = refs[:chunks]
    gate_grad_ref, o_grad_ref, gain_grad_ref, rows_ref = *refs[outs : outs + 3], refs[-1]
    count = grad_refs[0].shape[0]
    total = dealt_ref.shape[0]
    sums = jnp.zeros((1, DV), F32)
    for k in range(chunks):
        place = pl.ds(k * count, count)
        for h in range(heads):
            lanes = slice(h * DV, (h + 1) * DV)
            value = dealt_ref[place, lanes].astype(F32)
            grad = grad_refs[k][:, lanes].astype(F32)
            logit = gate_ref[place, lanes]
            scale = lax.rsqrt(jnp.mean(value * value, axis=1, keepdims=True) + 1e-05)
            unit = value * scale
            gate = jax.nn.sigmoid(logit)
            slid = logit * gate
            sums += jnp.sum(grad * unit * slid, axis=0, keepdims=True)
            grad = grad * gain_ref[...]
            slope = gate * (1.0 + logit * (1.0 - gate))
            gate_grad_ref[place, lanes] = (grad * unit * slope).astype(BF16)
            grad = grad * slid
            inner = jnp.mean(grad * unit, axis=1, keepdims=True)
            rows_ref[place, lanes] = (scale * (grad - unit * inner)).astype(BF16)
    gain_grad_ref[...] = sums
    for k in range(chunks):
        place = pl.ds(k * count, count)
        order = lax.broadcasted_iota(jnp.int32, (count, total), 1)
        picked = (col_ref[place, 4:5].astype(jnp.int32) == order).astype(F32)
        o_grad_ref[place, :] = mm(picked, rows_ref[...]).astype(BF16)


def ungate_rows(dealt_rows, cols, gate_logit, gain, grads, heads, passed, tokens):
    total, width = dealt_rows.shape
    whole = pl.BlockSpec(memory_space=pltpu.VMEM)
    first = 4 + len(grads)
    outs = pl.pallas_call(
        functools.partial(ungate_kernel, heads, len(grads), len(grads) + len(passed) + len(tokens)),
        in_specs=[whole] * first + [ANYWHERE] * (len(passed) + len(tokens)),
        out_specs=[whole] * 3 + [ANYWHERE] * len(passed),
        out_shape=[
            jax.ShapeDtypeStruct((total, width), BF16),
            jax.ShapeDtypeStruct((total, width), BF16),
            jax.ShapeDtypeStruct((1, DV), F32),
        ]
        + [jax.ShapeDtypeStruct(p.shape, p.dtype) for p in passed],
        input_output_aliases={first + i: 3 + i for i in range(len(passed))},
        scratch_shapes=[pltpu.VMEM((total, width), BF16)],
        compiler_params=pltpu.CompilerParams(vmem_limit_bytes=VMEM_BYTES),
        cost_estimate=SMALL_COST,
        name="ungate_rows",
    )(dealt_rows, cols, gate_logit, gain, *grads, *passed, *tokens)
    return outs[:3], list(outs[3:])


def turned_sums(values):
    sums = jnp.sum(values, axis=1, keepdims=True)
    return jnp.broadcast_to(sums, (values.shape[0], 128)).T[:1]


def put_rows(total, split, core_ref, refs):
    total = total.astype(BF16)
    if split is None:
        refs[0][...] = total
        return
    halves = total.reshape(*split, 2, -1, total.shape[1])
    for core in range(2):

        @pl.when(core_ref[0] == core)
        def _():
            refs[0][...] = halves[:, :, core]
            refs[1][...] = halves[:, :, 1 - core]


def row_outputs(split, width, cols, tile):
    if split is None:
        shape, block = (width, cols), (width, tile)
        spec = pl.BlockSpec(block, lambda i: (0, i))
        return [spec], [jax.ShapeDtypeStruct(shape, BF16)]
    shape = (*split, width // (2 * split[0] * split[1]))
    spec = pl.BlockSpec((*shape, tile), lambda i: (0, 0, 0, i))
    return [spec] * 2, [jax.ShapeDtypeStruct((*shape, cols), BF16)] * 2


def unpack_kernel(split, heads, words_ref, grad_ref, gates_ref, place_ref, normed_ref, w_ref, conv_ref, gain_ref, mid_ref, o_ref, first_sums_ref, *refs):
    count = 2 if split else 1
    dealt_ref, sums_ref = refs[-4 - count], refs[-3 - count]
    row_refs, small_ref, picked_ref = refs[-2 - count : -2], refs[-2], refs[-1]
    step = pl.program_id(0)
    total = grad_ref.shape[0]
    gates = gates_ref.shape[1]
    tile = grad_ref.shape[1] // 2

    @pl.when(step == 0)
    def _():
        part = 256
        for k in range(total // part):
            order = lax.broadcasted_iota(jnp.int32, (part, total), 0) + k * part
            picked = (place_ref[...].astype(jnp.int32) == order).astype(F32)
            picked_ref[k * part : (k + 1) * part, :] = picked.astype(BF16)
        dealt_ref[:, :gates] = gates_ref[...]
        dealt_ref[:, gates : gates + tile] = mm(picked_ref[...], grad_ref[:, :tile]).astype(BF16)
        share = mm(normed_ref[...], dealt_ref[:, gates : gates + tile])
        weights = w_ref[:, gates : gates + tile].astype(F32)
        sums_ref[...] = first_sums_ref[...] + turned_sums(share * weights)
        put_rows(share, split, words_ref, row_refs)

    @pl.when(step == 1)
    def _():
        dealt_ref[:, gates + tile :] = mm(picked_ref[...], grad_ref[:, tile:]).astype(BF16)
        share = mm(normed_ref[...], dealt_ref[:, gates + tile :])
        used = w_ref.shape[1] - gates - tile
        weights = w_ref[:, gates + tile :].astype(F32)
        sums_ref[...] += turned_sums(share[:, :used] * weights)
        if split:
            devices, rows = 2 * split[0] * split[1], share.shape[0] // (2 * split[0] * split[1])
            gin = sums_ref[...] / gain_ref[...]
            small_ref[...] = jnp.zeros_like(small_ref)
            gin = jnp.concatenate([gin[:, j * 128 : (j + 1) * 128] for j in range(8)], 0)
            mid = jnp.concatenate([mid_ref[:, j * 128 : (j + 1) * 128] for j in range(8)], 0)
            for d in range(devices):
                small_ref[d * rows + 4 : d * rows + 5, :] = o_ref[:, :128]
                small_ref[d * rows + 5 : d * rows + 6, :] = o_ref[:, 128:]
                small_ref[d * rows + 8 : d * rows + 16, :] = mid
                small_ref[d * rows + 16 : d * rows + 24, :] = gin
            rank = words_ref[2]
            keys = heads * DK // 128
            vals = heads * DV // 128
            owners = [rank * keys + j for j in range(keys)]
            owners += [HEAD_COUNT * DK // 128 + rank * keys + j for j in range(keys)]
            owners += [2 * HEAD_COUNT * DK // 128 + rank * vals + j for j in range(vals)]
            for j, owner in enumerate(owners):
                place = pl.ds(pl.multiple_of(owner * rows, rows), 8)
                old = small_ref[place, :]
                taps = lax.broadcasted_iota(jnp.int32, (8, 128), 0) < 4
                small_ref[place, :] = jnp.where(taps, conv_ref[:, j * 128 : (j + 1) * 128], old)
            share = jnp.concatenate([share[:, :-128], small_ref[...]], 1)
        put_rows(share, split, words_ref, row_refs)


def unpack(split, words, grad, gate_grad, place, normed, weights, g_conv, gain, g_mid, g_o, sums, heads, tokens):
    total = grad.shape[0]
    cols = grad.shape[1] + gate_grad.shape[1]
    width = normed.shape[0]
    operands = (grad, gate_grad, place, normed, weights, g_conv, gain, g_mid, g_o, sums)
    specs, shapes = row_outputs(split, width, grad.shape[1], grad.shape[1] // 2)
    return pl.pallas_call(
        functools.partial(unpack_kernel, split, heads),
        grid=(2,),
        in_specs=[SCALAR]
        + [pl.BlockSpec(a.shape, lambda i: (0, 0)) for a in operands]
        + [ANYWHERE] * len(tokens),
        out_specs=[
            pl.BlockSpec((total, cols), lambda i: (0, 0)),
            pl.BlockSpec((1, width), lambda i: (0, 0)),
        ]
        + specs,
        out_shape=[
            jax.ShapeDtypeStruct((total, cols), BF16),
            jax.ShapeDtypeStruct((1, width), F32),
        ]
        + shapes,
        scratch_shapes=[pltpu.VMEM((width, 128), F32), pltpu.VMEM((total, total), BF16)],
        compiler_params=params(),
        cost_estimate=SMALL_COST,
        name="unpack",
    )(words, *operands, *tokens)


def unproject_kernel(chunks, first, grad_ref, w_ref, *refs):
    part_refs, turned_ref = refs[first : first + chunks], refs[-1]
    step = pl.program_id(0)

    @pl.when(step == 0)
    def _():
        turned_ref[...] = w_ref[...].T

    part = mm(grad_ref[:, : turned_ref.shape[0]], turned_ref[...])
    for k in range(chunks):

        @pl.when(step == k)
        def _():
            part_refs[k][...] = part.astype(BF16)


def unproject(grad, weights, count, passed, tokens):
    total, cols = grad.shape
    width = weights.shape[0]
    chunks = total // count
    outs = pl.pallas_call(
        functools.partial(unproject_kernel, chunks, len(passed) + len(tokens)),
        grid=(chunks,),
        in_specs=[
            pl.BlockSpec((count, cols), lambda i: (i, 0)),
            pl.BlockSpec(weights.shape, lambda i: (0, 0)),
        ]
        + [ANYWHERE] * (len(passed) + len(tokens)),
        out_specs=[pl.BlockSpec((count, width), lambda i: (0, 0))] * chunks
        + [ANYWHERE] * len(passed),
        out_shape=[jax.ShapeDtypeStruct((count, width), BF16)] * chunks
        + [jax.ShapeDtypeStruct(p.shape, p.dtype) for p in passed],
        input_output_aliases={2 + i: chunks + i for i in range(len(passed))},
        scratch_shapes=[pltpu.VMEM(weights.shape[::-1], BF16)],
        compiler_params=params(56 * MIB),
        cost_estimate=SMALL_COST,
        name="unproject",
    )(grad, weights, *passed, *tokens)
    return list(outs[:chunks]), list(outs[chunks:])


def hand_kernel(*refs):
    refs[-1][...] = jnp.zeros_like(refs[-1])


def handed(passed, tokens):
    outs = pl.pallas_call(
        hand_kernel,
        in_specs=[ANYWHERE] * (len(passed) + len(tokens)),
        out_specs=[ANYWHERE] * len(passed) + [WHOLE],
        out_shape=[jax.ShapeDtypeStruct(p.shape, p.dtype) for p in passed]
        + [jax.ShapeDtypeStruct((8, 128), F32)],
        input_output_aliases={i: i for i in range(len(passed))},
        cost_estimate=SMALL_COST,
        name="handed",
    )(*passed, *tokens)
    return outs[:-1]


def weight_grad_kernel(split, tiles, sums, words_ref, *refs):
    row_refs = refs[-2:] if split else refs[-1:]
    step = pl.program_id(0)
    for tile, pairs in enumerate(tiles):

        @pl.when(step == tile)
        def _():
            total = mm_tn(refs[pairs[0][0]][...], refs[pairs[0][1]][...])
            for left, right in pairs[1:]:
                total += mm_tn(refs[left][...], refs[right][...])
            put_rows(total, split, words_ref, row_refs)
            if sums is not None and tile == 0:
                refs[sums[1]][...] = turned_sums(total * refs[sums[0]][...].astype(F32))


def weight_grad(split, words, groups, tile, tokens, weights=None, limit=VMEM_BYTES):
    width = groups[0][0][0].shape[1]
    operands, specs, tiles = [words], [SCALAR], []
    first = 0
    for lefts, rights in groups:
        count = rights[0].shape[1] // tile
        base = len(operands) - 1
        for left in lefts:
            operands.append(left)
            specs.append(pl.BlockSpec((rights[0].shape[0], width), lambda i: (0, 0)))
        for right in rights:
            operands.append(right)
            specs.append(
                pl.BlockSpec(
                    (right.shape[0], tile),
                    lambda i, first=first, count=count: (0, jnp.clip(i - first, 0, count - 1)),
                )
            )
        tiles += [[(base + k, base + len(lefts) + k) for k in range(len(lefts))]] * count
        first += count
    sums = None
    out_specs, out_shapes = row_outputs(split, width, first * tile, tile)
    if weights is not None:
        operands.append(weights)
        specs.append(pl.BlockSpec((width, tile), lambda i: (0, 0)))
        sums = (len(operands) - 2, len(operands) - 1 + len(tokens))
        out_specs = [pl.BlockSpec((1, width), lambda i: (0, 0))] + out_specs
        out_shapes = [jax.ShapeDtypeStruct((1, width), F32)] + out_shapes
    return pl.pallas_call(
        functools.partial(weight_grad_kernel, split, tiles, sums),
        grid=(first,),
        in_specs=specs + [ANYWHERE] * len(tokens),
        out_specs=out_specs,
        out_shape=out_shapes,
        compiler_params=params(limit),
        cost_estimate=SMALL_COST,
        name="weight_grad",
    )(*operands, *tokens)


def join_kernel(pairs, *refs):
    for chip in range(refs[0].shape[1]):
        place = 0
        for k in range(pairs):
            keep_ref, got_ref = refs[2 * k], refs[2 * k + 1]
            width = keep_ref.shape[3]
            total = keep_ref[:, chip].astype(F32) + got_ref[:, chip].astype(F32)
            refs[-1][chip, :, :, place : place + width] = total.astype(BF16)
            place += width


def joined(pairs, tokens):
    seq_count, chips, rows, _ = pairs[0][0].shape
    cols = sum(keep.shape[3] for keep, _ in pairs)
    return pl.pallas_call(
        functools.partial(join_kernel, len(pairs)),
        in_specs=[WHOLE] * (2 * len(pairs)) + [ANYWHERE] * len(tokens),
        out_specs=WHOLE,
        out_shape=jax.ShapeDtypeStruct((chips, seq_count, rows, cols), BF16),
        compiler_params=pltpu.CompilerParams(vmem_limit_bytes=VMEM_BYTES),
        cost_estimate=SMALL_COST,
        name="joined",
    )(*[a for pair in pairs for a in pair], *tokens)


def layer_kernel(chunks, w_ref, low_ref, *refs):
    weights = w_ref[...].T
    count = low_ref.shape[0]
    refs[chunks][...] = mm(refs[0][...], weights).astype(BF16)
    for k in range(1, chunks):
        refs[chunks + k][:count, :] = low_ref[...]
        refs[chunks + k][count:, :] = mm(refs[k][...], weights).astype(BF16)


def layer_products(hiddens, weights, low):
    count, wide = hiddens[0].shape
    width = weights.shape[0]
    chunks = len(hiddens)
    rows = [count] + [2 * count] * (chunks - 1)
    return pl.pallas_call(
        functools.partial(layer_kernel, chunks),
        grid=(1,),
        in_specs=[
            pl.BlockSpec((width, wide), lambda i: (0, weights.shape[1] // wide - 1)),
            pl.BlockSpec((count, width), lambda i: (0, 0)),
        ]
        + [pl.BlockSpec((count, wide), lambda i: (0, 0))] * chunks,
        out_specs=[pl.BlockSpec((r, width), lambda i: (0, 0)) for r in rows],
        out_shape=[jax.ShapeDtypeStruct((r, width), BF16) for r in rows],
        compiler_params=params(),
        cost_estimate=SMALL_COST,
        name="layer_products",
    )(weights, low, *hiddens)


def position_kernel(heads, chunks, words_ref, lengths_ref, order_ref, decay_ref, *refs):
    col_ref, row_ref, place_ref, cum_ref = refs[-4:]
    total = order_ref.shape[1]
    count = total // chunks
    blocks, near = total // BLOCK, count // BLOCK
    rank = words_ref[2]
    ends = [lengths_ref[0]]
    for e in range(1, lengths_ref.shape[0]):
        ends.append(ends[-1] + lengths_ref[e])

    def segment(position):
        found = jnp.zeros(position.shape, jnp.int32)
        for end in ends:
            found += (position >= end).astype(jnp.int32)
        return jnp.where(position < 0, -1, found)

    for k in range(chunks):
        for h in range(heads):
            for b in range(near):
                value = jnp.zeros((1, BLOCK), F32)
                for part in range(3):
                    row = (part * heads + h) * near + b
                    value += decay_ref[k, row : row + 1, :].astype(F32)
                cum_ref[pl.ds(h * blocks + (rank ^ k) * near + b, 1), :] = value
    rows, cols = masks()
    upper = (rows <= cols).astype(F32)
    cums = jnp.dot(
        cum_ref[...], upper, precision=lax.Precision.HIGHEST, preferred_element_type=F32
    )
    order = order_ref[...]
    chunk = jnp.zeros_like(order)
    for k in range(1, chunks):
        chunk += (order >= k * count).astype(jnp.int32)
    place = (order + ((chunk ^ rank) - chunk) * count).astype(F32)
    place_ref[...] = place
    row_ref[...] = jnp.zeros_like(row_ref)
    lane = lax.broadcasted_iota(jnp.int32, (1, BLOCK), 1)
    for b in range(blocks):
        position = lane + b * BLOCK
        here = segment(position)
        low, high = jnp.full((1, BLOCK), b * BLOCK - 1), jnp.full((1, BLOCK), b * BLOCK + BLOCK - 1)
        keep_in = (here == segment(low)).astype(F32)
        keep_out = (here == segment(high)).astype(F32)
        found = [(segment(position - 3 + tap) == here).astype(F32) for tap in range(3)]
        found += [here.astype(F32), place[:, b * BLOCK : (b + 1) * BLOCK]]
        mine = [cums[h * blocks + b : h * blocks + b + 1, :] for h in range(heads)]
        found += mine
        found += [jnp.exp(c) * keep_in for c in mine]
        found += [jnp.exp(c[:, BLOCK - 1 :] - c) * keep_out for c in mine]
        found.append(jnp.zeros((128 - len(found), BLOCK), F32))
        col_ref[b * BLOCK : (b + 1) * BLOCK, :] = jnp.concatenate(found, 0).T
        for h in range(heads):
            row_ref[h : h + 1, b * BLOCK : (b + 1) * BLOCK] = mine[h]
        row_ref[heads : heads + 1, b * BLOCK : (b + 1) * BLOCK] = here.astype(F32)


def positions(words, lengths, order, decays, heads, tokens):
    total = order.shape[1]
    return pl.pallas_call(
        functools.partial(position_kernel, heads, decays.shape[0]),
        in_specs=[SCALAR, SCALAR, WHOLE, WHOLE] + [ANYWHERE] * len(tokens),
        out_specs=[WHOLE] * 3,
        out_shape=(
            jax.ShapeDtypeStruct((total, 128), F32),
            jax.ShapeDtypeStruct((8, total), F32),
            jax.ShapeDtypeStruct((1, total), F32),
        ),
        scratch_shapes=[pltpu.VMEM((heads * total // BLOCK, BLOCK), F32)],
        cost_estimate=SMALL_COST,
        compiler_params=pltpu.CompilerParams(vmem_limit_bytes=VMEM_BYTES),
        name="positions",
    )(words, lengths, order, decays, *tokens)


def out_rows_kernel(others, words_ref, mine_ref, normed_ref, *refs):
    out_ref, turned_ref = refs[-2:]
    core, chip = words_ref[0], words_ref[1]
    if others:
        chunks, chips, rows, _ = mine_ref.shape
        for k in range(chunks):
            for j in range(chips):
                device = k * 2 * chips + 2 * (chip ^ j)
                for ref, side in ((mine_ref, core), (refs[0], 1 - core)):
                    place = pl.ds(pl.multiple_of((device + side) * rows, rows), rows)
                    out_ref[place, :] = ref[k, j]
    else:
        out_ref[...] = mine_ref[...]
    turned_ref[...] = normed_ref[...].T


def out_rows(words, mine, others, normed, rows, tokens):
    return pl.pallas_call(
        functools.partial(out_rows_kernel, len(others)),
        in_specs=[SCALAR] + [WHOLE] * (2 + len(others)) + [ANYWHERE] * len(tokens),
        out_specs=[WHOLE] * 2,
        out_shape=(
            jax.ShapeDtypeStruct((rows, mine.shape[-1]), BF16),
            jax.ShapeDtypeStruct(normed.shape[::-1], BF16),
        ),
        compiler_params=pltpu.CompilerParams(vmem_limit_bytes=VMEM_BYTES),
        cost_estimate=SMALL_COST,
        name="out_rows",
    )(words, mine, normed, *others, *tokens)


def ffn_rows_kernel(words_ref, ffn_ref, *refs):
    width = ffn_ref.shape[0] * ffn_ref.shape[2]
    for k in range(ffn_ref.shape[1]):
        place = pl.ds(pl.multiple_of((words_ref[2] ^ k) * width, width), width)
        refs[-1][place, :] = ffn_ref[:, k].reshape(width, ffn_ref.shape[3])


def ffn_rows(words, ffn, tokens):
    return pl.pallas_call(
        ffn_rows_kernel,
        in_specs=[SCALAR, WHOLE] + [ANYWHERE] * len(tokens),
        out_specs=WHOLE,
        out_shape=jax.ShapeDtypeStruct((ffn.shape[0] * ffn.shape[1] * ffn.shape[2], ffn.shape[3]), BF16),
        compiler_params=pltpu.CompilerParams(vmem_limit_bytes=VMEM_BYTES),
        cost_estimate=SMALL_COST,
        name="ffn_rows",
    )(words, ffn, *tokens)


def out_project_kernel(chunks, rank_ref, x_ref, gain_ref, w_ref, *refs):
    residual_ref, mid_ref, all_ref = refs[-3:]
    rank = rank_ref[0]
    for k in range(chunks):
        width = refs[k].shape[1]
        all_ref[:, pl.ds(pl.multiple_of((rank ^ k) * width, width), width)] = refs[k][...]
    residual = x_ref[...].astype(F32) + mm_nt(all_ref[...], w_ref[...])
    residual_ref[...] = residual
    scale = lax.rsqrt(jnp.mean(residual * residual, axis=1, keepdims=True) + 1e-05)
    mid_ref[...] = (residual * scale * gain_ref[...]).astype(BF16)


def out_project(rank, x, gain, attn, weights):
    count, width = x.shape
    return pl.pallas_call(
        functools.partial(out_project_kernel, len(attn)),
        in_specs=[SCALAR] + [WHOLE] * (3 + len(attn)),
        out_specs=[WHOLE] * 2,
        out_shape=(
            jax.ShapeDtypeStruct((count, width), F32),
            jax.ShapeDtypeStruct((count, width), BF16),
        ),
        scratch_shapes=[pltpu.VMEM((count, weights.shape[1]), BF16)],
        compiler_params=pltpu.CompilerParams(vmem_limit_bytes=VMEM_BYTES),
        cost_estimate=SMALL_COST,
        name="out_project",
    )(rank, x, gain, weights, *attn)


def mid_back_kernel(chunks, handed, rank_ref, grad_ref, residual_ref, gain_ref, w_ref, *refs):
    parts = refs[:chunks]
    outs, all_ref = refs[chunks + handed :], refs[-1]
    res_grad_ref, low_ref, gain_grad_ref, chunk_refs = outs[0], outs[1], outs[2], outs[3 : 3 + chunks]
    rank = rank_ref[0]
    mid_grad = parts[0][...].astype(F32)
    for k in range(1, chunks):
        mid_grad += parts[k][...].astype(F32)
    residual = residual_ref[...]
    scale = lax.rsqrt(jnp.mean(residual * residual, axis=1, keepdims=True) + 1e-05)
    unit = residual * scale
    gain_grad_ref[...] = jnp.sum(mid_grad * unit, axis=0, keepdims=True)
    scaled = mid_grad * gain_ref[...]
    inner = jnp.mean(scaled * unit, axis=1, keepdims=True)
    res_grad = grad_ref[...].astype(F32) + scale * (scaled - unit * inner)
    res_grad_ref[...] = res_grad
    low = res_grad.astype(BF16)
    low_ref[...] = low
    all_ref[...] = mm(low, w_ref[...]).astype(BF16)
    for k in range(chunks):
        width = chunk_refs[k].shape[1]
        chunk_refs[k][...] = all_ref[:, pl.ds(pl.multiple_of((rank ^ k) * width, width), width)]


def mid_back(rank, grad, residual, gain, parts, weights, passed):
    count, width = residual.shape
    chunks = len(parts)
    wide = weights.shape[1]
    first = 5 + chunks
    outs = pl.pallas_call(
        functools.partial(mid_back_kernel, chunks, len(passed)),
        in_specs=[SCALAR] + [WHOLE] * (first - 1) + [ANYWHERE] * len(passed),
        out_specs=[WHOLE] * (3 + chunks) + [ANYWHERE] * len(passed),
        out_shape=[
            jax.ShapeDtypeStruct((count, width), F32),
            jax.ShapeDtypeStruct((count, width), BF16),
            jax.ShapeDtypeStruct((1, width), F32),
        ]
        + [jax.ShapeDtypeStruct((count, wide // chunks), BF16)] * chunks
        + [jax.ShapeDtypeStruct(p.shape, p.dtype) for p in passed],
        input_output_aliases={first + i: 3 + chunks + i for i in range(len(passed))},
        scratch_shapes=[pltpu.VMEM((count, wide), BF16)],
        compiler_params=pltpu.CompilerParams(vmem_limit_bytes=VMEM_BYTES),
        cost_estimate=SMALL_COST,
        name="mid_back",
    )(rank, grad, residual, gain, weights, *parts, *passed)
    return (*outs[:3], outs[3 : 3 + chunks], list(outs[3 + chunks :]))


def in_back_kernel(chunks, x_ref, res_grad_ref, gain_ref, *refs):
    x = x_ref[...].astype(F32)
    grad = refs[0][...].astype(F32)
    for k in range(1, chunks):
        grad += refs[k][...].astype(F32)
    scale = lax.rsqrt(jnp.mean(x * x, axis=1, keepdims=True) + 1e-05)
    unit = x * scale
    scaled = grad * gain_ref[...]
    inner = jnp.mean(scaled * unit, axis=1, keepdims=True)
    refs[-1][...] = (res_grad_ref[...] + scale * (scaled - unit * inner)).astype(BF16)


def in_back(x, res_grad, gain, parts, tokens):
    return pl.pallas_call(
        functools.partial(in_back_kernel, len(parts)),
        in_specs=[WHOLE] * (3 + len(parts)) + [ANYWHERE] * len(tokens),
        out_specs=WHOLE,
        out_shape=jax.ShapeDtypeStruct(x.shape, BF16),
        compiler_params=pltpu.CompilerParams(vmem_limit_bytes=VMEM_BYTES),
        cost_estimate=SMALL_COST,
        name="in_back",
    )(x, res_grad, gain, *parts, *tokens)


def swapped(value, axis, mask):
    devices = lax.axis_size(axis)
    return lax.ppermute(value, axis, [(i, i ^ mask) for i in range(devices)])


def pinned(value, other):
    return value + 0 * other[:1, :1].astype(value.dtype)


def spread(value):
    return [value] + [swapped(value, "seq", k) for k in range(1, lax.axis_size("seq"))]


def returned(chunks):
    return [chunks[0]] + [swapped(chunks[k], "seq", k) for k in range(1, len(chunks))]


class RowSum:
    def __init__(self, outs):
        self.outs = list(outs)

    def pair(self):
        if len(self.outs) == 2:
            self.got = swapped(self.outs[1], "mp", 1)

    def join(self, *tokens):
        seq_count, mp_count = lax.axis_size("seq"), lax.axis_size("mp")
        if len(self.outs) == 1:
            (grad,) = self.outs
            cols = grad.shape[1]
            parts = grad.astype(F32).reshape(seq_count, mp_count, -1, cols).transpose(1, 0, 2, 3)
            own = lax.psum_scatter(parts.reshape(-1, cols), "mp", scatter_dimension=0, tiled=True)
            self.half = grad
            self.parts = own.reshape(1, seq_count, -1, cols)
            return
        self.half = joined([(self.outs[0], self.got)], tokens)
        self.between()

    def between(self):
        mp_count = lax.axis_size("mp")
        groups = [list(range(core, mp_count, 2)) for core in range(2)]
        self.parts = lax.all_to_all(self.half, "mp", 0, 0, axis_index_groups=groups, tiled=True)

    def beside(self, other):
        if len(self.outs) == 1:
            both = RowSum([jnp.concatenate([self.outs[0], other.outs[0]], 1)])
            both.join()
            return both
        both = RowSum([])
        both.half = joined([(s.outs[0], s.got) for s in (self, other)], [])
        both.between()
        return both


def row_sums(sums, tokens):
    groups = [part.parts for part in sums]
    shape = groups[0].shape[1:3]
    cols = [group.shape[3] for group in groups]

    def kernel(*refs):
        place = 0
        for ref, width in zip(refs, cols):
            total = ref[0].astype(F32)
            for k in range(1, ref.shape[0]):
                total += ref[k].astype(F32)
            refs[-1][:, :, place : place + width] = total.astype(BF16)
            place = place + width

    return pl.pallas_call(
        kernel,
        in_specs=[WHOLE] * len(groups) + [ANYWHERE] * len(tokens),
        out_specs=WHOLE,
        out_shape=jax.ShapeDtypeStruct(shape + (sum(cols),), BF16),
        cost_estimate=SMALL_COST,
        compiler_params=pltpu.CompilerParams(vmem_limit_bytes=VMEM_BYTES),
        name="row_sums",
    )(*groups, *tokens)


def finish_kernel(heads, wide, half, rows, pieces_ref, *refs):
    qkv_ref, gate_ref, beta_ref, conv_ref, out_ref, gu_ref, down_ref, small_ref = refs
    chunks = pieces_ref.shape[0]
    keys, vals = heads * DK, heads * DV
    ffn, mix = 0, 3 * wide
    gate_first, first, out_first = mix, mix + vals, pieces_ref.shape[2] - vals

    def piece(j, start, width):
        return pieces_ref[j, :, start : start + width].astype(F32)

    for j in range(chunks):
        gate_ref[:, j * vals : (j + 1) * vals] = piece(j, gate_first, vals)
        qkv_ref[:, j * keys : (j + 1) * keys] = piece(j, first, keys)
        place = chunks * keys + j * keys
        qkv_ref[:, place : place + keys] = piece(j, first + keys, keys)
        place = 2 * chunks * keys + j * vals
        qkv_ref[:, place : place + vals] = piece(j, first + 2 * keys, vals)
        out_ref[j * vals : (j + 1) * vals, :] = piece(j, out_first, vals).T
        down_ref[j * half : (j + 1) * half, :] = piece(j, ffn + 2 * wide, wide).T[:half]
        beta = piece(j, first + 2 * keys + vals, 128)
        beta_ref[:, j * heads : (j + 1) * heads] = beta[:, :heads]
    small = piece(0, out_first - 128, 128)
    for j in range(1, chunks):
        small += piece(j, out_first - 128, 128)
    small_ref[...] = small
    conv_ref[...] = small.T[:, : conv_ref.shape[1]]
    for part in range(2):
        whole = jnp.concatenate(
            [piece(j, ffn + part * wide, wide)[:, :half] for j in range(chunks)], 1
        )
        gu_ref[:, part * chunks * half : (part + 1) * chunks * half] = whole


def finish(pieces, heads, wide, half, taps):
    chunks, rows, _ = pieces.shape
    keys, vals = HEAD_COUNT * DK, HEAD_COUNT * DV
    ffn = chunks * half
    shapes = [(rows, 2 * keys + vals), (rows, vals), (rows, HEAD_COUNT), (128, taps)]
    shapes += [(vals, rows), (rows, 2 * ffn), (ffn, rows), (rows, 128)]
    return pl.pallas_call(
        functools.partial(finish_kernel, heads, wide, half, rows),
        in_specs=[WHOLE],
        out_specs=[WHOLE] * len(shapes),
        out_shape=[jax.ShapeDtypeStruct(shape, F32) for shape in shapes],
        compiler_params=pltpu.CompilerParams(vmem_limit_bytes=VMEM_BYTES),
        cost_estimate=SMALL_COST,
        name="finish",
    )(pieces)


def dealt(own):
    return lax.all_to_all(own, "seq", 0, 0, tiled=True)


def left_product(left, right):
    return lax.dot_general(
        left, right, (((0,), (0,)), ((), ())), preferred_element_type=jnp.float32
    )


def right_product(left, right):
    return lax.dot_general(
        left, right, (((1,), (1,)), ((), ())), preferred_element_type=jnp.float32
    )


def dot(left, right):
    return jnp.dot(left, right, preferred_element_type=jnp.float32)


def silu_slope(values):
    gate = jax.nn.sigmoid(values)
    return gate * (1.0 + values * (1.0 - gate))


def split_three(values):
    high = values.astype(BF16)
    rest = values - high.astype(F32)
    middle = rest.astype(BF16)
    return jnp.stack([high, middle, (rest - middle.astype(F32)).astype(BF16)])


def body(
    layer_in,
    out_grad,
    seq_lengths,
    dealing,
    log_decay,
    w_qkv,
    w_out_gate,
    w_beta,
    conv_w,
    gain_in,
    gain_o,
    w_out,
    gain_mid,
    w_gate_up,
    w_down,
):
    seq_count, mp_count = lax.axis_size("seq"), lax.axis_size("mp")
    rank, place_mp = lax.axis_index("seq"), lax.axis_index("mp")
    count = layer_in.shape[1]
    rows = w_qkv.shape[0]
    heads = HEAD_COUNT // seq_count
    key_cols, val_cols = heads * DK, heads * DV
    half = w_down.shape[0] // seq_count
    wide = -(-half // 256) * 256
    taps = conv_w.shape[1]
    total = dealing.shape[1]
    devices = seq_count * mp_count
    channels = 2 * key_cols + val_cols
    all_keys, ffn = HEAD_COUNT * DK, w_down.shape[0]
    split = (seq_count, mp_count // 2) if mp_count <= 8 else None
    words = jnp.stack([place_mp % 2, place_mp // 2, rank]).astype(jnp.int32)
    rank_word = rank.astype(jnp.int32).reshape(1)

    small = jnp.concatenate([conv_w.T.reshape(-1), gain_in, gain_mid, gain_o])
    small_count = small.shape[0]
    spare = 128 - heads
    filler = jnp.concatenate([small, jnp.zeros((rows * spare - small_count,), BF16)])
    filler = filler.reshape(rows, spare)
    wide_filler = jnp.zeros((rows, wide - half), BF16)
    turned_down = w_down.T
    decay_lanes = -(-3 * heads * count // (128 * rows)) * 128
    decays = split_three(log_decay[0].T)
    mix_cols = channels + 128 + val_cols
    pieces, ffn_pieces = [], []
    for j in range(seq_count):
        own_decay = decays[:, j * heads : (j + 1) * heads].reshape(-1)
        own_decay = jnp.concatenate(
            [own_decay, jnp.zeros((rows * decay_lanes - own_decay.shape[0],), BF16)]
        )
        pieces.append(
            jnp.concatenate(
                [
                    w_out_gate[:, j * val_cols : (j + 1) * val_cols],
                    w_qkv[:, j * key_cols : (j + 1) * key_cols],
                    w_qkv[:, all_keys + j * key_cols : all_keys + (j + 1) * key_cols],
                    w_qkv[:, 2 * all_keys + j * val_cols : 2 * all_keys + (j + 1) * val_cols],
                    w_beta[:, j * heads : (j + 1) * heads],
                    filler,
                    own_decay.reshape(rows, decay_lanes),
                ],
                1,
            )
        )
        ffn_pieces.append(
            jnp.concatenate(
                [
                    w_gate_up[:, j * half : (j + 1) * half],
                    wide_filler,
                    w_gate_up[:, ffn + j * half : ffn + (j + 1) * half],
                    wide_filler,
                    turned_down[:, j * half : (j + 1) * half],
                    wide_filler,
                ],
                1,
            )
        )
    def near(arrays):
        arrays = jnp.stack(arrays)
        return jnp.stack(
            returned(
                [lax.dynamic_index_in_dim(arrays, rank ^ k, 0, keepdims=False) for k in range(seq_count)]
            )
        )

    pieces = near([jnp.concatenate(p, 1) for p in zip(pieces, ffn_pieces)])
    ffn_pieces = pieces[:, :, -3 * wide :]
    gathered = lax.all_gather(pieces[:, :, :mix_cols], "mp", axis=0, tiled=False)
    chunks_in = spread(layer_in[0] + 0 * pieces[1, :1, :1])

    relative = rank ^ jnp.arange(seq_count)
    smalls = gathered[:, :, :, mix_cols - spare :].transpose(1, 0, 2, 3)
    smalls = jnp.take(smalls, relative, axis=0).reshape(devices, -1)[:, :small_count]
    own_taps = conv_w.shape[0] * taps
    full_conv = smalls[:, :own_taps].reshape(-1, taps, conv_w.shape[0]).transpose(1, 0, 2)
    full_conv = full_conv.reshape(taps, -1).astype(F32)
    conv = jnp.concatenate(
        [
            lax.dynamic_slice_in_dim(full_conv, rank * key_cols, key_cols, 1),
            lax.dynamic_slice_in_dim(full_conv, all_keys + rank * key_cols, key_cols, 1),
            lax.dynamic_slice_in_dim(full_conv, 2 * all_keys + rank * val_cols, val_cols, 1),
        ],
        1,
    )
    conv = jnp.concatenate([conv, jnp.zeros((8 - taps, channels), F32)], 0)
    gains = smalls[:, own_taps:].astype(F32)
    full_gin = gains[:, :rows].reshape(1, -1)
    full_gmid = gains[:, rows : 2 * rows].reshape(1, -1)
    full_go = gains[:, 2 * rows :].reshape(1, -1)

    out_turned = w_out.T
    out_near = []
    if split:
        out_near = [out_turned] + [swapped(out_turned, "mp", 2 * j) for j in range(1, mp_count // 2)]

    out_copies = []
    if split:
        out_copies = [
            jnp.broadcast_to(jnp.stack(out_near), (seq_count, mp_count // 2, *out_turned.shape))
        ]

    decays = pieces[:, :, mix_cols : -3 * wide].reshape(seq_count, -1)[:, : 3 * heads * count]
    col_info, row_info, place_row = positions(
        words, seq_lengths[0], dealing, decays.reshape(seq_count, -1, BLOCK), heads, out_copies
    )

    passed = [ffn_pieces, out_grad[0] + 0 * pieces[1, :1, :1]] + out_copies
    passed = handed(passed, chunks_in[1:] + [row_info])
    ffn_all = lax.all_gather(passed[0], "mp", axis=0, tiled=False)
    chunks_grad = spread(passed[1])
    out_mine = [lax.all_to_all(passed[2], "seq", 0, 0, tiled=True)] if split else []
    (normed, gate_logit, proj, logit_parts, mix), _ = project(
        rank_word, chunks_in, full_gin, gathered, col_info, channels,
        [], [conv, full_go, full_gmid],
    )
    outs = forward_recurrence(proj, conv, col_info, row_info, logit_parts, heads, [])
    dealt_rows, attn, out_mine = gate_rows(
        outs[0], place_row, gate_logit, full_go, count, heads, out_mine, chunks_grad[1:]
    )
    if split:
        out_others = [swapped(out_mine[0], "mp", 1)]
    else:
        out_mine, out_others = [lax.all_gather(out_turned, ("seq", "mp"), axis=0, tiled=True)], []
    attn_parts = returned(attn)
    out_w, normed_t = out_rows(words, out_mine[0], out_others, normed, devices * rows, [attn[0]])

    residual, mid_own = out_project(rank_word, layer_in[0], full_gmid, attn_parts, out_w)

    ffn_w = ffn_rows(words, ffn_all, [mid_own])
    w_gu, down_turned = ffn_w[:, : 2 * wide], ffn_w[:, 2 * wide :]
    mids = spread(mid_own)
    hiddens, gu_grads, mid_parts = ([None] * seq_count for _ in range(3))
    last_part = None
    for k in (0, 1, 3, 2):
        mid_k = mids[k] if last_part is None else pinned(mids[k], last_part)
        gate_up = dot(mid_k, w_gu)
        gate, up = gate_up[:, :wide], gate_up[:, wide:]
        hiddens[k] = (silu(gate) * up).astype(BF16)
        hidden_grad = dot(chunks_grad[k], down_turned)
        gu_grads[k] = jnp.concatenate(
            [hidden_grad * up * silu_slope(gate), hidden_grad * silu(gate)], 1
        ).astype(BF16)
        mid_parts[k] = last_part = right_product(gu_grads[k], w_gu).astype(BF16)
    mid_parts = returned(mid_parts)
    ffn_sum = RowSum(
        weight_grad(
            split, words, [(mids, gu_grads), (chunks_grad, hiddens)], wide, [last_part, mid_parts[1]]
        ),
    )
    res_grad, out_proj_grad, g_mid, attn_grads, ffn_sum.outs[-1:] = mid_back(
        rank_word, out_grad[0], residual, full_gmid, mid_parts, out_w, ffn_sum.outs[-1:]
    )
    attn_grads = returned(attn_grads)
    ffn_sum.pair()
    layer_own, *both = layer_products(hiddens, ffn_w, out_proj_grad)

    (gate_grad, o_grad, g_go), both = ungate_rows(
        dealt_rows, col_info, gate_logit, full_go, attn_grads, heads, both, []
    )
    gate_sums, *gate_outs = weight_grad(
        split, words, [([normed], [gate_grad])], val_cols, [], weights=mix
    )
    gate_sum = RowSum(gate_outs)
    gate_sum.pair()
    ffn_sum = ffn_sum.beside(gate_sum)
    both = returned([None] + both)[1:]
    proj_grad, g_conv = backward_recurrence(
        proj, conv, col_info, row_info, logit_parts, outs[1:], o_grad, heads, [ffn_sum.half]
    )
    mix_grad, mix_sums, *mix_outs = unpack(
        split, words, proj_grad, gate_grad, place_row, normed_t, mix, g_conv, full_gin, g_mid, g_go,
        gate_sums, heads, [],
    )
    mix_sum = RowSum(mix_outs)
    mix_sum.pair()
    normed_parts, _ = unproject(mix_grad, mix, count, [], [])
    normed_chunks = returned(normed_parts)
    out_sum = RowSum(
        weight_grad(split, words, [([out_proj_grad] + both, attn)], val_cols,
            [normed_parts[0], ffn_sum.parts], limit=56 * MIB,
        )
    )
    out_sum.pair()
    last_sum = mix_sum.beside(out_sum)
    in_grad = in_back(layer_in[0], res_grad, full_gin, normed_chunks, [last_sum.half])
    layer_out = residual + sum(
        c.astype(F32) for c in [layer_own] + [b[count:] for b in both]
    )
    all_pieces = dealt(row_sums([ffn_sum, last_sum], [in_grad]))
    layer_out = layer_out.astype(BF16)[None]
    if split:
        g_qkv, g_gate, g_beta, g_conv, g_out, g_gu, g_down, small_sum = finish(
            all_pieces, heads, wide, half, taps
        )
        device = rank * mp_count + place_mp
        grad_go = lax.dynamic_slice_in_dim(
            small_sum[4:6].reshape(-1), device * gain_o.shape[0], gain_o.shape[0]
        )
        grad_gmid = lax.dynamic_slice_in_dim(small_sum[8:16].reshape(-1), device * rows, rows)
        grad_gin = lax.dynamic_slice_in_dim(small_sum[16:24].reshape(-1), device * rows, rows)
        return (
            layer_out, in_grad[None], g_qkv, g_gate, g_beta, g_conv,
            grad_gin, grad_go, g_out, grad_gmid, g_gu, g_down,
        )

    def columns(first, width):
        parts = [all_pieces[j, :, first : first + width] for j in range(seq_count)]
        return jnp.concatenate(parts, 1).astype(F32)

    everywhere = ("seq", "mp")
    conv_full = jnp.zeros((taps, conv_w.shape[0] * devices), F32)
    for first, width in ((0, key_cols), (key_cols, key_cols), (2 * key_cols, val_cols)):
        conv_full = lax.dynamic_update_slice_in_dim(
            conv_full, g_conv[:taps, first : first + width], first * seq_count + rank * width, 1
        )
    grad_conv = lax.psum_scatter(conv_full.T, everywhere, scatter_dimension=0, tiled=True)
    g_gin = mix_sums[0] / full_gin[0]
    grad_gin, grad_gmid, grad_go = (
        lax.psum_scatter(g, everywhere, scatter_dimension=0, tiled=True)
        for g in (g_gin, g_mid[0], g_go[0])
    )
    first = 3 * wide + val_cols
    last = all_pieces.shape[2] - val_cols
    return (
        layer_out,
        in_grad[None],
        jnp.concatenate(
            [
                columns(first, key_cols),
                columns(first + key_cols, key_cols),
                columns(first + 2 * key_cols, val_cols),
            ],
            1,
        ),
        columns(3 * wide, val_cols),
        columns(first + channels, heads),
        grad_conv,
        grad_gin,
        grad_go,
        columns(last, val_cols).T,
        grad_gmid,
        jnp.concatenate([columns(0, half), columns(wide, half)], 1),
        columns(2 * wide, half).T,
    )


def solution(mesh):
    in_specs = (
        P("mp", "seq", None),
        P("mp", "seq", None),
        P("mp", None),
        P("mp", None),
        P("mp", "seq", None),
        P(("seq", "mp"), None),
        P(("seq", "mp"), None),
        P(("seq", "mp"), None),
        P(("seq", "mp"), None),
        P(("seq", "mp")),
        P(("seq", "mp")),
        P(None, ("seq", "mp")),
        P(("seq", "mp")),
        P(("seq", "mp"), None),
        P(None, ("seq", "mp")),
    )
    out_specs = (
        P("mp", "seq", None),
        P("mp", "seq", None),
        P(("seq", "mp"), None),
        P(("seq", "mp"), None),
        P(("seq", "mp"), None),
        P(("seq", "mp"), None),
        P(("seq", "mp")),
        P(("seq", "mp")),
        P(None, ("seq", "mp")),
        P(("seq", "mp")),
        P(("seq", "mp"), None),
        P(None, ("seq", "mp")),
    )
    return jax.shard_map(body, mesh=mesh, in_specs=in_specs, out_specs=out_specs, check_vma=False)
```

```python
import functools

import jax
import jax.numpy as jnp
from jax import lax
from jax.experimental import pallas as pl
from jax.experimental.pallas import tpu as pltpu
from jax.sharding import PartitionSpec as P

HEAD_COUNT = 8
DK = 128
DV = 256
BLOCK = 128
FORWARD_STEP = 6
BACKWARD_STEP = 2
F32 = jnp.float32
BF16 = jnp.bfloat16


def mm(left, right):
    return jnp.dot(left.astype(BF16), right.astype(BF16), preferred_element_type=F32)


def mm_nt(left, right):
    return lax.dot_general(
        left.astype(BF16),
        right.astype(BF16),
        (((1,), (1,)), ((), ())),
        preferred_element_type=F32,
    )


def mm_tn(left, right):
    return lax.dot_general(
        left.astype(BF16),
        right.astype(BF16),
        (((0,), (0,)), ((), ())),
        preferred_element_type=F32,
    )


def masks():
    rows = lax.broadcasted_iota(jnp.int32, (BLOCK, BLOCK), 0)
    cols = lax.broadcasted_iota(jnp.int32, (BLOCK, BLOCK), 1)
    return rows, cols


def unit_inverses(mats, rows, cols):
    ident = (rows == cols).astype(F32)
    near = (rows // 16) == (cols // 16)
    power = [jnp.where(near, a, 0.0) for a in mats]
    result = [ident - p for p in power]
    span = 2
    while span < 16:
        power = [mm(p, p) for p in power]
        result = [t + mm(t, p) for t, p in zip(result, power)]
        span *= 2
    size = 16
    while size < BLOCK:
        off = ((rows // (2 * size)) == (cols // (2 * size))) & ((rows // size) != (cols // size))
        reach = [mm(jnp.where(off, a, 0.0), t) for a, t in zip(mats, result)]
        result = [t - mm(t, x) for t, x in zip(result, reach)]
        size *= 2
    return result


def convolve(ext_ref, conv_ref, col_ref, start, first, width):
    cols = pl.ds(first, width)
    total = ext_ref[pl.ds(16 + start, BLOCK), cols] * conv_ref[3:4, cols]
    for tap in range(3):
        keep = col_ref[pl.ds(start, BLOCK), tap : tap + 1]
        total += ext_ref[pl.ds(13 + tap + start, BLOCK), cols] * keep * conv_ref[tap : tap + 1, cols]
    return total


def column(col_ref, start, index):
    return col_ref[pl.ds(start, BLOCK), index : index + 1]


def strength(logit_ref, start, head, heads):
    return jax.nn.sigmoid(column(logit_ref, start, head))


def exact_nt(left, right):
    left_high, right_high = left.astype(BF16), right.astype(BF16)
    left_low = left - left_high.astype(F32)
    right_low = right - right_high.astype(F32)
    return mm_nt(left_high, right_high) + (mm_nt(left_high, right_low) + mm_nt(left_low, right_high))


def decay_matrix(col_ref, row_ref, start, head, heads, rows, cols):
    cum_i = column(col_ref, start, 5 + head)
    cum_j = row_ref[head : head + 1, pl.ds(start, BLOCK)]
    seg_i = column(col_ref, start, 3)
    seg_j = row_ref[heads : heads + 1, pl.ds(start, BLOCK)]
    within = (rows >= cols) & (seg_i == seg_j)
    return jnp.where(within, jnp.exp(jnp.where(within, cum_i - cum_j, 0.0)), 0.0)


def silu(values):
    return values * jax.nn.sigmoid(values)


def forward_kernel(
    heads, edge_ref, proj_ref, conv_ref, col_ref, row_ref, logit_ref, *refs,
):
    o_ref, s_ref, n_ref, t_ref, w_ref, p_ref, pre_ref, ext_ref, state_ref = refs[-9:]
    steps = proj_ref.shape[0] // BLOCK

    @pl.when(pl.program_id(0) == 0)
    def _():
        state_ref[...] = jnp.zeros_like(state_ref)

    ext_ref[:16, :] = edge_ref[...].astype(F32)
    ext_ref[16:, :] = proj_ref[...].astype(F32)
    rows, cols = masks()
    strict = rows > cols
    units = [(g, h) for g in range(steps) for h in range(heads)]
    queries, keys, values, mats, decays, betas = {}, {}, {}, [], {}, {}
    for g, h in units:
        start = g * BLOCK

        def taken(first, width):
            value = convolve(ext_ref, conv_ref, col_ref, start, first, width)
            pre_ref[pl.ds(start, BLOCK), first : first + width] = value
            return value

        queries[g, h] = silu(taken(h * DK, DK))
        raw = silu(taken((heads + h) * DK, DK))
        keys[g, h] = raw * lax.rsqrt(jnp.sum(raw * raw, axis=1, keepdims=True) + 1e-06)
        values[g, h] = silu(taken(2 * heads * DK + h * DV, DV))
        decays[g, h] = decay_matrix(col_ref, row_ref, start, h, heads, rows, cols)
        betas[g, h] = strength(logit_ref, start, h, heads)
        beta = betas[g, h]
        inner = mm_nt(keys[g, h], keys[g, h])
        mats.append(jnp.where(strict, beta * inner * decays[g, h], 0.0))
    inverses = unit_inverses(mats, rows, cols)
    umats, wmats, pmats, boundary, reads = {}, {}, {}, {}, {}
    for (g, h), inverse in zip(units, inverses):
        start = g * BLOCK
        beta = betas[g, h]
        elog = column(col_ref, start, 5 + heads + h)
        flog = column(col_ref, start, 5 + 2 * heads + h)
        inverse = inverse.astype(BF16)
        t_ref[g, h] = inverse
        umats[g, h] = mm(inverse, beta * values[g, h])
        wmats[g, h] = mm(inverse, (beta * elog) * keys[g, h]).astype(BF16)
        w_ref[g, h] = wmats[g, h]
        pmats[g, h] = (exact_nt(queries[g, h], keys[g, h]) * decays[g, h]).astype(BF16)
        p_ref[g, h] = pmats[g, h]
        boundary[g, h] = (keys[g, h] * flog).T.astype(BF16)
        reads[g, h] = (queries[g, h] * elog).astype(BF16)
    for g in range(steps):
        start = g * BLOCK
        for h in range(heads):
            state = state_ref[h]
            low = state.astype(BF16)
            s_ref[g, h] = low
            news = (umats[g, h] - mm(wmats[g, h], low)).astype(BF16)
            n_ref[g, h] = news
            carried = col_ref[pl.ds(start + BLOCK - 1, 1), 5 + heads + h : 6 + heads + h]
            state_ref[h] = carried * state + mm(boundary[g, h], news)
            output = mm(reads[g, h], low) + mm(pmats[g, h], news)
            o_ref[pl.ds(start, BLOCK), h * DV : (h + 1) * DV] = output.astype(BF16)


def backward_kernel(
    heads, edge_ref, proj_ref, conv_ref, col_ref, row_ref, logit_ref,
    s_ref, n_ref, t_ref, w_ref, p_ref, pre_ref, do_ref, *refs,
):
    grad_ref, gconv_ref, ext_ref, shift_ref, dstate_ref, head_ref = refs[-6:]
    count = proj_ref.shape[0]
    steps = count // BLOCK
    channels = proj_ref.shape[1]

    @pl.when(pl.program_id(0) == 0)
    def _():
        dstate_ref[...] = jnp.zeros_like(dstate_ref)
        head_ref[...] = jnp.zeros_like(head_ref)
        gconv_ref[...] = jnp.zeros_like(gconv_ref)

    ext_ref[:16, :] = edge_ref[...].astype(F32)
    ext_ref[16:, :] = proj_ref[...].astype(F32)
    for tap in range(3):
        shift_ref[tap, count : count + 8, :] = head_ref[tap]
    rows, cols = masks()
    strict = rows > cols
    units = [(g, h) for g in reversed(range(steps)) for h in range(heads)]
    queries, keys, pre, reads, first, gains = {}, {}, {}, {}, {}, {}
    for g, h in units:
        start = g * BLOCK

        def taken(first, width):
            return pre_ref[pl.ds(start, BLOCK), first : first + width]

        elog = column(col_ref, start, 5 + heads + h)
        out_grad = do_ref[pl.ds(start, BLOCK), h * DV : (h + 1) * DV]
        queries[g, h] = silu(taken(h * DK, DK))
        raw = silu(taken((heads + h) * DK, DK))
        scale = lax.rsqrt(jnp.sum(raw * raw, axis=1, keepdims=True) + 1e-06)
        keys[g, h] = (raw * scale, scale)
        first[g, h] = mm_tn(p_ref[g, h], out_grad)
        gains[g, h] = mm_tn(queries[g, h] * elog, out_grad)
    news_grads, state_grads = {}, {}
    for g in reversed(range(steps)):
        start = g * BLOCK
        for h in range(heads):
            flog = column(col_ref, start, 5 + 2 * heads + h)
            dstate = dstate_ref[h]
            low = dstate.astype(BF16)
            state_grads[g, h] = low
            news_grad = (first[g, h] + mm(keys[g, h][0] * flog, low)).astype(BF16)
            news_grads[g, h] = news_grad
            carried = col_ref[pl.ds(start + BLOCK - 1, 1), 5 + heads + h : 6 + heads + h]
            dstate_ref[h] = gains[g, h] + carried * dstate - mm_tn(w_ref[g, h], news_grad)
    lane = lax.broadcasted_iota(jnp.int32, (BLOCK, 128), 1)

    def through_conv(g, first_col, width, grad):
        start = g * BLOCK
        cols_ = pl.ds(first_col, width)
        value = pre_ref[pl.ds(start, BLOCK), first_col : first_col + width]
        gate = jax.nn.sigmoid(value)
        grad = grad * (gate * (1.0 + value * (1.0 - gate)))
        shift_ref[3, pl.ds(start, BLOCK), cols_] = grad * conv_ref[3:4, cols_]
        sums = []
        for tap in range(3):
            kept = grad * col_ref[pl.ds(start, BLOCK), tap : tap + 1]
            shift_ref[tap, pl.ds(start, BLOCK), cols_] = kept * conv_ref[tap : tap + 1, cols_]
            sums.append(
                jnp.sum(kept * ext_ref[pl.ds(13 + tap + start, BLOCK), cols_], axis=0, keepdims=True)
            )
        sums.append(
            jnp.sum(grad * ext_ref[pl.ds(16 + start, BLOCK), cols_], axis=0, keepdims=True)
        )
        for tap in range(4):
            gconv_ref[tap : tap + 1, cols_] += sums[tap]

    logit_grads = {}
    for g, h in units:
        start = g * BLOCK
        beta = strength(logit_ref, start, h, heads)
        elog = column(col_ref, start, 5 + heads + h)
        flog = column(col_ref, start, 5 + 2 * heads + h)
        key, scale = keys[g, h]
        query = queries[g, h]
        out_grad = do_ref[pl.ds(start, BLOCK), h * DV : (h + 1) * DV]
        decay = decay_matrix(col_ref, row_ref, start, h, heads, rows, cols)
        key_low = key.astype(BF16)
        inner = mm_nt(key_low, key_low) * decay
        news, state, dstate = n_ref[g, h], s_ref[g, h], state_grads[g, h]
        rhs_grad = mm_tn(t_ref[g, h], news_grads[g, h])
        rhs_low = rhs_grad.astype(BF16)
        within = (mm_nt(out_grad, news) * decay).astype(BF16)
        mat_grad = jnp.where(strict, -mm_nt(rhs_low, news), 0.0)
        pair = (mat_grad * beta * decay).astype(BF16)
        back = mm_nt(rhs_low, state)
        q_grad = mm(within, key_low) + elog * mm_nt(out_grad, state)
        k_grad = (
            mm_tn(within, query)
            + mm(pair, key_low)
            + mm_tn(pair, key_low)
            + flog * mm_nt(news, dstate)
            - (beta * elog) * back
        )
        value = silu(pre_ref[pl.ds(start, BLOCK), pl.ds(2 * heads * DK + h * DV, DV)])
        beta_grad = (
            jnp.sum(mat_grad * inner - elog * (key * back), axis=1, keepdims=True)
            + jnp.sum(rhs_grad * value, axis=1, keepdims=True)
        )
        logit_grads[g, h] = beta_grad * beta * (1.0 - beta)
        raw_grad = scale * (k_grad - key * jnp.sum(k_grad * key, axis=1, keepdims=True))
        through_conv(g, h * DK, DK, q_grad)
        through_conv(g, (heads + h) * DK, DK, raw_grad)
        through_conv(g, 2 * heads * DK + h * DV, DV, beta * rhs_grad)
    for g in range(steps):
        total = jnp.zeros((BLOCK, 128), F32)
        for h in range(heads):
            total = jnp.where(lane == h, logit_grads[g, h], total)
        grad_ref[pl.ds(g * BLOCK, BLOCK), channels : channels + 128] = total.astype(BF16)
        grad_ref[pl.ds(g * BLOCK, BLOCK), channels + 128 :] = jnp.zeros((BLOCK, 128), BF16)
    total = shift_ref[3, :count, :]
    for tap in range(3):
        total += shift_ref[tap, pl.ds(3 - tap, count), :]
    grad_ref[:, :channels] = total.astype(BF16)
    for tap in range(3):
        head_ref[tap] = shift_ref[tap, :8, :]


def saved_shapes(blocks, heads):
    return (
        jax.ShapeDtypeStruct((blocks, heads, DK, DV), BF16),
        jax.ShapeDtypeStruct((blocks, heads, BLOCK, DV), BF16),
        jax.ShapeDtypeStruct((blocks, heads, BLOCK, BLOCK), BF16),
        jax.ShapeDtypeStruct((blocks, heads, BLOCK, DK), BF16),
        jax.ShapeDtypeStruct((blocks, heads, BLOCK, BLOCK), BF16),
        jax.ShapeDtypeStruct((blocks * BLOCK, heads * (2 * DK + DV)), F32),
    )


def saved_specs(shapes, per_step, index):
    return [
        pl.BlockSpec((per_step,) + shape.shape[1:], lambda i: (index(i), 0, 0, 0))
        for shape in shapes[:-1]
    ] + [pl.BlockSpec((per_step * BLOCK, shapes[-1].shape[1]), lambda i: (index(i), 0))]


def common_specs(step, channels, logits, index):
    return [
        pl.BlockSpec((16, channels), lambda i: (jnp.maximum(index(i) * (step // 16) - 1, 0), 0)),
        pl.BlockSpec((step, channels), lambda i: (index(i), 0)),
        pl.BlockSpec((8, channels), lambda i: (0, 0)),
        pl.BlockSpec((step, 128), lambda i: (index(i), 0)),
        pl.BlockSpec((8, step), lambda i: (0, index(i))),
        pl.BlockSpec((step, logits), lambda i: (index(i), 0)),
    ]


MIB = 1024 * 1024
VMEM_BYTES = 24 * MIB
SMALL_COST = pl.CostEstimate(flops=10**6, bytes_accessed=10**6, transcendentals=0)
ANYWHERE = pl.BlockSpec(memory_space=pl.ANY)
WHOLE = pl.BlockSpec(memory_space=pltpu.VMEM)
SCALAR = pl.BlockSpec(memory_space=pltpu.SMEM)


def params(limit=VMEM_BYTES):
    return pltpu.CompilerParams(dimension_semantics=("arbitrary",), vmem_limit_bytes=limit)


def forward_recurrence(proj, conv, cols, rows, logits, heads, tokens):
    count, channels = proj.shape
    step = BLOCK * FORWARD_STEP
    shapes = saved_shapes(count // BLOCK, heads)
    index = lambda i: i
    return pl.pallas_call(
        functools.partial(forward_kernel, heads),
        grid=(count // step,),
        in_specs=common_specs(step, channels, 128, index) + [ANYWHERE] * len(tokens),
        out_specs=[pl.BlockSpec((step, heads * DV), lambda i: (i, 0))] + saved_specs(shapes, FORWARD_STEP, index),
        out_shape=(jax.ShapeDtypeStruct((count, heads * DV), BF16),) + shapes,
        scratch_shapes=[
            pltpu.VMEM((step + 16, channels), F32),
            pltpu.VMEM((heads, DK, DV), F32),
        ],
        compiler_params=params(56 * MIB),
        cost_estimate=SMALL_COST,
        name="recurrence_forward",
    )(proj, proj, conv, cols, rows, logits, *tokens)


def backward_recurrence(proj, conv, cols, rows, logits, saved, out_grad, heads, tokens):
    count, channels = proj.shape
    step = BLOCK * BACKWARD_STEP
    last = count // step - 1
    index = lambda i: last - i
    return pl.pallas_call(
        functools.partial(backward_kernel, heads),
        grid=(count // step,),
        in_specs=common_specs(step, channels, 128, index)
        + saved_specs(saved, BACKWARD_STEP, index)
        + [pl.BlockSpec((step, heads * DV), lambda i: (index(i), 0))]
        + [ANYWHERE] * len(tokens),
        out_specs=[
            pl.BlockSpec((step, channels + 256), lambda i: (index(i), 0)),
            pl.BlockSpec((8, channels), lambda i: (0, 0)),
        ],
        out_shape=(
            jax.ShapeDtypeStruct((count, channels + 256), BF16),
            jax.ShapeDtypeStruct((8, channels), F32),
        ),
        scratch_shapes=[
            pltpu.VMEM((step + 16, channels), F32),
            pltpu.VMEM((4, step + 8, channels), F32),
            pltpu.VMEM((heads, DK, DV), F32),
            pltpu.VMEM((3, 8, channels), F32),
        ],
        compiler_params=params(56 * MIB),
        cost_estimate=SMALL_COST,
        name="recurrence_backward",
    )(proj, proj, conv, cols, rows, logits, *saved, out_grad, *tokens)


def project_kernel(
    channels, chunks, handed, rank_ref, gain_ref, w_ref, col_ref, *refs
):
    x_refs = refs[:chunks]
    normed_ref, gate_ref, proj_ref, logit_ref, all_ref = refs[chunks + handed : chunks + handed + 5]
    rows_ref = refs[-1]
    step = pl.program_id(0)
    count = x_refs[0].shape[0]

    @pl.when(step == 0)
    def _():
        width = w_ref.shape[0] * w_ref.shape[2]
        for k in range(w_ref.shape[1]):
            place = pl.ds(pl.multiple_of((rank_ref[0] ^ k) * width, width), width)
            all_ref[place, :] = w_ref[:, k].reshape(width, w_ref.shape[3])

    for k in range(chunks):

        @pl.when(step == k)
        def _():
            x = x_refs[k][...].astype(F32)
            scale = lax.rsqrt(jnp.mean(x * x, axis=1, keepdims=True) + 1e-05)
            normed = (x * scale * gain_ref[...]).astype(BF16)
            normed_ref[...] = normed
            total = mm(normed, all_ref[...])
            gates = gate_ref.shape[1]
            gate_ref[...] = total[:, :gates]
            logit = total[:, gates + channels :]
            high = logit.astype(BF16)
            place = slice(k * count, (k + 1) * count)
            rows_ref[place, : channels + 128] = total[:, gates:].astype(BF16)
            rows_ref[place, channels + 128 :] = (logit - high.astype(F32)).astype(BF16)

    @pl.when(step >= chunks)
    def _():
        order = lax.broadcasted_iota(jnp.int32, (proj_ref.shape[0], rows_ref.shape[0]), 1)
        picked = (col_ref[:, 4:5].astype(jnp.int32) == order).astype(F32)
        packed = mm(picked, rows_ref[...])
        proj_ref[...] = packed[:, :channels].astype(BF16)
        logit_ref[...] = packed[:, channels : channels + 128] + packed[:, channels + 128 :]


def project(rank, x_chunks, gain, weights, cols, channels, passed, tokens):
    count, width = x_chunks[0].shape
    total = count * len(x_chunks)
    gates = weights.shape[3] - channels - 128
    chunks = total // count
    block = total // 2
    first = lambda i: jnp.minimum(i, chunks - 1)
    later = lambda i: jnp.maximum(i - chunks, 0)
    outs = pl.pallas_call(
        functools.partial(project_kernel, channels, chunks, len(passed) + len(tokens)),
        grid=(chunks + total // block,),
        in_specs=[
            SCALAR,
            pl.BlockSpec((1, width), lambda i: (0, 0)),
            pl.BlockSpec(weights.shape, lambda i: (0, 0, 0, 0)),
            pl.BlockSpec((block, 128), lambda i: (later(i), 0)),
        ]
        + [pl.BlockSpec((count, width), lambda i: (0, 0))] * chunks
        + [ANYWHERE] * (len(passed) + len(tokens)),
        out_specs=[
            pl.BlockSpec((count, width), lambda i: (first(i), 0)),
            pl.BlockSpec((count, gates), lambda i: (first(i), 0)),
            pl.BlockSpec((block, channels), lambda i: (later(i), 0)),
            pl.BlockSpec((block, 128), lambda i: (later(i), 0)),
            pl.BlockSpec((width, weights.shape[3]), lambda i: (0, 0)),
        ]
        + [ANYWHERE] * len(passed),
        out_shape=[
            jax.ShapeDtypeStruct((total, width), BF16),
            jax.ShapeDtypeStruct((total, gates), F32),
            jax.ShapeDtypeStruct((total, channels), BF16),
            jax.ShapeDtypeStruct((total, 128), F32),
            jax.ShapeDtypeStruct((width, weights.shape[3]), BF16),
        ]
        + [jax.ShapeDtypeStruct(p.shape, p.dtype) for p in passed],
        input_output_aliases={4 + chunks + i: 5 + i for i in range(len(passed))},
        scratch_shapes=[pltpu.VMEM((total, channels + 256), BF16)],
        compiler_params=params(56 * MIB),
        cost_estimate=SMALL_COST,
        name="project",
    )(rank, gain, weights, cols, *x_chunks, *passed, *tokens)
    return outs[:5], outs[5:]


def gate_kernel(heads, count, first, o_ref, place_ref, gate_ref, gain_ref, *refs):
    chunks = place_ref.shape[1] // count
    dealt_ref, chunk_refs = refs[first], refs[first + 1 : first + 1 + chunks]
    for k, chunk_ref in enumerate(chunk_refs):
        order = lax.broadcasted_iota(jnp.int32, (count, o_ref.shape[0]), 0) + k * count
        picked = (place_ref[...].astype(jnp.int32) == order).astype(F32)
        rows = mm(picked, o_ref[...])
        place = pl.ds(k * count, count)
        dealt_ref[place, :] = rows.astype(BF16)
        for h in range(heads):
            lanes = slice(h * DV, (h + 1) * DV)
            value = rows[:, lanes]
            scale = lax.rsqrt(jnp.mean(value * value, axis=1, keepdims=True) + 1e-05)
            gated = value * scale * gain_ref[...] * silu(gate_ref[place, lanes])
            chunk_ref[:, lanes] = gated.astype(BF16)


def gate_rows(output, place, gate_logit, gain, count, heads, passed, tokens):
    total, cols = output.shape
    chunks = total // count
    others = len(passed) + len(tokens)
    outs = pl.pallas_call(
        functools.partial(gate_kernel, heads, count, others),
        in_specs=[WHOLE] * 4 + [ANYWHERE] * others,
        out_specs=[WHOLE] * (chunks + 1) + [ANYWHERE] * len(passed),
        out_shape=[jax.ShapeDtypeStruct((total, cols), BF16)]
        + [jax.ShapeDtypeStruct((count, cols), BF16)] * chunks
        + [jax.ShapeDtypeStruct(a.shape, a.dtype) for a in passed],
        input_output_aliases={4 + i: 1 + chunks + i for i in range(len(passed))},
        compiler_params=pltpu.CompilerParams(vmem_limit_bytes=VMEM_BYTES),
        cost_estimate=SMALL_COST,
        name="gate_rows",
    )(output, place, gate_logit, gain, *passed, *tokens)
    return outs[0], outs[1 : 1 + chunks], outs[1 + chunks :]


def ungate_kernel(heads, chunks, outs, dealt_ref, col_ref, gate_ref, gain_ref, *refs):
    grad_refs = refs[:chunks]
    gate_grad_ref, o_grad_ref, gain_grad_ref, rows_ref = *refs[outs : outs + 3], refs[-1]
    count = grad_refs[0].shape[0]
    total = dealt_ref.shape[0]
    sums = jnp.zeros((1, DV), F32)
    for k in range(chunks):
        place = pl.ds(k * count, count)
        for h in range(heads):
            lanes = slice(h * DV, (h + 1) * DV)
            value = dealt_ref[place, lanes].astype(F32)
            grad = grad_refs[k][:, lanes].astype(F32)
            logit = gate_ref[place, lanes]
            scale = lax.rsqrt(jnp.mean(value * value, axis=1, keepdims=True) + 1e-05)
            unit = value * scale
            gate = jax.nn.sigmoid(logit)
            slid = logit * gate
            sums += jnp.sum(grad * unit * slid, axis=0, keepdims=True)
            grad = grad * gain_ref[...]
            slope = gate * (1.0 + logit * (1.0 - gate))
            gate_grad_ref[place, lanes] = (grad * unit * slope).astype(BF16)
            grad = grad * slid
            inner = jnp.mean(grad * unit, axis=1, keepdims=True)
            rows_ref[place, lanes] = (scale * (grad - unit * inner)).astype(BF16)
    gain_grad_ref[...] = sums
    for k in range(chunks):
        place = pl.ds(k * count, count)
        order = lax.broadcasted_iota(jnp.int32, (count, total), 1)
        picked = (col_ref[place, 4:5].astype(jnp.int32) == order).astype(F32)
        o_grad_ref[place, :] = mm(picked, rows_ref[...]).astype(BF16)


def ungate_rows(dealt_rows, cols, gate_logit, gain, grads, heads, passed, tokens):
    total, width = dealt_rows.shape
    whole = pl.BlockSpec(memory_space=pltpu.VMEM)
    first = 4 + len(grads)
    outs = pl.pallas_call(
        functools.partial(ungate_kernel, heads, len(grads), len(grads) + len(passed) + len(tokens)),
        in_specs=[whole] * first + [ANYWHERE] * (len(passed) + len(tokens)),
        out_specs=[whole] * 3 + [ANYWHERE] * len(passed),
        out_shape=[
            jax.ShapeDtypeStruct((total, width), BF16),
            jax.ShapeDtypeStruct((total, width), BF16),
            jax.ShapeDtypeStruct((1, DV), F32),
        ]
        + [jax.ShapeDtypeStruct(p.shape, p.dtype) for p in passed],
        input_output_aliases={first + i: 3 + i for i in range(len(passed))},
        scratch_shapes=[pltpu.VMEM((total, width), BF16)],
        compiler_params=pltpu.CompilerParams(vmem_limit_bytes=VMEM_BYTES),
        cost_estimate=SMALL_COST,
        name="ungate_rows",
    )(dealt_rows, cols, gate_logit, gain, *grads, *passed, *tokens)
    return outs[:3], list(outs[3:])


def turned_sums(values):
    sums = jnp.sum(values, axis=1, keepdims=True)
    return jnp.broadcast_to(sums, (values.shape[0], 128)).T[:1]


def put_rows(total, split, core_ref, refs):
    total = total.astype(BF16)
    if split is None:
        refs[0][...] = total
        return
    halves = total.reshape(*split, 2, -1, total.shape[1])
    for core in range(2):

        @pl.when(core_ref[0] == core)
        def _():
            refs[0][...] = halves[:, :, core]
            refs[1][...] = halves[:, :, 1 - core]


def row_outputs(split, width, cols, tile):
    if split is None:
        shape, block = (width, cols), (width, tile)
        spec = pl.BlockSpec(block, lambda i: (0, i))
        return [spec], [jax.ShapeDtypeStruct(shape, BF16)]
    shape = (*split, width // (2 * split[0] * split[1]))
    spec = pl.BlockSpec((*shape, tile), lambda i: (0, 0, 0, i))
    return [spec] * 2, [jax.ShapeDtypeStruct((*shape, cols), BF16)] * 2


def unpack_kernel(split, heads, words_ref, grad_ref, gates_ref, place_ref, normed_ref, w_ref, conv_ref, gain_ref, mid_ref, o_ref, first_sums_ref, *refs):
    count = 2 if split else 1
    dealt_ref, sums_ref = refs[-4 - count], refs[-3 - count]
    row_refs, small_ref, picked_ref = refs[-2 - count : -2], refs[-2], refs[-1]
    step = pl.program_id(0)
    total = grad_ref.shape[0]
    gates = gates_ref.shape[1]
    tile = grad_ref.shape[1] // 2

    @pl.when(step == 0)
    def _():
        part = 256
        for k in range(total // part):
            order = lax.broadcasted_iota(jnp.int32, (part, total), 0) + k * part
            picked = (place_ref[...].astype(jnp.int32) == order).astype(F32)
            picked_ref[k * part : (k + 1) * part, :] = picked.astype(BF16)
        dealt_ref[:, :gates] = gates_ref[...]
        dealt_ref[:, gates : gates + tile] = mm(picked_ref[...], grad_ref[:, :tile]).astype(BF16)
        share = mm(normed_ref[...], dealt_ref[:, gates : gates + tile])
        weights = w_ref[:, gates : gates + tile].astype(F32)
        sums_ref[...] = first_sums_ref[...] + turned_sums(share * weights)
        put_rows(share, split, words_ref, row_refs)

    @pl.when(step == 1)
    def _():
        dealt_ref[:, gates + tile :] = mm(picked_ref[...], grad_ref[:, tile:]).astype(BF16)
        share = mm(normed_ref[...], dealt_ref[:, gates + tile :])
        used = w_ref.shape[1] - gates - tile
        weights = w_ref[:, gates + tile :].astype(F32)
        sums_ref[...] += turned_sums(share[:, :used] * weights)
        if split:
            devices, rows = 2 * split[0] * split[1], share.shape[0] // (2 * split[0] * split[1])
            gin = sums_ref[...] / gain_ref[...]
            small_ref[...] = jnp.zeros_like(small_ref)
            gin = jnp.concatenate([gin[:, j * 128 : (j + 1) * 128] for j in range(8)], 0)
            mid = jnp.concatenate([mid_ref[:, j * 128 : (j + 1) * 128] for j in range(8)], 0)
            for d in range(devices):
                small_ref[d * rows + 4 : d * rows + 5, :] = o_ref[:, :128]
                small_ref[d * rows + 5 : d * rows + 6, :] = o_ref[:, 128:]
                small_ref[d * rows + 8 : d * rows + 16, :] = mid
                small_ref[d * rows + 16 : d * rows + 24, :] = gin
            rank = words_ref[2]
            keys = heads * DK // 128
            vals = heads * DV // 128
            owners = [rank * keys + j for j in range(keys)]
            owners += [HEAD_COUNT * DK // 128 + rank * keys + j for j in range(keys)]
            owners += [2 * HEAD_COUNT * DK // 128 + rank * vals + j for j in range(vals)]
            for j, owner in enumerate(owners):
                place = pl.ds(pl.multiple_of(owner * rows, rows), 8)
                old = small_ref[place, :]
                taps = lax.broadcasted_iota(jnp.int32, (8, 128), 0) < 4
                small_ref[place, :] = jnp.where(taps, conv_ref[:, j * 128 : (j + 1) * 128], old)
            share = jnp.concatenate([share[:, :-128], small_ref[...]], 1)
        put_rows(share, split, words_ref, row_refs)


def unpack(split, words, grad, gate_grad, place, normed, weights, g_conv, gain, g_mid, g_o, sums, heads, tokens):
    total = grad.shape[0]
    cols = grad.shape[1] + gate_grad.shape[1]
    width = normed.shape[0]
    operands = (grad, gate_grad, place, normed, weights, g_conv, gain, g_mid, g_o, sums)
    specs, shapes = row_outputs(split, width, grad.shape[1], grad.shape[1] // 2)
    return pl.pallas_call(
        functools.partial(unpack_kernel, split, heads),
        grid=(2,),
        in_specs=[SCALAR]
        + [pl.BlockSpec(a.shape, lambda i: (0, 0)) for a in operands]
        + [ANYWHERE] * len(tokens),
        out_specs=[
            pl.BlockSpec((total, cols), lambda i: (0, 0)),
            pl.BlockSpec((1, width), lambda i: (0, 0)),
        ]
        + specs,
        out_shape=[
            jax.ShapeDtypeStruct((total, cols), BF16),
            jax.ShapeDtypeStruct((1, width), F32),
        ]
        + shapes,
        scratch_shapes=[pltpu.VMEM((width, 128), F32), pltpu.VMEM((total, total), BF16)],
        compiler_params=params(),
        cost_estimate=SMALL_COST,
        name="unpack",
    )(words, *operands, *tokens)


def unproject_kernel(chunks, first, grad_ref, w_ref, *refs):
    part_refs, turned_ref = refs[first : first + chunks], refs[-1]
    step = pl.program_id(0)

    @pl.when(step == 0)
    def _():
        turned_ref[...] = w_ref[...].T

    part = mm(grad_ref[:, : turned_ref.shape[0]], turned_ref[...])
    for k in range(chunks):

        @pl.when(step == k)
        def _():
            part_refs[k][...] = part.astype(BF16)


def unproject(grad, weights, count, passed, tokens):
    total, cols = grad.shape
    width = weights.shape[0]
    chunks = total // count
    outs = pl.pallas_call(
        functools.partial(unproject_kernel, chunks, len(passed) + len(tokens)),
        grid=(chunks,),
        in_specs=[
            pl.BlockSpec((count, cols), lambda i: (i, 0)),
            pl.BlockSpec(weights.shape, lambda i: (0, 0)),
        ]
        + [ANYWHERE] * (len(passed) + len(tokens)),
        out_specs=[pl.BlockSpec((count, width), lambda i: (0, 0))] * chunks
        + [ANYWHERE] * len(passed),
        out_shape=[jax.ShapeDtypeStruct((count, width), BF16)] * chunks
        + [jax.ShapeDtypeStruct(p.shape, p.dtype) for p in passed],
        input_output_aliases={2 + i: chunks + i for i in range(len(passed))},
        scratch_shapes=[pltpu.VMEM(weights.shape[::-1], BF16)],
        compiler_params=params(56 * MIB),
        cost_estimate=SMALL_COST,
        name="unproject",
    )(grad, weights, *passed, *tokens)
    return list(outs[:chunks]), list(outs[chunks:])


def hand_kernel(*refs):
    refs[-1][...] = jnp.zeros_like(refs[-1])


def handed(passed, tokens):
    outs = pl.pallas_call(
        hand_kernel,
        in_specs=[ANYWHERE] * (len(passed) + len(tokens)),
        out_specs=[ANYWHERE] * len(passed) + [WHOLE],
        out_shape=[jax.ShapeDtypeStruct(p.shape, p.dtype) for p in passed]
        + [jax.ShapeDtypeStruct((8, 128), F32)],
        input_output_aliases={i: i for i in range(len(passed))},
        cost_estimate=SMALL_COST,
        name="handed",
    )(*passed, *tokens)
    return outs[:-1]


def weight_grad_kernel(split, tiles, sums, words_ref, *refs):
    row_refs = refs[-2:] if split else refs[-1:]
    step = pl.program_id(0)
    for tile, pairs in enumerate(tiles):

        @pl.when(step == tile)
        def _():
            total = mm_tn(refs[pairs[0][0]][...], refs[pairs[0][1]][...])
            for left, right in pairs[1:]:
                total += mm_tn(refs[left][...], refs[right][...])
            put_rows(total, split, words_ref, row_refs)
            if sums is not None and tile == 0:
                refs[sums[1]][...] = turned_sums(total * refs[sums[0]][...].astype(F32))


def weight_grad(split, words, groups, tile, tokens, weights=None, limit=VMEM_BYTES):
    width = groups[0][0][0].shape[1]
    operands, specs, tiles = [words], [SCALAR], []
    first = 0
    for lefts, rights in groups:
        count = rights[0].shape[1] // tile
        base = len(operands) - 1
        for left in lefts:
            operands.append(left)
            specs.append(pl.BlockSpec((rights[0].shape[0], width), lambda i: (0, 0)))
        for right in rights:
            operands.append(right)
            specs.append(
                pl.BlockSpec(
                    (right.shape[0], tile),
                    lambda i, first=first, count=count: (0, jnp.clip(i - first, 0, count - 1)),
                )
            )
        tiles += [[(base + k, base + len(lefts) + k) for k in range(len(lefts))]] * count
        first += count
    sums = None
    out_specs, out_shapes = row_outputs(split, width, first * tile, tile)
    if weights is not None:
        operands.append(weights)
        specs.append(pl.BlockSpec((width, tile), lambda i: (0, 0)))
        sums = (len(operands) - 2, len(operands) - 1 + len(tokens))
        out_specs = [pl.BlockSpec((1, width), lambda i: (0, 0))] + out_specs
        out_shapes = [jax.ShapeDtypeStruct((1, width), F32)] + out_shapes
    return pl.pallas_call(
        functools.partial(weight_grad_kernel, split, tiles, sums),
        grid=(first,),
        in_specs=specs + [ANYWHERE] * len(tokens),
        out_specs=out_specs,
        out_shape=out_shapes,
        compiler_params=params(limit),
        cost_estimate=SMALL_COST,
        name="weight_grad",
    )(*operands, *tokens)


def join_kernel(pairs, *refs):
    for chip in range(refs[0].shape[1]):
        place = 0
        for k in range(pairs):
            keep_ref, got_ref = refs[2 * k], refs[2 * k + 1]
            width = keep_ref.shape[3]
            total = keep_ref[:, chip].astype(F32) + got_ref[:, chip].astype(F32)
            refs[-1][chip, :, :, place : place + width] = total.astype(BF16)
            place += width


def joined(pairs, tokens):
    seq_count, chips, rows, _ = pairs[0][0].shape
    cols = sum(keep.shape[3] for keep, _ in pairs)
    return pl.pallas_call(
        functools.partial(join_kernel, len(pairs)),
        in_specs=[WHOLE] * (2 * len(pairs)) + [ANYWHERE] * len(tokens),
        out_specs=WHOLE,
        out_shape=jax.ShapeDtypeStruct((chips, seq_count, rows, cols), BF16),
        compiler_params=pltpu.CompilerParams(vmem_limit_bytes=VMEM_BYTES),
        cost_estimate=SMALL_COST,
        name="joined",
    )(*[a for pair in pairs for a in pair], *tokens)


def layer_kernel(chunks, w_ref, low_ref, *refs):
    weights = w_ref[...].T
    count = low_ref.shape[0]
    refs[chunks][...] = mm(refs[0][...], weights).astype(BF16)
    for k in range(1, chunks):
        refs[chunks + k][:count, :] = low_ref[...]
        refs[chunks + k][count:, :] = mm(refs[k][...], weights).astype(BF16)


def layer_products(hiddens, weights, low):
    count, wide = hiddens[0].shape
    width = weights.shape[0]
    chunks = len(hiddens)
    rows = [count] + [2 * count] * (chunks - 1)
    return pl.pallas_call(
        functools.partial(layer_kernel, chunks),
        grid=(1,),
        in_specs=[
            pl.BlockSpec((width, wide), lambda i: (0, weights.shape[1] // wide - 1)),
            pl.BlockSpec((count, width), lambda i: (0, 0)),
        ]
        + [pl.BlockSpec((count, wide), lambda i: (0, 0))] * chunks,
        out_specs=[pl.BlockSpec((r, width), lambda i: (0, 0)) for r in rows],
        out_shape=[jax.ShapeDtypeStruct((r, width), BF16) for r in rows],
        compiler_params=params(),
        cost_estimate=SMALL_COST,
        name="layer_products",
    )(weights, low, *hiddens)


def position_kernel(heads, chunks, words_ref, lengths_ref, order_ref, decay_ref, *refs):
    col_ref, row_ref, place_ref, cum_ref = refs[-4:]
    total = order_ref.shape[1]
    count = total // chunks
    blocks, near = total // BLOCK, count // BLOCK
    rank = words_ref[2]
    ends = [lengths_ref[0]]
    for e in range(1, lengths_ref.shape[0]):
        ends.append(ends[-1] + lengths_ref[e])

    def segment(position):
        found = jnp.zeros(position.shape, jnp.int32)
        for end in ends:
            found += (position >= end).astype(jnp.int32)
        return jnp.where(position < 0, -1, found)

    for k in range(chunks):
        for h in range(heads):
            for b in range(near):
                value = jnp.zeros((1, BLOCK), F32)
                for part in range(3):
                    row = (part * heads + h) * near + b
                    value += decay_ref[k, row : row + 1, :].astype(F32)
                cum_ref[pl.ds(h * blocks + (rank ^ k) * near + b, 1), :] = value
    rows, cols = masks()
    upper = (rows <= cols).astype(F32)
    cums = jnp.dot(
        cum_ref[...], upper, precision=lax.Precision.HIGHEST, preferred_element_type=F32
    )
    order = order_ref[...]
    chunk = jnp.zeros_like(order)
    for k in range(1, chunks):
        chunk += (order >= k * count).astype(jnp.int32)
    place = (order + ((chunk ^ rank) - chunk) * count).astype(F32)
    place_ref[...] = place
    row_ref[...] = jnp.zeros_like(row_ref)
    lane = lax.broadcasted_iota(jnp.int32, (1, BLOCK), 1)
    for b in range(blocks):
        position = lane + b * BLOCK
        here = segment(position)
        low, high = jnp.full((1, BLOCK), b * BLOCK - 1), jnp.full((1, BLOCK), b * BLOCK + BLOCK - 1)
        keep_in = (here == segment(low)).astype(F32)
        keep_out = (here == segment(high)).astype(F32)
        found = [(segment(position - 3 + tap) == here).astype(F32) for tap in range(3)]
        found += [here.astype(F32), place[:, b * BLOCK : (b + 1) * BLOCK]]
        mine = [cums[h * blocks + b : h * blocks + b + 1, :] for h in range(heads)]
        found += mine
        found += [jnp.exp(c) * keep_in for c in mine]
        found += [jnp.exp(c[:, BLOCK - 1 :] - c) * keep_out for c in mine]
        found.append(jnp.zeros((128 - len(found), BLOCK), F32))
        col_ref[b * BLOCK : (b + 1) * BLOCK, :] = jnp.concatenate(found, 0).T
        for h in range(heads):
            row_ref[h : h + 1, b * BLOCK : (b + 1) * BLOCK] = mine[h]
        row_ref[heads : heads + 1, b * BLOCK : (b + 1) * BLOCK] = here.astype(F32)


def positions(words, lengths, order, decays, heads, tokens):
    total = order.shape[1]
    return pl.pallas_call(
        functools.partial(position_kernel, heads, decays.shape[0]),
        in_specs=[SCALAR, SCALAR, WHOLE, WHOLE] + [ANYWHERE] * len(tokens),
        out_specs=[WHOLE] * 3,
        out_shape=(
            jax.ShapeDtypeStruct((total, 128), F32),
            jax.ShapeDtypeStruct((8, total), F32),
            jax.ShapeDtypeStruct((1, total), F32),
        ),
        scratch_shapes=[pltpu.VMEM((heads * total // BLOCK, BLOCK), F32)],
        cost_estimate=SMALL_COST,
        compiler_params=pltpu.CompilerParams(vmem_limit_bytes=VMEM_BYTES),
        name="positions",
    )(words, lengths, order, decays, *tokens)


def out_rows_kernel(others, words_ref, mine_ref, normed_ref, *refs):
    out_ref, turned_ref = refs[-2:]
    core, chip = words_ref[0], words_ref[1]
    if others:
        chunks, chips, rows, _ = mine_ref.shape
        for k in range(chunks):
            for j in range(chips):
                device = k * 2 * chips + 2 * (chip ^ j)
                for ref, side in ((mine_ref, core), (refs[0], 1 - core)):
                    place = pl.ds(pl.multiple_of((device + side) * rows, rows), rows)
                    out_ref[place, :] = ref[k, j]
    else:
        out_ref[...] = mine_ref[...]
    turned_ref[...] = normed_ref[...].T


def out_rows(words, mine, others, normed, rows, tokens):
    return pl.pallas_call(
        functools.partial(out_rows_kernel, len(others)),
        in_specs=[SCALAR] + [WHOLE] * (2 + len(others)) + [ANYWHERE] * len(tokens),
        out_specs=[WHOLE] * 2,
        out_shape=(
            jax.ShapeDtypeStruct((rows, mine.shape[-1]), BF16),
            jax.ShapeDtypeStruct(normed.shape[::-1], BF16),
        ),
        compiler_params=pltpu.CompilerParams(vmem_limit_bytes=VMEM_BYTES),
        cost_estimate=SMALL_COST,
        name="out_rows",
    )(words, mine, normed, *others, *tokens)


def ffn_rows_kernel(words_ref, ffn_ref, *refs):
    width = ffn_ref.shape[0] * ffn_ref.shape[2]
    for k in range(ffn_ref.shape[1]):
        place = pl.ds(pl.multiple_of((words_ref[2] ^ k) * width, width), width)
        refs[-1][place, :] = ffn_ref[:, k].reshape(width, ffn_ref.shape[3])


def ffn_rows(words, ffn, tokens):
    return pl.pallas_call(
        ffn_rows_kernel,
        in_specs=[SCALAR, WHOLE] + [ANYWHERE] * len(tokens),
        out_specs=WHOLE,
        out_shape=jax.ShapeDtypeStruct((ffn.shape[0] * ffn.shape[1] * ffn.shape[2], ffn.shape[3]), BF16),
        compiler_params=pltpu.CompilerParams(vmem_limit_bytes=VMEM_BYTES),
        cost_estimate=SMALL_COST,
        name="ffn_rows",
    )(words, ffn, *tokens)


def out_project_kernel(chunks, rank_ref, x_ref, gain_ref, w_ref, *refs):
    residual_ref, mid_ref, all_ref = refs[-3:]
    rank = rank_ref[0]
    for k in range(chunks):
        width = refs[k].shape[1]
        all_ref[:, pl.ds(pl.multiple_of((rank ^ k) * width, width), width)] = refs[k][...]
    residual = x_ref[...].astype(F32) + mm_nt(all_ref[...], w_ref[...])
    residual_ref[...] = residual
    scale = lax.rsqrt(jnp.mean(residual * residual, axis=1, keepdims=True) + 1e-05)
    mid_ref[...] = (residual * scale * gain_ref[...]).astype(BF16)


def out_project(rank, x, gain, attn, weights):
    count, width = x.shape
    return pl.pallas_call(
        functools.partial(out_project_kernel, len(attn)),
        in_specs=[SCALAR] + [WHOLE] * (3 + len(attn)),
        out_specs=[WHOLE] * 2,
        out_shape=(
            jax.ShapeDtypeStruct((count, width), F32),
            jax.ShapeDtypeStruct((count, width), BF16),
        ),
        scratch_shapes=[pltpu.VMEM((count, weights.shape[1]), BF16)],
        compiler_params=pltpu.CompilerParams(vmem_limit_bytes=VMEM_BYTES),
        cost_estimate=SMALL_COST,
        name="out_project",
    )(rank, x, gain, weights, *attn)


def mid_back_kernel(chunks, handed, rank_ref, grad_ref, residual_ref, gain_ref, w_ref, *refs):
    parts = refs[:chunks]
    outs, all_ref = refs[chunks + handed :], refs[-1]
    res_grad_ref, low_ref, gain_grad_ref, chunk_refs = outs[0], outs[1], outs[2], outs[3 : 3 + chunks]
    rank = rank_ref[0]
    mid_grad = parts[0][...].astype(F32)
    for k in range(1, chunks):
        mid_grad += parts[k][...].astype(F32)
    residual = residual_ref[...]
    scale = lax.rsqrt(jnp.mean(residual * residual, axis=1, keepdims=True) + 1e-05)
    unit = residual * scale
    gain_grad_ref[...] = jnp.sum(mid_grad * unit, axis=0, keepdims=True)
    scaled = mid_grad * gain_ref[...]
    inner = jnp.mean(scaled * unit, axis=1, keepdims=True)
    res_grad = grad_ref[...].astype(F32) + scale * (scaled - unit * inner)
    res_grad_ref[...] = res_grad
    low = res_grad.astype(BF16)
    low_ref[...] = low
    all_ref[...] = mm(low, w_ref[...]).astype(BF16)
    for k in range(chunks):
        width = chunk_refs[k].shape[1]
        chunk_refs[k][...] = all_ref[:, pl.ds(pl.multiple_of((rank ^ k) * width, width), width)]


def mid_back(rank, grad, residual, gain, parts, weights, passed):
    count, width = residual.shape
    chunks = len(parts)
    wide = weights.shape[1]
    first = 5 + chunks
    outs = pl.pallas_call(
        functools.partial(mid_back_kernel, chunks, len(passed)),
        in_specs=[SCALAR] + [WHOLE] * (first - 1) + [ANYWHERE] * len(passed),
        out_specs=[WHOLE] * (3 + chunks) + [ANYWHERE] * len(passed),
        out_shape=[
            jax.ShapeDtypeStruct((count, width), F32),
            jax.ShapeDtypeStruct((count, width), BF16),
            jax.ShapeDtypeStruct((1, width), F32),
        ]
        + [jax.ShapeDtypeStruct((count, wide // chunks), BF16)] * chunks
        + [jax.ShapeDtypeStruct(p.shape, p.dtype) for p in passed],
        input_output_aliases={first + i: 3 + chunks + i for i in range(len(passed))},
        scratch_shapes=[pltpu.VMEM((count, wide), BF16)],
        compiler_params=pltpu.CompilerParams(vmem_limit_bytes=VMEM_BYTES),
        cost_estimate=SMALL_COST,
        name="mid_back",
    )(rank, grad, residual, gain, weights, *parts, *passed)
    return (*outs[:3], outs[3 : 3 + chunks], list(outs[3 + chunks :]))


def in_back_kernel(chunks, x_ref, res_grad_ref, gain_ref, *refs):
    x = x_ref[...].astype(F32)
    grad = refs[0][...].astype(F32)
    for k in range(1, chunks):
        grad += refs[k][...].astype(F32)
    scale = lax.rsqrt(jnp.mean(x * x, axis=1, keepdims=True) + 1e-05)
    unit = x * scale
    scaled = grad * gain_ref[...]
    inner = jnp.mean(scaled * unit, axis=1, keepdims=True)
    refs[-1][...] = (res_grad_ref[...] + scale * (scaled - unit * inner)).astype(BF16)


def in_back(x, res_grad, gain, parts, tokens):
    return pl.pallas_call(
        functools.partial(in_back_kernel, len(parts)),
        in_specs=[WHOLE] * (3 + len(parts)) + [ANYWHERE] * len(tokens),
        out_specs=WHOLE,
        out_shape=jax.ShapeDtypeStruct(x.shape, BF16),
        compiler_params=pltpu.CompilerParams(vmem_limit_bytes=VMEM_BYTES),
        cost_estimate=SMALL_COST,
        name="in_back",
    )(x, res_grad, gain, *parts, *tokens)


def swapped(value, axis, mask):
    devices = lax.axis_size(axis)
    return lax.ppermute(value, axis, [(i, i ^ mask) for i in range(devices)])


def pinned(value, other):
    return value + 0 * other[:1, :1].astype(value.dtype)


def spread(value):
    return [value] + [swapped(value, "seq", k) for k in range(1, lax.axis_size("seq"))]


def returned(chunks):
    return [chunks[0]] + [swapped(chunks[k], "seq", k) for k in range(1, len(chunks))]


class RowSum:
    def __init__(self, outs):
        self.outs = list(outs)

    def pair(self):
        if len(self.outs) == 2:
            self.got = swapped(self.outs[1], "mp", 1)

    def join(self, *tokens):
        seq_count, mp_count = lax.axis_size("seq"), lax.axis_size("mp")
        if len(self.outs) == 1:
            (grad,) = self.outs
            cols = grad.shape[1]
            parts = grad.astype(F32).reshape(seq_count, mp_count, -1, cols).transpose(1, 0, 2, 3)
            own = lax.psum_scatter(parts.reshape(-1, cols), "mp", scatter_dimension=0, tiled=True)
            self.half = grad
            self.parts = own.reshape(1, seq_count, -1, cols)
            return
        self.half = joined([(self.outs[0], self.got)], tokens)
        self.between()

    def between(self):
        mp_count = lax.axis_size("mp")
        groups = [list(range(core, mp_count, 2)) for core in range(2)]
        self.parts = lax.all_to_all(self.half, "mp", 0, 0, axis_index_groups=groups, tiled=True)

    def beside(self, other):
        if len(self.outs) == 1:
            both = RowSum([jnp.concatenate([self.outs[0], other.outs[0]], 1)])
            both.join()
            return both
        both = RowSum([])
        both.half = joined([(s.outs[0], s.got) for s in (self, other)], [])
        both.between()
        return both


def row_sums(sums, tokens):
    groups = [part.parts for part in sums]
    shape = groups[0].shape[1:3]
    cols = [group.shape[3] for group in groups]

    def kernel(*refs):
        place = 0
        for ref, width in zip(refs, cols):
            total = ref[0].astype(F32)
            for k in range(1, ref.shape[0]):
                total += ref[k].astype(F32)
            refs[-1][:, :, place : place + width] = total.astype(BF16)
            place = place + width

    return pl.pallas_call(
        kernel,
        in_specs=[WHOLE] * len(groups) + [ANYWHERE] * len(tokens),
        out_specs=WHOLE,
        out_shape=jax.ShapeDtypeStruct(shape + (sum(cols),), BF16),
        cost_estimate=SMALL_COST,
        compiler_params=pltpu.CompilerParams(vmem_limit_bytes=VMEM_BYTES),
        name="row_sums",
    )(*groups, *tokens)


def finish_kernel(heads, wide, half, rows, pieces_ref, *refs):
    qkv_ref, gate_ref, beta_ref, conv_ref, out_ref, gu_ref, down_ref, small_ref = refs
    chunks = pieces_ref.shape[0]
    keys, vals = heads * DK, heads * DV
    ffn, mix = 0, 3 * wide
    gate_first, first, out_first = mix, mix + vals, pieces_ref.shape[2] - vals

    def piece(j, start, width):
        return pieces_ref[j, :, start : start + width].astype(F32)

    for j in range(chunks):
        gate_ref[:, j * vals : (j + 1) * vals] = piece(j, gate_first, vals)
        qkv_ref[:, j * keys : (j + 1) * keys] = piece(j, first, keys)
        place = chunks * keys + j * keys
        qkv_ref[:, place : place + keys] = piece(j, first + keys, keys)
        place = 2 * chunks * keys + j * vals
        qkv_ref[:, place : place + vals] = piece(j, first + 2 * keys, vals)
        out_ref[:, j * vals : (j + 1) * vals] = piece(j, out_first, vals)
        beta = piece(j, first + 2 * keys + vals, 128)
        beta_ref[:, j * heads : (j + 1) * heads] = beta[:, :heads]
    small = piece(0, out_first - 128, 128)
    for j in range(1, chunks):
        small += piece(j, out_first - 128, 128)
    small_ref[...] = small
    conv_ref[...] = small[: conv_ref.shape[0]]
    for part in range(3):
        whole = jnp.concatenate(
            [piece(j, ffn + part * wide, wide)[:, :half] for j in range(chunks)], 1
        )
        if part < 2:
            gu_ref[:, part * chunks * half : (part + 1) * chunks * half] = whole
        else:
            down_ref[...] = whole


def finish(pieces, heads, wide, half, taps):
    chunks, rows, _ = pieces.shape
    keys, vals = HEAD_COUNT * DK, HEAD_COUNT * DV
    ffn = chunks * half
    shapes = [(rows, 2 * keys + vals), (rows, vals), (rows, HEAD_COUNT), (taps, 128)]
    shapes += [(rows, vals), (rows, 2 * ffn), (rows, ffn), (rows, 128)]
    return pl.pallas_call(
        functools.partial(finish_kernel, heads, wide, half, rows),
        in_specs=[WHOLE],
        out_specs=[WHOLE] * len(shapes),
        out_shape=[jax.ShapeDtypeStruct(shape, F32) for shape in shapes],
        compiler_params=pltpu.CompilerParams(vmem_limit_bytes=VMEM_BYTES),
        cost_estimate=SMALL_COST,
        name="finish",
    )(pieces)


def dealt(own):
    return lax.all_to_all(own, "seq", 0, 0, tiled=True)


def left_product(left, right):
    return lax.dot_general(
        left, right, (((0,), (0,)), ((), ())), preferred_element_type=jnp.float32
    )


def right_product(left, right):
    return lax.dot_general(
        left, right, (((1,), (1,)), ((), ())), preferred_element_type=jnp.float32
    )


def dot(left, right):
    return jnp.dot(left, right, preferred_element_type=jnp.float32)


def silu_slope(values):
    gate = jax.nn.sigmoid(values)
    return gate * (1.0 + values * (1.0 - gate))


def split_three(values):
    high = values.astype(BF16)
    rest = values - high.astype(F32)
    middle = rest.astype(BF16)
    return jnp.stack([high, middle, (rest - middle.astype(F32)).astype(BF16)])


def body(
    layer_in,
    out_grad,
    seq_lengths,
    dealing,
    log_decay,
    w_qkv,
    w_out_gate,
    w_beta,
    conv_w,
    gain_in,
    gain_o,
    w_out,
    gain_mid,
    w_gate_up,
    w_down,
):
    seq_count, mp_count = lax.axis_size("seq"), lax.axis_size("mp")
    rank, place_mp = lax.axis_index("seq"), lax.axis_index("mp")
    count = layer_in.shape[1]
    rows = w_qkv.shape[0]
    heads = HEAD_COUNT // seq_count
    key_cols, val_cols = heads * DK, heads * DV
    half = w_down.shape[0] // seq_count
    wide = -(-half // 256) * 256
    taps = conv_w.shape[1]
    total = dealing.shape[1]
    devices = seq_count * mp_count
    channels = 2 * key_cols + val_cols
    all_keys, ffn = HEAD_COUNT * DK, w_down.shape[0]
    split = (seq_count, mp_count // 2) if mp_count <= 8 else None
    words = jnp.stack([place_mp % 2, place_mp // 2, rank]).astype(jnp.int32)
    rank_word = rank.astype(jnp.int32).reshape(1)

    small = jnp.concatenate([conv_w.T.reshape(-1), gain_in, gain_mid, gain_o])
    small_count = small.shape[0]
    spare = 128 - heads
    filler = jnp.concatenate([small, jnp.zeros((rows * spare - small_count,), BF16)])
    filler = filler.reshape(rows, spare)
    wide_filler = jnp.zeros((rows, wide - half), BF16)
    turned_down = w_down.T
    decay_lanes = -(-3 * heads * count // (128 * rows)) * 128
    decays = split_three(log_decay[0].T)
    mix_cols = channels + 128 + val_cols
    pieces, ffn_pieces = [], []
    for j in range(seq_count):
        own_decay = decays[:, j * heads : (j + 1) * heads].reshape(-1)
        own_decay = jnp.concatenate(
            [own_decay, jnp.zeros((rows * decay_lanes - own_decay.shape[0],), BF16)]
        )
        pieces.append(
            jnp.concatenate(
                [
                    w_out_gate[:, j * val_cols : (j + 1) * val_cols],
                    w_qkv[:, j * key_cols : (j + 1) * key_cols],
                    w_qkv[:, all_keys + j * key_cols : all_keys + (j + 1) * key_cols],
                    w_qkv[:, 2 * all_keys + j * val_cols : 2 * all_keys + (j + 1) * val_cols],
                    w_beta[:, j * heads : (j + 1) * heads],
                    filler,
                    own_decay.reshape(rows, decay_lanes),
                ],
                1,
            )
        )
        ffn_pieces.append(
            jnp.concatenate(
                [
                    w_gate_up[:, j * half : (j + 1) * half],
                    wide_filler,
                    w_gate_up[:, ffn + j * half : ffn + (j + 1) * half],
                    wide_filler,
                    turned_down[:, j * half : (j + 1) * half],
                    wide_filler,
                ],
                1,
            )
        )
    def near(arrays):
        arrays = jnp.stack(arrays)
        return jnp.stack(
            returned(
                [lax.dynamic_index_in_dim(arrays, rank ^ k, 0, keepdims=False) for k in range(seq_count)]
            )
        )

    pieces, ffn_pieces = near(pieces), near(ffn_pieces)
    gathered = lax.all_gather(pieces[:, :, :mix_cols], "mp", axis=0, tiled=False)
    late = pieces[1, :1, :1] + jnp.sum(ffn_pieces[1:, :1, :1], axis=0)
    chunks_in = spread(layer_in[0] + 0 * late)

    relative = rank ^ jnp.arange(seq_count)
    smalls = gathered[:, :, :, mix_cols - spare :].transpose(1, 0, 2, 3)
    smalls = jnp.take(smalls, relative, axis=0).reshape(devices, -1)[:, :small_count]
    own_taps = conv_w.shape[0] * taps
    full_conv = smalls[:, :own_taps].reshape(-1, taps, conv_w.shape[0]).transpose(1, 0, 2)
    full_conv = full_conv.reshape(taps, -1).astype(F32)
    conv = jnp.concatenate(
        [
            lax.dynamic_slice_in_dim(full_conv, rank * key_cols, key_cols, 1),
            lax.dynamic_slice_in_dim(full_conv, all_keys + rank * key_cols, key_cols, 1),
            lax.dynamic_slice_in_dim(full_conv, 2 * all_keys + rank * val_cols, val_cols, 1),
        ],
        1,
    )
    conv = jnp.concatenate([conv, jnp.zeros((8 - taps, channels), F32)], 0)
    gains = smalls[:, own_taps:].astype(F32)
    full_gin = gains[:, :rows].reshape(1, -1)
    full_gmid = gains[:, rows : 2 * rows].reshape(1, -1)
    full_go = gains[:, 2 * rows :].reshape(1, -1)

    out_turned = w_out.T
    out_near = []
    if split:
        out_near = [out_turned] + [swapped(out_turned, "mp", 2 * j) for j in range(1, mp_count // 2)]

    out_copies = []
    if split:
        out_copies = [
            jnp.broadcast_to(jnp.stack(out_near), (seq_count, mp_count // 2, *out_turned.shape))
        ]

    decays = pieces[:, :, mix_cols:].reshape(seq_count, -1)[:, : 3 * heads * count]
    col_info, row_info, place_row = positions(
        words, seq_lengths[0], dealing, decays.reshape(seq_count, -1, BLOCK), heads, out_copies
    )

    passed = [ffn_pieces, out_grad[0] + 0 * pieces[1, :1, :1]] + out_copies
    passed = handed(passed, chunks_in[1:] + [row_info])
    ffn_all = lax.all_gather(passed[0], "mp", axis=0, tiled=False)
    chunks_grad = spread(passed[1])
    out_mine = [lax.all_to_all(passed[2], "seq", 0, 0, tiled=True)] if split else []
    (normed, gate_logit, proj, logit_parts, mix), _ = project(
        rank_word, chunks_in, full_gin, gathered, col_info, channels,
        [], [conv, full_go, full_gmid],
    )
    outs = forward_recurrence(proj, conv, col_info, row_info, logit_parts, heads, [])
    dealt_rows, attn, out_mine = gate_rows(
        outs[0], place_row, gate_logit, full_go, count, heads, out_mine, chunks_grad[1:]
    )
    if split:
        out_others = [swapped(out_mine[0], "mp", 1)]
    else:
        out_mine, out_others = [lax.all_gather(out_turned, ("seq", "mp"), axis=0, tiled=True)], []
    attn_parts = returned(attn)
    out_w, normed_t = out_rows(words, out_mine[0], out_others, normed, devices * rows, [attn[0]])

    residual, mid_own = out_project(rank_word, layer_in[0], full_gmid, attn_parts, out_w)

    ffn_w = ffn_rows(words, ffn_all, [mid_own])
    w_gu, down_turned = ffn_w[:, : 2 * wide], ffn_w[:, 2 * wide :]
    mids = spread(mid_own)
    hiddens, gu_grads, mid_parts = ([None] * seq_count for _ in range(3))
    last_part = None
    for k in (0, 1, 3, 2):
        mid_k = mids[k] if last_part is None else pinned(mids[k], last_part)
        gate_up = dot(mid_k, w_gu)
        gate, up = gate_up[:, :wide], gate_up[:, wide:]
        hiddens[k] = (silu(gate) * up).astype(BF16)
        hidden_grad = dot(chunks_grad[k], down_turned)
        gu_grads[k] = jnp.concatenate(
            [hidden_grad * up * silu_slope(gate), hidden_grad * silu(gate)], 1
        ).astype(BF16)
        mid_parts[k] = last_part = right_product(gu_grads[k], w_gu).astype(BF16)
    mid_parts = returned(mid_parts)
    ffn_sum = RowSum(
        weight_grad(
            split, words, [(mids, gu_grads), (chunks_grad, hiddens)], wide, [last_part, mid_parts[1]]
        ),
    )
    res_grad, out_proj_grad, g_mid, attn_grads, ffn_sum.outs[-1:] = mid_back(
        rank_word, out_grad[0], residual, full_gmid, mid_parts, out_w, ffn_sum.outs[-1:]
    )
    attn_grads = returned(attn_grads)
    ffn_sum.pair()
    layer_own, *both = layer_products(hiddens, ffn_w, out_proj_grad)

    (gate_grad, o_grad, g_go), both = ungate_rows(
        dealt_rows, col_info, gate_logit, full_go, attn_grads, heads, both, []
    )
    gate_sums, *gate_outs = weight_grad(
        split, words, [([normed], [gate_grad])], val_cols, [], weights=mix
    )
    gate_sum = RowSum(gate_outs)
    gate_sum.pair()
    ffn_sum = ffn_sum.beside(gate_sum)
    both = returned([None] + both)[1:]
    proj_grad, g_conv = backward_recurrence(
        proj, conv, col_info, row_info, logit_parts, outs[1:], o_grad, heads, [ffn_sum.half]
    )
    mix_grad, mix_sums, *mix_outs = unpack(
        split, words, proj_grad, gate_grad, place_row, normed_t, mix, g_conv, full_gin, g_mid, g_go,
        gate_sums, heads, [],
    )
    mix_sum = RowSum(mix_outs)
    mix_sum.pair()
    normed_parts, _ = unproject(mix_grad, mix, count, [], [])
    normed_chunks = returned(normed_parts)
    out_sum = RowSum(
        weight_grad(split, words, [([out_proj_grad] + both, attn)], val_cols,
            [normed_parts[0], ffn_sum.parts], limit=56 * MIB,
        )
    )
    out_sum.pair()
    last_sum = mix_sum.beside(out_sum)
    in_grad = in_back(layer_in[0], res_grad, full_gin, normed_chunks, [last_sum.half])
    layer_out = residual + sum(
        c.astype(F32) for c in [layer_own] + [b[count:] for b in both]
    )
    all_pieces = dealt(row_sums([ffn_sum, last_sum], [in_grad]))
    layer_out = layer_out.astype(BF16)[None]
    if split:
        g_qkv, g_gate, g_beta, g_conv, g_out, g_gu, g_down, small_sum = finish(
            all_pieces, heads, wide, half, taps
        )
        device = rank * mp_count + place_mp
        grad_go = lax.dynamic_slice_in_dim(
            small_sum[4:6].reshape(-1), device * gain_o.shape[0], gain_o.shape[0]
        )
        grad_gmid = lax.dynamic_slice_in_dim(small_sum[8:16].reshape(-1), device * rows, rows)
        grad_gin = lax.dynamic_slice_in_dim(small_sum[16:24].reshape(-1), device * rows, rows)
        return (
            layer_out, in_grad[None], g_qkv, g_gate, g_beta, g_conv.T,
            grad_gin, grad_go, g_out.T, grad_gmid, g_gu, g_down.T,
        )

    def columns(first, width):
        parts = [all_pieces[j, :, first : first + width] for j in range(seq_count)]
        return jnp.concatenate(parts, 1).astype(F32)

    everywhere = ("seq", "mp")
    conv_full = jnp.zeros((taps, conv_w.shape[0] * devices), F32)
    for first, width in ((0, key_cols), (key_cols, key_cols), (2 * key_cols, val_cols)):
        conv_full = lax.dynamic_update_slice_in_dim(
            conv_full, g_conv[:taps, first : first + width], first * seq_count + rank * width, 1
        )
    grad_conv = lax.psum_scatter(conv_full.T, everywhere, scatter_dimension=0, tiled=True)
    g_gin = mix_sums[0] / full_gin[0]
    grad_gin, grad_gmid, grad_go = (
        lax.psum_scatter(g, everywhere, scatter_dimension=0, tiled=True)
        for g in (g_gin, g_mid[0], g_go[0])
    )
    first = 3 * wide + val_cols
    last = all_pieces.shape[2] - val_cols
    return (
        layer_out,
        in_grad[None],
        jnp.concatenate(
            [
                columns(first, key_cols),
                columns(first + key_cols, key_cols),
                columns(first + 2 * key_cols, val_cols),
            ],
            1,
        ),
        columns(3 * wide, val_cols),
        columns(first + channels, heads),
        grad_conv,
        grad_gin,
        grad_go,
        columns(last, val_cols).T,
        grad_gmid,
        jnp.concatenate([columns(0, half), columns(wide, half)], 1),
        columns(2 * wide, half).T,
    )


def solution(mesh):
    in_specs = (
        P("mp", "seq", None),
        P("mp", "seq", None),
        P("mp", None),
        P("mp", None),
        P("mp", "seq", None),
        P(("seq", "mp"), None),
        P(("seq", "mp"), None),
        P(("seq", "mp"), None),
        P(("seq", "mp"), None),
        P(("seq", "mp")),
        P(("seq", "mp")),
        P(None, ("seq", "mp")),
        P(("seq", "mp")),
        P(("seq", "mp"), None),
        P(None, ("seq", "mp")),
    )
    out_specs = (
        P("mp", "seq", None),
        P("mp", "seq", None),
        P(("seq", "mp"), None),
        P(("seq", "mp"), None),
        P(("seq", "mp"), None),
        P(("seq", "mp"), None),
        P(("seq", "mp")),
        P(("seq", "mp")),
        P(None, ("seq", "mp")),
        P(("seq", "mp")),
        P(("seq", "mp"), None),
        P(None, ("seq", "mp")),
    )
    return jax.shard_map(body, mesh=mesh, in_specs=in_specs, out_specs=out_specs, check_vma=False)
```

```python
import functools

import jax
import jax.numpy as jnp
from jax import lax
from jax.experimental import pallas as pl
from jax.experimental.pallas import tpu as pltpu
from jax.sharding import PartitionSpec as P

HEAD_COUNT = 8
DK = 128
DV = 256
BLOCK = 128
FORWARD_STEP = 6
BACKWARD_STEP = 2
F32 = jnp.float32
BF16 = jnp.bfloat16


def mm(left, right):
    return jnp.dot(left.astype(BF16), right.astype(BF16), preferred_element_type=F32)


def mm_nt(left, right):
    return lax.dot_general(
        left.astype(BF16),
        right.astype(BF16),
        (((1,), (1,)), ((), ())),
        preferred_element_type=F32,
    )


def mm_tn(left, right):
    return lax.dot_general(
        left.astype(BF16),
        right.astype(BF16),
        (((0,), (0,)), ((), ())),
        preferred_element_type=F32,
    )


def masks():
    rows = lax.broadcasted_iota(jnp.int32, (BLOCK, BLOCK), 0)
    cols = lax.broadcasted_iota(jnp.int32, (BLOCK, BLOCK), 1)
    return rows, cols


def unit_inverses(mats, rows, cols):
    ident = (rows == cols).astype(F32)
    near = (rows // 16) == (cols // 16)
    power = [jnp.where(near, a, 0.0) for a in mats]
    result = [ident - p for p in power]
    span = 2
    while span < 16:
        power = [mm(p, p) for p in power]
        result = [t + mm(t, p) for t, p in zip(result, power)]
        span *= 2
    size = 16
    while size < BLOCK:
        off = ((rows // (2 * size)) == (cols // (2 * size))) & ((rows // size) != (cols // size))
        reach = [mm(jnp.where(off, a, 0.0), t) for a, t in zip(mats, result)]
        result = [t - mm(t, x) for t, x in zip(result, reach)]
        size *= 2
    return result


def convolve(ext_ref, conv_ref, col_ref, start, first, width):
    cols = pl.ds(first, width)
    total = ext_ref[pl.ds(16 + start, BLOCK), cols] * conv_ref[3:4, cols]
    for tap in range(3):
        keep = col_ref[pl.ds(start, BLOCK), tap : tap + 1]
        total += ext_ref[pl.ds(13 + tap + start, BLOCK), cols] * keep * conv_ref[tap : tap + 1, cols]
    return total


def column(col_ref, start, index):
    return col_ref[pl.ds(start, BLOCK), index : index + 1]


def strength(logit_ref, start, head, heads):
    return jax.nn.sigmoid(column(logit_ref, start, head))


def exact_nt(left, right):
    left_high, right_high = left.astype(BF16), right.astype(BF16)
    left_low = left - left_high.astype(F32)
    right_low = right - right_high.astype(F32)
    return mm_nt(left_high, right_high) + (mm_nt(left_high, right_low) + mm_nt(left_low, right_high))


def decay_matrix(col_ref, row_ref, start, head, heads, rows, cols):
    cum_i = column(col_ref, start, 5 + head)
    cum_j = row_ref[head : head + 1, pl.ds(start, BLOCK)]
    seg_i = column(col_ref, start, 3)
    seg_j = row_ref[heads : heads + 1, pl.ds(start, BLOCK)]
    within = (rows >= cols) & (seg_i == seg_j)
    return jnp.where(within, jnp.exp(jnp.where(within, cum_i - cum_j, 0.0)), 0.0)


def silu(values):
    return values * jax.nn.sigmoid(values)


def forward_kernel(
    heads, edge_ref, proj_ref, conv_ref, col_ref, row_ref, logit_ref, *refs,
):
    o_ref, s_ref, n_ref, t_ref, w_ref, p_ref, pre_ref, ext_ref, state_ref = refs[-9:]
    steps = proj_ref.shape[0] // BLOCK

    @pl.when(pl.program_id(0) == 0)
    def _():
        state_ref[...] = jnp.zeros_like(state_ref)

    ext_ref[:16, :] = edge_ref[...].astype(F32)
    ext_ref[16:, :] = proj_ref[...].astype(F32)
    rows, cols = masks()
    strict = rows > cols
    units = [(g, h) for g in range(steps) for h in range(heads)]
    queries, keys, values, mats, decays, betas = {}, {}, {}, [], {}, {}
    for g, h in units:
        start = g * BLOCK

        def taken(first, width):
            value = convolve(ext_ref, conv_ref, col_ref, start, first, width)
            pre_ref[pl.ds(start, BLOCK), first : first + width] = value
            return value

        queries[g, h] = silu(taken(h * DK, DK))
        raw = silu(taken((heads + h) * DK, DK))
        keys[g, h] = raw * lax.rsqrt(jnp.sum(raw * raw, axis=1, keepdims=True) + 1e-06)
        values[g, h] = silu(taken(2 * heads * DK + h * DV, DV))
        decays[g, h] = decay_matrix(col_ref, row_ref, start, h, heads, rows, cols)
        betas[g, h] = strength(logit_ref, start, h, heads)
        beta = betas[g, h]
        inner = mm_nt(keys[g, h], keys[g, h])
        mats.append(jnp.where(strict, beta * inner * decays[g, h], 0.0))
    inverses = unit_inverses(mats, rows, cols)
    umats, wmats, pmats, boundary, reads = {}, {}, {}, {}, {}
    for (g, h), inverse in zip(units, inverses):
        start = g * BLOCK
        beta = betas[g, h]
        elog = column(col_ref, start, 5 + heads + h)
        flog = column(col_ref, start, 5 + 2 * heads + h)
        inverse = inverse.astype(BF16)
        t_ref[g, h] = inverse
        umats[g, h] = mm(inverse, beta * values[g, h])
        wmats[g, h] = mm(inverse, (beta * elog) * keys[g, h]).astype(BF16)
        w_ref[g, h] = wmats[g, h]
        pmats[g, h] = (exact_nt(queries[g, h], keys[g, h]) * decays[g, h]).astype(BF16)
        p_ref[g, h] = pmats[g, h]
        boundary[g, h] = (keys[g, h] * flog).T.astype(BF16)
        reads[g, h] = (queries[g, h] * elog).astype(BF16)
    for g in range(steps):
        start = g * BLOCK
        for h in range(heads):
            state = state_ref[h]
            low = state.astype(BF16)
            s_ref[g, h] = low
            news = (umats[g, h] - mm(wmats[g, h], low)).astype(BF16)
            n_ref[g, h] = news
            carried = col_ref[pl.ds(start + BLOCK - 1, 1), 5 + heads + h : 6 + heads + h]
            state_ref[h] = carried * state + mm(boundary[g, h], news)
            output = mm(reads[g, h], low) + mm(pmats[g, h], news)
            o_ref[pl.ds(start, BLOCK), h * DV : (h + 1) * DV] = output.astype(BF16)


def backward_kernel(
    heads, edge_ref, proj_ref, conv_ref, col_ref, row_ref, logit_ref,
    s_ref, n_ref, t_ref, w_ref, p_ref, pre_ref, do_ref, *refs,
):
    grad_ref, gconv_ref, ext_ref, shift_ref, dstate_ref, head_ref = refs[-6:]
    count = proj_ref.shape[0]
    steps = count // BLOCK
    channels = proj_ref.shape[1]

    @pl.when(pl.program_id(0) == 0)
    def _():
        dstate_ref[...] = jnp.zeros_like(dstate_ref)
        head_ref[...] = jnp.zeros_like(head_ref)
        gconv_ref[...] = jnp.zeros_like(gconv_ref)

    ext_ref[:16, :] = edge_ref[...].astype(F32)
    ext_ref[16:, :] = proj_ref[...].astype(F32)
    for tap in range(3):
        shift_ref[tap, count : count + 8, :] = head_ref[tap]
    rows, cols = masks()
    strict = rows > cols
    units = [(g, h) for g in reversed(range(steps)) for h in range(heads)]
    queries, keys, pre, reads, first, gains = {}, {}, {}, {}, {}, {}
    for g, h in units:
        start = g * BLOCK

        def taken(first, width):
            return pre_ref[pl.ds(start, BLOCK), first : first + width]

        elog = column(col_ref, start, 5 + heads + h)
        out_grad = do_ref[pl.ds(start, BLOCK), h * DV : (h + 1) * DV]
        queries[g, h] = silu(taken(h * DK, DK))
        raw = silu(taken((heads + h) * DK, DK))
        scale = lax.rsqrt(jnp.sum(raw * raw, axis=1, keepdims=True) + 1e-06)
        keys[g, h] = (raw * scale, scale)
        first[g, h] = mm_tn(p_ref[g, h], out_grad)
        gains[g, h] = mm_tn(queries[g, h] * elog, out_grad)
    news_grads, state_grads = {}, {}
    for g in reversed(range(steps)):
        start = g * BLOCK
        for h in range(heads):
            flog = column(col_ref, start, 5 + 2 * heads + h)
            dstate = dstate_ref[h]
            low = dstate.astype(BF16)
            state_grads[g, h] = low
            news_grad = (first[g, h] + mm(keys[g, h][0] * flog, low)).astype(BF16)
            news_grads[g, h] = news_grad
            carried = col_ref[pl.ds(start + BLOCK - 1, 1), 5 + heads + h : 6 + heads + h]
            dstate_ref[h] = gains[g, h] + carried * dstate - mm_tn(w_ref[g, h], news_grad)
    lane = lax.broadcasted_iota(jnp.int32, (BLOCK, 128), 1)

    def through_conv(g, first_col, width, grad):
        start = g * BLOCK
        cols_ = pl.ds(first_col, width)
        value = pre_ref[pl.ds(start, BLOCK), first_col : first_col + width]
        gate = jax.nn.sigmoid(value)
        grad = grad * (gate * (1.0 + value * (1.0 - gate)))
        shift_ref[3, pl.ds(start, BLOCK), cols_] = grad * conv_ref[3:4, cols_]
        sums = []
        for tap in range(3):
            kept = grad * col_ref[pl.ds(start, BLOCK), tap : tap + 1]
            shift_ref[tap, pl.ds(start, BLOCK), cols_] = kept * conv_ref[tap : tap + 1, cols_]
            sums.append(
                jnp.sum(kept * ext_ref[pl.ds(13 + tap + start, BLOCK), cols_], axis=0, keepdims=True)
            )
        sums.append(
            jnp.sum(grad * ext_ref[pl.ds(16 + start, BLOCK), cols_], axis=0, keepdims=True)
        )
        for tap in range(4):
            gconv_ref[tap : tap + 1, cols_] += sums[tap]

    logit_grads = {}
    for g, h in units:
        start = g * BLOCK
        beta = strength(logit_ref, start, h, heads)
        elog = column(col_ref, start, 5 + heads + h)
        flog = column(col_ref, start, 5 + 2 * heads + h)
        key, scale = keys[g, h]
        query = queries[g, h]
        out_grad = do_ref[pl.ds(start, BLOCK), h * DV : (h + 1) * DV]
        decay = decay_matrix(col_ref, row_ref, start, h, heads, rows, cols)
        key_low = key.astype(BF16)
        inner = mm_nt(key_low, key_low) * decay
        news, state, dstate = n_ref[g, h], s_ref[g, h], state_grads[g, h]
        rhs_grad = mm_tn(t_ref[g, h], news_grads[g, h])
        rhs_low = rhs_grad.astype(BF16)
        within = (mm_nt(out_grad, news) * decay).astype(BF16)
        mat_grad = jnp.where(strict, -mm_nt(rhs_low, news), 0.0)
        pair = (mat_grad * beta * decay).astype(BF16)
        back = mm_nt(rhs_low, state)
        q_grad = mm(within, key_low) + elog * mm_nt(out_grad, state)
        k_grad = (
            mm_tn(within, query)
            + mm(pair, key_low)
            + mm_tn(pair, key_low)
            + flog * mm_nt(news, dstate)
            - (beta * elog) * back
        )
        value = silu(pre_ref[pl.ds(start, BLOCK), pl.ds(2 * heads * DK + h * DV, DV)])
        beta_grad = (
            jnp.sum(mat_grad * inner - elog * (key * back), axis=1, keepdims=True)
            + jnp.sum(rhs_grad * value, axis=1, keepdims=True)
        )
        logit_grads[g, h] = beta_grad * beta * (1.0 - beta)
        raw_grad = scale * (k_grad - key * jnp.sum(k_grad * key, axis=1, keepdims=True))
        through_conv(g, h * DK, DK, q_grad)
        through_conv(g, (heads + h) * DK, DK, raw_grad)
        through_conv(g, 2 * heads * DK + h * DV, DV, beta * rhs_grad)
    for g in range(steps):
        total = jnp.zeros((BLOCK, 128), F32)
        for h in range(heads):
            total = jnp.where(lane == h, logit_grads[g, h], total)
        grad_ref[pl.ds(g * BLOCK, BLOCK), channels : channels + 128] = total.astype(BF16)
        grad_ref[pl.ds(g * BLOCK, BLOCK), channels + 128 :] = jnp.zeros((BLOCK, 128), BF16)
    total = shift_ref[3, :count, :]
    for tap in range(3):
        total += shift_ref[tap, pl.ds(3 - tap, count), :]
    grad_ref[:, :channels] = total.astype(BF16)
    for tap in range(3):
        head_ref[tap] = shift_ref[tap, :8, :]


def saved_shapes(blocks, heads):
    return (
        jax.ShapeDtypeStruct((blocks, heads, DK, DV), BF16),
        jax.ShapeDtypeStruct((blocks, heads, BLOCK, DV), BF16),
        jax.ShapeDtypeStruct((blocks, heads, BLOCK, BLOCK), BF16),
        jax.ShapeDtypeStruct((blocks, heads, BLOCK, DK), BF16),
        jax.ShapeDtypeStruct((blocks, heads, BLOCK, BLOCK), BF16),
        jax.ShapeDtypeStruct((blocks * BLOCK, heads * (2 * DK + DV)), F32),
    )


def saved_specs(shapes, per_step, index):
    return [
        pl.BlockSpec((per_step,) + shape.shape[1:], lambda i: (index(i), 0, 0, 0))
        for shape in shapes[:-1]
    ] + [pl.BlockSpec((per_step * BLOCK, shapes[-1].shape[1]), lambda i: (index(i), 0))]


def common_specs(step, channels, logits, index):
    return [
        pl.BlockSpec((16, channels), lambda i: (jnp.maximum(index(i) * (step // 16) - 1, 0), 0)),
        pl.BlockSpec((step, channels), lambda i: (index(i), 0)),
        pl.BlockSpec((8, channels), lambda i: (0, 0)),
        pl.BlockSpec((step, 128), lambda i: (index(i), 0)),
        pl.BlockSpec((8, step), lambda i: (0, index(i))),
        pl.BlockSpec((step, logits), lambda i: (index(i), 0)),
    ]


MIB = 1024 * 1024
VMEM_BYTES = 24 * MIB
SMALL_COST = pl.CostEstimate(flops=10**6, bytes_accessed=10**6, transcendentals=0)
ANYWHERE = pl.BlockSpec(memory_space=pl.ANY)
WHOLE = pl.BlockSpec(memory_space=pltpu.VMEM)
SCALAR = pl.BlockSpec(memory_space=pltpu.SMEM)


def params(limit=VMEM_BYTES):
    return pltpu.CompilerParams(dimension_semantics=("arbitrary",), vmem_limit_bytes=limit)


def forward_recurrence(proj, conv, cols, rows, logits, heads, tokens):
    count, channels = proj.shape
    step = BLOCK * FORWARD_STEP
    shapes = saved_shapes(count // BLOCK, heads)
    index = lambda i: i
    return pl.pallas_call(
        functools.partial(forward_kernel, heads),
        grid=(count // step,),
        in_specs=common_specs(step, channels, 128, index) + [ANYWHERE] * len(tokens),
        out_specs=[pl.BlockSpec((step, heads * DV), lambda i: (i, 0))] + saved_specs(shapes, FORWARD_STEP, index),
        out_shape=(jax.ShapeDtypeStruct((count, heads * DV), BF16),) + shapes,
        scratch_shapes=[
            pltpu.VMEM((step + 16, channels), F32),
            pltpu.VMEM((heads, DK, DV), F32),
        ],
        compiler_params=params(56 * MIB),
        cost_estimate=SMALL_COST,
        name="recurrence_forward",
    )(proj, proj, conv, cols, rows, logits, *tokens)


def backward_recurrence(proj, conv, cols, rows, logits, saved, out_grad, heads, tokens):
    count, channels = proj.shape
    step = BLOCK * BACKWARD_STEP
    last = count // step - 1
    index = lambda i: last - i
    return pl.pallas_call(
        functools.partial(backward_kernel, heads),
        grid=(count // step,),
        in_specs=common_specs(step, channels, 128, index)
        + saved_specs(saved, BACKWARD_STEP, index)
        + [pl.BlockSpec((step, heads * DV), lambda i: (index(i), 0))]
        + [ANYWHERE] * len(tokens),
        out_specs=[
            pl.BlockSpec((step, channels + 256), lambda i: (index(i), 0)),
            pl.BlockSpec((8, channels), lambda i: (0, 0)),
        ],
        out_shape=(
            jax.ShapeDtypeStruct((count, channels + 256), BF16),
            jax.ShapeDtypeStruct((8, channels), F32),
        ),
        scratch_shapes=[
            pltpu.VMEM((step + 16, channels), F32),
            pltpu.VMEM((4, step + 8, channels), F32),
            pltpu.VMEM((heads, DK, DV), F32),
            pltpu.VMEM((3, 8, channels), F32),
        ],
        compiler_params=params(56 * MIB),
        cost_estimate=SMALL_COST,
        name="recurrence_backward",
    )(proj, proj, conv, cols, rows, logits, *saved, out_grad, *tokens)


def project_kernel(
    channels, chunks, handed, rank_ref, gain_ref, w_ref, col_ref, *refs
):
    x_refs = refs[:chunks]
    normed_ref, gate_ref, proj_ref, logit_ref, all_ref = refs[chunks + handed : chunks + handed + 5]
    rows_ref = refs[-1]
    step = pl.program_id(0)
    count = x_refs[0].shape[0]

    @pl.when(step == 0)
    def _():
        width = w_ref.shape[0] * w_ref.shape[2]
        for k in range(w_ref.shape[1]):
            place = pl.ds(pl.multiple_of((rank_ref[0] ^ k) * width, width), width)
            all_ref[place, :] = w_ref[:, k].reshape(width, w_ref.shape[3])

    for k in range(chunks):

        @pl.when(step == k)
        def _():
            x = x_refs[k][...].astype(F32)
            scale = lax.rsqrt(jnp.mean(x * x, axis=1, keepdims=True) + 1e-05)
            normed = (x * scale * gain_ref[...]).astype(BF16)
            normed_ref[...] = normed
            total = mm(normed, all_ref[...])
            gates = gate_ref.shape[1]
            gate_ref[...] = total[:, :gates]
            logit = total[:, gates + channels :]
            high = logit.astype(BF16)
            place = slice(k * count, (k + 1) * count)
            rows_ref[place, : channels + 128] = total[:, gates:].astype(BF16)
            rows_ref[place, channels + 128 :] = (logit - high.astype(F32)).astype(BF16)

    @pl.when(step >= chunks)
    def _():
        order = lax.broadcasted_iota(jnp.int32, (proj_ref.shape[0], rows_ref.shape[0]), 1)
        picked = (col_ref[:, 4:5].astype(jnp.int32) == order).astype(F32)
        packed = mm(picked, rows_ref[...])
        proj_ref[...] = packed[:, :channels].astype(BF16)
        logit_ref[...] = packed[:, channels : channels + 128] + packed[:, channels + 128 :]


def project(rank, x_chunks, gain, weights, cols, channels, passed, tokens):
    count, width = x_chunks[0].shape
    total = count * len(x_chunks)
    gates = weights.shape[3] - channels - 128
    chunks = total // count
    block = total // 2
    first = lambda i: jnp.minimum(i, chunks - 1)
    later = lambda i: jnp.maximum(i - chunks, 0)
    outs = pl.pallas_call(
        functools.partial(project_kernel, channels, chunks, len(passed) + len(tokens)),
        grid=(chunks + total // block,),
        in_specs=[
            SCALAR,
            pl.BlockSpec((1, width), lambda i: (0, 0)),
            pl.BlockSpec(weights.shape, lambda i: (0, 0, 0, 0)),
            pl.BlockSpec((block, 128), lambda i: (later(i), 0)),
        ]
        + [pl.BlockSpec((count, width), lambda i: (0, 0))] * chunks
        + [ANYWHERE] * (len(passed) + len(tokens)),
        out_specs=[
            pl.BlockSpec((count, width), lambda i: (first(i), 0)),
            pl.BlockSpec((count, gates), lambda i: (first(i), 0)),
            pl.BlockSpec((block, channels), lambda i: (later(i), 0)),
            pl.BlockSpec((block, 128), lambda i: (later(i), 0)),
            pl.BlockSpec((width, weights.shape[3]), lambda i: (0, 0)),
        ]
        + [ANYWHERE] * len(passed),
        out_shape=[
            jax.ShapeDtypeStruct((total, width), BF16),
            jax.ShapeDtypeStruct((total, gates), F32),
            jax.ShapeDtypeStruct((total, channels), BF16),
            jax.ShapeDtypeStruct((total, 128), F32),
            jax.ShapeDtypeStruct((width, weights.shape[3]), BF16),
        ]
        + [jax.ShapeDtypeStruct(p.shape, p.dtype) for p in passed],
        input_output_aliases={4 + chunks + i: 5 + i for i in range(len(passed))},
        scratch_shapes=[pltpu.VMEM((total, channels + 256), BF16)],
        compiler_params=params(56 * MIB),
        cost_estimate=SMALL_COST,
        name="project",
    )(rank, gain, weights, cols, *x_chunks, *passed, *tokens)
    return outs[:5], outs[5:]


def gate_kernel(heads, count, first, o_ref, place_ref, gate_ref, gain_ref, *refs):
    chunks = place_ref.shape[1] // count
    dealt_ref, chunk_refs = refs[first], refs[first + 1 : first + 1 + chunks]
    for k, chunk_ref in enumerate(chunk_refs):
        order = lax.broadcasted_iota(jnp.int32, (count, o_ref.shape[0]), 0) + k * count
        picked = (place_ref[...].astype(jnp.int32) == order).astype(F32)
        rows = mm(picked, o_ref[...])
        place = pl.ds(k * count, count)
        dealt_ref[place, :] = rows.astype(BF16)
        for h in range(heads):
            lanes = slice(h * DV, (h + 1) * DV)
            value = rows[:, lanes]
            scale = lax.rsqrt(jnp.mean(value * value, axis=1, keepdims=True) + 1e-05)
            gated = value * scale * gain_ref[...] * silu(gate_ref[place, lanes])
            chunk_ref[:, lanes] = gated.astype(BF16)


def gate_rows(output, place, gate_logit, gain, count, heads, passed, tokens):
    total, cols = output.shape
    chunks = total // count
    others = len(passed) + len(tokens)
    outs = pl.pallas_call(
        functools.partial(gate_kernel, heads, count, others),
        in_specs=[WHOLE] * 4 + [ANYWHERE] * others,
        out_specs=[WHOLE] * (chunks + 1) + [ANYWHERE] * len(passed),
        out_shape=[jax.ShapeDtypeStruct((total, cols), BF16)]
        + [jax.ShapeDtypeStruct((count, cols), BF16)] * chunks
        + [jax.ShapeDtypeStruct(a.shape, a.dtype) for a in passed],
        input_output_aliases={4 + i: 1 + chunks + i for i in range(len(passed))},
        compiler_params=pltpu.CompilerParams(vmem_limit_bytes=VMEM_BYTES),
        cost_estimate=SMALL_COST,
        name="gate_rows",
    )(output, place, gate_logit, gain, *passed, *tokens)
    return outs[0], outs[1 : 1 + chunks], outs[1 + chunks :]


def ungate_kernel(heads, chunks, outs, dealt_ref, col_ref, gate_ref, gain_ref, *refs):
    grad_refs = refs[:chunks]
    gate_grad_ref, o_grad_ref, gain_grad_ref, rows_ref = *refs[outs : outs + 3], refs[-1]
    count = grad_refs[0].shape[0]
    total = dealt_ref.shape[0]
    sums = jnp.zeros((1, DV), F32)
    for k in range(chunks):
        place = pl.ds(k * count, count)
        for h in range(heads):
            lanes = slice(h * DV, (h + 1) * DV)
            value = dealt_ref[place, lanes].astype(F32)
            grad = grad_refs[k][:, lanes].astype(F32)
            logit = gate_ref[place, lanes]
            scale = lax.rsqrt(jnp.mean(value * value, axis=1, keepdims=True) + 1e-05)
            unit = value * scale
            gate = jax.nn.sigmoid(logit)
            slid = logit * gate
            sums += jnp.sum(grad * unit * slid, axis=0, keepdims=True)
            grad = grad * gain_ref[...]
            slope = gate * (1.0 + logit * (1.0 - gate))
            gate_grad_ref[place, lanes] = (grad * unit * slope).astype(BF16)
            grad = grad * slid
            inner = jnp.mean(grad * unit, axis=1, keepdims=True)
            rows_ref[place, lanes] = (scale * (grad - unit * inner)).astype(BF16)
    gain_grad_ref[...] = sums
    for k in range(chunks):
        place = pl.ds(k * count, count)
        order = lax.broadcasted_iota(jnp.int32, (count, total), 1)
        picked = (col_ref[place, 4:5].astype(jnp.int32) == order).astype(F32)
        o_grad_ref[place, :] = mm(picked, rows_ref[...]).astype(BF16)


def ungate_rows(dealt_rows, cols, gate_logit, gain, grads, heads, passed, tokens):
    total, width = dealt_rows.shape
    whole = pl.BlockSpec(memory_space=pltpu.VMEM)
    first = 4 + len(grads)
    outs = pl.pallas_call(
        functools.partial(ungate_kernel, heads, len(grads), len(grads) + len(passed) + len(tokens)),
        in_specs=[whole] * first + [ANYWHERE] * (len(passed) + len(tokens)),
        out_specs=[whole] * 3 + [ANYWHERE] * len(passed),
        out_shape=[
            jax.ShapeDtypeStruct((total, width), BF16),
            jax.ShapeDtypeStruct((total, width), BF16),
            jax.ShapeDtypeStruct((1, DV), F32),
        ]
        + [jax.ShapeDtypeStruct(p.shape, p.dtype) for p in passed],
        input_output_aliases={first + i: 3 + i for i in range(len(passed))},
        scratch_shapes=[pltpu.VMEM((total, width), BF16)],
        compiler_params=pltpu.CompilerParams(vmem_limit_bytes=VMEM_BYTES),
        cost_estimate=SMALL_COST,
        name="ungate_rows",
    )(dealt_rows, cols, gate_logit, gain, *grads, *passed, *tokens)
    return outs[:3], list(outs[3:])


def turned_sums(values):
    sums = jnp.sum(values, axis=1, keepdims=True)
    return jnp.broadcast_to(sums, (values.shape[0], 128)).T[:1]


def put_rows(total, split, core_ref, refs):
    total = total.astype(BF16)
    if split is None:
        refs[0][...] = total
        return
    halves = total.reshape(*split, 2, -1, total.shape[1])
    for core in range(2):

        @pl.when(core_ref[0] == core)
        def _():
            refs[0][...] = halves[:, :, core]
            refs[1][...] = halves[:, :, 1 - core]


def row_outputs(split, width, cols, tile):
    if split is None:
        shape, block = (width, cols), (width, tile)
        spec = pl.BlockSpec(block, lambda i: (0, i))
        return [spec], [jax.ShapeDtypeStruct(shape, BF16)]
    shape = (*split, width // (2 * split[0] * split[1]))
    spec = pl.BlockSpec((*shape, tile), lambda i: (0, 0, 0, i))
    return [spec] * 2, [jax.ShapeDtypeStruct((*shape, cols), BF16)] * 2


def unpack_kernel(split, heads, words_ref, grad_ref, gates_ref, place_ref, normed_ref, w_ref, conv_ref, gain_ref, mid_ref, o_ref, first_sums_ref, *refs):
    count = 2 if split else 1
    dealt_ref, sums_ref = refs[-4 - count], refs[-3 - count]
    row_refs, small_ref, picked_ref = refs[-2 - count : -2], refs[-2], refs[-1]
    step = pl.program_id(0)
    total = grad_ref.shape[0]
    gates = gates_ref.shape[1]
    tile = grad_ref.shape[1] // 2

    @pl.when(step == 0)
    def _():
        part = 256
        for k in range(total // part):
            order = lax.broadcasted_iota(jnp.int32, (part, total), 0) + k * part
            picked = (place_ref[...].astype(jnp.int32) == order).astype(F32)
            picked_ref[k * part : (k + 1) * part, :] = picked.astype(BF16)
        dealt_ref[:, :gates] = gates_ref[...]
        dealt_ref[:, gates : gates + tile] = mm(picked_ref[...], grad_ref[:, :tile]).astype(BF16)
        share = mm(normed_ref[...], dealt_ref[:, gates : gates + tile])
        weights = w_ref[:, gates : gates + tile].astype(F32)
        sums_ref[...] = first_sums_ref[...] + turned_sums(share * weights)
        put_rows(share, split, words_ref, row_refs)

    @pl.when(step == 1)
    def _():
        dealt_ref[:, gates + tile :] = mm(picked_ref[...], grad_ref[:, tile:]).astype(BF16)
        share = mm(normed_ref[...], dealt_ref[:, gates + tile :])
        used = w_ref.shape[1] - gates - tile
        weights = w_ref[:, gates + tile :].astype(F32)
        sums_ref[...] += turned_sums(share[:, :used] * weights)
        if split:
            devices, rows = 2 * split[0] * split[1], share.shape[0] // (2 * split[0] * split[1])
            gin = sums_ref[...] / gain_ref[...]
            small_ref[...] = jnp.zeros_like(small_ref)
            gin = jnp.concatenate([gin[:, j * 128 : (j + 1) * 128] for j in range(8)], 0)
            mid = jnp.concatenate([mid_ref[:, j * 128 : (j + 1) * 128] for j in range(8)], 0)
            for d in range(devices):
                small_ref[d * rows + 4 : d * rows + 5, :] = o_ref[:, :128]
                small_ref[d * rows + 5 : d * rows + 6, :] = o_ref[:, 128:]
                small_ref[d * rows + 8 : d * rows + 16, :] = mid
                small_ref[d * rows + 16 : d * rows + 24, :] = gin
            rank = words_ref[2]
            keys = heads * DK // 128
            vals = heads * DV // 128
            owners = [rank * keys + j for j in range(keys)]
            owners += [HEAD_COUNT * DK // 128 + rank * keys + j for j in range(keys)]
            owners += [2 * HEAD_COUNT * DK // 128 + rank * vals + j for j in range(vals)]
            for j, owner in enumerate(owners):
                place = pl.ds(pl.multiple_of(owner * rows, rows), 8)
                old = small_ref[place, :]
                taps = lax.broadcasted_iota(jnp.int32, (8, 128), 0) < 4
                small_ref[place, :] = jnp.where(taps, conv_ref[:, j * 128 : (j + 1) * 128], old)
            share = jnp.concatenate([share[:, :-128], small_ref[...]], 1)
        put_rows(share, split, words_ref, row_refs)


def unpack(split, words, grad, gate_grad, place, normed, weights, g_conv, gain, g_mid, g_o, sums, heads, tokens):
    total = grad.shape[0]
    cols = grad.shape[1] + gate_grad.shape[1]
    width = normed.shape[0]
    operands = (grad, gate_grad, place, normed, weights, g_conv, gain, g_mid, g_o, sums)
    specs, shapes = row_outputs(split, width, grad.shape[1], grad.shape[1] // 2)
    return pl.pallas_call(
        functools.partial(unpack_kernel, split, heads),
        grid=(2,),
        in_specs=[SCALAR]
        + [pl.BlockSpec(a.shape, lambda i: (0, 0)) for a in operands]
        + [ANYWHERE] * len(tokens),
        out_specs=[
            pl.BlockSpec((total, cols), lambda i: (0, 0)),
            pl.BlockSpec((1, width), lambda i: (0, 0)),
        ]
        + specs,
        out_shape=[
            jax.ShapeDtypeStruct((total, cols), BF16),
            jax.ShapeDtypeStruct((1, width), F32),
        ]
        + shapes,
        scratch_shapes=[pltpu.VMEM((width, 128), F32), pltpu.VMEM((total, total), BF16)],
        compiler_params=params(),
        cost_estimate=SMALL_COST,
        name="unpack",
    )(words, *operands, *tokens)


def unproject_kernel(chunks, first, grad_ref, w_ref, *refs):
    part_refs, turned_ref = refs[first : first + chunks], refs[-1]
    step = pl.program_id(0)

    @pl.when(step == 0)
    def _():
        turned_ref[...] = w_ref[...].T

    part = mm(grad_ref[:, : turned_ref.shape[0]], turned_ref[...])
    for k in range(chunks):

        @pl.when(step == k)
        def _():
            part_refs[k][...] = part.astype(BF16)


def unproject(grad, weights, count, passed, tokens):
    total, cols = grad.shape
    width = weights.shape[0]
    chunks = total // count
    outs = pl.pallas_call(
        functools.partial(unproject_kernel, chunks, len(passed) + len(tokens)),
        grid=(chunks,),
        in_specs=[
            pl.BlockSpec((count, cols), lambda i: (i, 0)),
            pl.BlockSpec(weights.shape, lambda i: (0, 0)),
        ]
        + [ANYWHERE] * (len(passed) + len(tokens)),
        out_specs=[pl.BlockSpec((count, width), lambda i: (0, 0))] * chunks
        + [ANYWHERE] * len(passed),
        out_shape=[jax.ShapeDtypeStruct((count, width), BF16)] * chunks
        + [jax.ShapeDtypeStruct(p.shape, p.dtype) for p in passed],
        input_output_aliases={2 + i: chunks + i for i in range(len(passed))},
        scratch_shapes=[pltpu.VMEM(weights.shape[::-1], BF16)],
        compiler_params=params(56 * MIB),
        cost_estimate=SMALL_COST,
        name="unproject",
    )(grad, weights, *passed, *tokens)
    return list(outs[:chunks]), list(outs[chunks:])


def hand_kernel(*refs):
    refs[-1][...] = jnp.zeros_like(refs[-1])


def handed(passed, tokens):
    outs = pl.pallas_call(
        hand_kernel,
        in_specs=[ANYWHERE] * (len(passed) + len(tokens)),
        out_specs=[ANYWHERE] * len(passed) + [WHOLE],
        out_shape=[jax.ShapeDtypeStruct(p.shape, p.dtype) for p in passed]
        + [jax.ShapeDtypeStruct((8, 128), F32)],
        input_output_aliases={i: i for i in range(len(passed))},
        cost_estimate=SMALL_COST,
        name="handed",
    )(*passed, *tokens)
    return outs[:-1]


def weight_grad_kernel(split, tiles, sums, words_ref, *refs):
    row_refs = refs[-2:] if split else refs[-1:]
    step = pl.program_id(0)
    for tile, pairs in enumerate(tiles):

        @pl.when(step == tile)
        def _():
            total = mm_tn(refs[pairs[0][0]][...], refs[pairs[0][1]][...])
            for left, right in pairs[1:]:
                total += mm_tn(refs[left][...], refs[right][...])
            put_rows(total, split, words_ref, row_refs)
            if sums is not None and tile == 0:
                refs[sums[1]][...] = turned_sums(total * refs[sums[0]][...].astype(F32))


def weight_grad(split, words, groups, tile, tokens, weights=None, limit=VMEM_BYTES):
    width = groups[0][0][0].shape[1]
    operands, specs, tiles = [words], [SCALAR], []
    first = 0
    for lefts, rights in groups:
        count = rights[0].shape[1] // tile
        base = len(operands) - 1
        for left in lefts:
            operands.append(left)
            specs.append(pl.BlockSpec((rights[0].shape[0], width), lambda i: (0, 0)))
        for right in rights:
            operands.append(right)
            specs.append(
                pl.BlockSpec(
                    (right.shape[0], tile),
                    lambda i, first=first, count=count: (0, jnp.clip(i - first, 0, count - 1)),
                )
            )
        tiles += [[(base + k, base + len(lefts) + k) for k in range(len(lefts))]] * count
        first += count
    sums = None
    out_specs, out_shapes = row_outputs(split, width, first * tile, tile)
    if weights is not None:
        operands.append(weights)
        specs.append(pl.BlockSpec((width, tile), lambda i: (0, 0)))
        sums = (len(operands) - 2, len(operands) - 1 + len(tokens))
        out_specs = [pl.BlockSpec((1, width), lambda i: (0, 0))] + out_specs
        out_shapes = [jax.ShapeDtypeStruct((1, width), F32)] + out_shapes
    return pl.pallas_call(
        functools.partial(weight_grad_kernel, split, tiles, sums),
        grid=(first,),
        in_specs=specs + [ANYWHERE] * len(tokens),
        out_specs=out_specs,
        out_shape=out_shapes,
        compiler_params=params(limit),
        cost_estimate=SMALL_COST,
        name="weight_grad",
    )(*operands, *tokens)


def join_kernel(pairs, *refs):
    for chip in range(refs[0].shape[1]):
        place = 0
        for k in range(pairs):
            keep_ref, got_ref = refs[2 * k], refs[2 * k + 1]
            width = keep_ref.shape[3]
            total = keep_ref[:, chip].astype(F32) + got_ref[:, chip].astype(F32)
            refs[-1][chip, :, :, place : place + width] = total.astype(BF16)
            place += width


def joined(pairs, tokens):
    seq_count, chips, rows, _ = pairs[0][0].shape
    cols = sum(keep.shape[3] for keep, _ in pairs)
    return pl.pallas_call(
        functools.partial(join_kernel, len(pairs)),
        in_specs=[WHOLE] * (2 * len(pairs)) + [ANYWHERE] * len(tokens),
        out_specs=WHOLE,
        out_shape=jax.ShapeDtypeStruct((chips, seq_count, rows, cols), BF16),
        compiler_params=pltpu.CompilerParams(vmem_limit_bytes=VMEM_BYTES),
        cost_estimate=SMALL_COST,
        name="joined",
    )(*[a for pair in pairs for a in pair], *tokens)


def layer_kernel(chunks, w_ref, low_ref, *refs):
    weights = w_ref[...].T
    count = low_ref.shape[0]
    refs[chunks][...] = mm(refs[0][...], weights).astype(BF16)
    for k in range(1, chunks):
        refs[chunks + k][:count, :] = low_ref[...]
        refs[chunks + k][count:, :] = mm(refs[k][...], weights).astype(BF16)


def layer_products(hiddens, weights, low):
    count, wide = hiddens[0].shape
    width = weights.shape[0]
    chunks = len(hiddens)
    rows = [count] + [2 * count] * (chunks - 1)
    return pl.pallas_call(
        functools.partial(layer_kernel, chunks),
        grid=(1,),
        in_specs=[
            pl.BlockSpec((width, wide), lambda i: (0, weights.shape[1] // wide - 1)),
            pl.BlockSpec((count, width), lambda i: (0, 0)),
        ]
        + [pl.BlockSpec((count, wide), lambda i: (0, 0))] * chunks,
        out_specs=[pl.BlockSpec((r, width), lambda i: (0, 0)) for r in rows],
        out_shape=[jax.ShapeDtypeStruct((r, width), BF16) for r in rows],
        compiler_params=params(),
        cost_estimate=SMALL_COST,
        name="layer_products",
    )(weights, low, *hiddens)


def position_kernel(heads, chunks, words_ref, lengths_ref, order_ref, decay_ref, *refs):
    col_ref, row_ref, place_ref, cum_ref = refs[-4:]
    total = order_ref.shape[1]
    count = total // chunks
    blocks, near = total // BLOCK, count // BLOCK
    rank = words_ref[2]
    ends = [lengths_ref[0]]
    for e in range(1, lengths_ref.shape[0]):
        ends.append(ends[-1] + lengths_ref[e])

    def segment(position):
        found = jnp.zeros(position.shape, jnp.int32)
        for end in ends:
            found += (position >= end).astype(jnp.int32)
        return jnp.where(position < 0, -1, found)

    for k in range(chunks):
        for h in range(heads):
            for b in range(near):
                value = jnp.zeros((1, BLOCK), F32)
                for part in range(3):
                    row = (part * heads + h) * near + b
                    value += decay_ref[k, row : row + 1, :].astype(F32)
                cum_ref[pl.ds(h * blocks + (rank ^ k) * near + b, 1), :] = value
    rows, cols = masks()
    upper = (rows <= cols).astype(F32)
    cums = jnp.dot(
        cum_ref[...], upper, precision=lax.Precision.HIGHEST, preferred_element_type=F32
    )
    order = order_ref[...]
    chunk = jnp.zeros_like(order)
    for k in range(1, chunks):
        chunk += (order >= k * count).astype(jnp.int32)
    place = (order + ((chunk ^ rank) - chunk) * count).astype(F32)
    place_ref[...] = place
    row_ref[...] = jnp.zeros_like(row_ref)
    lane = lax.broadcasted_iota(jnp.int32, (1, BLOCK), 1)
    for b in range(blocks):
        position = lane + b * BLOCK
        here = segment(position)
        low, high = jnp.full((1, BLOCK), b * BLOCK - 1), jnp.full((1, BLOCK), b * BLOCK + BLOCK - 1)
        keep_in = (here == segment(low)).astype(F32)
        keep_out = (here == segment(high)).astype(F32)
        found = [(segment(position - 3 + tap) == here).astype(F32) for tap in range(3)]
        found += [here.astype(F32), place[:, b * BLOCK : (b + 1) * BLOCK]]
        mine = [cums[h * blocks + b : h * blocks + b + 1, :] for h in range(heads)]
        found += mine
        found += [jnp.exp(c) * keep_in for c in mine]
        found += [jnp.exp(c[:, BLOCK - 1 :] - c) * keep_out for c in mine]
        found.append(jnp.zeros((128 - len(found), BLOCK), F32))
        col_ref[b * BLOCK : (b + 1) * BLOCK, :] = jnp.concatenate(found, 0).T
        for h in range(heads):
            row_ref[h : h + 1, b * BLOCK : (b + 1) * BLOCK] = mine[h]
        row_ref[heads : heads + 1, b * BLOCK : (b + 1) * BLOCK] = here.astype(F32)


def positions(words, lengths, order, decays, heads, tokens):
    total = order.shape[1]
    return pl.pallas_call(
        functools.partial(position_kernel, heads, decays.shape[0]),
        in_specs=[SCALAR, SCALAR, WHOLE, WHOLE] + [ANYWHERE] * len(tokens),
        out_specs=[WHOLE] * 3,
        out_shape=(
            jax.ShapeDtypeStruct((total, 128), F32),
            jax.ShapeDtypeStruct((8, total), F32),
            jax.ShapeDtypeStruct((1, total), F32),
        ),
        scratch_shapes=[pltpu.VMEM((heads * total // BLOCK, BLOCK), F32)],
        cost_estimate=SMALL_COST,
        compiler_params=pltpu.CompilerParams(vmem_limit_bytes=VMEM_BYTES),
        name="positions",
    )(words, lengths, order, decays, *tokens)


def out_rows_kernel(others, words_ref, mine_ref, normed_ref, *refs):
    out_ref, turned_ref = refs[-2:]
    core, chip = words_ref[0], words_ref[1]
    if others:
        chunks, chips, rows, _ = mine_ref.shape
        for k in range(chunks):
            for j in range(chips):
                device = k * 2 * chips + 2 * (chip ^ j)
                for ref, side in ((mine_ref, core), (refs[0], 1 - core)):
                    place = pl.ds(pl.multiple_of((device + side) * rows, rows), rows)
                    out_ref[place, :] = ref[k, j]
    else:
        out_ref[...] = mine_ref[...]
    turned_ref[...] = normed_ref[...].T


def out_rows(words, mine, others, normed, rows, tokens):
    return pl.pallas_call(
        functools.partial(out_rows_kernel, len(others)),
        in_specs=[SCALAR] + [WHOLE] * (2 + len(others)) + [ANYWHERE] * len(tokens),
        out_specs=[WHOLE] * 2,
        out_shape=(
            jax.ShapeDtypeStruct((rows, mine.shape[-1]), BF16),
            jax.ShapeDtypeStruct(normed.shape[::-1], BF16),
        ),
        compiler_params=pltpu.CompilerParams(vmem_limit_bytes=VMEM_BYTES),
        cost_estimate=SMALL_COST,
        name="out_rows",
    )(words, mine, normed, *others, *tokens)


def ffn_rows_kernel(words_ref, ffn_ref, *refs):
    width = ffn_ref.shape[0] * ffn_ref.shape[2]
    for k in range(ffn_ref.shape[1]):
        place = pl.ds(pl.multiple_of((words_ref[2] ^ k) * width, width), width)
        refs[-1][place, :] = ffn_ref[:, k].reshape(width, ffn_ref.shape[3])


def ffn_rows(words, ffn, tokens):
    return pl.pallas_call(
        ffn_rows_kernel,
        in_specs=[SCALAR, WHOLE] + [ANYWHERE] * len(tokens),
        out_specs=WHOLE,
        out_shape=jax.ShapeDtypeStruct((ffn.shape[0] * ffn.shape[1] * ffn.shape[2], ffn.shape[3]), BF16),
        compiler_params=pltpu.CompilerParams(vmem_limit_bytes=VMEM_BYTES),
        cost_estimate=SMALL_COST,
        name="ffn_rows",
    )(words, ffn, *tokens)


def out_project_kernel(chunks, rank_ref, x_ref, gain_ref, w_ref, *refs):
    residual_ref, mid_ref, all_ref = refs[-3:]
    rank = rank_ref[0]
    for k in range(chunks):
        width = refs[k].shape[1]
        all_ref[:, pl.ds(pl.multiple_of((rank ^ k) * width, width), width)] = refs[k][...]
    residual = x_ref[...].astype(F32) + mm_nt(all_ref[...], w_ref[...])
    residual_ref[...] = residual
    scale = lax.rsqrt(jnp.mean(residual * residual, axis=1, keepdims=True) + 1e-05)
    mid_ref[...] = (residual * scale * gain_ref[...]).astype(BF16)


def out_project(rank, x, gain, attn, weights):
    count, width = x.shape
    return pl.pallas_call(
        functools.partial(out_project_kernel, len(attn)),
        in_specs=[SCALAR] + [WHOLE] * (3 + len(attn)),
        out_specs=[WHOLE] * 2,
        out_shape=(
            jax.ShapeDtypeStruct((count, width), F32),
            jax.ShapeDtypeStruct((count, width), BF16),
        ),
        scratch_shapes=[pltpu.VMEM((count, weights.shape[1]), BF16)],
        compiler_params=pltpu.CompilerParams(vmem_limit_bytes=VMEM_BYTES),
        cost_estimate=SMALL_COST,
        name="out_project",
    )(rank, x, gain, weights, *attn)


def mid_back_kernel(chunks, handed, rank_ref, grad_ref, residual_ref, gain_ref, w_ref, *refs):
    parts = refs[:chunks]
    outs, all_ref = refs[chunks + handed :], refs[-1]
    res_grad_ref, low_ref, gain_grad_ref, chunk_refs = outs[0], outs[1], outs[2], outs[3 : 3 + chunks]
    rank = rank_ref[0]
    mid_grad = parts[0][...].astype(F32)
    for k in range(1, chunks):
        mid_grad += parts[k][...].astype(F32)
    residual = residual_ref[...]
    scale = lax.rsqrt(jnp.mean(residual * residual, axis=1, keepdims=True) + 1e-05)
    unit = residual * scale
    gain_grad_ref[...] = jnp.sum(mid_grad * unit, axis=0, keepdims=True)
    scaled = mid_grad * gain_ref[...]
    inner = jnp.mean(scaled * unit, axis=1, keepdims=True)
    res_grad = grad_ref[...].astype(F32) + scale * (scaled - unit * inner)
    res_grad_ref[...] = res_grad
    low = res_grad.astype(BF16)
    low_ref[...] = low
    all_ref[...] = mm(low, w_ref[...]).astype(BF16)
    for k in range(chunks):
        width = chunk_refs[k].shape[1]
        chunk_refs[k][...] = all_ref[:, pl.ds(pl.multiple_of((rank ^ k) * width, width), width)]


def mid_back(rank, grad, residual, gain, parts, weights, passed):
    count, width = residual.shape
    chunks = len(parts)
    wide = weights.shape[1]
    first = 5 + chunks
    outs = pl.pallas_call(
        functools.partial(mid_back_kernel, chunks, len(passed)),
        in_specs=[SCALAR] + [WHOLE] * (first - 1) + [ANYWHERE] * len(passed),
        out_specs=[WHOLE] * (3 + chunks) + [ANYWHERE] * len(passed),
        out_shape=[
            jax.ShapeDtypeStruct((count, width), F32),
            jax.ShapeDtypeStruct((count, width), BF16),
            jax.ShapeDtypeStruct((1, width), F32),
        ]
        + [jax.ShapeDtypeStruct((count, wide // chunks), BF16)] * chunks
        + [jax.ShapeDtypeStruct(p.shape, p.dtype) for p in passed],
        input_output_aliases={first + i: 3 + chunks + i for i in range(len(passed))},
        scratch_shapes=[pltpu.VMEM((count, wide), BF16)],
        compiler_params=pltpu.CompilerParams(vmem_limit_bytes=VMEM_BYTES),
        cost_estimate=SMALL_COST,
        name="mid_back",
    )(rank, grad, residual, gain, weights, *parts, *passed)
    return (*outs[:3], outs[3 : 3 + chunks], list(outs[3 + chunks :]))


def in_back_kernel(chunks, x_ref, res_grad_ref, gain_ref, *refs):
    x = x_ref[...].astype(F32)
    grad = refs[0][...].astype(F32)
    for k in range(1, chunks):
        grad += refs[k][...].astype(F32)
    scale = lax.rsqrt(jnp.mean(x * x, axis=1, keepdims=True) + 1e-05)
    unit = x * scale
    scaled = grad * gain_ref[...]
    inner = jnp.mean(scaled * unit, axis=1, keepdims=True)
    refs[-1][...] = (res_grad_ref[...] + scale * (scaled - unit * inner)).astype(BF16)


def in_back(x, res_grad, gain, parts, tokens):
    return pl.pallas_call(
        functools.partial(in_back_kernel, len(parts)),
        in_specs=[WHOLE] * (3 + len(parts)) + [ANYWHERE] * len(tokens),
        out_specs=WHOLE,
        out_shape=jax.ShapeDtypeStruct(x.shape, BF16),
        compiler_params=pltpu.CompilerParams(vmem_limit_bytes=VMEM_BYTES),
        cost_estimate=SMALL_COST,
        name="in_back",
    )(x, res_grad, gain, *parts, *tokens)


def swapped(value, axis, mask):
    devices = lax.axis_size(axis)
    return lax.ppermute(value, axis, [(i, i ^ mask) for i in range(devices)])


def pinned(value, other):
    return value + 0 * other[:1, :1].astype(value.dtype)


def spread(value):
    return [value] + [swapped(value, "seq", k) for k in range(1, lax.axis_size("seq"))]


def returned(chunks):
    return [chunks[0]] + [swapped(chunks[k], "seq", k) for k in range(1, len(chunks))]


class RowSum:
    def __init__(self, outs):
        self.outs = list(outs)

    def pair(self):
        if len(self.outs) == 2:
            self.got = swapped(self.outs[1], "mp", 1)

    def join(self, *tokens):
        seq_count, mp_count = lax.axis_size("seq"), lax.axis_size("mp")
        if len(self.outs) == 1:
            (grad,) = self.outs
            cols = grad.shape[1]
            parts = grad.astype(F32).reshape(seq_count, mp_count, -1, cols).transpose(1, 0, 2, 3)
            own = lax.psum_scatter(parts.reshape(-1, cols), "mp", scatter_dimension=0, tiled=True)
            self.half = grad
            self.parts = own.reshape(1, seq_count, -1, cols)
            return
        self.half = joined([(self.outs[0], self.got)], tokens)
        self.between()

    def between(self):
        mp_count = lax.axis_size("mp")
        groups = [list(range(core, mp_count, 2)) for core in range(2)]
        self.parts = lax.all_to_all(self.half, "mp", 0, 0, axis_index_groups=groups, tiled=True)

    def beside(self, other):
        if len(self.outs) == 1:
            both = RowSum([jnp.concatenate([self.outs[0], other.outs[0]], 1)])
            both.join()
            return both
        both = RowSum([])
        both.half = joined([(s.outs[0], s.got) for s in (self, other)], [])
        both.between()
        return both


def row_sums(sums, tokens):
    groups = [part.parts for part in sums]
    shape = groups[0].shape[1:3]
    cols = [group.shape[3] for group in groups]

    def kernel(*refs):
        place = 0
        for ref, width in zip(refs, cols):
            total = ref[0].astype(F32)
            for k in range(1, ref.shape[0]):
                total += ref[k].astype(F32)
            refs[-1][:, :, place : place + width] = total.astype(BF16)
            place = place + width

    return pl.pallas_call(
        kernel,
        in_specs=[WHOLE] * len(groups) + [ANYWHERE] * len(tokens),
        out_specs=WHOLE,
        out_shape=jax.ShapeDtypeStruct(shape + (sum(cols),), BF16),
        cost_estimate=SMALL_COST,
        compiler_params=pltpu.CompilerParams(vmem_limit_bytes=VMEM_BYTES),
        name="row_sums",
    )(*groups, *tokens)


def finish_kernel(heads, wide, half, rows, pieces_ref, *refs):
    qkv_ref, gate_ref, beta_ref, conv_ref, out_ref, gu_ref, down_ref, small_ref = refs
    chunks = pieces_ref.shape[0]
    keys, vals = heads * DK, heads * DV
    ffn, mix = 0, 3 * wide
    gate_first, first, out_first = mix, mix + vals, pieces_ref.shape[2] - vals

    def piece(j, start, width):
        return pieces_ref[j, :, start : start + width].astype(F32)

    for j in range(chunks):
        gate_ref[:, j * vals : (j + 1) * vals] = piece(j, gate_first, vals)
        qkv_ref[:, j * keys : (j + 1) * keys] = piece(j, first, keys)
        place = chunks * keys + j * keys
        qkv_ref[:, place : place + keys] = piece(j, first + keys, keys)
        place = 2 * chunks * keys + j * vals
        qkv_ref[:, place : place + vals] = piece(j, first + 2 * keys, vals)
        out_ref[:, j * vals : (j + 1) * vals] = piece(j, out_first, vals)
        beta = piece(j, first + 2 * keys + vals, 128)
        beta_ref[:, j * heads : (j + 1) * heads] = beta[:, :heads]
    small = piece(0, out_first - 128, 128)
    for j in range(1, chunks):
        small += piece(j, out_first - 128, 128)
    small_ref[...] = small
    conv_ref[...] = small[: conv_ref.shape[0]]
    for part in range(3):
        whole = jnp.concatenate(
            [piece(j, ffn + part * wide, wide)[:, :half] for j in range(chunks)], 1
        )
        if part < 2:
            gu_ref[:, part * chunks * half : (part + 1) * chunks * half] = whole
        else:
            down_ref[...] = whole


def finish(pieces, heads, wide, half, taps):
    chunks, rows, _ = pieces.shape
    keys, vals = HEAD_COUNT * DK, HEAD_COUNT * DV
    ffn = chunks * half
    shapes = [(rows, 2 * keys + vals), (rows, vals), (rows, HEAD_COUNT), (taps, 128)]
    shapes += [(rows, vals), (rows, 2 * ffn), (rows, ffn), (rows, 128)]
    return pl.pallas_call(
        functools.partial(finish_kernel, heads, wide, half, rows),
        in_specs=[WHOLE],
        out_specs=[WHOLE] * len(shapes),
        out_shape=[jax.ShapeDtypeStruct(shape, F32) for shape in shapes],
        compiler_params=pltpu.CompilerParams(vmem_limit_bytes=VMEM_BYTES),
        cost_estimate=SMALL_COST,
        name="finish",
    )(pieces)


def dealt(own):
    return lax.all_to_all(own, "seq", 0, 0, tiled=True)


def left_product(left, right):
    return lax.dot_general(
        left, right, (((0,), (0,)), ((), ())), preferred_element_type=jnp.float32
    )


def right_product(left, right):
    return lax.dot_general(
        left, right, (((1,), (1,)), ((), ())), preferred_element_type=jnp.float32
    )


def dot(left, right):
    return jnp.dot(left, right, preferred_element_type=jnp.float32)


def silu_slope(values):
    gate = jax.nn.sigmoid(values)
    return gate * (1.0 + values * (1.0 - gate))


def split_three(values):
    high = values.astype(BF16)
    rest = values - high.astype(F32)
    middle = rest.astype(BF16)
    return jnp.stack([high, middle, (rest - middle.astype(F32)).astype(BF16)])


def body(
    layer_in,
    out_grad,
    seq_lengths,
    dealing,
    log_decay,
    w_qkv,
    w_out_gate,
    w_beta,
    conv_w,
    gain_in,
    gain_o,
    w_out,
    gain_mid,
    w_gate_up,
    w_down,
):
    seq_count, mp_count = lax.axis_size("seq"), lax.axis_size("mp")
    rank, place_mp = lax.axis_index("seq"), lax.axis_index("mp")
    count = layer_in.shape[1]
    rows = w_qkv.shape[0]
    heads = HEAD_COUNT // seq_count
    key_cols, val_cols = heads * DK, heads * DV
    half = w_down.shape[0] // seq_count
    wide = -(-half // 256) * 256
    taps = conv_w.shape[1]
    total = dealing.shape[1]
    devices = seq_count * mp_count
    channels = 2 * key_cols + val_cols
    all_keys, ffn = HEAD_COUNT * DK, w_down.shape[0]
    split = (seq_count, mp_count // 2) if mp_count <= 8 else None
    words = jnp.stack([place_mp % 2, place_mp // 2, rank]).astype(jnp.int32)
    rank_word = rank.astype(jnp.int32).reshape(1)

    small = jnp.concatenate([conv_w.T.reshape(-1), gain_in, gain_mid, gain_o])
    small_count = small.shape[0]
    spare = 128 - heads
    filler = jnp.concatenate([small, jnp.zeros((rows * spare - small_count,), BF16)])
    filler = filler.reshape(rows, spare)
    wide_filler = jnp.zeros((rows, wide - half), BF16)
    turned_down = w_down.T
    decay_lanes = -(-3 * heads * count // (128 * rows)) * 128
    decays = split_three(log_decay[0].T)
    mix_cols = channels + 128 + val_cols
    pieces, ffn_pieces = [], []
    for j in range(seq_count):
        own_decay = decays[:, j * heads : (j + 1) * heads].reshape(-1)
        own_decay = jnp.concatenate(
            [own_decay, jnp.zeros((rows * decay_lanes - own_decay.shape[0],), BF16)]
        )
        pieces.append(
            jnp.concatenate(
                [
                    w_out_gate[:, j * val_cols : (j + 1) * val_cols],
                    w_qkv[:, j * key_cols : (j + 1) * key_cols],
                    w_qkv[:, all_keys + j * key_cols : all_keys + (j + 1) * key_cols],
                    w_qkv[:, 2 * all_keys + j * val_cols : 2 * all_keys + (j + 1) * val_cols],
                    w_beta[:, j * heads : (j + 1) * heads],
                    filler,
                ],
                1,
            )
        )
        ffn_pieces.append(
            jnp.concatenate(
                [
                    w_gate_up[:, j * half : (j + 1) * half],
                    wide_filler,
                    w_gate_up[:, ffn + j * half : ffn + (j + 1) * half],
                    wide_filler,
                    turned_down[:, j * half : (j + 1) * half],
                    wide_filler,
                    own_decay.reshape(rows, decay_lanes),
                ],
                1,
            )
        )
    def near(arrays):
        arrays = jnp.stack(arrays)
        return jnp.stack(
            returned(
                [lax.dynamic_index_in_dim(arrays, rank ^ k, 0, keepdims=False) for k in range(seq_count)]
            )
        )

    pieces, ffn_pieces = near(pieces), near(ffn_pieces)
    gathered = lax.all_gather(pieces, "mp", axis=0, tiled=False)
    late = pieces[1, :1, :1] + jnp.sum(ffn_pieces[1:, :1, :1], axis=0)
    chunks_in = spread(layer_in[0] + 0 * late)

    relative = rank ^ jnp.arange(seq_count)
    smalls = gathered[:, :, :, mix_cols - spare :].transpose(1, 0, 2, 3)
    smalls = jnp.take(smalls, relative, axis=0).reshape(devices, -1)[:, :small_count]
    own_taps = conv_w.shape[0] * taps
    full_conv = smalls[:, :own_taps].reshape(-1, taps, conv_w.shape[0]).transpose(1, 0, 2)
    full_conv = full_conv.reshape(taps, -1).astype(F32)
    conv = jnp.concatenate(
        [
            lax.dynamic_slice_in_dim(full_conv, rank * key_cols, key_cols, 1),
            lax.dynamic_slice_in_dim(full_conv, all_keys + rank * key_cols, key_cols, 1),
            lax.dynamic_slice_in_dim(full_conv, 2 * all_keys + rank * val_cols, val_cols, 1),
        ],
        1,
    )
    conv = jnp.concatenate([conv, jnp.zeros((8 - taps, channels), F32)], 0)
    gains = smalls[:, own_taps:].astype(F32)
    full_gin = gains[:, :rows].reshape(1, -1)
    full_gmid = gains[:, rows : 2 * rows].reshape(1, -1)
    full_go = gains[:, 2 * rows :].reshape(1, -1)

    out_turned = w_out.T
    out_near = []
    if split:
        out_near = [out_turned] + [swapped(out_turned, "mp", 2 * j) for j in range(1, mp_count // 2)]

    out_copies = []
    if split:
        out_copies = [
            jnp.broadcast_to(jnp.stack(out_near), (seq_count, mp_count // 2, *out_turned.shape))
        ]

    decays = ffn_pieces[:, :, 3 * wide :].reshape(seq_count, -1)[:, : 3 * heads * count]
    col_info, row_info, place_row = positions(
        words, seq_lengths[0], dealing, decays.reshape(seq_count, -1, BLOCK), heads, out_copies
    )

    passed = [ffn_pieces[:, :, : 3 * wide], out_grad[0] + 0 * pieces[1, :1, :1]] + out_copies
    passed = handed(passed, chunks_in[1:] + [row_info])
    ffn_all = lax.all_gather(passed[0], "mp", axis=0, tiled=False)
    chunks_grad = spread(passed[1])
    out_mine = [lax.all_to_all(passed[2], "seq", 0, 0, tiled=True)] if split else []
    (normed, gate_logit, proj, logit_parts, mix), _ = project(
        rank_word, chunks_in, full_gin, gathered, col_info, channels,
        [], [conv, full_go, full_gmid],
    )
    outs = forward_recurrence(proj, conv, col_info, row_info, logit_parts, heads, [])
    dealt_rows, attn, out_mine = gate_rows(
        outs[0], place_row, gate_logit, full_go, count, heads, out_mine, chunks_grad[1:]
    )
    if split:
        out_others = [swapped(out_mine[0], "mp", 1)]
    else:
        out_mine, out_others = [lax.all_gather(out_turned, ("seq", "mp"), axis=0, tiled=True)], []
    attn_parts = returned(attn)
    out_w, normed_t = out_rows(words, out_mine[0], out_others, normed, devices * rows, [attn[0]])

    residual, mid_own = out_project(rank_word, layer_in[0], full_gmid, attn_parts, out_w)

    ffn_w = ffn_rows(words, ffn_all, [mid_own])
    w_gu, down_turned = ffn_w[:, : 2 * wide], ffn_w[:, 2 * wide :]
    mids = spread(mid_own)
    hiddens, gu_grads, mid_parts = ([None] * seq_count for _ in range(3))
    last_part = None
    for k in (0, 1, 3, 2):
        mid_k = mids[k] if last_part is None else pinned(mids[k], last_part)
        gate_up = dot(mid_k, w_gu)
        gate, up = gate_up[:, :wide], gate_up[:, wide:]
        hiddens[k] = (silu(gate) * up).astype(BF16)
        hidden_grad = dot(chunks_grad[k], down_turned)
        gu_grads[k] = jnp.concatenate(
            [hidden_grad * up * silu_slope(gate), hidden_grad * silu(gate)], 1
        ).astype(BF16)
        mid_parts[k] = last_part = right_product(gu_grads[k], w_gu).astype(BF16)
    mid_parts = returned(mid_parts)
    ffn_sum = RowSum(
        weight_grad(
            split, words, [(mids, gu_grads), (chunks_grad, hiddens)], wide, [last_part, mid_parts[1]]
        ),
    )
    res_grad, out_proj_grad, g_mid, attn_grads, ffn_sum.outs[-1:] = mid_back(
        rank_word, out_grad[0], residual, full_gmid, mid_parts, out_w, ffn_sum.outs[-1:]
    )
    attn_grads = returned(attn_grads)
    ffn_sum.pair()
    layer_own, *both = layer_products(hiddens, ffn_w, out_proj_grad)

    (gate_grad, o_grad, g_go), both = ungate_rows(
        dealt_rows, col_info, gate_logit, full_go, attn_grads, heads, both, []
    )
    gate_sums, *gate_outs = weight_grad(
        split, words, [([normed], [gate_grad])], val_cols, [], weights=mix
    )
    gate_sum = RowSum(gate_outs)
    gate_sum.pair()
    ffn_sum = ffn_sum.beside(gate_sum)
    both = returned([None] + both)[1:]
    proj_grad, g_conv = backward_recurrence(
        proj, conv, col_info, row_info, logit_parts, outs[1:], o_grad, heads, [ffn_sum.half]
    )
    mix_grad, mix_sums, *mix_outs = unpack(
        split, words, proj_grad, gate_grad, place_row, normed_t, mix, g_conv, full_gin, g_mid, g_go,
        gate_sums, heads, [],
    )
    mix_sum = RowSum(mix_outs)
    mix_sum.pair()
    normed_parts, _ = unproject(mix_grad, mix, count, [], [])
    normed_chunks = returned(normed_parts)
    out_sum = RowSum(
        weight_grad(split, words, [([out_proj_grad] + both, attn)], val_cols,
            [normed_parts[0], ffn_sum.parts], limit=56 * MIB,
        )
    )
    out_sum.pair()
    last_sum = mix_sum.beside(out_sum)
    in_grad = in_back(layer_in[0], res_grad, full_gin, normed_chunks, [last_sum.half])
    layer_out = residual + sum(
        c.astype(F32) for c in [layer_own] + [b[count:] for b in both]
    )
    all_pieces = dealt(row_sums([ffn_sum, last_sum], [in_grad]))
    layer_out = layer_out.astype(BF16)[None]
    if split:
        g_qkv, g_gate, g_beta, g_conv, g_out, g_gu, g_down, small_sum = finish(
            all_pieces, heads, wide, half, taps
        )
        device = rank * mp_count + place_mp
        grad_go = lax.dynamic_slice_in_dim(
            small_sum[4:6].reshape(-1), device * gain_o.shape[0], gain_o.shape[0]
        )
        grad_gmid = lax.dynamic_slice_in_dim(small_sum[8:16].reshape(-1), device * rows, rows)
        grad_gin = lax.dynamic_slice_in_dim(small_sum[16:24].reshape(-1), device * rows, rows)
        return (
            layer_out, in_grad[None], g_qkv, g_gate, g_beta, g_conv.T,
            grad_gin, grad_go, g_out.T, grad_gmid, g_gu, g_down.T,
        )

    def columns(first, width):
        parts = [all_pieces[j, :, first : first + width] for j in range(seq_count)]
        return jnp.concatenate(parts, 1).astype(F32)

    everywhere = ("seq", "mp")
    conv_full = jnp.zeros((taps, conv_w.shape[0] * devices), F32)
    for first, width in ((0, key_cols), (key_cols, key_cols), (2 * key_cols, val_cols)):
        conv_full = lax.dynamic_update_slice_in_dim(
            conv_full, g_conv[:taps, first : first + width], first * seq_count + rank * width, 1
        )
    grad_conv = lax.psum_scatter(conv_full.T, everywhere, scatter_dimension=0, tiled=True)
    g_gin = mix_sums[0] / full_gin[0]
    grad_gin, grad_gmid, grad_go = (
        lax.psum_scatter(g, everywhere, scatter_dimension=0, tiled=True)
        for g in (g_gin, g_mid[0], g_go[0])
    )
    first = 3 * wide + val_cols
    last = all_pieces.shape[2] - val_cols
    return (
        layer_out,
        in_grad[None],
        jnp.concatenate(
            [
                columns(first, key_cols),
                columns(first + key_cols, key_cols),
                columns(first + 2 * key_cols, val_cols),
            ],
            1,
        ),
        columns(3 * wide, val_cols),
        columns(first + channels, heads),
        grad_conv,
        grad_gin,
        grad_go,
        columns(last, val_cols).T,
        grad_gmid,
        jnp.concatenate([columns(0, half), columns(wide, half)], 1),
        columns(2 * wide, half).T,
    )


def solution(mesh):
    in_specs = (
        P("mp", "seq", None),
        P("mp", "seq", None),
        P("mp", None),
        P("mp", None),
        P("mp", "seq", None),
        P(("seq", "mp"), None),
        P(("seq", "mp"), None),
        P(("seq", "mp"), None),
        P(("seq", "mp"), None),
        P(("seq", "mp")),
        P(("seq", "mp")),
        P(None, ("seq", "mp")),
        P(("seq", "mp")),
        P(("seq", "mp"), None),
        P(None, ("seq", "mp")),
    )
    out_specs = (
        P("mp", "seq", None),
        P("mp", "seq", None),
        P(("seq", "mp"), None),
        P(("seq", "mp"), None),
        P(("seq", "mp"), None),
        P(("seq", "mp"), None),
        P(("seq", "mp")),
        P(("seq", "mp")),
        P(None, ("seq", "mp")),
        P(("seq", "mp")),
        P(("seq", "mp"), None),
        P(None, ("seq", "mp")),
    )
    return jax.shard_map(body, mesh=mesh, in_specs=in_specs, out_specs=out_specs, check_vma=False)
```

```python
import functools

import jax
import jax.numpy as jnp
from jax import lax
from jax.experimental import pallas as pl
from jax.experimental.pallas import tpu as pltpu
from jax.sharding import PartitionSpec as P

HEAD_COUNT = 8
DK = 128
DV = 256
BLOCK = 128
FORWARD_STEP = 6
BACKWARD_STEP = 2
F32 = jnp.float32
BF16 = jnp.bfloat16


def mm(left, right):
    return jnp.dot(left.astype(BF16), right.astype(BF16), preferred_element_type=F32)


def mm_nt(left, right):
    return lax.dot_general(
        left.astype(BF16),
        right.astype(BF16),
        (((1,), (1,)), ((), ())),
        preferred_element_type=F32,
    )


def mm_tn(left, right):
    return lax.dot_general(
        left.astype(BF16),
        right.astype(BF16),
        (((0,), (0,)), ((), ())),
        preferred_element_type=F32,
    )


def masks():
    rows = lax.broadcasted_iota(jnp.int32, (BLOCK, BLOCK), 0)
    cols = lax.broadcasted_iota(jnp.int32, (BLOCK, BLOCK), 1)
    return rows, cols


def unit_inverses(mats, rows, cols):
    ident = (rows == cols).astype(F32)
    near = (rows // 16) == (cols // 16)
    power = [jnp.where(near, a, 0.0) for a in mats]
    result = [ident - p for p in power]
    span = 2
    while span < 16:
        power = [mm(p, p) for p in power]
        result = [t + mm(t, p) for t, p in zip(result, power)]
        span *= 2
    size = 16
    while size < BLOCK:
        off = ((rows // (2 * size)) == (cols // (2 * size))) & ((rows // size) != (cols // size))
        reach = [mm(jnp.where(off, a, 0.0), t) for a, t in zip(mats, result)]
        result = [t - mm(t, x) for t, x in zip(result, reach)]
        size *= 2
    return result


def convolve(ext_ref, conv_ref, col_ref, start, first, width):
    cols = pl.ds(first, width)
    total = ext_ref[pl.ds(16 + start, BLOCK), cols] * conv_ref[3:4, cols]
    for tap in range(3):
        keep = col_ref[pl.ds(start, BLOCK), tap : tap + 1]
        total += ext_ref[pl.ds(13 + tap + start, BLOCK), cols] * keep * conv_ref[tap : tap + 1, cols]
    return total


def column(col_ref, start, index):
    return col_ref[pl.ds(start, BLOCK), index : index + 1]


def strength(logit_ref, start, head, heads):
    return jax.nn.sigmoid(column(logit_ref, start, head))


def exact_nt(left, right):
    left_high, right_high = left.astype(BF16), right.astype(BF16)
    left_low = left - left_high.astype(F32)
    right_low = right - right_high.astype(F32)
    return mm_nt(left_high, right_high) + (mm_nt(left_high, right_low) + mm_nt(left_low, right_high))


def decay_matrix(col_ref, row_ref, start, head, heads, rows, cols):
    cum_i = column(col_ref, start, 5 + head)
    cum_j = row_ref[head : head + 1, pl.ds(start, BLOCK)]
    seg_i = column(col_ref, start, 3)
    seg_j = row_ref[heads : heads + 1, pl.ds(start, BLOCK)]
    within = (rows >= cols) & (seg_i == seg_j)
    return jnp.where(within, jnp.exp(jnp.where(within, cum_i - cum_j, 0.0)), 0.0)


def silu(values):
    return values * jax.nn.sigmoid(values)


def forward_kernel(
    heads, edge_ref, proj_ref, conv_ref, col_ref, row_ref, logit_ref, *refs,
):
    o_ref, s_ref, n_ref, t_ref, w_ref, p_ref, pre_ref, ext_ref, state_ref = refs[-9:]
    steps = proj_ref.shape[0] // BLOCK

    @pl.when(pl.program_id(0) == 0)
    def _():
        state_ref[...] = jnp.zeros_like(state_ref)

    ext_ref[:16, :] = edge_ref[...].astype(F32)
    ext_ref[16:, :] = proj_ref[...].astype(F32)
    rows, cols = masks()
    strict = rows > cols
    units = [(g, h) for g in range(steps) for h in range(heads)]
    queries, keys, values, mats, decays, betas = {}, {}, {}, [], {}, {}
    for g, h in units:
        start = g * BLOCK

        def taken(first, width):
            value = convolve(ext_ref, conv_ref, col_ref, start, first, width)
            pre_ref[pl.ds(start, BLOCK), first : first + width] = value
            return value

        queries[g, h] = silu(taken(h * DK, DK))
        raw = silu(taken((heads + h) * DK, DK))
        keys[g, h] = raw * lax.rsqrt(jnp.sum(raw * raw, axis=1, keepdims=True) + 1e-06)
        values[g, h] = silu(taken(2 * heads * DK + h * DV, DV))
        decays[g, h] = decay_matrix(col_ref, row_ref, start, h, heads, rows, cols)
        betas[g, h] = strength(logit_ref, start, h, heads)
        beta = betas[g, h]
        inner = mm_nt(keys[g, h], keys[g, h])
        mats.append(jnp.where(strict, beta * inner * decays[g, h], 0.0))
    inverses = unit_inverses(mats, rows, cols)
    umats, wmats, pmats, boundary, reads = {}, {}, {}, {}, {}
    for (g, h), inverse in zip(units, inverses):
        start = g * BLOCK
        beta = betas[g, h]
        elog = column(col_ref, start, 5 + heads + h)
        flog = column(col_ref, start, 5 + 2 * heads + h)
        inverse = inverse.astype(BF16)
        t_ref[g, h] = inverse
        umats[g, h] = mm(inverse, beta * values[g, h])
        wmats[g, h] = mm(inverse, (beta * elog) * keys[g, h]).astype(BF16)
        w_ref[g, h] = wmats[g, h]
        pmats[g, h] = (exact_nt(queries[g, h], keys[g, h]) * decays[g, h]).astype(BF16)
        p_ref[g, h] = pmats[g, h]
        boundary[g, h] = (keys[g, h] * flog).T.astype(BF16)
        reads[g, h] = (queries[g, h] * elog).astype(BF16)
    for g in range(steps):
        start = g * BLOCK
        for h in range(heads):
            state = state_ref[h]
            low = state.astype(BF16)
            s_ref[g, h] = low
            news = (umats[g, h] - mm(wmats[g, h], low)).astype(BF16)
            n_ref[g, h] = news
            carried = col_ref[pl.ds(start + BLOCK - 1, 1), 5 + heads + h : 6 + heads + h]
            state_ref[h] = carried * state + mm(boundary[g, h], news)
            output = mm(reads[g, h], low) + mm(pmats[g, h], news)
            o_ref[pl.ds(start, BLOCK), h * DV : (h + 1) * DV] = output.astype(BF16)


def backward_kernel(
    heads, edge_ref, proj_ref, conv_ref, col_ref, row_ref, logit_ref,
    s_ref, n_ref, t_ref, w_ref, p_ref, pre_ref, do_ref, *refs,
):
    grad_ref, gconv_ref, ext_ref, shift_ref, dstate_ref, head_ref = refs[-6:]
    count = proj_ref.shape[0]
    steps = count // BLOCK
    channels = proj_ref.shape[1]

    @pl.when(pl.program_id(0) == 0)
    def _():
        dstate_ref[...] = jnp.zeros_like(dstate_ref)
        head_ref[...] = jnp.zeros_like(head_ref)
        gconv_ref[...] = jnp.zeros_like(gconv_ref)

    ext_ref[:16, :] = edge_ref[...].astype(F32)
    ext_ref[16:, :] = proj_ref[...].astype(F32)
    for tap in range(3):
        shift_ref[tap, count : count + 8, :] = head_ref[tap]
    rows, cols = masks()
    strict = rows > cols
    units = [(g, h) for g in reversed(range(steps)) for h in range(heads)]
    queries, keys, pre, reads, first, gains = {}, {}, {}, {}, {}, {}
    for g, h in units:
        start = g * BLOCK

        def taken(first, width):
            return pre_ref[pl.ds(start, BLOCK), first : first + width]

        elog = column(col_ref, start, 5 + heads + h)
        out_grad = do_ref[pl.ds(start, BLOCK), h * DV : (h + 1) * DV]
        queries[g, h] = silu(taken(h * DK, DK))
        raw = silu(taken((heads + h) * DK, DK))
        scale = lax.rsqrt(jnp.sum(raw * raw, axis=1, keepdims=True) + 1e-06)
        keys[g, h] = (raw * scale, scale)
        first[g, h] = mm_tn(p_ref[g, h], out_grad)
        gains[g, h] = mm_tn(queries[g, h] * elog, out_grad)
    news_grads, state_grads = {}, {}
    for g in reversed(range(steps)):
        start = g * BLOCK
        for h in range(heads):
            flog = column(col_ref, start, 5 + 2 * heads + h)
            dstate = dstate_ref[h]
            low = dstate.astype(BF16)
            state_grads[g, h] = low
            news_grad = (first[g, h] + mm(keys[g, h][0] * flog, low)).astype(BF16)
            news_grads[g, h] = news_grad
            carried = col_ref[pl.ds(start + BLOCK - 1, 1), 5 + heads + h : 6 + heads + h]
            dstate_ref[h] = gains[g, h] + carried * dstate - mm_tn(w_ref[g, h], news_grad)
    lane = lax.broadcasted_iota(jnp.int32, (BLOCK, 128), 1)

    def through_conv(g, first_col, width, grad):
        start = g * BLOCK
        cols_ = pl.ds(first_col, width)
        value = pre_ref[pl.ds(start, BLOCK), first_col : first_col + width]
        gate = jax.nn.sigmoid(value)
        grad = grad * (gate * (1.0 + value * (1.0 - gate)))
        shift_ref[3, pl.ds(start, BLOCK), cols_] = grad * conv_ref[3:4, cols_]
        sums = []
        for tap in range(3):
            kept = grad * col_ref[pl.ds(start, BLOCK), tap : tap + 1]
            shift_ref[tap, pl.ds(start, BLOCK), cols_] = kept * conv_ref[tap : tap + 1, cols_]
            sums.append(
                jnp.sum(kept * ext_ref[pl.ds(13 + tap + start, BLOCK), cols_], axis=0, keepdims=True)
            )
        sums.append(
            jnp.sum(grad * ext_ref[pl.ds(16 + start, BLOCK), cols_], axis=0, keepdims=True)
        )
        for tap in range(4):
            gconv_ref[tap : tap + 1, cols_] += sums[tap]

    logit_grads = {}
    for g, h in units:
        start = g * BLOCK
        beta = strength(logit_ref, start, h, heads)
        elog = column(col_ref, start, 5 + heads + h)
        flog = column(col_ref, start, 5 + 2 * heads + h)
        key, scale = keys[g, h]
        query = queries[g, h]
        out_grad = do_ref[pl.ds(start, BLOCK), h * DV : (h + 1) * DV]
        decay = decay_matrix(col_ref, row_ref, start, h, heads, rows, cols)
        key_low = key.astype(BF16)
        inner = mm_nt(key_low, key_low) * decay
        news, state, dstate = n_ref[g, h], s_ref[g, h], state_grads[g, h]
        rhs_grad = mm_tn(t_ref[g, h], news_grads[g, h])
        rhs_low = rhs_grad.astype(BF16)
        within = (mm_nt(out_grad, news) * decay).astype(BF16)
        mat_grad = jnp.where(strict, -mm_nt(rhs_low, news), 0.0)
        pair = (mat_grad * beta * decay).astype(BF16)
        back = mm_nt(rhs_low, state)
        q_grad = mm(within, key_low) + elog * mm_nt(out_grad, state)
        k_grad = (
            mm_tn(within, query)
            + mm(pair, key_low)
            + mm_tn(pair, key_low)
            + flog * mm_nt(news, dstate)
            - (beta * elog) * back
        )
        value = silu(pre_ref[pl.ds(start, BLOCK), pl.ds(2 * heads * DK + h * DV, DV)])
        beta_grad = (
            jnp.sum(mat_grad * inner - elog * (key * back), axis=1, keepdims=True)
            + jnp.sum(rhs_grad * value, axis=1, keepdims=True)
        )
        logit_grads[g, h] = beta_grad * beta * (1.0 - beta)
        raw_grad = scale * (k_grad - key * jnp.sum(k_grad * key, axis=1, keepdims=True))
        through_conv(g, h * DK, DK, q_grad)
        through_conv(g, (heads + h) * DK, DK, raw_grad)
        through_conv(g, 2 * heads * DK + h * DV, DV, beta * rhs_grad)
    for g in range(steps):
        total = jnp.zeros((BLOCK, 128), F32)
        for h in range(heads):
            total = jnp.where(lane == h, logit_grads[g, h], total)
        grad_ref[pl.ds(g * BLOCK, BLOCK), channels : channels + 128] = total.astype(BF16)
        grad_ref[pl.ds(g * BLOCK, BLOCK), channels + 128 :] = jnp.zeros((BLOCK, 128), BF16)
    total = shift_ref[3, :count, :]
    for tap in range(3):
        total += shift_ref[tap, pl.ds(3 - tap, count), :]
    grad_ref[:, :channels] = total.astype(BF16)
    for tap in range(3):
        head_ref[tap] = shift_ref[tap, :8, :]


def saved_shapes(blocks, heads):
    return (
        jax.ShapeDtypeStruct((blocks, heads, DK, DV), BF16),
        jax.ShapeDtypeStruct((blocks, heads, BLOCK, DV), BF16),
        jax.ShapeDtypeStruct((blocks, heads, BLOCK, BLOCK), BF16),
        jax.ShapeDtypeStruct((blocks, heads, BLOCK, DK), BF16),
        jax.ShapeDtypeStruct((blocks, heads, BLOCK, BLOCK), BF16),
        jax.ShapeDtypeStruct((blocks * BLOCK, heads * (2 * DK + DV)), F32),
    )


def saved_specs(shapes, per_step, index):
    return [
        pl.BlockSpec((per_step,) + shape.shape[1:], lambda i: (index(i), 0, 0, 0))
        for shape in shapes[:-1]
    ] + [pl.BlockSpec((per_step * BLOCK, shapes[-1].shape[1]), lambda i: (index(i), 0))]


def common_specs(step, channels, logits, index):
    return [
        pl.BlockSpec((16, channels), lambda i: (jnp.maximum(index(i) * (step // 16) - 1, 0), 0)),
        pl.BlockSpec((step, channels), lambda i: (index(i), 0)),
        pl.BlockSpec((8, channels), lambda i: (0, 0)),
        pl.BlockSpec((step, 128), lambda i: (index(i), 0)),
        pl.BlockSpec((8, step), lambda i: (0, index(i))),
        pl.BlockSpec((step, logits), lambda i: (index(i), 0)),
    ]


MIB = 1024 * 1024
VMEM_BYTES = 24 * MIB
SMALL_COST = pl.CostEstimate(flops=10**6, bytes_accessed=10**6, transcendentals=0)
ANYWHERE = pl.BlockSpec(memory_space=pl.ANY)
WHOLE = pl.BlockSpec(memory_space=pltpu.VMEM)
SCALAR = pl.BlockSpec(memory_space=pltpu.SMEM)


def params(limit=VMEM_BYTES):
    return pltpu.CompilerParams(dimension_semantics=("arbitrary",), vmem_limit_bytes=limit)


def forward_recurrence(proj, conv, cols, rows, logits, heads, tokens):
    count, channels = proj.shape
    step = BLOCK * FORWARD_STEP
    shapes = saved_shapes(count // BLOCK, heads)
    index = lambda i: i
    return pl.pallas_call(
        functools.partial(forward_kernel, heads),
        grid=(count // step,),
        in_specs=common_specs(step, channels, 128, index) + [ANYWHERE] * len(tokens),
        out_specs=[pl.BlockSpec((step, heads * DV), lambda i: (i, 0))] + saved_specs(shapes, FORWARD_STEP, index),
        out_shape=(jax.ShapeDtypeStruct((count, heads * DV), BF16),) + shapes,
        scratch_shapes=[
            pltpu.VMEM((step + 16, channels), F32),
            pltpu.VMEM((heads, DK, DV), F32),
        ],
        compiler_params=params(56 * MIB),
        cost_estimate=SMALL_COST,
        name="recurrence_forward",
    )(proj, proj, conv, cols, rows, logits, *tokens)


def backward_recurrence(proj, conv, cols, rows, logits, saved, out_grad, heads, tokens):
    count, channels = proj.shape
    step = BLOCK * BACKWARD_STEP
    last = count // step - 1
    index = lambda i: last - i
    return pl.pallas_call(
        functools.partial(backward_kernel, heads),
        grid=(count // step,),
        in_specs=common_specs(step, channels, 128, index)
        + saved_specs(saved, BACKWARD_STEP, index)
        + [pl.BlockSpec((step, heads * DV), lambda i: (index(i), 0))]
        + [ANYWHERE] * len(tokens),
        out_specs=[
            pl.BlockSpec((step, channels + 256), lambda i: (index(i), 0)),
            pl.BlockSpec((8, channels), lambda i: (0, 0)),
        ],
        out_shape=(
            jax.ShapeDtypeStruct((count, channels + 256), BF16),
            jax.ShapeDtypeStruct((8, channels), F32),
        ),
        scratch_shapes=[
            pltpu.VMEM((step + 16, channels), F32),
            pltpu.VMEM((4, step + 8, channels), F32),
            pltpu.VMEM((heads, DK, DV), F32),
            pltpu.VMEM((3, 8, channels), F32),
        ],
        compiler_params=params(56 * MIB),
        cost_estimate=SMALL_COST,
        name="recurrence_backward",
    )(proj, proj, conv, cols, rows, logits, *saved, out_grad, *tokens)


def project_kernel(
    channels, chunks, handed, rank_ref, gain_ref, w_ref, col_ref, *refs
):
    x_refs = refs[:chunks]
    normed_ref, gate_ref, proj_ref, logit_ref, all_ref = refs[chunks + handed : chunks + handed + 5]
    rows_ref = refs[-1]
    step = pl.program_id(0)
    count = x_refs[0].shape[0]

    @pl.when(step == 0)
    def _():
        width = w_ref.shape[0] * w_ref.shape[2]
        for k in range(w_ref.shape[1]):
            place = pl.ds(pl.multiple_of((rank_ref[0] ^ k) * width, width), width)
            all_ref[place, :] = w_ref[:, k].reshape(width, w_ref.shape[3])

    for k in range(chunks):

        @pl.when(step == k)
        def _():
            x = x_refs[k][...].astype(F32)
            scale = lax.rsqrt(jnp.mean(x * x, axis=1, keepdims=True) + 1e-05)
            normed = (x * scale * gain_ref[...]).astype(BF16)
            normed_ref[...] = normed
            total = mm(normed, all_ref[...])
            gates = gate_ref.shape[1]
            gate_ref[...] = total[:, :gates]
            logit = total[:, gates + channels :]
            high = logit.astype(BF16)
            place = slice(k * count, (k + 1) * count)
            rows_ref[place, : channels + 128] = total[:, gates:].astype(BF16)
            rows_ref[place, channels + 128 :] = (logit - high.astype(F32)).astype(BF16)

    @pl.when(step >= chunks)
    def _():
        order = lax.broadcasted_iota(jnp.int32, (proj_ref.shape[0], rows_ref.shape[0]), 1)
        picked = (col_ref[:, 4:5].astype(jnp.int32) == order).astype(F32)
        packed = mm(picked, rows_ref[...])
        proj_ref[...] = packed[:, :channels].astype(BF16)
        logit_ref[...] = packed[:, channels : channels + 128] + packed[:, channels + 128 :]


def project(rank, x_chunks, gain, weights, cols, channels, passed, tokens):
    count, width = x_chunks[0].shape
    total = count * len(x_chunks)
    gates = weights.shape[3] - channels - 128
    chunks = total // count
    block = total // 2
    first = lambda i: jnp.minimum(i, chunks - 1)
    later = lambda i: jnp.maximum(i - chunks, 0)
    outs = pl.pallas_call(
        functools.partial(project_kernel, channels, chunks, len(passed) + len(tokens)),
        grid=(chunks + total // block,),
        in_specs=[
            SCALAR,
            pl.BlockSpec((1, width), lambda i: (0, 0)),
            pl.BlockSpec(weights.shape, lambda i: (0, 0, 0, 0)),
            pl.BlockSpec((block, 128), lambda i: (later(i), 0)),
        ]
        + [pl.BlockSpec((count, width), lambda i: (0, 0))] * chunks
        + [ANYWHERE] * (len(passed) + len(tokens)),
        out_specs=[
            pl.BlockSpec((count, width), lambda i: (first(i), 0)),
            pl.BlockSpec((count, gates), lambda i: (first(i), 0)),
            pl.BlockSpec((block, channels), lambda i: (later(i), 0)),
            pl.BlockSpec((block, 128), lambda i: (later(i), 0)),
            pl.BlockSpec((width, weights.shape[3]), lambda i: (0, 0)),
        ]
        + [ANYWHERE] * len(passed),
        out_shape=[
            jax.ShapeDtypeStruct((total, width), BF16),
            jax.ShapeDtypeStruct((total, gates), F32),
            jax.ShapeDtypeStruct((total, channels), BF16),
            jax.ShapeDtypeStruct((total, 128), F32),
            jax.ShapeDtypeStruct((width, weights.shape[3]), BF16),
        ]
        + [jax.ShapeDtypeStruct(p.shape, p.dtype) for p in passed],
        input_output_aliases={4 + chunks + i: 5 + i for i in range(len(passed))},
        scratch_shapes=[pltpu.VMEM((total, channels + 256), BF16)],
        compiler_params=params(56 * MIB),
        cost_estimate=SMALL_COST,
        name="project",
    )(rank, gain, weights, cols, *x_chunks, *passed, *tokens)
    return outs[:5], outs[5:]


def gate_kernel(heads, count, first, o_ref, place_ref, gate_ref, gain_ref, *refs):
    chunks = place_ref.shape[1] // count
    dealt_ref, chunk_refs = refs[first], refs[first + 1 : first + 1 + chunks]
    for k, chunk_ref in enumerate(chunk_refs):
        order = lax.broadcasted_iota(jnp.int32, (count, o_ref.shape[0]), 0) + k * count
        picked = (place_ref[...].astype(jnp.int32) == order).astype(F32)
        rows = mm(picked, o_ref[...])
        place = pl.ds(k * count, count)
        dealt_ref[place, :] = rows.astype(BF16)
        for h in range(heads):
            lanes = slice(h * DV, (h + 1) * DV)
            value = rows[:, lanes]
            scale = lax.rsqrt(jnp.mean(value * value, axis=1, keepdims=True) + 1e-05)
            gated = value * scale * gain_ref[...] * silu(gate_ref[place, lanes])
            chunk_ref[:, lanes] = gated.astype(BF16)


def gate_rows(output, place, gate_logit, gain, count, heads, passed, tokens):
    total, cols = output.shape
    chunks = total // count
    others = len(passed) + len(tokens)
    outs = pl.pallas_call(
        functools.partial(gate_kernel, heads, count, others),
        in_specs=[WHOLE] * 4 + [ANYWHERE] * others,
        out_specs=[WHOLE] * (chunks + 1) + [ANYWHERE] * len(passed),
        out_shape=[jax.ShapeDtypeStruct((total, cols), BF16)]
        + [jax.ShapeDtypeStruct((count, cols), BF16)] * chunks
        + [jax.ShapeDtypeStruct(a.shape, a.dtype) for a in passed],
        input_output_aliases={4 + i: 1 + chunks + i for i in range(len(passed))},
        compiler_params=pltpu.CompilerParams(vmem_limit_bytes=VMEM_BYTES),
        cost_estimate=SMALL_COST,
        name="gate_rows",
    )(output, place, gate_logit, gain, *passed, *tokens)
    return outs[0], outs[1 : 1 + chunks], outs[1 + chunks :]


def ungate_kernel(heads, chunks, outs, dealt_ref, col_ref, gate_ref, gain_ref, *refs):
    grad_refs = refs[:chunks]
    gate_grad_ref, o_grad_ref, gain_grad_ref, rows_ref = *refs[outs : outs + 3], refs[-1]
    count = grad_refs[0].shape[0]
    total = dealt_ref.shape[0]
    sums = jnp.zeros((1, DV), F32)
    for k in range(chunks):
        place = pl.ds(k * count, count)
        for h in range(heads):
            lanes = slice(h * DV, (h + 1) * DV)
            value = dealt_ref[place, lanes].astype(F32)
            grad = grad_refs[k][:, lanes].astype(F32)
            logit = gate_ref[place, lanes]
            scale = lax.rsqrt(jnp.mean(value * value, axis=1, keepdims=True) + 1e-05)
            unit = value * scale
            gate = jax.nn.sigmoid(logit)
            slid = logit * gate
            sums += jnp.sum(grad * unit * slid, axis=0, keepdims=True)
            grad = grad * gain_ref[...]
            slope = gate * (1.0 + logit * (1.0 - gate))
            gate_grad_ref[place, lanes] = (grad * unit * slope).astype(BF16)
            grad = grad * slid
            inner = jnp.mean(grad * unit, axis=1, keepdims=True)
            rows_ref[place, lanes] = (scale * (grad - unit * inner)).astype(BF16)
    gain_grad_ref[...] = sums
    for k in range(chunks):
        place = pl.ds(k * count, count)
        order = lax.broadcasted_iota(jnp.int32, (count, total), 1)
        picked = (col_ref[place, 4:5].astype(jnp.int32) == order).astype(F32)
        o_grad_ref[place, :] = mm(picked, rows_ref[...]).astype(BF16)


def ungate_rows(dealt_rows, cols, gate_logit, gain, grads, heads, passed, tokens):
    total, width = dealt_rows.shape
    whole = pl.BlockSpec(memory_space=pltpu.VMEM)
    first = 4 + len(grads)
    outs = pl.pallas_call(
        functools.partial(ungate_kernel, heads, len(grads), len(grads) + len(passed) + len(tokens)),
        in_specs=[whole] * first + [ANYWHERE] * (len(passed) + len(tokens)),
        out_specs=[whole] * 3 + [ANYWHERE] * len(passed),
        out_shape=[
            jax.ShapeDtypeStruct((total, width), BF16),
            jax.ShapeDtypeStruct((total, width), BF16),
            jax.ShapeDtypeStruct((1, DV), F32),
        ]
        + [jax.ShapeDtypeStruct(p.shape, p.dtype) for p in passed],
        input_output_aliases={first + i: 3 + i for i in range(len(passed))},
        scratch_shapes=[pltpu.VMEM((total, width), BF16)],
        compiler_params=pltpu.CompilerParams(vmem_limit_bytes=VMEM_BYTES),
        cost_estimate=SMALL_COST,
        name="ungate_rows",
    )(dealt_rows, cols, gate_logit, gain, *grads, *passed, *tokens)
    return outs[:3], list(outs[3:])


def turned_sums(values):
    sums = jnp.sum(values, axis=1, keepdims=True)
    return jnp.broadcast_to(sums, (values.shape[0], 128)).T[:1]


def put_rows(total, split, core_ref, refs):
    total = total.astype(BF16)
    if split is None:
        refs[0][...] = total
        return
    halves = total.reshape(*split, 2, -1, total.shape[1])
    for core in range(2):

        @pl.when(core_ref[0] == core)
        def _():
            refs[0][...] = halves[:, :, core]
            refs[1][...] = halves[:, :, 1 - core]


def row_outputs(split, width, cols, tile):
    if split is None:
        shape, block = (width, cols), (width, tile)
        spec = pl.BlockSpec(block, lambda i: (0, i))
        return [spec], [jax.ShapeDtypeStruct(shape, BF16)]
    shape = (*split, width // (2 * split[0] * split[1]))
    spec = pl.BlockSpec((*shape, tile), lambda i: (0, 0, 0, i))
    return [spec] * 2, [jax.ShapeDtypeStruct((*shape, cols), BF16)] * 2


def unpack_kernel(split, heads, words_ref, grad_ref, gates_ref, place_ref, normed_ref, w_ref, conv_ref, gain_ref, mid_ref, o_ref, first_sums_ref, *refs):
    count = 2 if split else 1
    dealt_ref, sums_ref = refs[-4 - count], refs[-3 - count]
    row_refs, small_ref, picked_ref = refs[-2 - count : -2], refs[-2], refs[-1]
    step = pl.program_id(0)
    total = grad_ref.shape[0]
    gates = gates_ref.shape[1]
    tile = grad_ref.shape[1] // 2

    @pl.when(step == 0)
    def _():
        part = 256
        for k in range(total // part):
            order = lax.broadcasted_iota(jnp.int32, (part, total), 0) + k * part
            picked = (place_ref[...].astype(jnp.int32) == order).astype(F32)
            picked_ref[k * part : (k + 1) * part, :] = picked.astype(BF16)
        dealt_ref[:, :gates] = gates_ref[...]
        dealt_ref[:, gates : gates + tile] = mm(picked_ref[...], grad_ref[:, :tile]).astype(BF16)
        share = mm(normed_ref[...], dealt_ref[:, gates : gates + tile])
        weights = w_ref[:, gates : gates + tile].astype(F32)
        sums_ref[...] = first_sums_ref[...] + turned_sums(share * weights)
        put_rows(share, split, words_ref, row_refs)

    @pl.when(step == 1)
    def _():
        dealt_ref[:, gates + tile :] = mm(picked_ref[...], grad_ref[:, tile:]).astype(BF16)
        share = mm(normed_ref[...], dealt_ref[:, gates + tile :])
        used = w_ref.shape[1] - gates - tile
        weights = w_ref[:, gates + tile :].astype(F32)
        sums_ref[...] += turned_sums(share[:, :used] * weights)
        if split:
            devices, rows = 2 * split[0] * split[1], share.shape[0] // (2 * split[0] * split[1])
            gin = sums_ref[...] / gain_ref[...]
            small_ref[...] = jnp.zeros_like(small_ref)
            gin = jnp.concatenate([gin[:, j * 128 : (j + 1) * 128] for j in range(8)], 0)
            mid = jnp.concatenate([mid_ref[:, j * 128 : (j + 1) * 128] for j in range(8)], 0)
            for d in range(devices):
                small_ref[d * rows + 4 : d * rows + 5, :] = o_ref[:, :128]
                small_ref[d * rows + 5 : d * rows + 6, :] = o_ref[:, 128:]
                small_ref[d * rows + 8 : d * rows + 16, :] = mid
                small_ref[d * rows + 16 : d * rows + 24, :] = gin
            rank = words_ref[2]
            keys = heads * DK // 128
            vals = heads * DV // 128
            owners = [rank * keys + j for j in range(keys)]
            owners += [HEAD_COUNT * DK // 128 + rank * keys + j for j in range(keys)]
            owners += [2 * HEAD_COUNT * DK // 128 + rank * vals + j for j in range(vals)]
            for j, owner in enumerate(owners):
                place = pl.ds(pl.multiple_of(owner * rows, rows), 8)
                old = small_ref[place, :]
                taps = lax.broadcasted_iota(jnp.int32, (8, 128), 0) < 4
                small_ref[place, :] = jnp.where(taps, conv_ref[:, j * 128 : (j + 1) * 128], old)
            share = jnp.concatenate([share[:, :-128], small_ref[...]], 1)
        put_rows(share, split, words_ref, row_refs)


def unpack(split, words, grad, gate_grad, place, normed, weights, g_conv, gain, g_mid, g_o, sums, heads, tokens):
    total = grad.shape[0]
    cols = grad.shape[1] + gate_grad.shape[1]
    width = normed.shape[0]
    operands = (grad, gate_grad, place, normed, weights, g_conv, gain, g_mid, g_o, sums)
    specs, shapes = row_outputs(split, width, grad.shape[1], grad.shape[1] // 2)
    return pl.pallas_call(
        functools.partial(unpack_kernel, split, heads),
        grid=(2,),
        in_specs=[SCALAR]
        + [pl.BlockSpec(a.shape, lambda i: (0, 0)) for a in operands]
        + [ANYWHERE] * len(tokens),
        out_specs=[
            pl.BlockSpec((total, cols), lambda i: (0, 0)),
            pl.BlockSpec((1, width), lambda i: (0, 0)),
        ]
        + specs,
        out_shape=[
            jax.ShapeDtypeStruct((total, cols), BF16),
            jax.ShapeDtypeStruct((1, width), F32),
        ]
        + shapes,
        scratch_shapes=[pltpu.VMEM((width, 128), F32), pltpu.VMEM((total, total), BF16)],
        compiler_params=params(),
        cost_estimate=SMALL_COST,
        name="unpack",
    )(words, *operands, *tokens)


def unproject_kernel(chunks, first, grad_ref, w_ref, *refs):
    part_refs, turned_ref = refs[first : first + chunks], refs[-1]
    step = pl.program_id(0)

    @pl.when(step == 0)
    def _():
        turned_ref[...] = w_ref[...].T

    part = mm(grad_ref[:, : turned_ref.shape[0]], turned_ref[...])
    for k in range(chunks):

        @pl.when(step == k)
        def _():
            part_refs[k][...] = part.astype(BF16)


def unproject(grad, weights, count, passed, tokens):
    total, cols = grad.shape
    width = weights.shape[0]
    chunks = total // count
    outs = pl.pallas_call(
        functools.partial(unproject_kernel, chunks, len(passed) + len(tokens)),
        grid=(chunks,),
        in_specs=[
            pl.BlockSpec((count, cols), lambda i: (i, 0)),
            pl.BlockSpec(weights.shape, lambda i: (0, 0)),
        ]
        + [ANYWHERE] * (len(passed) + len(tokens)),
        out_specs=[pl.BlockSpec((count, width), lambda i: (0, 0))] * chunks
        + [ANYWHERE] * len(passed),
        out_shape=[jax.ShapeDtypeStruct((count, width), BF16)] * chunks
        + [jax.ShapeDtypeStruct(p.shape, p.dtype) for p in passed],
        input_output_aliases={2 + i: chunks + i for i in range(len(passed))},
        scratch_shapes=[pltpu.VMEM(weights.shape[::-1], BF16)],
        compiler_params=params(56 * MIB),
        cost_estimate=SMALL_COST,
        name="unproject",
    )(grad, weights, *passed, *tokens)
    return list(outs[:chunks]), list(outs[chunks:])


def hand_kernel(*refs):
    refs[-1][...] = jnp.zeros_like(refs[-1])


def handed(passed, tokens):
    outs = pl.pallas_call(
        hand_kernel,
        in_specs=[ANYWHERE] * (len(passed) + len(tokens)),
        out_specs=[ANYWHERE] * len(passed) + [WHOLE],
        out_shape=[jax.ShapeDtypeStruct(p.shape, p.dtype) for p in passed]
        + [jax.ShapeDtypeStruct((8, 128), F32)],
        input_output_aliases={i: i for i in range(len(passed))},
        cost_estimate=SMALL_COST,
        name="handed",
    )(*passed, *tokens)
    return outs[:-1]


def weight_grad_kernel(split, tiles, sums, words_ref, *refs):
    row_refs = refs[-2:] if split else refs[-1:]
    step = pl.program_id(0)
    for tile, pairs in enumerate(tiles):

        @pl.when(step == tile)
        def _():
            total = mm_tn(refs[pairs[0][0]][...], refs[pairs[0][1]][...])
            for left, right in pairs[1:]:
                total += mm_tn(refs[left][...], refs[right][...])
            put_rows(total, split, words_ref, row_refs)
            if sums is not None and tile == 0:
                refs[sums[1]][...] = turned_sums(total * refs[sums[0]][...].astype(F32))


def weight_grad(split, words, groups, tile, tokens, weights=None, limit=VMEM_BYTES):
    width = groups[0][0][0].shape[1]
    operands, specs, tiles = [words], [SCALAR], []
    first = 0
    for lefts, rights in groups:
        count = rights[0].shape[1] // tile
        base = len(operands) - 1
        for left in lefts:
            operands.append(left)
            specs.append(pl.BlockSpec((rights[0].shape[0], width), lambda i: (0, 0)))
        for right in rights:
            operands.append(right)
            specs.append(
                pl.BlockSpec(
                    (right.shape[0], tile),
                    lambda i, first=first, count=count: (0, jnp.clip(i - first, 0, count - 1)),
                )
            )
        tiles += [[(base + k, base + len(lefts) + k) for k in range(len(lefts))]] * count
        first += count
    sums = None
    out_specs, out_shapes = row_outputs(split, width, first * tile, tile)
    if weights is not None:
        operands.append(weights)
        specs.append(pl.BlockSpec((width, tile), lambda i: (0, 0)))
        sums = (len(operands) - 2, len(operands) - 1 + len(tokens))
        out_specs = [pl.BlockSpec((1, width), lambda i: (0, 0))] + out_specs
        out_shapes = [jax.ShapeDtypeStruct((1, width), F32)] + out_shapes
    return pl.pallas_call(
        functools.partial(weight_grad_kernel, split, tiles, sums),
        grid=(first,),
        in_specs=specs + [ANYWHERE] * len(tokens),
        out_specs=out_specs,
        out_shape=out_shapes,
        compiler_params=params(limit),
        cost_estimate=SMALL_COST,
        name="weight_grad",
    )(*operands, *tokens)


def join_kernel(pairs, *refs):
    for chip in range(refs[0].shape[1]):
        place = 0
        for k in range(pairs):
            keep_ref, got_ref = refs[2 * k], refs[2 * k + 1]
            width = keep_ref.shape[3]
            total = keep_ref[:, chip].astype(F32) + got_ref[:, chip].astype(F32)
            refs[-1][chip, :, :, place : place + width] = total.astype(BF16)
            place += width


def joined(pairs, tokens):
    seq_count, chips, rows, _ = pairs[0][0].shape
    cols = sum(keep.shape[3] for keep, _ in pairs)
    return pl.pallas_call(
        functools.partial(join_kernel, len(pairs)),
        in_specs=[WHOLE] * (2 * len(pairs)) + [ANYWHERE] * len(tokens),
        out_specs=WHOLE,
        out_shape=jax.ShapeDtypeStruct((chips, seq_count, rows, cols), BF16),
        compiler_params=pltpu.CompilerParams(vmem_limit_bytes=VMEM_BYTES),
        cost_estimate=SMALL_COST,
        name="joined",
    )(*[a for pair in pairs for a in pair], *tokens)


def layer_kernel(chunks, w_ref, low_ref, *refs):
    weights = w_ref[...].T
    count = low_ref.shape[0]
    refs[chunks][...] = mm(refs[0][...], weights).astype(BF16)
    for k in range(1, chunks):
        refs[chunks + k][:count, :] = low_ref[...]
        refs[chunks + k][count:, :] = mm(refs[k][...], weights).astype(BF16)


def layer_products(hiddens, weights, low):
    count, wide = hiddens[0].shape
    width = weights.shape[0]
    chunks = len(hiddens)
    rows = [count] + [2 * count] * (chunks - 1)
    return pl.pallas_call(
        functools.partial(layer_kernel, chunks),
        grid=(1,),
        in_specs=[
            pl.BlockSpec((width, wide), lambda i: (0, weights.shape[1] // wide - 1)),
            pl.BlockSpec((count, width), lambda i: (0, 0)),
        ]
        + [pl.BlockSpec((count, wide), lambda i: (0, 0))] * chunks,
        out_specs=[pl.BlockSpec((r, width), lambda i: (0, 0)) for r in rows],
        out_shape=[jax.ShapeDtypeStruct((r, width), BF16) for r in rows],
        compiler_params=params(),
        cost_estimate=SMALL_COST,
        name="layer_products",
    )(weights, low, *hiddens)


def position_kernel(heads, chunks, words_ref, lengths_ref, order_ref, decay_ref, *refs):
    col_ref, row_ref, place_ref, cum_ref = refs[-4:]
    total = order_ref.shape[1]
    count = total // chunks
    blocks, near = total // BLOCK, count // BLOCK
    rank = words_ref[2]
    ends = [lengths_ref[0]]
    for e in range(1, lengths_ref.shape[0]):
        ends.append(ends[-1] + lengths_ref[e])

    def segment(position):
        found = jnp.zeros(position.shape, jnp.int32)
        for end in ends:
            found += (position >= end).astype(jnp.int32)
        return jnp.where(position < 0, -1, found)

    for k in range(chunks):
        for h in range(heads):
            for b in range(near):
                value = jnp.zeros((1, BLOCK), F32)
                for part in range(3):
                    row = (part * heads + h) * near + b
                    value += decay_ref[k, row : row + 1, :].astype(F32)
                cum_ref[pl.ds(h * blocks + (rank ^ k) * near + b, 1), :] = value
    rows, cols = masks()
    upper = (rows <= cols).astype(F32)
    cums = jnp.dot(
        cum_ref[...], upper, precision=lax.Precision.HIGHEST, preferred_element_type=F32
    )
    order = order_ref[...]
    chunk = jnp.zeros_like(order)
    for k in range(1, chunks):
        chunk += (order >= k * count).astype(jnp.int32)
    place = (order + ((chunk ^ rank) - chunk) * count).astype(F32)
    place_ref[...] = place
    row_ref[...] = jnp.zeros_like(row_ref)
    lane = lax.broadcasted_iota(jnp.int32, (1, BLOCK), 1)
    for b in range(blocks):
        position = lane + b * BLOCK
        here = segment(position)
        low, high = jnp.full((1, BLOCK), b * BLOCK - 1), jnp.full((1, BLOCK), b * BLOCK + BLOCK - 1)
        keep_in = (here == segment(low)).astype(F32)
        keep_out = (here == segment(high)).astype(F32)
        found = [(segment(position - 3 + tap) == here).astype(F32) for tap in range(3)]
        found += [here.astype(F32), place[:, b * BLOCK : (b + 1) * BLOCK]]
        mine = [cums[h * blocks + b : h * blocks + b + 1, :] for h in range(heads)]
        found += mine
        found += [jnp.exp(c) * keep_in for c in mine]
        found += [jnp.exp(c[:, BLOCK - 1 :] - c) * keep_out for c in mine]
        found.append(jnp.zeros((128 - len(found), BLOCK), F32))
        col_ref[b * BLOCK : (b + 1) * BLOCK, :] = jnp.concatenate(found, 0).T
        for h in range(heads):
            row_ref[h : h + 1, b * BLOCK : (b + 1) * BLOCK] = mine[h]
        row_ref[heads : heads + 1, b * BLOCK : (b + 1) * BLOCK] = here.astype(F32)


def positions(words, lengths, order, decays, heads, tokens):
    total = order.shape[1]
    return pl.pallas_call(
        functools.partial(position_kernel, heads, decays.shape[0]),
        in_specs=[SCALAR, SCALAR, WHOLE, WHOLE] + [ANYWHERE] * len(tokens),
        out_specs=[WHOLE] * 3,
        out_shape=(
            jax.ShapeDtypeStruct((total, 128), F32),
            jax.ShapeDtypeStruct((8, total), F32),
            jax.ShapeDtypeStruct((1, total), F32),
        ),
        scratch_shapes=[pltpu.VMEM((heads * total // BLOCK, BLOCK), F32)],
        cost_estimate=SMALL_COST,
        compiler_params=pltpu.CompilerParams(vmem_limit_bytes=VMEM_BYTES),
        name="positions",
    )(words, lengths, order, decays, *tokens)


def out_rows_kernel(others, words_ref, mine_ref, normed_ref, *refs):
    out_ref, turned_ref = refs[-2:]
    core, chip = words_ref[0], words_ref[1]
    if others:
        chunks, chips, rows, _ = mine_ref.shape
        for k in range(chunks):
            for j in range(chips):
                device = k * 2 * chips + 2 * (chip ^ j)
                for ref, side in ((mine_ref, core), (refs[0], 1 - core)):
                    place = pl.ds(pl.multiple_of((device + side) * rows, rows), rows)
                    out_ref[place, :] = ref[k, j]
    else:
        out_ref[...] = mine_ref[...]
    turned_ref[...] = normed_ref[...].T


def out_rows(words, mine, others, normed, rows, tokens):
    return pl.pallas_call(
        functools.partial(out_rows_kernel, len(others)),
        in_specs=[SCALAR] + [WHOLE] * (2 + len(others)) + [ANYWHERE] * len(tokens),
        out_specs=[WHOLE] * 2,
        out_shape=(
            jax.ShapeDtypeStruct((rows, mine.shape[-1]), BF16),
            jax.ShapeDtypeStruct(normed.shape[::-1], BF16),
        ),
        compiler_params=pltpu.CompilerParams(vmem_limit_bytes=VMEM_BYTES),
        cost_estimate=SMALL_COST,
        name="out_rows",
    )(words, mine, normed, *others, *tokens)


def ffn_rows_kernel(words_ref, ffn_ref, *refs):
    width = ffn_ref.shape[0] * ffn_ref.shape[2]
    for k in range(ffn_ref.shape[1]):
        place = pl.ds(pl.multiple_of((words_ref[2] ^ k) * width, width), width)
        refs[-1][place, :] = ffn_ref[:, k].reshape(width, ffn_ref.shape[3])


def ffn_rows(words, ffn, tokens):
    return pl.pallas_call(
        ffn_rows_kernel,
        in_specs=[SCALAR, WHOLE] + [ANYWHERE] * len(tokens),
        out_specs=WHOLE,
        out_shape=jax.ShapeDtypeStruct((ffn.shape[0] * ffn.shape[1] * ffn.shape[2], ffn.shape[3]), BF16),
        compiler_params=pltpu.CompilerParams(vmem_limit_bytes=VMEM_BYTES),
        cost_estimate=SMALL_COST,
        name="ffn_rows",
    )(words, ffn, *tokens)


def out_project_kernel(chunks, rank_ref, x_ref, gain_ref, w_ref, *refs):
    residual_ref, mid_ref, all_ref = refs[-3:]
    rank = rank_ref[0]
    for k in range(chunks):
        width = refs[k].shape[1]
        all_ref[:, pl.ds(pl.multiple_of((rank ^ k) * width, width), width)] = refs[k][...]
    residual = x_ref[...].astype(F32) + mm_nt(all_ref[...], w_ref[...])
    residual_ref[...] = residual
    scale = lax.rsqrt(jnp.mean(residual * residual, axis=1, keepdims=True) + 1e-05)
    mid_ref[...] = (residual * scale * gain_ref[...]).astype(BF16)


def out_project(rank, x, gain, attn, weights):
    count, width = x.shape
    return pl.pallas_call(
        functools.partial(out_project_kernel, len(attn)),
        in_specs=[SCALAR] + [WHOLE] * (3 + len(attn)),
        out_specs=[WHOLE] * 2,
        out_shape=(
            jax.ShapeDtypeStruct((count, width), F32),
            jax.ShapeDtypeStruct((count, width), BF16),
        ),
        scratch_shapes=[pltpu.VMEM((count, weights.shape[1]), BF16)],
        compiler_params=pltpu.CompilerParams(vmem_limit_bytes=VMEM_BYTES),
        cost_estimate=SMALL_COST,
        name="out_project",
    )(rank, x, gain, weights, *attn)


def mid_back_kernel(chunks, handed, rank_ref, grad_ref, residual_ref, gain_ref, w_ref, *refs):
    parts = refs[:chunks]
    outs, all_ref = refs[chunks + handed :], refs[-1]
    res_grad_ref, low_ref, gain_grad_ref, chunk_refs = outs[0], outs[1], outs[2], outs[3 : 3 + chunks]
    rank = rank_ref[0]
    mid_grad = parts[0][...].astype(F32)
    for k in range(1, chunks):
        mid_grad += parts[k][...].astype(F32)
    residual = residual_ref[...]
    scale = lax.rsqrt(jnp.mean(residual * residual, axis=1, keepdims=True) + 1e-05)
    unit = residual * scale
    gain_grad_ref[...] = jnp.sum(mid_grad * unit, axis=0, keepdims=True)
    scaled = mid_grad * gain_ref[...]
    inner = jnp.mean(scaled * unit, axis=1, keepdims=True)
    res_grad = grad_ref[...].astype(F32) + scale * (scaled - unit * inner)
    res_grad_ref[...] = res_grad
    low = res_grad.astype(BF16)
    low_ref[...] = low
    all_ref[...] = mm(low, w_ref[...]).astype(BF16)
    for k in range(chunks):
        width = chunk_refs[k].shape[1]
        chunk_refs[k][...] = all_ref[:, pl.ds(pl.multiple_of((rank ^ k) * width, width), width)]


def mid_back(rank, grad, residual, gain, parts, weights, passed):
    count, width = residual.shape
    chunks = len(parts)
    wide = weights.shape[1]
    first = 5 + chunks
    outs = pl.pallas_call(
        functools.partial(mid_back_kernel, chunks, len(passed)),
        in_specs=[SCALAR] + [WHOLE] * (first - 1) + [ANYWHERE] * len(passed),
        out_specs=[WHOLE] * (3 + chunks) + [ANYWHERE] * len(passed),
        out_shape=[
            jax.ShapeDtypeStruct((count, width), F32),
            jax.ShapeDtypeStruct((count, width), BF16),
            jax.ShapeDtypeStruct((1, width), F32),
        ]
        + [jax.ShapeDtypeStruct((count, wide // chunks), BF16)] * chunks
        + [jax.ShapeDtypeStruct(p.shape, p.dtype) for p in passed],
        input_output_aliases={first + i: 3 + chunks + i for i in range(len(passed))},
        scratch_shapes=[pltpu.VMEM((count, wide), BF16)],
        compiler_params=pltpu.CompilerParams(vmem_limit_bytes=VMEM_BYTES),
        cost_estimate=SMALL_COST,
        name="mid_back",
    )(rank, grad, residual, gain, weights, *parts, *passed)
    return (*outs[:3], outs[3 : 3 + chunks], list(outs[3 + chunks :]))


def in_back_kernel(chunks, x_ref, res_grad_ref, gain_ref, *refs):
    x = x_ref[...].astype(F32)
    grad = refs[0][...].astype(F32)
    for k in range(1, chunks):
        grad += refs[k][...].astype(F32)
    scale = lax.rsqrt(jnp.mean(x * x, axis=1, keepdims=True) + 1e-05)
    unit = x * scale
    scaled = grad * gain_ref[...]
    inner = jnp.mean(scaled * unit, axis=1, keepdims=True)
    refs[-1][...] = (res_grad_ref[...] + scale * (scaled - unit * inner)).astype(BF16)


def in_back(x, res_grad, gain, parts, tokens):
    return pl.pallas_call(
        functools.partial(in_back_kernel, len(parts)),
        in_specs=[WHOLE] * (3 + len(parts)) + [ANYWHERE] * len(tokens),
        out_specs=WHOLE,
        out_shape=jax.ShapeDtypeStruct(x.shape, BF16),
        compiler_params=pltpu.CompilerParams(vmem_limit_bytes=VMEM_BYTES),
        cost_estimate=SMALL_COST,
        name="in_back",
    )(x, res_grad, gain, *parts, *tokens)


def swapped(value, axis, mask):
    devices = lax.axis_size(axis)
    return lax.ppermute(value, axis, [(i, i ^ mask) for i in range(devices)])


def pinned(value, other):
    return value + 0 * other[:1, :1].astype(value.dtype)


def spread(value):
    return [value] + [swapped(value, "seq", k) for k in range(1, lax.axis_size("seq"))]


def returned(chunks):
    return [chunks[0]] + [swapped(chunks[k], "seq", k) for k in range(1, len(chunks))]


class RowSum:
    def __init__(self, outs):
        self.outs = list(outs)

    def pair(self):
        if len(self.outs) == 2:
            self.got = swapped(self.outs[1], "mp", 1)

    def join(self, *tokens):
        seq_count, mp_count = lax.axis_size("seq"), lax.axis_size("mp")
        if len(self.outs) == 1:
            (grad,) = self.outs
            cols = grad.shape[1]
            parts = grad.astype(F32).reshape(seq_count, mp_count, -1, cols).transpose(1, 0, 2, 3)
            own = lax.psum_scatter(parts.reshape(-1, cols), "mp", scatter_dimension=0, tiled=True)
            self.half = grad
            self.parts = own.reshape(1, seq_count, -1, cols)
            return
        self.half = joined([(self.outs[0], self.got)], tokens)
        self.between()

    def between(self):
        mp_count = lax.axis_size("mp")
        groups = [list(range(core, mp_count, 2)) for core in range(2)]
        self.parts = lax.all_to_all(self.half, "mp", 0, 0, axis_index_groups=groups, tiled=True)

    def beside(self, other):
        if len(self.outs) == 1:
            both = RowSum([jnp.concatenate([self.outs[0], other.outs[0]], 1)])
            both.join()
            return both
        both = RowSum([])
        both.half = joined([(s.outs[0], s.got) for s in (self, other)], [])
        both.between()
        return both


def row_sums(sums, tokens):
    groups = [part.parts for part in sums]
    shape = groups[0].shape[1:3]
    cols = [group.shape[3] for group in groups]

    def kernel(*refs):
        place = 0
        for ref, width in zip(refs, cols):
            total = ref[0].astype(F32)
            for k in range(1, ref.shape[0]):
                total += ref[k].astype(F32)
            refs[-1][:, :, place : place + width] = total.astype(BF16)
            place = place + width

    return pl.pallas_call(
        kernel,
        in_specs=[WHOLE] * len(groups) + [ANYWHERE] * len(tokens),
        out_specs=WHOLE,
        out_shape=jax.ShapeDtypeStruct(shape + (sum(cols),), BF16),
        cost_estimate=SMALL_COST,
        compiler_params=pltpu.CompilerParams(vmem_limit_bytes=VMEM_BYTES),
        name="row_sums",
    )(*groups, *tokens)


def finish_kernel(heads, wide, half, rows, pieces_ref, *refs):
    qkv_ref, gate_ref, beta_ref, conv_ref, out_ref, gu_ref, down_ref, small_ref = refs
    chunks = pieces_ref.shape[0]
    keys, vals = heads * DK, heads * DV
    ffn, mix = 0, 3 * wide
    gate_first, first, out_first = mix, mix + vals, pieces_ref.shape[2] - vals

    def piece(j, start, width):
        return pieces_ref[j, :, start : start + width].astype(F32)

    for j in range(chunks):
        gate_ref[:, j * vals : (j + 1) * vals] = piece(j, gate_first, vals)
        qkv_ref[:, j * keys : (j + 1) * keys] = piece(j, first, keys)
        place = chunks * keys + j * keys
        qkv_ref[:, place : place + keys] = piece(j, first + keys, keys)
        place = 2 * chunks * keys + j * vals
        qkv_ref[:, place : place + vals] = piece(j, first + 2 * keys, vals)
        out_ref[:, j * vals : (j + 1) * vals] = piece(j, out_first, vals)
        beta = piece(j, first + 2 * keys + vals, 128)
        beta_ref[:, j * heads : (j + 1) * heads] = beta[:, :heads]
    small = piece(0, out_first - 128, 128)
    for j in range(1, chunks):
        small += piece(j, out_first - 128, 128)
    small_ref[...] = small
    conv_ref[...] = small[: conv_ref.shape[0]]
    for part in range(3):
        whole = jnp.concatenate(
            [piece(j, ffn + part * wide, wide)[:, :half] for j in range(chunks)], 1
        )
        if part < 2:
            gu_ref[:, part * chunks * half : (part + 1) * chunks * half] = whole
        else:
            down_ref[...] = whole


def finish(pieces, heads, wide, half, taps):
    chunks, rows, _ = pieces.shape
    keys, vals = HEAD_COUNT * DK, HEAD_COUNT * DV
    ffn = chunks * half
    shapes = [(rows, 2 * keys + vals), (rows, vals), (rows, HEAD_COUNT), (taps, 128)]
    shapes += [(rows, vals), (rows, 2 * ffn), (rows, ffn), (rows, 128)]
    return pl.pallas_call(
        functools.partial(finish_kernel, heads, wide, half, rows),
        in_specs=[WHOLE],
        out_specs=[WHOLE] * len(shapes),
        out_shape=[jax.ShapeDtypeStruct(shape, F32) for shape in shapes],
        compiler_params=pltpu.CompilerParams(vmem_limit_bytes=VMEM_BYTES),
        cost_estimate=SMALL_COST,
        name="finish",
    )(pieces)


def dealt(own):
    return lax.all_to_all(own, "seq", 0, 0, tiled=True)


def left_product(left, right):
    return lax.dot_general(
        left, right, (((0,), (0,)), ((), ())), preferred_element_type=jnp.float32
    )


def right_product(left, right):
    return lax.dot_general(
        left, right, (((1,), (1,)), ((), ())), preferred_element_type=jnp.float32
    )


def dot(left, right):
    return jnp.dot(left, right, preferred_element_type=jnp.float32)


def silu_slope(values):
    gate = jax.nn.sigmoid(values)
    return gate * (1.0 + values * (1.0 - gate))


def split_three(values):
    high = values.astype(BF16)
    rest = values - high.astype(F32)
    middle = rest.astype(BF16)
    return jnp.stack([high, middle, (rest - middle.astype(F32)).astype(BF16)])


def body(
    layer_in,
    out_grad,
    seq_lengths,
    dealing,
    log_decay,
    w_qkv,
    w_out_gate,
    w_beta,
    conv_w,
    gain_in,
    gain_o,
    w_out,
    gain_mid,
    w_gate_up,
    w_down,
):
    seq_count, mp_count = lax.axis_size("seq"), lax.axis_size("mp")
    rank, place_mp = lax.axis_index("seq"), lax.axis_index("mp")
    count = layer_in.shape[1]
    rows = w_qkv.shape[0]
    heads = HEAD_COUNT // seq_count
    key_cols, val_cols = heads * DK, heads * DV
    half = w_down.shape[0] // seq_count
    wide = -(-half // 256) * 256
    taps = conv_w.shape[1]
    total = dealing.shape[1]
    devices = seq_count * mp_count
    channels = 2 * key_cols + val_cols
    all_keys, ffn = HEAD_COUNT * DK, w_down.shape[0]
    split = (seq_count, mp_count // 2) if mp_count <= 8 else None
    words = jnp.stack([place_mp % 2, place_mp // 2, rank]).astype(jnp.int32)
    rank_word = rank.astype(jnp.int32).reshape(1)

    small = jnp.concatenate([conv_w.T.reshape(-1), gain_in, gain_mid, gain_o])
    small_count = small.shape[0]
    spare = 128 - heads
    filler = jnp.concatenate([small, jnp.zeros((rows * spare - small_count,), BF16)])
    filler = filler.reshape(rows, spare)
    wide_filler = jnp.zeros((rows, wide - half), BF16)
    turned_down = w_down.T
    decay_lanes = -(-3 * heads * count // (128 * rows)) * 128
    decays = split_three(log_decay[0].T)
    mix_cols = channels + 128 + val_cols
    pieces, ffn_pieces = [], []
    for j in range(seq_count):
        own_decay = decays[:, j * heads : (j + 1) * heads].reshape(-1)
        own_decay = jnp.concatenate(
            [own_decay, jnp.zeros((rows * decay_lanes - own_decay.shape[0],), BF16)]
        )
        pieces.append(
            jnp.concatenate(
                [
                    w_out_gate[:, j * val_cols : (j + 1) * val_cols],
                    w_qkv[:, j * key_cols : (j + 1) * key_cols],
                    w_qkv[:, all_keys + j * key_cols : all_keys + (j + 1) * key_cols],
                    w_qkv[:, 2 * all_keys + j * val_cols : 2 * all_keys + (j + 1) * val_cols],
                    w_beta[:, j * heads : (j + 1) * heads],
                    filler,
                ],
                1,
            )
        )
        ffn_pieces.append(
            jnp.concatenate(
                [
                    w_gate_up[:, j * half : (j + 1) * half],
                    wide_filler,
                    w_gate_up[:, ffn + j * half : ffn + (j + 1) * half],
                    wide_filler,
                    turned_down[:, j * half : (j + 1) * half],
                    wide_filler,
                    own_decay.reshape(rows, decay_lanes),
                ],
                1,
            )
        )
    def near(arrays):
        arrays = jnp.stack(arrays)
        return jnp.stack(
            returned(
                [lax.dynamic_index_in_dim(arrays, rank ^ k, 0, keepdims=False) for k in range(seq_count)]
            )
        )

    pieces, ffn_pieces = near(pieces), near(ffn_pieces)
    gathered = lax.all_gather(pieces, "mp", axis=0, tiled=False)
    late = pieces[1, :1, :1] + jnp.sum(ffn_pieces[1:, :1, :1], axis=0)
    chunks_in = spread(layer_in[0] + 0 * late)

    relative = rank ^ jnp.arange(seq_count)
    smalls = gathered[:, :, :, mix_cols - spare :].transpose(1, 0, 2, 3)
    smalls = jnp.take(smalls, relative, axis=0).reshape(devices, -1)[:, :small_count]
    own_taps = conv_w.shape[0] * taps
    full_conv = smalls[:, :own_taps].reshape(-1, taps, conv_w.shape[0]).transpose(1, 0, 2)
    full_conv = full_conv.reshape(taps, -1).astype(F32)
    conv = jnp.concatenate(
        [
            lax.dynamic_slice_in_dim(full_conv, rank * key_cols, key_cols, 1),
            lax.dynamic_slice_in_dim(full_conv, all_keys + rank * key_cols, key_cols, 1),
            lax.dynamic_slice_in_dim(full_conv, 2 * all_keys + rank * val_cols, val_cols, 1),
        ],
        1,
    )
    conv = jnp.concatenate([conv, jnp.zeros((8 - taps, channels), F32)], 0)
    gains = smalls[:, own_taps:].astype(F32)
    full_gin = gains[:, :rows].reshape(1, -1)
    full_gmid = gains[:, rows : 2 * rows].reshape(1, -1)
    full_go = gains[:, 2 * rows :].reshape(1, -1)

    out_turned = w_out.T
    out_near = []
    if split:
        out_near = [out_turned] + [swapped(out_turned, "mp", 2 * j) for j in range(1, mp_count // 2)]

    out_copies = []
    if split:
        out_copies = [
            jnp.broadcast_to(jnp.stack(out_near), (seq_count, mp_count // 2, *out_turned.shape))
        ]

    decays = ffn_pieces[:, :, 3 * wide :].reshape(seq_count, -1)[:, : 3 * heads * count]
    col_info, row_info, place_row = positions(
        words, seq_lengths[0], dealing, decays.reshape(seq_count, -1, BLOCK), heads, out_copies
    )

    passed = [ffn_pieces[:, :, : 3 * wide], out_grad[0] + 0 * pieces[1, :1, :1]] + out_copies
    passed = handed(passed, chunks_in[1:] + [row_info])
    ffn_all = lax.all_gather(passed[0], "mp", axis=0, tiled=False)
    chunks_grad = spread(passed[1])
    out_mine = [lax.all_to_all(passed[2], "seq", 0, 0, tiled=True)] if split else []
    (normed, gate_logit, proj, logit_parts, mix), _ = project(
        rank_word, chunks_in, full_gin, gathered, col_info, channels,
        [], [conv, full_go, full_gmid],
    )
    outs = forward_recurrence(proj, conv, col_info, row_info, logit_parts, heads, [])
    dealt_rows, attn, out_mine = gate_rows(
        outs[0], place_row, gate_logit, full_go, count, heads, out_mine, chunks_grad[1:]
    )
    if split:
        out_others = [swapped(out_mine[0], "mp", 1)]
    else:
        out_mine, out_others = [lax.all_gather(out_turned, ("seq", "mp"), axis=0, tiled=True)], []
    attn_parts = returned(attn)
    out_w, normed_t = out_rows(words, out_mine[0], out_others, normed, devices * rows, [attn[0]])

    residual, mid_own = out_project(rank_word, layer_in[0], full_gmid, attn_parts, out_w)

    ffn_w = ffn_rows(words, ffn_all, [mid_own])
    w_gu, down_turned = ffn_w[:, : 2 * wide], ffn_w[:, 2 * wide :]
    mids = spread(mid_own)
    hiddens, gu_grads, mid_parts = ([None] * seq_count for _ in range(3))
    last_part = None
    for k in (0, 1, 3, 2):
        mid_k = mids[k] if last_part is None else pinned(mids[k], last_part)
        gate_up = dot(mid_k, w_gu)
        gate, up = gate_up[:, :wide], gate_up[:, wide:]
        hiddens[k] = (silu(gate) * up).astype(BF16)
        hidden_grad = dot(chunks_grad[k], down_turned)
        gu_grads[k] = jnp.concatenate(
            [hidden_grad * up * silu_slope(gate), hidden_grad * silu(gate)], 1
        ).astype(BF16)
        mid_parts[k] = last_part = right_product(gu_grads[k], w_gu).astype(BF16)
    mid_parts = returned(mid_parts)
    ffn_sum = RowSum(
        weight_grad(
            split, words, [(mids, gu_grads), (chunks_grad, hiddens)], wide, [last_part, mid_parts[1]]
        ),
    )
    res_grad, out_proj_grad, g_mid, attn_grads, ffn_sum.outs[-1:] = mid_back(
        rank_word, out_grad[0], residual, full_gmid, mid_parts, out_w, ffn_sum.outs[-1:]
    )
    attn_grads = returned(attn_grads)
    ffn_sum.pair()
    layer_own, *both = layer_products(hiddens, ffn_w, out_proj_grad)

    (gate_grad, o_grad, g_go), both = ungate_rows(
        dealt_rows, col_info, gate_logit, full_go, attn_grads, heads, both, []
    )
    gate_sums, *gate_outs = weight_grad(
        split, words, [([normed], [gate_grad])], val_cols, [], weights=mix
    )
    gate_sum = RowSum(gate_outs)
    gate_sum.pair()
    ffn_sum = ffn_sum.beside(gate_sum)
    both = returned([None] + both)[1:]
    proj_grad, g_conv = backward_recurrence(
        proj, conv, col_info, row_info, logit_parts, outs[1:], o_grad, heads, [ffn_sum.half]
    )
    mix_grad, mix_sums, *mix_outs = unpack(
        split, words, proj_grad, gate_grad, place_row, normed_t, mix, g_conv, full_gin, g_mid, g_go,
        gate_sums, heads, [],
    )
    mix_sum = RowSum(mix_outs)
    mix_sum.pair()
    normed_parts, _ = unproject(mix_grad, mix, count, [], [])
    normed_chunks = returned(normed_parts)
    out_sum = RowSum(
        weight_grad(split, words, [([out_proj_grad] + both, attn)], val_cols,
            [normed_parts[0], ffn_sum.parts], limit=56 * MIB,
        )
    )
    out_sum.pair()
    last_sum = mix_sum.beside(out_sum)
    ffn_total = row_sums([ffn_sum], [last_sum.half])
    in_grad = in_back(layer_in[0], res_grad, full_gin, normed_chunks, [ffn_total])
    ffn_sum.parts = ffn_total[None]
    layer_out = residual + sum(
        c.astype(F32) for c in [layer_own] + [b[count:] for b in both]
    )
    all_pieces = dealt(row_sums([ffn_sum, last_sum], [in_grad]))
    layer_out = layer_out.astype(BF16)[None]
    if split:
        g_qkv, g_gate, g_beta, g_conv, g_out, g_gu, g_down, small_sum = finish(
            all_pieces, heads, wide, half, taps
        )
        device = rank * mp_count + place_mp
        grad_go = lax.dynamic_slice_in_dim(
            small_sum[4:6].reshape(-1), device * gain_o.shape[0], gain_o.shape[0]
        )
        grad_gmid = lax.dynamic_slice_in_dim(small_sum[8:16].reshape(-1), device * rows, rows)
        grad_gin = lax.dynamic_slice_in_dim(small_sum[16:24].reshape(-1), device * rows, rows)
        return (
            layer_out, in_grad[None], g_qkv, g_gate, g_beta, g_conv.T,
            grad_gin, grad_go, g_out.T, grad_gmid, g_gu, g_down.T,
        )

    def columns(first, width):
        parts = [all_pieces[j, :, first : first + width] for j in range(seq_count)]
        return jnp.concatenate(parts, 1).astype(F32)

    everywhere = ("seq", "mp")
    conv_full = jnp.zeros((taps, conv_w.shape[0] * devices), F32)
    for first, width in ((0, key_cols), (key_cols, key_cols), (2 * key_cols, val_cols)):
        conv_full = lax.dynamic_update_slice_in_dim(
            conv_full, g_conv[:taps, first : first + width], first * seq_count + rank * width, 1
        )
    grad_conv = lax.psum_scatter(conv_full.T, everywhere, scatter_dimension=0, tiled=True)
    g_gin = mix_sums[0] / full_gin[0]
    grad_gin, grad_gmid, grad_go = (
        lax.psum_scatter(g, everywhere, scatter_dimension=0, tiled=True)
        for g in (g_gin, g_mid[0], g_go[0])
    )
    first = 3 * wide + val_cols
    last = all_pieces.shape[2] - val_cols
    return (
        layer_out,
        in_grad[None],
        jnp.concatenate(
            [
                columns(first, key_cols),
                columns(first + key_cols, key_cols),
                columns(first + 2 * key_cols, val_cols),
            ],
            1,
        ),
        columns(3 * wide, val_cols),
        columns(first + channels, heads),
        grad_conv,
        grad_gin,
        grad_go,
        columns(last, val_cols).T,
        grad_gmid,
        jnp.concatenate([columns(0, half), columns(wide, half)], 1),
        columns(2 * wide, half).T,
    )


def solution(mesh):
    in_specs = (
        P("mp", "seq", None),
        P("mp", "seq", None),
        P("mp", None),
        P("mp", None),
        P("mp", "seq", None),
        P(("seq", "mp"), None),
        P(("seq", "mp"), None),
        P(("seq", "mp"), None),
        P(("seq", "mp"), None),
        P(("seq", "mp")),
        P(("seq", "mp")),
        P(None, ("seq", "mp")),
        P(("seq", "mp")),
        P(("seq", "mp"), None),
        P(None, ("seq", "mp")),
    )
    out_specs = (
        P("mp", "seq", None),
        P("mp", "seq", None),
        P(("seq", "mp"), None),
        P(("seq", "mp"), None),
        P(("seq", "mp"), None),
        P(("seq", "mp"), None),
        P(("seq", "mp")),
        P(("seq", "mp")),
        P(None, ("seq", "mp")),
        P(("seq", "mp")),
        P(("seq", "mp"), None),
        P(None, ("seq", "mp")),
    )
    return jax.shard_map(body, mesh=mesh, in_specs=in_specs, out_specs=out_specs, check_vma=False)
```

```python
import functools

import jax
import jax.numpy as jnp
from jax import lax
from jax.experimental import pallas as pl
from jax.experimental.pallas import tpu as pltpu
from jax.sharding import PartitionSpec as P

HEAD_COUNT = 8
DK = 128
DV = 256
BLOCK = 128
FORWARD_STEP = 6
BACKWARD_STEP = 2
F32 = jnp.float32
BF16 = jnp.bfloat16


def mm(left, right):
    return jnp.dot(left.astype(BF16), right.astype(BF16), preferred_element_type=F32)


def mm_nt(left, right):
    return lax.dot_general(
        left.astype(BF16),
        right.astype(BF16),
        (((1,), (1,)), ((), ())),
        preferred_element_type=F32,
    )


def mm_tn(left, right):
    return lax.dot_general(
        left.astype(BF16),
        right.astype(BF16),
        (((0,), (0,)), ((), ())),
        preferred_element_type=F32,
    )


def masks():
    rows = lax.broadcasted_iota(jnp.int32, (BLOCK, BLOCK), 0)
    cols = lax.broadcasted_iota(jnp.int32, (BLOCK, BLOCK), 1)
    return rows, cols


def unit_inverses(mats, rows, cols):
    ident = (rows == cols).astype(F32)
    near = (rows // 16) == (cols // 16)
    power = [jnp.where(near, a, 0.0) for a in mats]
    result = [ident - p for p in power]
    span = 2
    while span < 16:
        power = [mm(p, p) for p in power]
        result = [t + mm(t, p) for t, p in zip(result, power)]
        span *= 2
    size = 16
    while size < BLOCK:
        off = ((rows // (2 * size)) == (cols // (2 * size))) & ((rows // size) != (cols // size))
        reach = [mm(jnp.where(off, a, 0.0), t) for a, t in zip(mats, result)]
        result = [t - mm(t, x) for t, x in zip(result, reach)]
        size *= 2
    return result


def convolve(ext_ref, conv_ref, col_ref, start, first, width):
    cols = pl.ds(first, width)
    total = ext_ref[pl.ds(16 + start, BLOCK), cols] * conv_ref[3:4, cols]
    for tap in range(3):
        keep = col_ref[pl.ds(start, BLOCK), tap : tap + 1]
        total += ext_ref[pl.ds(13 + tap + start, BLOCK), cols] * keep * conv_ref[tap : tap + 1, cols]
    return total


def column(col_ref, start, index):
    return col_ref[pl.ds(start, BLOCK), index : index + 1]


def strength(logit_ref, start, head, heads):
    return jax.nn.sigmoid(column(logit_ref, start, head))


def exact_nt(left, right):
    left_high, right_high = left.astype(BF16), right.astype(BF16)
    left_low = left - left_high.astype(F32)
    right_low = right - right_high.astype(F32)
    return mm_nt(left_high, right_high) + (mm_nt(left_high, right_low) + mm_nt(left_low, right_high))


def decay_matrix(col_ref, row_ref, start, head, heads, rows, cols):
    cum_i = column(col_ref, start, 5 + head)
    cum_j = row_ref[head : head + 1, pl.ds(start, BLOCK)]
    seg_i = column(col_ref, start, 3)
    seg_j = row_ref[heads : heads + 1, pl.ds(start, BLOCK)]
    within = (rows >= cols) & (seg_i == seg_j)
    return jnp.where(within, jnp.exp(jnp.where(within, cum_i - cum_j, 0.0)), 0.0)


def silu(values):
    return values * jax.nn.sigmoid(values)


def forward_kernel(
    heads, edge_ref, proj_ref, conv_ref, col_ref, row_ref, logit_ref, *refs,
):
    o_ref, s_ref, n_ref, t_ref, w_ref, p_ref, pre_ref, ext_ref, state_ref = refs[-9:]
    steps = proj_ref.shape[0] // BLOCK

    @pl.when(pl.program_id(0) == 0)
    def _():
        state_ref[...] = jnp.zeros_like(state_ref)

    ext_ref[:16, :] = edge_ref[...].astype(F32)
    ext_ref[16:, :] = proj_ref[...].astype(F32)
    rows, cols = masks()
    strict = rows > cols
    units = [(g, h) for g in range(steps) for h in range(heads)]
    queries, keys, values, mats, decays, betas = {}, {}, {}, [], {}, {}
    for g, h in units:
        start = g * BLOCK

        def taken(first, width):
            value = convolve(ext_ref, conv_ref, col_ref, start, first, width)
            pre_ref[pl.ds(start, BLOCK), first : first + width] = value
            return value

        queries[g, h] = silu(taken(h * DK, DK))
        raw = silu(taken((heads + h) * DK, DK))
        keys[g, h] = raw * lax.rsqrt(jnp.sum(raw * raw, axis=1, keepdims=True) + 1e-06)
        values[g, h] = silu(taken(2 * heads * DK + h * DV, DV))
        decays[g, h] = decay_matrix(col_ref, row_ref, start, h, heads, rows, cols)
        betas[g, h] = strength(logit_ref, start, h, heads)
        beta = betas[g, h]
        inner = mm_nt(keys[g, h], keys[g, h])
        mats.append(jnp.where(strict, beta * inner * decays[g, h], 0.0))
    inverses = unit_inverses(mats, rows, cols)
    umats, wmats, pmats, boundary, reads = {}, {}, {}, {}, {}
    for (g, h), inverse in zip(units, inverses):
        start = g * BLOCK
        beta = betas[g, h]
        elog = column(col_ref, start, 5 + heads + h)
        flog = column(col_ref, start, 5 + 2 * heads + h)
        inverse = inverse.astype(BF16)
        t_ref[g, h] = inverse
        umats[g, h] = mm(inverse, beta * values[g, h])
        wmats[g, h] = mm(inverse, (beta * elog) * keys[g, h]).astype(BF16)
        w_ref[g, h] = wmats[g, h]
        pmats[g, h] = (exact_nt(queries[g, h], keys[g, h]) * decays[g, h]).astype(BF16)
        p_ref[g, h] = pmats[g, h]
        boundary[g, h] = (keys[g, h] * flog).T.astype(BF16)
        reads[g, h] = (queries[g, h] * elog).astype(BF16)
    for g in range(steps):
        start = g * BLOCK
        for h in range(heads):
            state = state_ref[h]
            low = state.astype(BF16)
            s_ref[g, h] = low
            news = (umats[g, h] - mm(wmats[g, h], low)).astype(BF16)
            n_ref[g, h] = news
            carried = col_ref[pl.ds(start + BLOCK - 1, 1), 5 + heads + h : 6 + heads + h]
            state_ref[h] = carried * state + mm(boundary[g, h], news)
            output = mm(reads[g, h], low) + mm(pmats[g, h], news)
            o_ref[pl.ds(start, BLOCK), h * DV : (h + 1) * DV] = output.astype(BF16)


def backward_kernel(
    heads, edge_ref, proj_ref, conv_ref, col_ref, row_ref, logit_ref,
    s_ref, n_ref, t_ref, w_ref, p_ref, pre_ref, do_ref, *refs,
):
    grad_ref, gconv_ref, ext_ref, shift_ref, dstate_ref, head_ref = refs[-6:]
    count = proj_ref.shape[0]
    steps = count // BLOCK
    channels = proj_ref.shape[1]

    @pl.when(pl.program_id(0) == 0)
    def _():
        dstate_ref[...] = jnp.zeros_like(dstate_ref)
        head_ref[...] = jnp.zeros_like(head_ref)
        gconv_ref[...] = jnp.zeros_like(gconv_ref)

    ext_ref[:16, :] = edge_ref[...].astype(F32)
    ext_ref[16:, :] = proj_ref[...].astype(F32)
    for tap in range(3):
        shift_ref[tap, count : count + 8, :] = head_ref[tap]
    rows, cols = masks()
    strict = rows > cols
    units = [(g, h) for g in reversed(range(steps)) for h in range(heads)]
    queries, keys, pre, reads, first, gains = {}, {}, {}, {}, {}, {}
    for g, h in units:
        start = g * BLOCK

        def taken(first, width):
            return pre_ref[pl.ds(start, BLOCK), first : first + width]

        elog = column(col_ref, start, 5 + heads + h)
        out_grad = do_ref[pl.ds(start, BLOCK), h * DV : (h + 1) * DV]
        queries[g, h] = silu(taken(h * DK, DK))
        raw = silu(taken((heads + h) * DK, DK))
        scale = lax.rsqrt(jnp.sum(raw * raw, axis=1, keepdims=True) + 1e-06)
        keys[g, h] = (raw * scale, scale)
        first[g, h] = mm_tn(p_ref[g, h], out_grad)
        gains[g, h] = mm_tn(queries[g, h] * elog, out_grad)
    news_grads, state_grads = {}, {}
    for g in reversed(range(steps)):
        start = g * BLOCK
        for h in range(heads):
            flog = column(col_ref, start, 5 + 2 * heads + h)
            dstate = dstate_ref[h]
            low = dstate.astype(BF16)
            state_grads[g, h] = low
            news_grad = (first[g, h] + mm(keys[g, h][0] * flog, low)).astype(BF16)
            news_grads[g, h] = news_grad
            carried = col_ref[pl.ds(start + BLOCK - 1, 1), 5 + heads + h : 6 + heads + h]
            dstate_ref[h] = gains[g, h] + carried * dstate - mm_tn(w_ref[g, h], news_grad)
    lane = lax.broadcasted_iota(jnp.int32, (BLOCK, 128), 1)

    def through_conv(g, first_col, width, grad):
        start = g * BLOCK
        cols_ = pl.ds(first_col, width)
        value = pre_ref[pl.ds(start, BLOCK), first_col : first_col + width]
        gate = jax.nn.sigmoid(value)
        grad = grad * (gate * (1.0 + value * (1.0 - gate)))
        shift_ref[3, pl.ds(start, BLOCK), cols_] = grad * conv_ref[3:4, cols_]
        sums = []
        for tap in range(3):
            kept = grad * col_ref[pl.ds(start, BLOCK), tap : tap + 1]
            shift_ref[tap, pl.ds(start, BLOCK), cols_] = kept * conv_ref[tap : tap + 1, cols_]
            sums.append(
                jnp.sum(kept * ext_ref[pl.ds(13 + tap + start, BLOCK), cols_], axis=0, keepdims=True)
            )
        sums.append(
            jnp.sum(grad * ext_ref[pl.ds(16 + start, BLOCK), cols_], axis=0, keepdims=True)
        )
        for tap in range(4):
            gconv_ref[tap : tap + 1, cols_] += sums[tap]

    logit_grads = {}
    for g, h in units:
        start = g * BLOCK
        beta = strength(logit_ref, start, h, heads)
        elog = column(col_ref, start, 5 + heads + h)
        flog = column(col_ref, start, 5 + 2 * heads + h)
        key, scale = keys[g, h]
        query = queries[g, h]
        out_grad = do_ref[pl.ds(start, BLOCK), h * DV : (h + 1) * DV]
        decay = decay_matrix(col_ref, row_ref, start, h, heads, rows, cols)
        key_low = key.astype(BF16)
        inner = mm_nt(key_low, key_low) * decay
        news, state, dstate = n_ref[g, h], s_ref[g, h], state_grads[g, h]
        rhs_grad = mm_tn(t_ref[g, h], news_grads[g, h])
        rhs_low = rhs_grad.astype(BF16)
        within = (mm_nt(out_grad, news) * decay).astype(BF16)
        mat_grad = jnp.where(strict, -mm_nt(rhs_low, news), 0.0)
        pair = (mat_grad * beta * decay).astype(BF16)
        back = mm_nt(rhs_low, state)
        q_grad = mm(within, key_low) + elog * mm_nt(out_grad, state)
        k_grad = (
            mm_tn(within, query)
            + mm(pair, key_low)
            + mm_tn(pair, key_low)
            + flog * mm_nt(news, dstate)
            - (beta * elog) * back
        )
        value = silu(pre_ref[pl.ds(start, BLOCK), pl.ds(2 * heads * DK + h * DV, DV)])
        beta_grad = (
            jnp.sum(mat_grad * inner - elog * (key * back), axis=1, keepdims=True)
            + jnp.sum(rhs_grad * value, axis=1, keepdims=True)
        )
        logit_grads[g, h] = beta_grad * beta * (1.0 - beta)
        raw_grad = scale * (k_grad - key * jnp.sum(k_grad * key, axis=1, keepdims=True))
        through_conv(g, h * DK, DK, q_grad)
        through_conv(g, (heads + h) * DK, DK, raw_grad)
        through_conv(g, 2 * heads * DK + h * DV, DV, beta * rhs_grad)
    for g in range(steps):
        total = jnp.zeros((BLOCK, 128), F32)
        for h in range(heads):
            total = jnp.where(lane == h, logit_grads[g, h], total)
        grad_ref[pl.ds(g * BLOCK, BLOCK), channels : channels + 128] = total.astype(BF16)
        grad_ref[pl.ds(g * BLOCK, BLOCK), channels + 128 :] = jnp.zeros((BLOCK, 128), BF16)
    total = shift_ref[3, :count, :]
    for tap in range(3):
        total += shift_ref[tap, pl.ds(3 - tap, count), :]
    grad_ref[:, :channels] = total.astype(BF16)
    for tap in range(3):
        head_ref[tap] = shift_ref[tap, :8, :]


def saved_shapes(blocks, heads):
    return (
        jax.ShapeDtypeStruct((blocks, heads, DK, DV), BF16),
        jax.ShapeDtypeStruct((blocks, heads, BLOCK, DV), BF16),
        jax.ShapeDtypeStruct((blocks, heads, BLOCK, BLOCK), BF16),
        jax.ShapeDtypeStruct((blocks, heads, BLOCK, DK), BF16),
        jax.ShapeDtypeStruct((blocks, heads, BLOCK, BLOCK), BF16),
        jax.ShapeDtypeStruct((blocks * BLOCK, heads * (2 * DK + DV)), F32),
    )


def saved_specs(shapes, per_step, index):
    return [
        pl.BlockSpec((per_step,) + shape.shape[1:], lambda i: (index(i), 0, 0, 0))
        for shape in shapes[:-1]
    ] + [pl.BlockSpec((per_step * BLOCK, shapes[-1].shape[1]), lambda i: (index(i), 0))]


def common_specs(step, channels, logits, index):
    return [
        pl.BlockSpec((16, channels), lambda i: (jnp.maximum(index(i) * (step // 16) - 1, 0), 0)),
        pl.BlockSpec((step, channels), lambda i: (index(i), 0)),
        pl.BlockSpec((8, channels), lambda i: (0, 0)),
        pl.BlockSpec((step, 128), lambda i: (index(i), 0)),
        pl.BlockSpec((8, step), lambda i: (0, index(i))),
        pl.BlockSpec((step, logits), lambda i: (index(i), 0)),
    ]


MIB = 1024 * 1024
VMEM_BYTES = 24 * MIB
SMALL_COST = pl.CostEstimate(flops=10**6, bytes_accessed=10**6, transcendentals=0)
ANYWHERE = pl.BlockSpec(memory_space=pl.ANY)
WHOLE = pl.BlockSpec(memory_space=pltpu.VMEM)
SCALAR = pl.BlockSpec(memory_space=pltpu.SMEM)


def params(limit=VMEM_BYTES):
    return pltpu.CompilerParams(dimension_semantics=("arbitrary",), vmem_limit_bytes=limit)


def forward_recurrence(proj, conv, cols, rows, logits, heads, tokens):
    count, channels = proj.shape
    step = BLOCK * FORWARD_STEP
    shapes = saved_shapes(count // BLOCK, heads)
    index = lambda i: i
    return pl.pallas_call(
        functools.partial(forward_kernel, heads),
        grid=(count // step,),
        in_specs=common_specs(step, channels, 128, index) + [ANYWHERE] * len(tokens),
        out_specs=[pl.BlockSpec((step, heads * DV), lambda i: (i, 0))] + saved_specs(shapes, FORWARD_STEP, index),
        out_shape=(jax.ShapeDtypeStruct((count, heads * DV), BF16),) + shapes,
        scratch_shapes=[
            pltpu.VMEM((step + 16, channels), F32),
            pltpu.VMEM((heads, DK, DV), F32),
        ],
        compiler_params=params(56 * MIB),
        cost_estimate=SMALL_COST,
        name="recurrence_forward",
    )(proj, proj, conv, cols, rows, logits, *tokens)


def backward_recurrence(proj, conv, cols, rows, logits, saved, out_grad, heads, tokens):
    count, channels = proj.shape
    step = BLOCK * BACKWARD_STEP
    last = count // step - 1
    index = lambda i: last - i
    return pl.pallas_call(
        functools.partial(backward_kernel, heads),
        grid=(count // step,),
        in_specs=common_specs(step, channels, 128, index)
        + saved_specs(saved, BACKWARD_STEP, index)
        + [pl.BlockSpec((step, heads * DV), lambda i: (index(i), 0))]
        + [ANYWHERE] * len(tokens),
        out_specs=[
            pl.BlockSpec((step, channels + 256), lambda i: (index(i), 0)),
            pl.BlockSpec((8, channels), lambda i: (0, 0)),
        ],
        out_shape=(
            jax.ShapeDtypeStruct((count, channels + 256), BF16),
            jax.ShapeDtypeStruct((8, channels), F32),
        ),
        scratch_shapes=[
            pltpu.VMEM((step + 16, channels), F32),
            pltpu.VMEM((4, step + 8, channels), F32),
            pltpu.VMEM((heads, DK, DV), F32),
            pltpu.VMEM((3, 8, channels), F32),
        ],
        compiler_params=params(56 * MIB),
        cost_estimate=SMALL_COST,
        name="recurrence_backward",
    )(proj, proj, conv, cols, rows, logits, *saved, out_grad, *tokens)


def project_kernel(
    channels, chunks, handed, rank_ref, gain_ref, w_ref, col_ref, *refs
):
    x_refs = refs[:chunks]
    normed_ref, gate_ref, proj_ref, logit_ref, all_ref = refs[chunks + handed : chunks + handed + 5]
    rows_ref = refs[-1]
    step = pl.program_id(0)
    count = x_refs[0].shape[0]

    @pl.when(step == 0)
    def _():
        width = w_ref.shape[0] * w_ref.shape[2]
        for k in range(w_ref.shape[1]):
            place = pl.ds(pl.multiple_of((rank_ref[0] ^ k) * width, width), width)
            all_ref[place, :] = w_ref[:, k].reshape(width, w_ref.shape[3])

    for k in range(chunks):

        @pl.when(step == k)
        def _():
            x = x_refs[k][...].astype(F32)
            scale = lax.rsqrt(jnp.mean(x * x, axis=1, keepdims=True) + 1e-05)
            normed = (x * scale * gain_ref[...]).astype(BF16)
            normed_ref[...] = normed
            total = mm(normed, all_ref[...])
            gates = gate_ref.shape[1]
            gate_ref[...] = total[:, :gates]
            logit = total[:, gates + channels :]
            high = logit.astype(BF16)
            place = slice(k * count, (k + 1) * count)
            rows_ref[place, : channels + 128] = total[:, gates:].astype(BF16)
            rows_ref[place, channels + 128 :] = (logit - high.astype(F32)).astype(BF16)

    @pl.when(step >= chunks)
    def _():
        order = lax.broadcasted_iota(jnp.int32, (proj_ref.shape[0], rows_ref.shape[0]), 1)
        picked = (col_ref[:, 4:5].astype(jnp.int32) == order).astype(F32)
        packed = mm(picked, rows_ref[...])
        proj_ref[...] = packed[:, :channels].astype(BF16)
        logit_ref[...] = packed[:, channels : channels + 128] + packed[:, channels + 128 :]


def project(rank, x_chunks, gain, weights, cols, channels, passed, tokens):
    count, width = x_chunks[0].shape
    total = count * len(x_chunks)
    gates = weights.shape[3] - channels - 128
    chunks = total // count
    block = total // 2
    first = lambda i: jnp.minimum(i, chunks - 1)
    later = lambda i: jnp.maximum(i - chunks, 0)
    outs = pl.pallas_call(
        functools.partial(project_kernel, channels, chunks, len(passed) + len(tokens)),
        grid=(chunks + total // block,),
        in_specs=[
            SCALAR,
            pl.BlockSpec((1, width), lambda i: (0, 0)),
            pl.BlockSpec(weights.shape, lambda i: (0, 0, 0, 0)),
            pl.BlockSpec((block, 128), lambda i: (later(i), 0)),
        ]
        + [pl.BlockSpec((count, width), lambda i: (0, 0))] * chunks
        + [ANYWHERE] * (len(passed) + len(tokens)),
        out_specs=[
            pl.BlockSpec((count, width), lambda i: (first(i), 0)),
            pl.BlockSpec((count, gates), lambda i: (first(i), 0)),
            pl.BlockSpec((block, channels), lambda i: (later(i), 0)),
            pl.BlockSpec((block, 128), lambda i: (later(i), 0)),
            pl.BlockSpec((width, weights.shape[3]), lambda i: (0, 0)),
        ]
        + [ANYWHERE] * len(passed),
        out_shape=[
            jax.ShapeDtypeStruct((total, width), BF16),
            jax.ShapeDtypeStruct((total, gates), F32),
            jax.ShapeDtypeStruct((total, channels), BF16),
            jax.ShapeDtypeStruct((total, 128), F32),
            jax.ShapeDtypeStruct((width, weights.shape[3]), BF16),
        ]
        + [jax.ShapeDtypeStruct(p.shape, p.dtype) for p in passed],
        input_output_aliases={4 + chunks + i: 5 + i for i in range(len(passed))},
        scratch_shapes=[pltpu.VMEM((total, channels + 256), BF16)],
        compiler_params=params(56 * MIB),
        cost_estimate=SMALL_COST,
        name="project",
    )(rank, gain, weights, cols, *x_chunks, *passed, *tokens)
    return outs[:5], outs[5:]


def gate_kernel(heads, count, first, o_ref, place_ref, gate_ref, gain_ref, *refs):
    chunks = place_ref.shape[1] // count
    dealt_ref, chunk_refs = refs[first], refs[first + 1 : first + 1 + chunks]
    for k, chunk_ref in enumerate(chunk_refs):
        order = lax.broadcasted_iota(jnp.int32, (count, o_ref.shape[0]), 0) + k * count
        picked = (place_ref[...].astype(jnp.int32) == order).astype(F32)
        rows = mm(picked, o_ref[...])
        place = pl.ds(k * count, count)
        dealt_ref[place, :] = rows.astype(BF16)
        for h in range(heads):
            lanes = slice(h * DV, (h + 1) * DV)
            value = rows[:, lanes]
            scale = lax.rsqrt(jnp.mean(value * value, axis=1, keepdims=True) + 1e-05)
            gated = value * scale * gain_ref[...] * silu(gate_ref[place, lanes])
            chunk_ref[:, lanes] = gated.astype(BF16)


def gate_rows(output, place, gate_logit, gain, count, heads, passed, tokens):
    total, cols = output.shape
    chunks = total // count
    others = len(passed) + len(tokens)
    outs = pl.pallas_call(
        functools.partial(gate_kernel, heads, count, others),
        in_specs=[WHOLE] * 4 + [ANYWHERE] * others,
        out_specs=[WHOLE] * (chunks + 1) + [ANYWHERE] * len(passed),
        out_shape=[jax.ShapeDtypeStruct((total, cols), BF16)]
        + [jax.ShapeDtypeStruct((count, cols), BF16)] * chunks
        + [jax.ShapeDtypeStruct(a.shape, a.dtype) for a in passed],
        input_output_aliases={4 + i: 1 + chunks + i for i in range(len(passed))},
        compiler_params=pltpu.CompilerParams(vmem_limit_bytes=VMEM_BYTES),
        cost_estimate=SMALL_COST,
        name="gate_rows",
    )(output, place, gate_logit, gain, *passed, *tokens)
    return outs[0], outs[1 : 1 + chunks], outs[1 + chunks :]


def ungate_kernel(heads, chunks, outs, dealt_ref, col_ref, gate_ref, gain_ref, *refs):
    grad_refs = refs[:chunks]
    gate_grad_ref, o_grad_ref, gain_grad_ref, rows_ref = *refs[outs : outs + 3], refs[-1]
    count = grad_refs[0].shape[0]
    total = dealt_ref.shape[0]
    sums = jnp.zeros((1, DV), F32)
    for k in range(chunks):
        place = pl.ds(k * count, count)
        for h in range(heads):
            lanes = slice(h * DV, (h + 1) * DV)
            value = dealt_ref[place, lanes].astype(F32)
            grad = grad_refs[k][:, lanes].astype(F32)
            logit = gate_ref[place, lanes]
            scale = lax.rsqrt(jnp.mean(value * value, axis=1, keepdims=True) + 1e-05)
            unit = value * scale
            gate = jax.nn.sigmoid(logit)
            slid = logit * gate
            sums += jnp.sum(grad * unit * slid, axis=0, keepdims=True)
            grad = grad * gain_ref[...]
            slope = gate * (1.0 + logit * (1.0 - gate))
            gate_grad_ref[place, lanes] = (grad * unit * slope).astype(BF16)
            grad = grad * slid
            inner = jnp.mean(grad * unit, axis=1, keepdims=True)
            rows_ref[place, lanes] = (scale * (grad - unit * inner)).astype(BF16)
    gain_grad_ref[...] = sums
    for k in range(chunks):
        place = pl.ds(k * count, count)
        order = lax.broadcasted_iota(jnp.int32, (count, total), 1)
        picked = (col_ref[place, 4:5].astype(jnp.int32) == order).astype(F32)
        o_grad_ref[place, :] = mm(picked, rows_ref[...]).astype(BF16)


def ungate_rows(dealt_rows, cols, gate_logit, gain, grads, heads, passed, tokens):
    total, width = dealt_rows.shape
    whole = pl.BlockSpec(memory_space=pltpu.VMEM)
    first = 4 + len(grads)
    outs = pl.pallas_call(
        functools.partial(ungate_kernel, heads, len(grads), len(grads) + len(passed) + len(tokens)),
        in_specs=[whole] * first + [ANYWHERE] * (len(passed) + len(tokens)),
        out_specs=[whole] * 3 + [ANYWHERE] * len(passed),
        out_shape=[
            jax.ShapeDtypeStruct((total, width), BF16),
            jax.ShapeDtypeStruct((total, width), BF16),
            jax.ShapeDtypeStruct((1, DV), F32),
        ]
        + [jax.ShapeDtypeStruct(p.shape, p.dtype) for p in passed],
        input_output_aliases={first + i: 3 + i for i in range(len(passed))},
        scratch_shapes=[pltpu.VMEM((total, width), BF16)],
        compiler_params=pltpu.CompilerParams(vmem_limit_bytes=VMEM_BYTES),
        cost_estimate=SMALL_COST,
        name="ungate_rows",
    )(dealt_rows, cols, gate_logit, gain, *grads, *passed, *tokens)
    return outs[:3], list(outs[3:])


def turned_sums(values):
    sums = jnp.sum(values, axis=1, keepdims=True)
    return jnp.broadcast_to(sums, (values.shape[0], 128)).T[:1]


def put_rows(total, split, core_ref, refs):
    total = total.astype(BF16)
    if split is None:
        refs[0][...] = total
        return
    halves = total.reshape(*split, 2, -1, total.shape[1])
    for core in range(2):

        @pl.when(core_ref[0] == core)
        def _():
            refs[0][...] = halves[:, :, core]
            refs[1][...] = halves[:, :, 1 - core]


def row_outputs(split, width, cols, tile):
    if split is None:
        shape, block = (width, cols), (width, tile)
        spec = pl.BlockSpec(block, lambda i: (0, i))
        return [spec], [jax.ShapeDtypeStruct(shape, BF16)]
    shape = (*split, width // (2 * split[0] * split[1]))
    spec = pl.BlockSpec((*shape, tile), lambda i: (0, 0, 0, i))
    return [spec] * 2, [jax.ShapeDtypeStruct((*shape, cols), BF16)] * 2


def unpack_kernel(split, heads, words_ref, grad_ref, gates_ref, place_ref, normed_ref, w_ref, conv_ref, gain_ref, mid_ref, o_ref, first_sums_ref, *refs):
    count = 2 if split else 1
    dealt_ref, sums_ref = refs[-4 - count], refs[-3 - count]
    row_refs, small_ref, picked_ref = refs[-2 - count : -2], refs[-2], refs[-1]
    step = pl.program_id(0)
    total = grad_ref.shape[0]
    gates = gates_ref.shape[1]
    tile = grad_ref.shape[1] // 2

    @pl.when(step == 0)
    def _():
        part = 256
        for k in range(total // part):
            order = lax.broadcasted_iota(jnp.int32, (part, total), 0) + k * part
            picked = (place_ref[...].astype(jnp.int32) == order).astype(F32)
            picked_ref[k * part : (k + 1) * part, :] = picked.astype(BF16)
        dealt_ref[:, :gates] = gates_ref[...]
        dealt_ref[:, gates : gates + tile] = mm(picked_ref[...], grad_ref[:, :tile]).astype(BF16)
        share = mm(normed_ref[...], dealt_ref[:, gates : gates + tile])
        weights = w_ref[:, gates : gates + tile].astype(F32)
        sums_ref[...] = first_sums_ref[...] + turned_sums(share * weights)
        put_rows(share, split, words_ref, row_refs)

    @pl.when(step == 1)
    def _():
        dealt_ref[:, gates + tile :] = mm(picked_ref[...], grad_ref[:, tile:]).astype(BF16)
        share = mm(normed_ref[...], dealt_ref[:, gates + tile :])
        used = w_ref.shape[1] - gates - tile
        weights = w_ref[:, gates + tile :].astype(F32)
        sums_ref[...] += turned_sums(share[:, :used] * weights)
        if split:
            devices, rows = 2 * split[0] * split[1], share.shape[0] // (2 * split[0] * split[1])
            gin = sums_ref[...] / gain_ref[...]
            small_ref[...] = jnp.zeros_like(small_ref)
            gin = jnp.concatenate([gin[:, j * 128 : (j + 1) * 128] for j in range(8)], 0)
            mid = jnp.concatenate([mid_ref[:, j * 128 : (j + 1) * 128] for j in range(8)], 0)
            for d in range(devices):
                small_ref[d * rows + 4 : d * rows + 5, :] = o_ref[:, :128]
                small_ref[d * rows + 5 : d * rows + 6, :] = o_ref[:, 128:]
                small_ref[d * rows + 8 : d * rows + 16, :] = mid
                small_ref[d * rows + 16 : d * rows + 24, :] = gin
            rank = words_ref[2]
            keys = heads * DK // 128
            vals = heads * DV // 128
            owners = [rank * keys + j for j in range(keys)]
            owners += [HEAD_COUNT * DK // 128 + rank * keys + j for j in range(keys)]
            owners += [2 * HEAD_COUNT * DK // 128 + rank * vals + j for j in range(vals)]
            for j, owner in enumerate(owners):
                place = pl.ds(pl.multiple_of(owner * rows, rows), 8)
                old = small_ref[place, :]
                taps = lax.broadcasted_iota(jnp.int32, (8, 128), 0) < 4
                small_ref[place, :] = jnp.where(taps, conv_ref[:, j * 128 : (j + 1) * 128], old)
            share = jnp.concatenate([share[:, :-128], small_ref[...]], 1)
        put_rows(share, split, words_ref, row_refs)


def unpack(split, words, grad, gate_grad, place, normed, weights, g_conv, gain, g_mid, g_o, sums, heads, tokens):
    total = grad.shape[0]
    cols = grad.shape[1] + gate_grad.shape[1]
    width = normed.shape[0]
    operands = (grad, gate_grad, place, normed, weights, g_conv, gain, g_mid, g_o, sums)
    specs, shapes = row_outputs(split, width, grad.shape[1], grad.shape[1] // 2)
    return pl.pallas_call(
        functools.partial(unpack_kernel, split, heads),
        grid=(2,),
        in_specs=[SCALAR]
        + [pl.BlockSpec(a.shape, lambda i: (0, 0)) for a in operands]
        + [ANYWHERE] * len(tokens),
        out_specs=[
            pl.BlockSpec((total, cols), lambda i: (0, 0)),
            pl.BlockSpec((1, width), lambda i: (0, 0)),
        ]
        + specs,
        out_shape=[
            jax.ShapeDtypeStruct((total, cols), BF16),
            jax.ShapeDtypeStruct((1, width), F32),
        ]
        + shapes,
        scratch_shapes=[pltpu.VMEM((width, 128), F32), pltpu.VMEM((total, total), BF16)],
        compiler_params=params(),
        cost_estimate=SMALL_COST,
        name="unpack",
    )(words, *operands, *tokens)


def unproject_kernel(chunks, first, grad_ref, w_ref, *refs):
    part_refs, turned_ref = refs[first : first + chunks], refs[-1]
    step = pl.program_id(0)

    @pl.when(step == 0)
    def _():
        turned_ref[...] = w_ref[...].T

    part = mm(grad_ref[:, : turned_ref.shape[0]], turned_ref[...])
    for k in range(chunks):

        @pl.when(step == k)
        def _():
            part_refs[k][...] = part.astype(BF16)


def unproject(grad, weights, count, passed, tokens):
    total, cols = grad.shape
    width = weights.shape[0]
    chunks = total // count
    outs = pl.pallas_call(
        functools.partial(unproject_kernel, chunks, len(passed) + len(tokens)),
        grid=(chunks,),
        in_specs=[
            pl.BlockSpec((count, cols), lambda i: (i, 0)),
            pl.BlockSpec(weights.shape, lambda i: (0, 0)),
        ]
        + [ANYWHERE] * (len(passed) + len(tokens)),
        out_specs=[pl.BlockSpec((count, width), lambda i: (0, 0))] * chunks
        + [ANYWHERE] * len(passed),
        out_shape=[jax.ShapeDtypeStruct((count, width), BF16)] * chunks
        + [jax.ShapeDtypeStruct(p.shape, p.dtype) for p in passed],
        input_output_aliases={2 + i: chunks + i for i in range(len(passed))},
        scratch_shapes=[pltpu.VMEM(weights.shape[::-1], BF16)],
        compiler_params=params(56 * MIB),
        cost_estimate=SMALL_COST,
        name="unproject",
    )(grad, weights, *passed, *tokens)
    return list(outs[:chunks]), list(outs[chunks:])


def hand_kernel(*refs):
    refs[-1][...] = jnp.zeros_like(refs[-1])


def handed(passed, tokens):
    outs = pl.pallas_call(
        hand_kernel,
        in_specs=[ANYWHERE] * (len(passed) + len(tokens)),
        out_specs=[ANYWHERE] * len(passed) + [WHOLE],
        out_shape=[jax.ShapeDtypeStruct(p.shape, p.dtype) for p in passed]
        + [jax.ShapeDtypeStruct((8, 128), F32)],
        input_output_aliases={i: i for i in range(len(passed))},
        cost_estimate=SMALL_COST,
        name="handed",
    )(*passed, *tokens)
    return outs[:-1]


def weight_grad_kernel(split, tiles, sums, words_ref, *refs):
    row_refs = refs[-2:] if split else refs[-1:]
    step = pl.program_id(0)
    for tile, pairs in enumerate(tiles):

        @pl.when(step == tile)
        def _():
            total = mm_tn(refs[pairs[0][0]][...], refs[pairs[0][1]][...])
            for left, right in pairs[1:]:
                total += mm_tn(refs[left][...], refs[right][...])
            put_rows(total, split, words_ref, row_refs)
            if sums is not None and tile == 0:
                refs[sums[1]][...] = turned_sums(total * refs[sums[0]][...].astype(F32))


def weight_grad(split, words, groups, tile, tokens, weights=None, limit=VMEM_BYTES):
    width = groups[0][0][0].shape[1]
    operands, specs, tiles = [words], [SCALAR], []
    first = 0
    for lefts, rights in groups:
        count = rights[0].shape[1] // tile
        base = len(operands) - 1
        for left in lefts:
            operands.append(left)
            specs.append(pl.BlockSpec((rights[0].shape[0], width), lambda i: (0, 0)))
        for right in rights:
            operands.append(right)
            specs.append(
                pl.BlockSpec(
                    (right.shape[0], tile),
                    lambda i, first=first, count=count: (0, jnp.clip(i - first, 0, count - 1)),
                )
            )
        tiles += [[(base + k, base + len(lefts) + k) for k in range(len(lefts))]] * count
        first += count
    sums = None
    out_specs, out_shapes = row_outputs(split, width, first * tile, tile)
    if weights is not None:
        operands.append(weights)
        specs.append(pl.BlockSpec((width, tile), lambda i: (0, 0)))
        sums = (len(operands) - 2, len(operands) - 1 + len(tokens))
        out_specs = [pl.BlockSpec((1, width), lambda i: (0, 0))] + out_specs
        out_shapes = [jax.ShapeDtypeStruct((1, width), F32)] + out_shapes
    return pl.pallas_call(
        functools.partial(weight_grad_kernel, split, tiles, sums),
        grid=(first,),
        in_specs=specs + [ANYWHERE] * len(tokens),
        out_specs=out_specs,
        out_shape=out_shapes,
        compiler_params=params(limit),
        cost_estimate=SMALL_COST,
        name="weight_grad",
    )(*operands, *tokens)


def join_kernel(pairs, *refs):
    for chip in range(refs[0].shape[1]):
        place = 0
        for k in range(pairs):
            keep_ref, got_ref = refs[2 * k], refs[2 * k + 1]
            width = keep_ref.shape[3]
            total = keep_ref[:, chip].astype(F32) + got_ref[:, chip].astype(F32)
            refs[-1][chip, :, :, place : place + width] = total.astype(BF16)
            place += width


def joined(pairs, tokens):
    seq_count, chips, rows, _ = pairs[0][0].shape
    cols = sum(keep.shape[3] for keep, _ in pairs)
    return pl.pallas_call(
        functools.partial(join_kernel, len(pairs)),
        in_specs=[WHOLE] * (2 * len(pairs)) + [ANYWHERE] * len(tokens),
        out_specs=WHOLE,
        out_shape=jax.ShapeDtypeStruct((chips, seq_count, rows, cols), BF16),
        compiler_params=pltpu.CompilerParams(vmem_limit_bytes=VMEM_BYTES),
        cost_estimate=SMALL_COST,
        name="joined",
    )(*[a for pair in pairs for a in pair], *tokens)


def layer_kernel(chunks, w_ref, low_ref, *refs):
    weights = w_ref[...].T
    count = low_ref.shape[0]
    refs[chunks][...] = mm(refs[0][...], weights).astype(BF16)
    for k in range(1, chunks):
        refs[chunks + k][:count, :] = low_ref[...]
        refs[chunks + k][count:, :] = mm(refs[k][...], weights).astype(BF16)


def layer_products(hiddens, weights, low):
    count, wide = hiddens[0].shape
    width = weights.shape[0]
    chunks = len(hiddens)
    rows = [count] + [2 * count] * (chunks - 1)
    return pl.pallas_call(
        functools.partial(layer_kernel, chunks),
        grid=(1,),
        in_specs=[
            pl.BlockSpec((width, wide), lambda i: (0, weights.shape[1] // wide - 1)),
            pl.BlockSpec((count, width), lambda i: (0, 0)),
        ]
        + [pl.BlockSpec((count, wide), lambda i: (0, 0))] * chunks,
        out_specs=[pl.BlockSpec((r, width), lambda i: (0, 0)) for r in rows],
        out_shape=[jax.ShapeDtypeStruct((r, width), BF16) for r in rows],
        compiler_params=params(),
        cost_estimate=SMALL_COST,
        name="layer_products",
    )(weights, low, *hiddens)


def position_kernel(heads, chunks, words_ref, lengths_ref, order_ref, decay_ref, *refs):
    col_ref, row_ref, place_ref, cum_ref = refs[-4:]
    total = order_ref.shape[1]
    count = total // chunks
    blocks, near = total // BLOCK, count // BLOCK
    rank = words_ref[2]
    ends = [lengths_ref[0]]
    for e in range(1, lengths_ref.shape[0]):
        ends.append(ends[-1] + lengths_ref[e])

    def segment(position):
        found = jnp.zeros(position.shape, jnp.int32)
        for end in ends:
            found += (position >= end).astype(jnp.int32)
        return jnp.where(position < 0, -1, found)

    for k in range(chunks):
        for h in range(heads):
            for b in range(near):
                value = jnp.zeros((1, BLOCK), F32)
                for part in range(3):
                    row = (part * heads + h) * near + b
                    value += decay_ref[k, row : row + 1, :].astype(F32)
                cum_ref[pl.ds(h * blocks + (rank ^ k) * near + b, 1), :] = value
    rows, cols = masks()
    upper = (rows <= cols).astype(F32)
    cums = jnp.dot(
        cum_ref[...], upper, precision=lax.Precision.HIGHEST, preferred_element_type=F32
    )
    order = order_ref[...]
    chunk = jnp.zeros_like(order)
    for k in range(1, chunks):
        chunk += (order >= k * count).astype(jnp.int32)
    place = (order + ((chunk ^ rank) - chunk) * count).astype(F32)
    place_ref[...] = place
    row_ref[...] = jnp.zeros_like(row_ref)
    lane = lax.broadcasted_iota(jnp.int32, (1, BLOCK), 1)
    for b in range(blocks):
        position = lane + b * BLOCK
        here = segment(position)
        low, high = jnp.full((1, BLOCK), b * BLOCK - 1), jnp.full((1, BLOCK), b * BLOCK + BLOCK - 1)
        keep_in = (here == segment(low)).astype(F32)
        keep_out = (here == segment(high)).astype(F32)
        found = [(segment(position - 3 + tap) == here).astype(F32) for tap in range(3)]
        found += [here.astype(F32), place[:, b * BLOCK : (b + 1) * BLOCK]]
        mine = [cums[h * blocks + b : h * blocks + b + 1, :] for h in range(heads)]
        found += mine
        found += [jnp.exp(c) * keep_in for c in mine]
        found += [jnp.exp(c[:, BLOCK - 1 :] - c) * keep_out for c in mine]
        found.append(jnp.zeros((128 - len(found), BLOCK), F32))
        col_ref[b * BLOCK : (b + 1) * BLOCK, :] = jnp.concatenate(found, 0).T
        for h in range(heads):
            row_ref[h : h + 1, b * BLOCK : (b + 1) * BLOCK] = mine[h]
        row_ref[heads : heads + 1, b * BLOCK : (b + 1) * BLOCK] = here.astype(F32)


def positions(words, lengths, order, decays, heads, tokens):
    total = order.shape[1]
    return pl.pallas_call(
        functools.partial(position_kernel, heads, decays.shape[0]),
        in_specs=[SCALAR, SCALAR, WHOLE, WHOLE] + [ANYWHERE] * len(tokens),
        out_specs=[WHOLE] * 3,
        out_shape=(
            jax.ShapeDtypeStruct((total, 128), F32),
            jax.ShapeDtypeStruct((8, total), F32),
            jax.ShapeDtypeStruct((1, total), F32),
        ),
        scratch_shapes=[pltpu.VMEM((heads * total // BLOCK, BLOCK), F32)],
        cost_estimate=SMALL_COST,
        compiler_params=pltpu.CompilerParams(vmem_limit_bytes=VMEM_BYTES),
        name="positions",
    )(words, lengths, order, decays, *tokens)


def out_rows_kernel(others, words_ref, mine_ref, normed_ref, *refs):
    out_ref, turned_ref = refs[-2:]
    core, chip = words_ref[0], words_ref[1]
    if others:
        chunks, chips, rows, _ = mine_ref.shape
        for k in range(chunks):
            for j in range(chips):
                device = k * 2 * chips + 2 * (chip ^ j)
                for ref, side in ((mine_ref, core), (refs[0], 1 - core)):
                    place = pl.ds(pl.multiple_of((device + side) * rows, rows), rows)
                    out_ref[place, :] = ref[k, j]
    else:
        out_ref[...] = mine_ref[...]
    turned_ref[...] = normed_ref[...].T


def out_rows(words, mine, others, normed, rows, tokens):
    return pl.pallas_call(
        functools.partial(out_rows_kernel, len(others)),
        in_specs=[SCALAR] + [WHOLE] * (2 + len(others)) + [ANYWHERE] * len(tokens),
        out_specs=[WHOLE] * 2,
        out_shape=(
            jax.ShapeDtypeStruct((rows, mine.shape[-1]), BF16),
            jax.ShapeDtypeStruct(normed.shape[::-1], BF16),
        ),
        compiler_params=pltpu.CompilerParams(vmem_limit_bytes=VMEM_BYTES),
        cost_estimate=SMALL_COST,
        name="out_rows",
    )(words, mine, normed, *others, *tokens)


def ffn_rows_kernel(words_ref, ffn_ref, *refs):
    width = ffn_ref.shape[0] * ffn_ref.shape[2]
    for k in range(ffn_ref.shape[1]):
        place = pl.ds(pl.multiple_of((words_ref[2] ^ k) * width, width), width)
        refs[-1][place, :] = ffn_ref[:, k].reshape(width, ffn_ref.shape[3])


def ffn_rows(words, ffn, tokens):
    return pl.pallas_call(
        ffn_rows_kernel,
        in_specs=[SCALAR, WHOLE] + [ANYWHERE] * len(tokens),
        out_specs=WHOLE,
        out_shape=jax.ShapeDtypeStruct((ffn.shape[0] * ffn.shape[1] * ffn.shape[2], ffn.shape[3]), BF16),
        compiler_params=pltpu.CompilerParams(vmem_limit_bytes=VMEM_BYTES),
        cost_estimate=SMALL_COST,
        name="ffn_rows",
    )(words, ffn, *tokens)


def out_project_kernel(chunks, rank_ref, x_ref, gain_ref, w_ref, *refs):
    residual_ref, mid_ref, all_ref = refs[-3:]
    rank = rank_ref[0]
    for k in range(chunks):
        width = refs[k].shape[1]
        all_ref[:, pl.ds(pl.multiple_of((rank ^ k) * width, width), width)] = refs[k][...]
    residual = x_ref[...].astype(F32) + mm_nt(all_ref[...], w_ref[...])
    residual_ref[...] = residual
    scale = lax.rsqrt(jnp.mean(residual * residual, axis=1, keepdims=True) + 1e-05)
    mid_ref[...] = (residual * scale * gain_ref[...]).astype(BF16)


def out_project(rank, x, gain, attn, weights):
    count, width = x.shape
    return pl.pallas_call(
        functools.partial(out_project_kernel, len(attn)),
        in_specs=[SCALAR] + [WHOLE] * (3 + len(attn)),
        out_specs=[WHOLE] * 2,
        out_shape=(
            jax.ShapeDtypeStruct((count, width), F32),
            jax.ShapeDtypeStruct((count, width), BF16),
        ),
        scratch_shapes=[pltpu.VMEM((count, weights.shape[1]), BF16)],
        compiler_params=pltpu.CompilerParams(vmem_limit_bytes=VMEM_BYTES),
        cost_estimate=SMALL_COST,
        name="out_project",
    )(rank, x, gain, weights, *attn)


def mid_back_kernel(chunks, handed, rank_ref, grad_ref, residual_ref, gain_ref, w_ref, *refs):
    parts = refs[:chunks]
    outs, all_ref = refs[chunks + handed :], refs[-1]
    res_grad_ref, low_ref, gain_grad_ref, chunk_refs = outs[0], outs[1], outs[2], outs[3 : 3 + chunks]
    rank = rank_ref[0]
    mid_grad = parts[0][...].astype(F32)
    for k in range(1, chunks):
        mid_grad += parts[k][...].astype(F32)
    residual = residual_ref[...]
    scale = lax.rsqrt(jnp.mean(residual * residual, axis=1, keepdims=True) + 1e-05)
    unit = residual * scale
    gain_grad_ref[...] = jnp.sum(mid_grad * unit, axis=0, keepdims=True)
    scaled = mid_grad * gain_ref[...]
    inner = jnp.mean(scaled * unit, axis=1, keepdims=True)
    res_grad = grad_ref[...].astype(F32) + scale * (scaled - unit * inner)
    res_grad_ref[...] = res_grad
    low = res_grad.astype(BF16)
    low_ref[...] = low
    all_ref[...] = mm(low, w_ref[...]).astype(BF16)
    for k in range(chunks):
        width = chunk_refs[k].shape[1]
        chunk_refs[k][...] = all_ref[:, pl.ds(pl.multiple_of((rank ^ k) * width, width), width)]


def mid_back(rank, grad, residual, gain, parts, weights, passed):
    count, width = residual.shape
    chunks = len(parts)
    wide = weights.shape[1]
    first = 5 + chunks
    outs = pl.pallas_call(
        functools.partial(mid_back_kernel, chunks, len(passed)),
        in_specs=[SCALAR] + [WHOLE] * (first - 1) + [ANYWHERE] * len(passed),
        out_specs=[WHOLE] * (3 + chunks) + [ANYWHERE] * len(passed),
        out_shape=[
            jax.ShapeDtypeStruct((count, width), F32),
            jax.ShapeDtypeStruct((count, width), BF16),
            jax.ShapeDtypeStruct((1, width), F32),
        ]
        + [jax.ShapeDtypeStruct((count, wide // chunks), BF16)] * chunks
        + [jax.ShapeDtypeStruct(p.shape, p.dtype) for p in passed],
        input_output_aliases={first + i: 3 + chunks + i for i in range(len(passed))},
        scratch_shapes=[pltpu.VMEM((count, wide), BF16)],
        compiler_params=pltpu.CompilerParams(vmem_limit_bytes=VMEM_BYTES),
        cost_estimate=SMALL_COST,
        name="mid_back",
    )(rank, grad, residual, gain, weights, *parts, *passed)
    return (*outs[:3], outs[3 : 3 + chunks], list(outs[3 + chunks :]))


def in_back_kernel(chunks, x_ref, res_grad_ref, gain_ref, *refs):
    x = x_ref[...].astype(F32)
    grad = refs[0][...].astype(F32)
    for k in range(1, chunks):
        grad += refs[k][...].astype(F32)
    scale = lax.rsqrt(jnp.mean(x * x, axis=1, keepdims=True) + 1e-05)
    unit = x * scale
    scaled = grad * gain_ref[...]
    inner = jnp.mean(scaled * unit, axis=1, keepdims=True)
    refs[-1][...] = (res_grad_ref[...] + scale * (scaled - unit * inner)).astype(BF16)


def in_back(x, res_grad, gain, parts, tokens):
    return pl.pallas_call(
        functools.partial(in_back_kernel, len(parts)),
        in_specs=[WHOLE] * (3 + len(parts)) + [ANYWHERE] * len(tokens),
        out_specs=WHOLE,
        out_shape=jax.ShapeDtypeStruct(x.shape, BF16),
        compiler_params=pltpu.CompilerParams(vmem_limit_bytes=VMEM_BYTES),
        cost_estimate=SMALL_COST,
        name="in_back",
    )(x, res_grad, gain, *parts, *tokens)


def swapped(value, axis, mask):
    devices = lax.axis_size(axis)
    return lax.ppermute(value, axis, [(i, i ^ mask) for i in range(devices)])


def pinned(value, other):
    return value + 0 * other[:1, :1].astype(value.dtype)


def spread(value):
    return [value] + [swapped(value, "seq", k) for k in range(1, lax.axis_size("seq"))]


def returned(chunks):
    return [chunks[0]] + [swapped(chunks[k], "seq", k) for k in range(1, len(chunks))]


class RowSum:
    def __init__(self, outs):
        self.outs = list(outs)

    def pair(self):
        if len(self.outs) == 2:
            self.got = swapped(self.outs[1], "mp", 1)

    def join(self, *tokens):
        seq_count, mp_count = lax.axis_size("seq"), lax.axis_size("mp")
        if len(self.outs) == 1:
            (grad,) = self.outs
            cols = grad.shape[1]
            parts = grad.astype(F32).reshape(seq_count, mp_count, -1, cols).transpose(1, 0, 2, 3)
            own = lax.psum_scatter(parts.reshape(-1, cols), "mp", scatter_dimension=0, tiled=True)
            self.half = grad
            self.parts = own.reshape(1, seq_count, -1, cols)
            return
        self.half = joined([(self.outs[0], self.got)], tokens)
        self.between()

    def between(self):
        mp_count = lax.axis_size("mp")
        groups = [list(range(core, mp_count, 2)) for core in range(2)]
        self.parts = lax.all_to_all(self.half, "mp", 0, 0, axis_index_groups=groups, tiled=True)

    def beside(self, other):
        if len(self.outs) == 1:
            both = RowSum([jnp.concatenate([self.outs[0], other.outs[0]], 1)])
            both.join()
            return both
        both = RowSum([])
        both.half = joined([(s.outs[0], s.got) for s in (self, other)], [])
        both.between()
        return both


def row_sums(sums, tokens):
    groups = [part.parts for part in sums]
    shape = groups[0].shape[1:3]
    cols = [group.shape[3] for group in groups]

    def kernel(*refs):
        place = 0
        for ref, width in zip(refs, cols):
            total = ref[0].astype(F32)
            for k in range(1, ref.shape[0]):
                total += ref[k].astype(F32)
            refs[-1][:, :, place : place + width] = total.astype(BF16)
            place = place + width

    return pl.pallas_call(
        kernel,
        in_specs=[WHOLE] * len(groups) + [ANYWHERE] * len(tokens),
        out_specs=WHOLE,
        out_shape=jax.ShapeDtypeStruct(shape + (sum(cols),), BF16),
        cost_estimate=SMALL_COST,
        compiler_params=pltpu.CompilerParams(vmem_limit_bytes=VMEM_BYTES),
        name="row_sums",
    )(*groups, *tokens)


def finish_kernel(heads, wide, half, rows, pieces_ref, *refs):
    qkv_ref, gate_ref, beta_ref, conv_ref, out_ref, gu_ref, down_ref, small_ref = refs
    chunks = pieces_ref.shape[0]
    keys, vals = heads * DK, heads * DV
    ffn, mix = 0, 3 * wide
    gate_first, first, out_first = mix, mix + vals, pieces_ref.shape[2] - vals

    def piece(j, start, width):
        return pieces_ref[j, :, start : start + width].astype(F32)

    for j in range(chunks):
        gate_ref[:, j * vals : (j + 1) * vals] = piece(j, gate_first, vals)
        qkv_ref[:, j * keys : (j + 1) * keys] = piece(j, first, keys)
        place = chunks * keys + j * keys
        qkv_ref[:, place : place + keys] = piece(j, first + keys, keys)
        place = 2 * chunks * keys + j * vals
        qkv_ref[:, place : place + vals] = piece(j, first + 2 * keys, vals)
        out_ref[:, j * vals : (j + 1) * vals] = piece(j, out_first, vals)
        beta = piece(j, first + 2 * keys + vals, 128)
        beta_ref[:, j * heads : (j + 1) * heads] = beta[:, :heads]
    small = piece(0, out_first - 128, 128)
    for j in range(1, chunks):
        small += piece(j, out_first - 128, 128)
    small_ref[...] = small
    conv_ref[...] = small[: conv_ref.shape[0]]
    for part in range(3):
        whole = jnp.concatenate(
            [piece(j, ffn + part * wide, wide)[:, :half] for j in range(chunks)], 1
        )
        if part < 2:
            gu_ref[:, part * chunks * half : (part + 1) * chunks * half] = whole
        else:
            down_ref[...] = whole


def finish(pieces, heads, wide, half, taps):
    chunks, rows, _ = pieces.shape
    keys, vals = HEAD_COUNT * DK, HEAD_COUNT * DV
    ffn = chunks * half
    shapes = [(rows, 2 * keys + vals), (rows, vals), (rows, HEAD_COUNT), (taps, 128)]
    shapes += [(rows, vals), (rows, 2 * ffn), (rows, ffn), (rows, 128)]
    return pl.pallas_call(
        functools.partial(finish_kernel, heads, wide, half, rows),
        in_specs=[WHOLE],
        out_specs=[WHOLE] * len(shapes),
        out_shape=[jax.ShapeDtypeStruct(shape, F32) for shape in shapes],
        compiler_params=pltpu.CompilerParams(vmem_limit_bytes=VMEM_BYTES),
        cost_estimate=SMALL_COST,
        name="finish",
    )(pieces)


def dealt(own):
    return lax.all_to_all(own, "seq", 0, 0, tiled=True)


def left_product(left, right):
    return lax.dot_general(
        left, right, (((0,), (0,)), ((), ())), preferred_element_type=jnp.float32
    )


def right_product(left, right):
    return lax.dot_general(
        left, right, (((1,), (1,)), ((), ())), preferred_element_type=jnp.float32
    )


def dot(left, right):
    return jnp.dot(left, right, preferred_element_type=jnp.float32)


def silu_slope(values):
    gate = jax.nn.sigmoid(values)
    return gate * (1.0 + values * (1.0 - gate))


def split_three(values):
    high = values.astype(BF16)
    rest = values - high.astype(F32)
    middle = rest.astype(BF16)
    return jnp.stack([high, middle, (rest - middle.astype(F32)).astype(BF16)])


def body(
    layer_in,
    out_grad,
    seq_lengths,
    dealing,
    log_decay,
    w_qkv,
    w_out_gate,
    w_beta,
    conv_w,
    gain_in,
    gain_o,
    w_out,
    gain_mid,
    w_gate_up,
    w_down,
):
    seq_count, mp_count = lax.axis_size("seq"), lax.axis_size("mp")
    rank, place_mp = lax.axis_index("seq"), lax.axis_index("mp")
    count = layer_in.shape[1]
    rows = w_qkv.shape[0]
    heads = HEAD_COUNT // seq_count
    key_cols, val_cols = heads * DK, heads * DV
    half = w_down.shape[0] // seq_count
    wide = -(-half // 256) * 256
    taps = conv_w.shape[1]
    total = dealing.shape[1]
    devices = seq_count * mp_count
    channels = 2 * key_cols + val_cols
    all_keys, ffn = HEAD_COUNT * DK, w_down.shape[0]
    split = (seq_count, mp_count // 2) if mp_count <= 8 else None
    words = jnp.stack([place_mp % 2, place_mp // 2, rank]).astype(jnp.int32)
    rank_word = rank.astype(jnp.int32).reshape(1)

    small = jnp.concatenate([conv_w.T.reshape(-1), gain_in, gain_mid, gain_o])
    small_count = small.shape[0]
    spare = 128 - heads
    filler = jnp.concatenate([small, jnp.zeros((rows * spare - small_count,), BF16)])
    filler = filler.reshape(rows, spare)
    wide_filler = jnp.zeros((rows, wide - half), BF16)
    turned_down = w_down.T
    decay_lanes = -(-3 * heads * count // (128 * rows)) * 128
    decays = split_three(log_decay[0].T)
    mix_cols = channels + 128 + val_cols
    pieces, ffn_pieces = [], []
    for j in range(seq_count):
        own_decay = decays[:, j * heads : (j + 1) * heads].reshape(-1)
        own_decay = jnp.concatenate(
            [own_decay, jnp.zeros((rows * decay_lanes - own_decay.shape[0],), BF16)]
        )
        pieces.append(
            jnp.concatenate(
                [
                    w_out_gate[:, j * val_cols : (j + 1) * val_cols],
                    w_qkv[:, j * key_cols : (j + 1) * key_cols],
                    w_qkv[:, all_keys + j * key_cols : all_keys + (j + 1) * key_cols],
                    w_qkv[:, 2 * all_keys + j * val_cols : 2 * all_keys + (j + 1) * val_cols],
                    w_beta[:, j * heads : (j + 1) * heads],
                    filler,
                ],
                1,
            )
        )
        ffn_pieces.append(
            jnp.concatenate(
                [
                    w_gate_up[:, j * half : (j + 1) * half],
                    wide_filler,
                    w_gate_up[:, ffn + j * half : ffn + (j + 1) * half],
                    wide_filler,
                    turned_down[:, j * half : (j + 1) * half],
                    wide_filler,
                    own_decay.reshape(rows, decay_lanes),
                ],
                1,
            )
        )
    def near(arrays):
        arrays = jnp.stack(arrays)
        return jnp.stack(
            returned(
                [lax.dynamic_index_in_dim(arrays, rank ^ k, 0, keepdims=False) for k in range(seq_count)]
            )
        )

    pieces, ffn_pieces = near(pieces), near(ffn_pieces)
    gathered = lax.all_gather(pieces, "mp", axis=0, tiled=False)
    late = pieces[1, :1, :1] + jnp.sum(ffn_pieces[1:, :1, :1], axis=0)
    chunks_in = spread(layer_in[0] + 0 * late)

    relative = rank ^ jnp.arange(seq_count)
    smalls = gathered[:, :, :, mix_cols - spare :].transpose(1, 0, 2, 3)
    smalls = jnp.take(smalls, relative, axis=0).reshape(devices, -1)[:, :small_count]
    own_taps = conv_w.shape[0] * taps
    full_conv = smalls[:, :own_taps].reshape(-1, taps, conv_w.shape[0]).transpose(1, 0, 2)
    full_conv = full_conv.reshape(taps, -1).astype(F32)
    conv = jnp.concatenate(
        [
            lax.dynamic_slice_in_dim(full_conv, rank * key_cols, key_cols, 1),
            lax.dynamic_slice_in_dim(full_conv, all_keys + rank * key_cols, key_cols, 1),
            lax.dynamic_slice_in_dim(full_conv, 2 * all_keys + rank * val_cols, val_cols, 1),
        ],
        1,
    )
    conv = jnp.concatenate([conv, jnp.zeros((8 - taps, channels), F32)], 0)
    gains = smalls[:, own_taps:].astype(F32)
    full_gin = gains[:, :rows].reshape(1, -1)
    full_gmid = gains[:, rows : 2 * rows].reshape(1, -1)
    full_go = gains[:, 2 * rows :].reshape(1, -1)

    out_turned = w_out.T
    out_near = []
    if split:
        out_near = [out_turned] + [swapped(out_turned, "mp", 2 * j) for j in range(1, mp_count // 2)]

    out_copies = []
    if split:
        out_copies = [
            jnp.broadcast_to(jnp.stack(out_near), (seq_count, mp_count // 2, *out_turned.shape))
        ]

    decays = ffn_pieces[:, :, 3 * wide :].reshape(seq_count, -1)[:, : 3 * heads * count]
    col_info, row_info, place_row = positions(
        words, seq_lengths[0], dealing, decays.reshape(seq_count, -1, BLOCK), heads, out_copies
    )

    passed = [ffn_pieces[:, :, : 3 * wide], out_grad[0] + 0 * pieces[1, :1, :1]] + out_copies
    passed = handed(passed, chunks_in[1:] + [row_info])
    ffn_all = lax.all_gather(passed[0], "mp", axis=0, tiled=False)
    chunks_grad = spread(passed[1])
    out_mine = [lax.all_to_all(passed[2], "seq", 0, 0, tiled=True)] if split else []
    (normed, gate_logit, proj, logit_parts, mix), _ = project(
        rank_word, chunks_in, full_gin, gathered, col_info, channels,
        [], [conv, full_go, full_gmid],
    )
    outs = forward_recurrence(proj, conv, col_info, row_info, logit_parts, heads, [])
    dealt_rows, attn, out_mine = gate_rows(
        outs[0], place_row, gate_logit, full_go, count, heads, out_mine, chunks_grad[1:]
    )
    if split:
        out_others = [swapped(out_mine[0], "mp", 1)]
    else:
        out_mine, out_others = [lax.all_gather(out_turned, ("seq", "mp"), axis=0, tiled=True)], []
    attn_parts = returned(attn)
    out_w, normed_t = out_rows(words, out_mine[0], out_others, normed, devices * rows, [attn[0]])

    residual, mid_own = out_project(rank_word, layer_in[0], full_gmid, attn_parts, out_w)

    ffn_w = ffn_rows(words, ffn_all, [mid_own])
    w_gu, down_turned = ffn_w[:, : 2 * wide], ffn_w[:, 2 * wide :]
    mids = spread(mid_own)
    hiddens, gu_grads, mid_parts = ([None] * seq_count for _ in range(3))
    last_part = None
    for k in (0, 1, 3, 2):
        mid_k = mids[k] if last_part is None else pinned(mids[k], last_part)
        gate_up = dot(mid_k, w_gu)
        gate, up = gate_up[:, :wide], gate_up[:, wide:]
        hiddens[k] = (silu(gate) * up).astype(BF16)
        hidden_grad = dot(chunks_grad[k], down_turned)
        gu_grads[k] = jnp.concatenate(
            [hidden_grad * up * silu_slope(gate), hidden_grad * silu(gate)], 1
        ).astype(BF16)
        mid_parts[k] = last_part = right_product(gu_grads[k], w_gu).astype(BF16)
    mid_parts = returned(mid_parts)
    ffn_sum = RowSum(
        weight_grad(
            split, words, [(mids, gu_grads), (chunks_grad, hiddens)], wide, [last_part, mid_parts[1]]
        ),
    )
    res_grad, out_proj_grad, g_mid, attn_grads, ffn_sum.outs[-1:] = mid_back(
        rank_word, out_grad[0], residual, full_gmid, mid_parts, out_w, ffn_sum.outs[-1:]
    )
    attn_grads = returned(attn_grads)
    ffn_sum.pair()
    layer_own, *both = layer_products(hiddens, ffn_w, out_proj_grad)

    (gate_grad, o_grad, g_go), both = ungate_rows(
        dealt_rows, col_info, gate_logit, full_go, attn_grads, heads, both, []
    )
    gate_sums, *gate_outs = weight_grad(
        split, words, [([normed], [gate_grad])], val_cols, [], weights=mix
    )
    gate_sum = RowSum(gate_outs)
    gate_sum.pair()
    ffn_sum = ffn_sum.beside(gate_sum)
    both = returned([None] + both)[1:]
    proj_grad, g_conv = backward_recurrence(
        proj, conv, col_info, row_info, logit_parts, outs[1:], o_grad, heads, [ffn_sum.half]
    )
    mix_grad, mix_sums, *mix_outs = unpack(
        split, words, proj_grad, gate_grad, place_row, normed_t, mix, g_conv, full_gin, g_mid, g_go,
        gate_sums, heads, [],
    )
    mix_sum = RowSum(mix_outs)
    mix_sum.pair()
    normed_parts, _ = unproject(mix_grad, mix, count, [], [])
    normed_chunks = returned(normed_parts)
    out_sum = RowSum(
        weight_grad(split, words, [([out_proj_grad] + both, attn)], val_cols,
            [normed_parts[0], ffn_sum.parts], limit=56 * MIB,
        )
    )
    out_sum.pair()
    last_sum = mix_sum.beside(out_sum)
    ffn_total = row_sums([ffn_sum], [last_sum.half])
    in_grad = in_back(layer_in[0], res_grad, full_gin, normed_chunks, [ffn_total])
    ffn_sum.parts = ffn_total[None]
    layer_out = residual + sum(
        c.astype(F32) for c in [layer_own] + [b[count:] for b in both]
    )
    all_pieces = dealt(row_sums([ffn_sum, last_sum], [in_grad]))
    layer_out = layer_out.astype(BF16)[None]
    if split:
        g_qkv, g_gate, g_beta, g_conv, g_out, g_gu, g_down, small_sum = finish(
            all_pieces, heads, wide, half, taps
        )
        device = rank * mp_count + place_mp
        grad_go = lax.dynamic_slice_in_dim(
            small_sum[4:6].reshape(-1), device * gain_o.shape[0], gain_o.shape[0]
        )
        grad_gmid, grad_gin = lax.dynamic_slice_in_dim(
            small_sum[8:24].reshape(2, -1), device * rows, rows, 1
        )
        return (
            layer_out, in_grad[None], g_qkv, g_gate, g_beta, g_conv.T,
            grad_gin, grad_go, g_out.T, grad_gmid, g_gu, g_down.T,
        )

    def columns(first, width):
        parts = [all_pieces[j, :, first : first + width] for j in range(seq_count)]
        return jnp.concatenate(parts, 1).astype(F32)

    everywhere = ("seq", "mp")
    conv_full = jnp.zeros((taps, conv_w.shape[0] * devices), F32)
    for first, width in ((0, key_cols), (key_cols, key_cols), (2 * key_cols, val_cols)):
        conv_full = lax.dynamic_update_slice_in_dim(
            conv_full, g_conv[:taps, first : first + width], first * seq_count + rank * width, 1
        )
    grad_conv = lax.psum_scatter(conv_full.T, everywhere, scatter_dimension=0, tiled=True)
    g_gin = mix_sums[0] / full_gin[0]
    grad_gin, grad_gmid, grad_go = (
        lax.psum_scatter(g, everywhere, scatter_dimension=0, tiled=True)
        for g in (g_gin, g_mid[0], g_go[0])
    )
    first = 3 * wide + val_cols
    last = all_pieces.shape[2] - val_cols
    return (
        layer_out,
        in_grad[None],
        jnp.concatenate(
            [
                columns(first, key_cols),
                columns(first + key_cols, key_cols),
                columns(first + 2 * key_cols, val_cols),
            ],
            1,
        ),
        columns(3 * wide, val_cols),
        columns(first + channels, heads),
        grad_conv,
        grad_gin,
        grad_go,
        columns(last, val_cols).T,
        grad_gmid,
        jnp.concatenate([columns(0, half), columns(wide, half)], 1),
        columns(2 * wide, half).T,
    )


def solution(mesh):
    in_specs = (
        P("mp", "seq", None),
        P("mp", "seq", None),
        P("mp", None),
        P("mp", None),
        P("mp", "seq", None),
        P(("seq", "mp"), None),
        P(("seq", "mp"), None),
        P(("seq", "mp"), None),
        P(("seq", "mp"), None),
        P(("seq", "mp")),
        P(("seq", "mp")),
        P(None, ("seq", "mp")),
        P(("seq", "mp")),
        P(("seq", "mp"), None),
        P(None, ("seq", "mp")),
    )
    out_specs = (
        P("mp", "seq", None),
        P("mp", "seq", None),
        P(("seq", "mp"), None),
        P(("seq", "mp"), None),
        P(("seq", "mp"), None),
        P(("seq", "mp"), None),
        P(("seq", "mp")),
        P(("seq", "mp")),
        P(None, ("seq", "mp")),
        P(("seq", "mp")),
        P(("seq", "mp"), None),
        P(None, ("seq", "mp")),
    )
    return jax.shard_map(body, mesh=mesh, in_specs=in_specs, out_specs=out_specs, check_vma=False)
```
